128 devices in a mesh: seq: 16 (over z, y), head: 8 (over x, core).
Axes of the slice: x: 4, y: 4, z: 4, core: 2. Of those that a mesh axis runs over, the one named last changes fastest.
Arguments:
- tokens: bfloat16 [8192, 2048], P(('seq', 'head')), may hold values from -6 to 6
- mixer_gain: float32 [2048], replicated, may hold values from 0.5 to 1.5
- mixer_weight: bfloat16 [2048, 16, 768], P(None, 'head'), may hold values from -0.125 to 0.125
- rate_weight: bfloat16 [2048, 2, 16], P(None, None, 'head'), may hold values from -0.125 to 0.125
- conv_weight: bfloat16 [4, 16, 512], P(None, 'head'), may hold values from -3 to 3
- decay_log: float32 [16], P('head')
- decay_bias: float32 [16], P('head'), may hold values from -2 to 1
- head_gain: float32 [256], replicated, may hold values from 0.5 to 1.5
- output_weight: bfloat16 [16, 256, 2048], P('head'), may hold values from -0.1875 to 0.1875
- feed_gain: float32 [2048], replicated, may hold values from 0.5 to 1.5
- gate_up_weight: bfloat16 [2048, 2, 5504], P(None, None, 'head'), may hold values from -0.125 to 0.125
- down_weight: bfloat16 [5504, 2048], P('head'), may hold values from -0.15625 to 0.15625
- doc_starts: int32 [4], replicated, may hold values from 1 to 8191, as said below
- cotangent: bfloat16 [8192, 2048], P(('seq', 'head')), may hold values from -6 to 6
Outputs:
- layer_out: bfloat16 [8192, 2048], P(('seq', 'head'))
- grad_tokens: float32 [8192, 2048], P(('seq', 'head'))
- grad_mixer_gain: float32 [2048], replicated
- grad_mixer_weight: float32 [2048, 16, 768], P('seq', 'head')
- grad_rate_weight: float32 [2048, 2, 16], P('seq', None, 'head')
- grad_conv_weight: float32 [4, 16, 512], P(None, 'head')
- grad_decay_log: float32 [16], P('head')
- grad_decay_bias: float32 [16], P('head')
- grad_head_gain: float32 [256], replicated
- grad_output_weight: float32 [16, 256, 2048], P('head', None, 'seq')
- grad_feed_gain: float32 [2048], replicated
- grad_gate_up_weight: float32 [2048, 2, 5504], P('seq', None, 'head')
- grad_down_weight: float32 [5504, 2048], P('head', 'seq')
The draws below stay inside these ranges and needn't reach their ends.
Inputs may be any that keep to these rules, and one draw needn't show every extreme that they name: `doc_starts`: 4 increasing positions at which a new document begins: the first two lie within the first 512 positions, the last two within the last 512 positions.
All inputs are finite; a program needn't handle non-finite values.
Results may differ from the reference program's by a relative error of at most 0.022.
The reference program's roundings to bfloat16 on the way count: a program that leaves them out, or rounds other values in their place, can miss the bound.
Values may be sent and summed in bfloat16 or wider, within the bound.
A program may use at most 192 MiB of HBM per device.

```python
import jax
import jax.numpy as jnp
from jax import lax

D = 2048
HEADS = 16
DK = 128
DV = 256
FF = 5504
KCONV = 4
GROUP = 64
NB = 4
TOK_DEV = 512
TOKENS = 8192
MIXW = 768
CONVW = 512


def draw_decay_log(key, part):
    key = jax.random.fold_in(key, 5)
    spread = jax.random.uniform(key, (HEADS,), jnp.float32)
    return jnp.log(0.3 / TOKENS) + spread * (jnp.log(0.05) - jnp.log(0.3 / TOKENS))


def draw_doc_starts(key, part):
    key = jax.random.fold_in(key, 11)
    half_dev = TOK_DEV // 2
    lowest = jnp.array([1, half_dev, TOKENS - TOK_DEV, TOKENS - half_dev], jnp.int32)
    highest_end = jnp.array([half_dev, TOK_DEV, TOKENS - half_dev, TOKENS], jnp.int32)
    return jax.random.randint(key, (NB,), lowest, highest_end, dtype=jnp.int32)


def levels(rng, shape, split, low, largest):
    loudness, own = 1.0, jax.random.fold_in(rng, 6)
    for position, blocks in split:
        draws = jnp.exp(jax.random.uniform(jax.random.fold_in(own, position), (blocks,), jnp.float32, low / len(split), largest / len(split)))
        loudness = loudness * jnp.repeat(draws, shape[position] // blocks).reshape([-1 if axis == position else 1 for axis in range(len(shape))])
    return loudness


def gaussian(own_key, extent, width, limit, split=(), held_as=jnp.bfloat16):
    factor_of = levels(own_key, extent, split, -0.22, 0.18) if split else 1.0
    values = jax.random.normal(own_key, extent, jnp.float32) * width * factor_of
    return jnp.minimum(jnp.maximum(values, -limit), limit).astype(held_as)


def setup_inputs(seed: int = 0) -> dict:
    splits = jax.random.split(jax.random.key(seed), 15)
    return {
        "tokens": gaussian(splits[0], (TOKENS, D), 1.0, 6.0, ((0, 128),)),
        "mixer_gain": jnp.clip(1.0 + 0.1 * jax.random.normal(splits[1], (D,), jnp.float32), 0.5, 1.5),
        "mixer_weight": gaussian(splits[2], (D, HEADS, MIXW), D ** -0.5, 0.125, ((1, 8),)),
        "rate_weight": gaussian(splits[3], (D, 2, HEADS), D ** -0.5, 0.125, ((2, 8),)),
        "conv_weight": gaussian(splits[4], (KCONV, HEADS, CONVW), KCONV ** -0.5, 3.0, ((1, 8),)),
        "decay_log": draw_decay_log(jax.random.fold_in(splits[14], 71), 0),
        "decay_bias": jnp.clip(-2.0 + 3.0 * jax.random.uniform(splits[6], (HEADS,), jnp.float32) ** levels(splits[6], (HEADS,), ((0, 8),), -0.2, 0.2), -2.0, 1.0),
        "head_gain": jnp.clip(1.0 + 0.1 * jax.random.normal(splits[7], (DV,), jnp.float32), 0.5, 1.5),
        "output_weight": gaussian(splits[8], (HEADS, DV, D), (HEADS * DV // 4) ** -0.5, 0.1875, ((0, 8),)),
        "feed_gain": jnp.clip(1.0 + 0.1 * jax.random.normal(splits[9], (D,), jnp.float32), 0.5, 1.5),
        "gate_up_weight": gaussian(splits[10], (D, 2, FF), D ** -0.5, 0.125, ((2, 8),)),
        "down_weight": gaussian(splits[11], (FF, D), (FF // 4) ** -0.5, 0.15625, ((0, 8),)),
        "doc_starts": draw_doc_starts(jax.random.fold_in(splits[14], 71), 0),
        "cotangent": gaussian(splits[13], (TOKENS, D), 1.0, 6.0, ((0, 128),)),
    }


highest = lax.Precision.HIGHEST

@jax.custom_vjp
def low(v):
    return lax.optimization_barrier(v.astype(jnp.bfloat16)).astype(jnp.float32)

@jax.custom_vjp
def low_back(v):
    return v

def low_keep(v):
    return (low(v), None)

def low_pass(kept, grad):
    return (grad,)

def back_keep(v):
    return (v, None)

def back_low(kept, grad):
    return (low(grad),)
low.defvjp(low_keep, low_pass)
low_back.defvjp(back_keep, back_low)

def rms_scale(values, gain):
    return values * lax.rsqrt(lax.optimization_barrier(jnp.mean(values * values, axis=-1, keepdims=True)) + 1e-05) * gain

def doc_index(doc_starts, positions):
    inside = lax.optimization_barrier(jnp.sum((doc_starts[None, :] <= positions[:, None]).astype(jnp.int32), axis=1)).astype(jnp.int32)
    return jnp.where(positions < 0, -1, inside).astype(jnp.int32)

def mixer_inputs(padded, doc_pad, rate_proj, conv_weight, decay_log, decay_bias):
    length = rate_proj.shape[0]
    conv_sum = jnp.zeros((length,) + padded.shape[1:], padded.dtype)
    for tap_index in range(KCONV):
        window = padded[tap_index:tap_index + length]
        valid = (doc_pad[tap_index:tap_index + length] == doc_pad[KCONV - 1:]).astype(padded.dtype)
        conv_sum = conv_sum + conv_weight[tap_index] * window * valid[:, None, None]
    active = jax.nn.silu(conv_sum)
    query_vecs = active[..., :DK]
    key_vecs = active[..., DK:2 * DK]
    val_vecs = active[..., 2 * DK:]
    query_vecs = query_vecs * lax.rsqrt(lax.optimization_barrier(jnp.sum(query_vecs * query_vecs, axis=-1, keepdims=True)) + 1e-06) * DK ** (-0.5)
    key_vecs = key_vecs * lax.rsqrt(lax.optimization_barrier(jnp.sum(key_vecs * key_vecs, axis=-1, keepdims=True)) + 1e-06)
    strength = jax.nn.sigmoid(rate_proj[:, 1])
    log_decay = -jnp.exp(decay_log) * jax.nn.softplus(rate_proj[:, 0] + decay_bias)
    return (query_vecs, key_vecs, val_vecs, strength, log_decay)

def solve_lower(system, rhs_vals):
    return jax.scipy.linalg.solve_triangular(system, rhs_vals, lower=True, unit_diagonal=True)

def group_step(carried, query_vecs, key_vecs, val_vecs, strength, log_decay, doc_part, prev_doc):
    queries = jnp.swapaxes(query_vecs, 0, 1)
    keyset = jnp.swapaxes(key_vecs, 0, 1)
    valset = jnp.swapaxes(val_vecs, 0, 1)
    beta_head = strength.T
    cumulative = jnp.cumsum(log_decay.T, axis=1)
    length = doc_part.shape[0]
    row_pos = lax.broadcasted_iota(jnp.int32, (length, length), 0)
    col_pos = lax.broadcasted_iota(jnp.int32, (length, length), 1)
    same_doc = (doc_part[:, None] == doc_part[None, :]) & (col_pos <= row_pos)
    spread = jnp.where(same_doc[None], cumulative[:, :, None] - cumulative[:, None, :], 0.0)
    decay_mat = jnp.where(same_doc[None], jnp.exp(spread), 0.0)
    carry_in = jnp.where((doc_part == prev_doc)[None, :], jnp.exp(cumulative), 0.0)
    key_gram = jnp.einsum('hcd,hsd->hcs', keyset, keyset, precision=highest)
    lower_part = jnp.where((col_pos < row_pos)[None], beta_head[:, :, None] * decay_mat * key_gram, 0.0)
    system = lower_part + jnp.eye(length, dtype=lower_part.dtype)
    rhs_vals = beta_head[:, :, None] * valset - (beta_head * carry_in)[:, :, None] * jnp.einsum('hcd,hvd->hcv', keyset, carried, precision=highest)
    fresh = jax.vmap(solve_lower)(system, rhs_vals)
    scores = decay_mat * jnp.einsum('hcd,hsd->hcs', queries, keyset, precision=highest)
    outputs = carry_in[:, :, None] * jnp.einsum('hcd,hvd->hcv', queries, carried, precision=highest) + jnp.einsum('hcs,hsv->hcv', scores, fresh, precision=highest)
    weighted = decay_mat[:, -1, :, None] * keyset
    updated = carry_in[:, -1, None, None] * carried + jnp.einsum('hsv,hsd->hvd', fresh, weighted, precision=highest)
    return (updated, jnp.swapaxes(outputs, 0, 1))

def run_groups(start_state, query_vecs, key_vecs, val_vecs, strength, log_decay, doc_part, prev_docs):
    pieces = tuple((member.reshape((-1, GROUP) + member.shape[1:]) for member in (query_vecs, key_vecs, val_vecs, strength, log_decay, doc_part))) + (prev_docs,)

    def advance(carried, piece):
        return group_step(carried, *piece)
    final, outputs = lax.scan(jax.checkpoint(advance), start_state, pieces)
    return (final, outputs.reshape((-1,) + outputs.shape[2:]))

def forward(tokens, mixer_gain, mixer_weight, rate_weight, conv_weight, decay_log, decay_bias, head_gain, output_weight, feed_gain, gate_up_weight, down_weight, doc_starts):
    conv_width = 2 * DK + DV
    positions = jnp.arange(-(KCONV - 1), TOKENS, dtype=jnp.int32)
    doc_pad = doc_index(doc_starts, positions)
    prev_docs = doc_pad[KCONV - 2:KCONV - 2 + TOKENS:GROUP]
    normed = low(rms_scale(tokens, mixer_gain))
    projected = low_back(jnp.dot(normed, mixer_weight.reshape(D, HEADS * MIXW), precision=highest)).reshape(TOKENS, HEADS, MIXW)
    rate_proj = low_back(jnp.einsum('td,dgh->tgh', normed, rate_weight, precision=highest))
    pre_conv = low(projected[..., :conv_width])
    gate_out = projected[..., conv_width:]
    padded = jnp.concatenate([jnp.zeros((KCONV - 1, HEADS, conv_width), pre_conv.dtype), pre_conv])
    query_vecs, key_vecs, val_vecs, strength, log_decay = mixer_inputs(padded, doc_pad, rate_proj, conv_weight, decay_log, decay_bias)
    start_state = jnp.zeros((HEADS, DV, DK), pre_conv.dtype)
    final, head_out = run_groups(start_state, query_vecs, key_vecs, val_vecs, strength, log_decay, doc_pad[KCONV - 1:], prev_docs)
    gated = low(rms_scale(head_out, head_gain) * jax.nn.silu(gate_out))
    mixed = low_back(jnp.dot(gated.reshape(TOKENS, HEADS * DV), output_weight.reshape(HEADS * DV, D), precision=highest))
    hidden = tokens + mixed
    normed_two = low(rms_scale(hidden, feed_gain))
    gate_up = low_back(jnp.einsum('td,dgf->tgf', normed_two, gate_up_weight, precision=highest))
    middle = low(jax.nn.silu(gate_up[:, 0]) * gate_up[:, 1])
    return hidden + jnp.dot(middle, down_weight, precision=highest)

def reference(tokens, mixer_gain, mixer_weight, rate_weight, conv_weight, decay_log, decay_bias, head_gain, output_weight, feed_gain, gate_up_weight, down_weight, doc_starts, cotangent):
    floats = tuple((member.astype(jnp.float32) for member in (tokens, mixer_gain, mixer_weight, rate_weight, conv_weight, decay_log, decay_bias, head_gain, output_weight, feed_gain, gate_up_weight, down_weight)))

    def closed(*params):
        return forward(*params, doc_starts)
    layer_out, backward = jax.vjp(closed, *floats)
    gradients = backward(cotangent.astype(jnp.float32))
    return (layer_out.astype(jnp.bfloat16), gradients[0], gradients[1], gradients[2], gradients[3], gradients[4], gradients[5], gradients[6], gradients[7], gradients[8], gradients[9], gradients[10], gradients[11])
```

```python
import functools

import jax
import jax.numpy as jnp
from jax import lax
from jax.experimental import pallas as pl
from jax.experimental.pallas import tpu as pltpu
from jax.sharding import PartitionSpec as P

D = 2048
DK = 128
DV = 256
KCONV = 4
MIXW = 768
CONVW = 512
NB = 4
BLK = 256
PAD = 8
F32 = jnp.float32
BF16 = jnp.bfloat16

VMEM = pl.BlockSpec(memory_space=pltpu.VMEM)
SMEM = pl.BlockSpec(memory_space=pltpu.SMEM)


def dot(a, b, form="nn"):
    dims = {"nn": ((1,), (0,)), "nt": ((1,), (1,)), "tn": ((0,), (0,))}[form]
    return lax.dot_general(a.astype(BF16), b.astype(BF16), (dims, ((), ())), preferred_element_type=F32)


def halves(a):
    hi = a.astype(BF16)
    return hi, (a - hi.astype(F32)).astype(BF16)


def dot3(a, b, form="nn"):
    ah, al = halves(a)
    bh, bl = halves(b)
    return dot(ah, bh, form) + (dot(ah, bl, form) + dot(al, bh, form))


def dot_exact_left(a, b, form="nn"):
    b1, rest = halves(b)
    rest = b - b1.astype(F32)
    b2 = rest.astype(BF16)
    b3 = (rest - b2.astype(F32)).astype(BF16)
    return dot(a, b1, form) + (dot(a, b2, form) + dot(a, b3, form))


def iota(shape, axis):
    return lax.broadcasted_iota(jnp.int32, shape, axis)


def doc_of(info, pos):
    count = jnp.zeros(pos.shape, jnp.int32)
    for i in range(NB):
        count = count + jnp.where(pos >= info[i], 1, 0)
    return jnp.where(pos < 0, -1, count)


def sigmoid(v):
    return 1.0 / (1.0 + jnp.exp(-v))


def softplus(v):
    return jnp.maximum(v, 0.0) + jnp.log1p(jnp.exp(-jnp.abs(v)))


def unit_lower_inverse(low):
    n = low.shape[0]
    row, col = iota((n, n), 0), iota((n, n), 1)
    eye = jnp.where(row == col, 1.0, 0.0)

    def same(b):
        return row // b == col // b

    x = jnp.where(same(8), -low, 0.0)
    inv = eye + x
    x = dot3(x, x)
    inv = inv + dot3(inv, x)
    x = dot3(x, x)
    inv = inv + dot3(inv, x)
    b = 8
    while b < n:
        off = jnp.where(same(2 * b) & jnp.logical_not(same(b)), low, 0.0)
        inv = inv - dot3(inv, dot3(off, inv))
        b *= 2
    return inv


def valid_column(info, rows, back):
    pos = info[NB] + iota((rows, 1), 0)
    return jnp.where(doc_of(info, pos) == doc_of(info, pos - back), 1.0, 0.0)


def vectors(conv):
    act = conv * sigmoid(conv)
    qa, ka, va = act[:, :DK], act[:, DK : 2 * DK], act[:, 2 * DK :]
    rq = lax.rsqrt(jnp.sum(qa * qa, axis=1, keepdims=True) + 1e-06)
    rk = lax.rsqrt(jnp.sum(ka * ka, axis=1, keepdims=True) + 1e-06)
    return qa, ka, va, rq, rk


def rates(rate_ref, dlog_ref, dbias_ref):
    heads = dlog_ref.shape[1]
    pre = rate_ref[:, :heads] + dbias_ref[...]
    log_decay = -jnp.exp(dlog_ref[...]) * softplus(pre)
    return sigmoid(rate_ref[:, heads:]), log_decay, pre


def block_masks(info, c):
    row, col = iota((BLK, BLK), 0), iota((BLK, BLK), 1)
    base = info[NB] + c * BLK
    docs_r, docs_c = doc_of(info, base + row), doc_of(info, base + col)
    keep = (docs_r == docs_c) & (col <= row)
    column = doc_of(info, base + iota((BLK, 1), 0))
    first = jnp.where(column == doc_of(info, base - 1 + iota((BLK, 1), 0) * 0), 1.0, 0.0)
    last = jnp.where(column == doc_of(info, base + BLK - 1 + iota((BLK, 1), 0) * 0), 1.0, 0.0)
    tri = jnp.where(col <= row, 1.0, 0.0)
    strict = jnp.where(col < row, 1.0, 0.0)
    return keep, first, last, tri, strict


def decays(g, first, last, tri):
    cum = dot_exact_left(tri, jnp.broadcast_to(g, (BLK, DK)))[:, :1]
    carry = first * jnp.exp(cum)
    to_end = last * jnp.exp(cum[BLK - 1 :, :] - cum)
    return carry, to_end


def fwd_prep(info, proj, halo, rate, convw, dlog, dbias, conv_o, dec_o, inv_o, wu_o, qe_o, ol_o, step_o, ab_o, xpad):
    rows = proj.shape[0]
    heads = dlog.shape[1]
    blocks = rows // BLK
    strength, log_decay, _ = rates(rate, dlog, dbias)
    valid = [valid_column(info, rows, KCONV - 1 - j) for j in range(KCONV)]
    for h in range(heads):
        src, dst = pl.ds(h * MIXW, CONVW), pl.ds(h * CONVW, CONVW)
        xpad[:PAD, :] = halo[:, dst]
        xpad[PAD:, :] = proj[:, src].astype(BF16).astype(F32)
        conv = jnp.zeros((rows, CONVW), F32)
        for j in range(KCONV):
            lo = PAD - (KCONV - 1) + j
            conv = conv + convw[j : j + 1, dst].astype(F32) * xpad[lo : lo + rows, :] * valid[j]
        conv_o[:, dst] = conv
    for c in range(blocks):
        keep, first, last, tri, strict = block_masks(info, c)
        here = pl.ds(c * BLK, BLK)
        for h in range(heads):
            qa, ka, va, rq, rk = vectors(conv_o[here, pl.ds(h * CONVW, CONVW)])
            q, k = qa * (rq * DK**-0.5), ka * rk
            beta = strength[c * BLK : (c + 1) * BLK, h : h + 1]
            g = log_decay[c * BLK : (c + 1) * BLK, h : h + 1]
            spread = dot_exact_left(tri, g * strict)
            dec = jnp.where(keep, jnp.exp(jnp.where(keep, spread, 0.0)), 0.0)
            carry, to_end = decays(g, first, last, tri)
            low = strict * (beta * dec * dot(k, k, "nt"))
            inv = unit_lower_inverse(low)
            u = h * blocks + c
            dec_o[u] = dec
            inv_o[u] = inv.astype(BF16)
            rhs = jnp.concatenate([(beta * carry) * k, beta * va], axis=1)
            wu = dot(inv, rhs)
            wu_o[u] = wu
            out = dot(dec * dot(q, k, "nt"), wu)
            qe_o[here, pl.ds(h * DK, DK)] = carry * q - out[:, :DK]
            ol_o[here, pl.ds(h * DV, DV)] = out[:, DK:]
            step = dot(wu, to_end * k, "tn")
            eye = jnp.where(iota((DK, DK), 0) == iota((DK, DK), 1), 1.0, 0.0)
            step_o[u, :DK] = carry[BLK - 1 :, :] * eye - step[:DK]
            step_o[u, DK:] = step[DK:]
    for h in range(heads):
        ab = step_o[h * blocks]
        for c in range(1, blocks):
            nxt = step_o[h * blocks + c]
            ab = dot3(ab, nxt[:DK])
            ab_o_tail = nxt[DK:]
            ab = jnp.concatenate([ab[:DK], ab[DK:] + ab_o_tail], axis=0)
        ab_o[h] = ab.astype(ab_o.dtype)


def fwd_out(info, all_ab, step, qe, ol, proj, gain, states_o, head_o, gated_o):
    rows = qe.shape[0]
    heads = all_ab.shape[1]
    blocks = rows // BLK
    me = info[NB + 1]

    def chain(j, held):
        return tuple(
            dot_left2(held[h], all_ab[j, h, :DK, :]) + all_ab[j, h, DK:, :].astype(F32) for h in range(heads)
        )

    start = lax.fori_loop(0, me, chain, tuple(jnp.zeros((DV, DK), F32) for _ in range(heads)))
    for h in range(heads):
        state = start[h]
        for c in range(blocks):
            u = h * blocks + c
            here = pl.ds(c * BLK, BLK)
            states_o[u] = state
            out = ol[here, pl.ds(h * DV, DV)] + dot(qe[here, pl.ds(h * DK, DK)], state, "nt")
            head_o[here, pl.ds(h * DV, DV)] = out
            gate = proj[here, pl.ds(h * MIXW + CONVW, DV)]
            scale = lax.rsqrt(jnp.mean(out * out, axis=1, keepdims=True) + 1e-05)
            gated_o[here, pl.ds(h * DV, DV)] = (out * scale * gain[...] * (gate * sigmoid(gate))).astype(BF16)
            if c + 1 < blocks:
                state = dot3(state, step[u, :DK, :]) + step[u, DK:, :]


def dot_left2(a, b, form="nn"):
    ah, al = halves(a)
    return dot(ah, b, form) + dot(al, b, form)


def bwd_head(d_gated, head_out, proj, gain, qe, step, d_out_o, d_gate_o, d_gain_o, y_o, inc_o):
    rows = qe.shape[0]
    blocks = rows // BLK
    heads = qe.shape[1] // DK
    total = jnp.zeros((1, DV), F32)
    for h in range(heads):
        cols = pl.ds(h * DV, DV)
        for c in range(blocks):
            here = pl.ds(c * BLK, BLK)
            dg, out = d_gated[here, cols], head_out[here, cols]
            gate = proj[here, pl.ds(h * MIXW + CONVW, DV)]
            s = sigmoid(gate)
            silu = gate * s
            scale = lax.rsqrt(jnp.mean(out * out, axis=1, keepdims=True) + 1e-05)
            n = out * scale
            dn = dg * n
            d_gate_o[here, cols] = (dn * gain[...] * (s * (1.0 + gate * (1.0 - s)))).astype(BF16)
            total = total + jnp.sum(dn * silu, axis=0, keepdims=True)
            f = dg * gain[...] * silu
            d_out = scale * f - out * (scale * scale * scale) * jnp.mean(f * out, axis=1, keepdims=True)
            d_out_o[here, cols] = d_out
            y_o[h * blocks + c] = dot(d_out, qe[here, pl.ds(h * DK, DK)], "tn")
        inc = y_o[h * blocks + blocks - 1]
        for c in range(blocks - 2, -1, -1):
            inc = y_o[h * blocks + c] + dot3(inc, step[h * blocks + c, :DK, :], "nt")
        inc_o[h] = inc.astype(inc_o.dtype)
    d_gain_o[...] = total


def bwd_mix(
    info, all_ab, all_inc, conv, dec, inv, wu, states, step, y, d_out, rate, proj, halo, convw, dlog, dbias,
    d_pre_o, d_edge_o, d_rate_o, d_convw_o, d_decay_o, xpad, dpad, dsend, cols_s
):
    rows = d_out.shape[0]
    heads = all_ab.shape[1]
    blocks = rows // BLK
    me = info[NB + 1]
    last_dev = all_ab.shape[0] - 1
    strength, log_decay, pre = rates(rate, dlog, dbias)
    valid = [valid_column(info, rows, KCONV - 1 - j) for j in range(KCONV)]

    def chain(i, held):
        j = last_dev - i
        return tuple(
            dot_left2(held[h], all_ab[j, h, :DK, :], "nt") + all_inc[j, h].astype(F32) for h in range(heads)
        )

    later = lax.fori_loop(0, last_dev - me, chain, tuple(jnp.zeros((DV, DK), F32) for _ in range(heads)))
    for h in range(heads):
        grad = later[h]
        for c in range(blocks - 1, -1, -1):
            u = h * blocks + c
            dsend[u] = grad
            if c:
                grad = dot3(grad, step[u, :DK, :], "nt") + y[u]
    for c in range(blocks):
        keep, first, last, tri, strict = block_masks(info, c)
        here = pl.ds(c * BLK, BLK)
        for h in range(heads):
            u = h * blocks + c
            cv = conv[here, pl.ds(h * CONVW, CONVW)]
            sg = sigmoid(cv)
            qa, ka, va, rq, rk = vectors(cv)
            rqs = rq * DK**-0.5
            q, k = qa * rqs, ka * rk
            beta = strength[c * BLK : (c + 1) * BLK, h : h + 1]
            g = log_decay[c * BLK : (c + 1) * BLK, h : h + 1]
            carry, to_end = decays(g, first, last, tri)
            dm = dec[u]
            sc = dm * dot(q, k, "nt")
            gm = dm * dot(k, k, "nt") * strict
            state, d_end = states[u], dsend[u]
            do = d_out[here, pl.ds(h * DV, DV)]
            ks = dot(k, state, "nt")
            qs = dot(q, state, "nt")
            fresh = wu[u, :, DK:] - dot(wu[u, :, :DK], state, "nt")
            kd = to_end * k
            d_fresh = dot(sc, do, "tn") + dot(kd, d_end, "nt")
            d_rhs = dot(inv[u], d_fresh, "tn")
            d_low = -dot(d_rhs, fresh, "nt")
            d_sc = dot(do, fresh, "nt")
            d_val = beta * d_rhs
            ebar = d_low * gm
            d_beta = jnp.sum(d_rhs * (va - carry * ks), axis=1, keepdims=True) + jnp.sum(ebar, axis=1, keepdims=True)
            e = d_sc * sc + beta * ebar
            d_scd = d_sc * dm
            d_gm = (beta * d_low) * (dm * strict)
            d_kd = dot(fresh, d_end)
            d_q = dot(d_scd, k) + carry * dot(do, state)
            d_k = (
                dot(d_scd, q, "tn")
                - (beta * carry) * dot(d_rhs, state)
                + to_end * d_kd
                + dot(d_gm, k)
                + dot(d_gm, k, "tn")
            )
            hcol = carry * jnp.sum(do * qs - beta * d_rhs * ks, axis=1, keepdims=True)
            fcol = jnp.sum(kd * d_kd, axis=1, keepdims=True)
            tail = carry[BLK - 1 :, :] * jnp.sum(
                jnp.sum(state * d_end, axis=1, keepdims=True), axis=0, keepdims=True
            )
            lane = iota((BLK, DK), 1)
            d_g = (
                jnp.sum(dot_exact_left(tri, e, "tn") * strict, axis=1, keepdims=True)
                + dot_exact_left(tri, jnp.where(lane == 0, hcol, 0.0), "tn")[:, :1]
                + dot_exact_left(strict, jnp.where(lane == 0, fcol, 0.0))[:, :1]
                + tail
            )
            cols_s[here, h : h + 1] = d_g
            cols_s[here, heads + h : heads + h + 1] = d_beta
            d_qa = rqs * d_q - qa * (rqs * rq * rq * jnp.sum(d_q * qa, axis=1, keepdims=True))
            d_ka = rk * d_k - ka * (rk * rk * rk * jnp.sum(d_k * ka, axis=1, keepdims=True))
            d_act = jnp.concatenate([d_qa, d_ka, d_val], axis=1)
            d_pre_o[here, pl.ds(h * CONVW, CONVW)] = d_act * (sg * (1.0 + cv * (1.0 - sg)))
    d_g, d_beta = cols_s[:, :heads], cols_s[:, heads : 2 * heads]
    d_bias = -d_g * jnp.exp(dlog[...]) * sigmoid(pre)
    d_rate_o[:, :heads] = d_bias
    d_rate_o[:, heads:] = d_beta * strength * (1.0 - strength)
    d_decay_o[:, :heads] = jnp.sum(d_g * log_decay, axis=0, keepdims=True)
    d_decay_o[:, heads:] = jnp.sum(d_bias, axis=0, keepdims=True)
    for h in range(heads):
        src, dst = pl.ds(h * MIXW, CONVW), pl.ds(h * CONVW, CONVW)
        xpad[:PAD, :] = halo[:, dst]
        xpad[PAD:, :] = proj[:, src].astype(BF16).astype(F32)
        dpad[...] = jnp.zeros_like(dpad)
        d_conv = d_pre_o[:, dst]
        for j in range(KCONV):
            lo = PAD - (KCONV - 1) + j
            masked = d_conv * valid[j]
            d_convw_o[j : j + 1, dst] = jnp.sum(masked * xpad[lo : lo + rows, :], axis=0, keepdims=True)
            dpad[lo : lo + rows, :] += convw[j : j + 1, dst].astype(F32) * masked
        d_edge_o[:, dst] = dpad[:PAD, :]
        d_pre_o[:, dst] = dpad[PAD:, :]


def call(kernel, outs, scratch, limit, *args, flops=2_000_000_000, nbytes=16_000_000):
    def spec(a):
        return SMEM if a.dtype == jnp.int32 else VMEM

    return pl.pallas_call(
        kernel,
        out_shape=outs,
        in_specs=[spec(a) for a in args],
        out_specs=[VMEM for _ in outs],
        scratch_shapes=scratch,
        compiler_params=pltpu.CompilerParams(vmem_limit_bytes=limit << 20),
        cost_estimate=pl.CostEstimate(flops=flops, bytes_accessed=nbytes, transcendentals=0),
    )(*args)


def sds(shape, dtype=F32):
    return jax.ShapeDtypeStruct(shape, dtype)


def passed_along(shard, axis, by):
    length = lax.axis_size(axis)
    pairs = [(i, i + by) for i in range(length) if 0 <= i + by < length]
    return lax.ppermute(shard, axis, pairs)


def rms_scale(values, gain):
    return values * lax.rsqrt(jnp.mean(values * values, axis=-1, keepdims=True) + 1e-05) * gain


def swiglu(gate_up):
    return jax.nn.silu(gate_up[:, 0]) * gate_up[:, 1]


def local(
    tokens, mixer_gain, mixer_weight, rate_weight, conv_weight, decay_log, decay_bias, head_gain,
    output_weight, feed_gain, gate_up_weight, down_weight, doc_starts, cotangent,
):
    resid = tokens.astype(F32)
    norm_one, norm_one_back = jax.vjp(rms_scale, resid, mixer_gain)
    normed = norm_one.astype(BF16)
    gathered = lax.all_gather(normed, "head", axis=0, tiled=True)
    rows = gathered.shape[0]
    heads = mixer_weight.shape[1]
    blocks = rows // BLK
    units = heads * blocks
    seq = lax.axis_size("seq")
    mixer_flat = mixer_weight.reshape(D, heads * MIXW)
    projected = jnp.dot(gathered, mixer_flat, preferred_element_type=F32)
    rate_proj = jnp.einsum("td,dgh->tgh", gathered, rate_weight, preferred_element_type=F32).reshape(rows, 2 * heads)
    rim = projected[rows - PAD :].reshape(PAD, heads, MIXW)[:, :, :CONVW].reshape(PAD, heads * CONVW).astype(BF16)
    halo = passed_along(rim, "seq", 1).astype(F32)
    convw = conv_weight.reshape(KCONV, heads * CONVW)
    info = jnp.concatenate(
        [doc_starts, jnp.stack([lax.axis_index("seq") * rows, lax.axis_index("seq")]).astype(jnp.int32)]
    )
    dlog, dbias = decay_log.reshape(1, heads), decay_bias.reshape(1, heads)
    gain = head_gain.reshape(1, DV)

    conv, dec, inv, wu, qe, ol, step, ab = call(
        fwd_prep,
        [
            sds((rows, heads * CONVW)), sds((units, BLK, BLK)), sds((units, BLK, BLK), BF16),
            sds((units, BLK, DK + DV)), sds((rows, heads * DK)), sds((rows, heads * DV)),
            sds((units, DK + DV, DK)), sds((heads, DK + DV, DK), BF16),
        ],
        [pltpu.VMEM((PAD + rows, CONVW), F32)],
        56, info, projected, halo, rate_proj, convw, dlog, dbias,
    )
    all_ab = lax.all_gather(ab, "seq", axis=0)
    states, head_out, gated = call(
        fwd_out,
        [sds((units, DV, DK)), sds((rows, heads * DV)), sds((rows, heads * DV), BF16)],
        [], 48, info, all_ab, step, qe, ol, projected, gain,
    )
    out_flat = output_weight.reshape(heads * DV, D)
    mixed = lax.psum_scatter(
        jnp.dot(gated, out_flat, preferred_element_type=F32), "head", scatter_dimension=0, tiled=True
    )
    hidden = resid + mixed
    norm_two, norm_two_back = jax.vjp(rms_scale, hidden, feed_gain)
    normed_two = norm_two.astype(BF16)
    gathered_two = lax.all_gather(normed_two, "head", axis=0, tiled=True)
    cot_rows = lax.all_gather(cotangent, "head", axis=0, tiled=True)
    gate_up = jnp.einsum("td,dgf->tgf", gathered_two, gate_up_weight, preferred_element_type=F32)
    middle, swiglu_back = jax.vjp(swiglu, gate_up)
    middle_low = middle.astype(BF16)
    feed_sum = lax.psum_scatter(
        jnp.dot(middle_low, down_weight, preferred_element_type=F32).astype(BF16),
        "head", scatter_dimension=0, tiled=True,
    ).astype(F32)
    layer_out = (hidden + feed_sum).astype(BF16)
    d_middle = jnp.einsum("td,fd->tf", cot_rows, down_weight, preferred_element_type=F32)
    grad_down = jnp.einsum("tf,td->fd", middle_low, cot_rows, preferred_element_type=F32)
    d_gate_up = swiglu_back(d_middle)[0].astype(BF16)
    grad_gate_up = jnp.einsum("td,tgf->dgf", gathered_two, d_gate_up, preferred_element_type=F32)
    d_normed_two = lax.psum_scatter(
        jnp.einsum("tgf,dgf->td", d_gate_up, gate_up_weight, preferred_element_type=F32).astype(BF16),
        "head", scatter_dimension=0, tiled=True,
    ).astype(F32)
    d_hidden_norm, grad_feed_gain = norm_two_back(d_normed_two)
    d_hidden = cotangent.astype(F32) + d_hidden_norm
    d_mixed = lax.all_gather(d_hidden.astype(BF16), "head", axis=0, tiled=True)
    d_gated = jnp.einsum("td,vd->tv", d_mixed, out_flat, preferred_element_type=F32)
    grad_output = jnp.einsum("tv,td->vd", gated, d_mixed, preferred_element_type=F32)
    d_out, d_gate, grad_head_gain, y, inc = call(
        bwd_head,
        [
            sds((rows, heads * DV)), sds((rows, heads * DV), BF16), sds((1, DV)),
            sds((units, DV, DK)), sds((heads, DV, DK), BF16),
        ],
        [], 48, d_gated, head_out, projected, gain, qe, step,
    )
    all_inc = lax.all_gather(inc, "seq", axis=0)
    d_pre, d_edge, d_rate, d_convw, d_decay = call(
        bwd_mix,
        [
            sds((rows, heads * CONVW)), sds((PAD, heads * CONVW)), sds((rows, 2 * heads)),
            sds((KCONV, heads * CONVW)), sds((1, 2 * heads)),
        ],
        [
            pltpu.VMEM((PAD + rows, CONVW), F32), pltpu.VMEM((PAD + rows, CONVW), F32),
            pltpu.VMEM((units, DV, DK), F32), pltpu.VMEM((rows, DK), F32),
        ],
        60, info, all_ab, all_inc, conv, dec, inv, wu, states, step, y, d_out, rate_proj, projected, halo, convw,
        dlog, dbias,
    )
    returned = passed_along(d_edge, "seq", -1)
    d_pre = d_pre.at[rows - PAD :].add(returned).reshape(rows, heads, CONVW)
    d_projected = jnp.concatenate([d_pre.astype(BF16), d_gate.reshape(rows, heads, DV)], axis=2).reshape(
        rows, heads * MIXW
    )
    d_rate_low = d_rate.astype(BF16)
    grad_mixer = jnp.einsum("td,tw->dw", gathered, d_projected, preferred_element_type=F32)
    grad_rate = jnp.einsum("td,tg->dg", gathered, d_rate_low, preferred_element_type=F32)
    d_normed = lax.psum_scatter(
        (
            jnp.einsum("tw,dw->td", d_projected, mixer_flat, preferred_element_type=F32)
            + jnp.einsum("tg,dg->td", d_rate_low, rate_weight.reshape(D, 2 * heads), preferred_element_type=F32)
        ).astype(BF16),
        "head", scatter_dimension=0, tiled=True,
    ).astype(F32)
    d_resid, grad_mixer_gain = norm_one_back(d_normed)
    grad_tokens = d_hidden + d_resid

    def over_seq(grad, dim):
        return lax.psum_scatter(grad.astype(BF16), "seq", scatter_dimension=dim, tiled=True).astype(F32)

    grad_mixer = over_seq(grad_mixer, 0).reshape(D // seq, heads, MIXW)
    grad_rate = over_seq(grad_rate, 0).reshape(D // seq, 2, heads)
    grad_output = over_seq(grad_output, 1).reshape(heads, DV, D // seq)
    grad_gate_up = over_seq(grad_gate_up, 0)
    grad_down = over_seq(grad_down, 1)
    d_convw, d_decay = lax.psum((d_convw, d_decay), "seq")
    grad_conv = d_convw.reshape(KCONV, heads, CONVW)
    grad_decay_log, grad_decay_bias = d_decay[0, :heads], d_decay[0, heads:]
    grad_mixer_gain, grad_feed_gain, grad_head_gain = lax.psum(
        (grad_mixer_gain, grad_feed_gain, grad_head_gain[0]), ("seq", "head")
    )
    return (
        layer_out, grad_tokens, grad_mixer_gain, grad_mixer, grad_rate, grad_conv, grad_decay_log, grad_decay_bias,
        grad_head_gain, grad_output, grad_feed_gain, grad_gate_up, grad_down,
    )


def solution(mesh):
    rows = P(("seq", "head"), None)
    return jax.shard_map(
        local,
        mesh=mesh,
        in_specs=(
            rows, P(), P(None, "head", None), P(None, None, "head"), P(None, "head", None), P("head"), P("head"),
            P(), P("head", None, None), P(), P(None, None, "head"), P("head", None), P(), rows,
        ),
        out_specs=(
            rows, rows, P(), P("seq", "head", None), P("seq", None, "head"), P(None, "head", None), P("head"),
            P("head"), P(), P("head", None, "seq"), P(), P("seq", None, "head"), P("head", "seq"),
        ),
        check_vma=False,
    )
```

```python
import functools

import jax
import jax.numpy as jnp
from jax import lax
from jax.experimental import pallas as pl
from jax.experimental.pallas import tpu as pltpu
from jax.sharding import PartitionSpec as P

D = 2048
DK = 128
DV = 256
KCONV = 4
MIXW = 768
CONVW = 512
NB = 4
BLK = 256
PAD = 8
F32 = jnp.float32
BF16 = jnp.bfloat16

VMEM = pl.BlockSpec(memory_space=pltpu.VMEM)
SMEM = pl.BlockSpec(memory_space=pltpu.SMEM)


def dot(a, b, form="nn"):
    dims = {"nn": ((1,), (0,)), "nt": ((1,), (1,)), "tn": ((0,), (0,))}[form]
    return lax.dot_general(a.astype(BF16), b.astype(BF16), (dims, ((), ())), preferred_element_type=F32)


def halves(a):
    hi = a.astype(BF16)
    return hi, (a - hi.astype(F32)).astype(BF16)


def dot3(a, b, form="nn"):
    ah, al = halves(a)
    bh, bl = halves(b)
    return dot(ah, bh, form) + (dot(ah, bl, form) + dot(al, bh, form))


def dot_exact_left(a, b, form="nn"):
    b1, rest = halves(b)
    rest = b - b1.astype(F32)
    b2 = rest.astype(BF16)
    b3 = (rest - b2.astype(F32)).astype(BF16)
    return dot(a, b1, form) + (dot(a, b2, form) + dot(a, b3, form))


def iota(shape, axis):
    return lax.broadcasted_iota(jnp.int32, shape, axis)


def doc_of(info, pos):
    count = jnp.zeros(pos.shape, jnp.int32)
    for i in range(NB):
        count = count + jnp.where(pos >= info[i], 1, 0)
    return jnp.where(pos < 0, -1, count)


def sigmoid(v):
    return 1.0 / (1.0 + jnp.exp(-v))


def softplus(v):
    return jnp.maximum(v, 0.0) + jnp.log1p(jnp.exp(-jnp.abs(v)))


def unit_lower_inverse(low):
    n = low.shape[0]
    row, col = iota((n, n), 0), iota((n, n), 1)
    eye = jnp.where(row == col, 1.0, 0.0)

    def same(b):
        return row // b == col // b

    x = jnp.where(same(8), -low, 0.0)
    inv = eye + x
    x = dot3(x, x)
    inv = inv + dot3(inv, x)
    x = dot3(x, x)
    inv = inv + dot3(inv, x)
    b = 8
    while b < n:
        off = jnp.where(same(2 * b) & jnp.logical_not(same(b)), low, 0.0)
        inv = inv - dot3(inv, dot3(off, inv))
        b *= 2
    return inv


def valid_column(info, rows, back):
    pos = info[NB] + iota((rows, 1), 0)
    return jnp.where(doc_of(info, pos) == doc_of(info, pos - back), 1.0, 0.0)


def vectors(conv):
    act = conv * sigmoid(conv)
    qa, ka, va = act[:, :DK], act[:, DK : 2 * DK], act[:, 2 * DK :]
    rq = lax.rsqrt(jnp.sum(qa * qa, axis=1, keepdims=True) + 1e-06)
    rk = lax.rsqrt(jnp.sum(ka * ka, axis=1, keepdims=True) + 1e-06)
    return qa, ka, va, rq, rk


def rates(rate_ref, dlog_ref, dbias_ref):
    heads = dlog_ref.shape[1]
    pre = rate_ref[:, :heads] + dbias_ref[...]
    log_decay = -jnp.exp(dlog_ref[...]) * softplus(pre)
    return sigmoid(rate_ref[:, heads:]), log_decay, pre


def block_masks(info, c):
    row, col = iota((BLK, BLK), 0), iota((BLK, BLK), 1)
    base = info[NB] + c * BLK
    docs_r, docs_c = doc_of(info, base + row), doc_of(info, base + col)
    keep = (docs_r == docs_c) & (col <= row)
    column = doc_of(info, base + iota((BLK, 1), 0))
    first = jnp.where(column == doc_of(info, base - 1 + iota((BLK, 1), 0) * 0), 1.0, 0.0)
    last = jnp.where(column == doc_of(info, base + BLK - 1 + iota((BLK, 1), 0) * 0), 1.0, 0.0)
    tri = jnp.where(col <= row, 1.0, 0.0)
    strict = jnp.where(col < row, 1.0, 0.0)
    return keep, first, last, tri, strict


def decays(g, first, last, tri):
    cum = dot_exact_left(tri, jnp.broadcast_to(g, (BLK, DK)))[:, :1]
    carry = first * jnp.exp(cum)
    to_end = last * jnp.exp(cum[BLK - 1 :, :] - cum)
    return carry, to_end


def fwd_prep(info, proj, halo, rate, convw, dlog, dbias, conv_o, dec_o, inv_o, wu_o, qe_o, ol_o, step_o, ab_o, xpad):
    rows = proj.shape[0]
    heads = dlog.shape[1]
    blocks = rows // BLK
    strength, log_decay, _ = rates(rate, dlog, dbias)
    valid = [valid_column(info, rows, KCONV - 1 - j) for j in range(KCONV)]
    for h in range(heads):
        src, dst = pl.ds(h * MIXW, CONVW), pl.ds(h * CONVW, CONVW)
        xpad[:PAD, :] = halo[:, dst]
        xpad[PAD:, :] = proj[:, src].astype(BF16).astype(F32)
        conv = jnp.zeros((rows, CONVW), F32)
        for j in range(KCONV):
            lo = PAD - (KCONV - 1) + j
            conv = conv + convw[j : j + 1, dst].astype(F32) * xpad[lo : lo + rows, :] * valid[j]
        conv_o[:, dst] = conv
    for c in range(blocks):
        keep, first, last, tri, strict = block_masks(info, c)
        here = pl.ds(c * BLK, BLK)
        for h in range(heads):
            qa, ka, va, rq, rk = vectors(conv_o[here, pl.ds(h * CONVW, CONVW)])
            q, k = qa * (rq * DK**-0.5), ka * rk
            beta = strength[c * BLK : (c + 1) * BLK, h : h + 1]
            g = log_decay[c * BLK : (c + 1) * BLK, h : h + 1]
            spread = dot_exact_left(tri, g * strict)
            dec = jnp.where(keep, jnp.exp(jnp.where(keep, spread, 0.0)), 0.0)
            carry, to_end = decays(g, first, last, tri)
            low = strict * (beta * dec * dot(k, k, "nt"))
            inv = unit_lower_inverse(low)
            u = h * blocks + c
            dec_o[u] = dec
            inv_o[u] = inv.astype(BF16)
            rhs = jnp.concatenate([(beta * carry) * k, beta * va], axis=1)
            wu = dot(inv, rhs)
            wu_o[u] = wu
            out = dot(dec * dot(q, k, "nt"), wu)
            qe_o[here, pl.ds(h * DK, DK)] = carry * q - out[:, :DK]
            ol_o[here, pl.ds(h * DV, DV)] = out[:, DK:]
            step = dot(wu, to_end * k, "tn")
            eye = jnp.where(iota((DK, DK), 0) == iota((DK, DK), 1), 1.0, 0.0)
            step_o[u, :DK] = carry[BLK - 1 :, :] * eye - step[:DK]
            step_o[u, DK:] = step[DK:]
    for h in range(heads):
        ab = step_o[h * blocks]
        for c in range(1, blocks):
            nxt = step_o[h * blocks + c]
            ab = dot3(ab, nxt[:DK])
            ab_o_tail = nxt[DK:]
            ab = jnp.concatenate([ab[:DK], ab[DK:] + ab_o_tail], axis=0)
        ab_o[h] = ab.astype(ab_o.dtype)


def fwd_out(start, step, qe, ol, proj, gain, states_o, head_o, gated_o):
    rows = qe.shape[0]
    heads = start.shape[0]
    blocks = rows // BLK
    for h in range(heads):
        state = start[h]
        for c in range(blocks):
            u = h * blocks + c
            here = pl.ds(c * BLK, BLK)
            states_o[u] = state
            out = ol[here, pl.ds(h * DV, DV)] + dot(qe[here, pl.ds(h * DK, DK)], state, "nt")
            head_o[here, pl.ds(h * DV, DV)] = out
            gate = proj[here, pl.ds(h * MIXW + CONVW, DV)]
            scale = lax.rsqrt(jnp.mean(out * out, axis=1, keepdims=True) + 1e-05)
            gated_o[here, pl.ds(h * DV, DV)] = (out * scale * gain[...] * (gate * sigmoid(gate))).astype(BF16)
            if c + 1 < blocks:
                state = dot3(state, step[u, :DK, :]) + step[u, DK:, :]


def dot_left2(a, b, form="nn"):
    ah, al = halves(a)
    return dot(ah, b, form) + dot(al, b, form)


def bwd_head(d_gated, head_out, proj, gain, qe, step, d_out_o, d_gate_o, d_gain_o, y_o, inc_o):
    rows = qe.shape[0]
    blocks = rows // BLK
    heads = qe.shape[1] // DK
    total = jnp.zeros((1, DV), F32)
    for h in range(heads):
        cols = pl.ds(h * DV, DV)
        for c in range(blocks):
            here = pl.ds(c * BLK, BLK)
            dg, out = d_gated[here, cols], head_out[here, cols]
            gate = proj[here, pl.ds(h * MIXW + CONVW, DV)]
            s = sigmoid(gate)
            silu = gate * s
            scale = lax.rsqrt(jnp.mean(out * out, axis=1, keepdims=True) + 1e-05)
            n = out * scale
            dn = dg * n
            d_gate_o[here, cols] = (dn * gain[...] * (s * (1.0 + gate * (1.0 - s)))).astype(BF16)
            total = total + jnp.sum(dn * silu, axis=0, keepdims=True)
            f = dg * gain[...] * silu
            d_out = scale * f - out * (scale * scale * scale) * jnp.mean(f * out, axis=1, keepdims=True)
            d_out_o[here, cols] = d_out
            y_o[h * blocks + c] = dot(d_out, qe[here, pl.ds(h * DK, DK)], "tn")
        inc = y_o[h * blocks + blocks - 1]
        for c in range(blocks - 2, -1, -1):
            inc = y_o[h * blocks + c] + dot3(inc, step[h * blocks + c, :DK, :], "nt")
        inc_o[h] = inc.astype(inc_o.dtype)
    d_gain_o[...] = total


def bwd_mix(
    info, later, conv, dec, inv, wu, states, step, y, d_out, d_gate, rate, proj, halo, convw, dlog, dbias,
    d_proj_o, d_tail_o, d_edge_o, d_rate_o, d_convw_o, d_decay_o, xpad, dpad, dsend, cols_s, d_pre_o
):
    rows = d_out.shape[0]
    heads = later.shape[0]
    blocks = rows // BLK
    strength, log_decay, pre = rates(rate, dlog, dbias)
    valid = [valid_column(info, rows, KCONV - 1 - j) for j in range(KCONV)]
    for h in range(heads):
        grad = later[h]
        for c in range(blocks - 1, -1, -1):
            u = h * blocks + c
            dsend[u] = grad
            if c:
                grad = dot3(grad, step[u, :DK, :], "nt") + y[u]
    for c in range(blocks):
        keep, first, last, tri, strict = block_masks(info, c)
        here = pl.ds(c * BLK, BLK)
        for h in range(heads):
            u = h * blocks + c
            cv = conv[here, pl.ds(h * CONVW, CONVW)]
            sg = sigmoid(cv)
            qa, ka, va, rq, rk = vectors(cv)
            rqs = rq * DK**-0.5
            q, k = qa * rqs, ka * rk
            beta = strength[c * BLK : (c + 1) * BLK, h : h + 1]
            g = log_decay[c * BLK : (c + 1) * BLK, h : h + 1]
            carry, to_end = decays(g, first, last, tri)
            dm = dec[u]
            sc = dm * dot(q, k, "nt")
            gm = dm * dot(k, k, "nt") * strict
            state, d_end = states[u], dsend[u]
            do = d_out[here, pl.ds(h * DV, DV)]
            ks = dot(k, state, "nt")
            qs = dot(q, state, "nt")
            fresh = wu[u, :, DK:] - dot(wu[u, :, :DK], state, "nt")
            kd = to_end * k
            d_fresh = dot(sc, do, "tn") + dot(kd, d_end, "nt")
            d_rhs = dot(inv[u], d_fresh, "tn")
            d_low = -dot(d_rhs, fresh, "nt")
            d_sc = dot(do, fresh, "nt")
            d_val = beta * d_rhs
            ebar = d_low * gm
            d_beta = jnp.sum(d_rhs * (va - carry * ks), axis=1, keepdims=True) + jnp.sum(ebar, axis=1, keepdims=True)
            e = d_sc * sc + beta * ebar
            d_scd = d_sc * dm
            d_gm = (beta * d_low) * (dm * strict)
            d_kd = dot(fresh, d_end)
            d_q = dot(d_scd, k) + carry * dot(do, state)
            d_k = (
                dot(d_scd, q, "tn")
                - (beta * carry) * dot(d_rhs, state)
                + to_end * d_kd
                + dot(d_gm, k)
                + dot(d_gm, k, "tn")
            )
            hcol = carry * jnp.sum(do * qs - beta * d_rhs * ks, axis=1, keepdims=True)
            fcol = jnp.sum(kd * d_kd, axis=1, keepdims=True)
            tail = carry[BLK - 1 :, :] * jnp.sum(
                jnp.sum(state * d_end, axis=1, keepdims=True), axis=0, keepdims=True
            )
            lane = iota((BLK, DK), 1)
            d_g = (
                jnp.sum(dot_exact_left(tri, e, "tn") * strict, axis=1, keepdims=True)
                + dot_exact_left(tri, jnp.where(lane == 0, hcol, 0.0), "tn")[:, :1]
                + dot_exact_left(strict, jnp.where(lane == 0, fcol, 0.0))[:, :1]
                + tail
            )
            cols_s[here, h : h + 1] = d_g
            cols_s[here, heads + h : heads + h + 1] = d_beta
            d_qa = rqs * d_q - qa * (rqs * rq * rq * jnp.sum(d_q * qa, axis=1, keepdims=True))
            d_ka = rk * d_k - ka * (rk * rk * rk * jnp.sum(d_k * ka, axis=1, keepdims=True))
            d_act = jnp.concatenate([d_qa, d_ka, d_val], axis=1)
            d_pre_o[here, pl.ds(h * CONVW, CONVW)] = d_act * (sg * (1.0 + cv * (1.0 - sg)))
    d_g, d_beta = cols_s[:, :heads], cols_s[:, heads : 2 * heads]
    d_bias = -d_g * jnp.exp(dlog[...]) * sigmoid(pre)
    d_rate_o[:, :heads] = d_bias
    d_rate_o[:, heads:] = d_beta * strength * (1.0 - strength)
    d_decay_o[:, :heads] = jnp.sum(d_g * log_decay, axis=0, keepdims=True)
    d_decay_o[:, heads:] = jnp.sum(d_bias, axis=0, keepdims=True)
    for h in range(heads):
        src, dst = pl.ds(h * MIXW, CONVW), pl.ds(h * CONVW, CONVW)
        xpad[:PAD, :] = halo[:, dst]
        xpad[PAD:, :] = proj[:, src].astype(BF16).astype(F32)
        dpad[...] = jnp.zeros_like(dpad)
        d_conv = d_pre_o[:, dst]
        for j in range(KCONV):
            lo = PAD - (KCONV - 1) + j
            masked = d_conv * valid[j]
            d_convw_o[j : j + 1, dst] = jnp.sum(masked * xpad[lo : lo + rows, :], axis=0, keepdims=True)
            dpad[lo : lo + rows, :] += convw[j : j + 1, dst].astype(F32) * masked
        d_edge_o[:, dst] = dpad[:PAD, :]
        d_tail_o[:, dst] = dpad[rows:, :]
        d_proj_o[:, src] = dpad[PAD:, :].astype(BF16)
        d_proj_o[:, pl.ds(h * MIXW + CONVW, DV)] = d_gate[:, pl.ds(h * DV, DV)]


def call(kernel, outs, scratch, limit, *args, flops=2_000_000_000, nbytes=16_000_000):
    def spec(a):
        return SMEM if a.dtype == jnp.int32 else VMEM

    return pl.pallas_call(
        kernel,
        out_shape=outs,
        in_specs=[spec(a) for a in args],
        out_specs=[VMEM for _ in outs],
        scratch_shapes=scratch,
        compiler_params=pltpu.CompilerParams(vmem_limit_bytes=limit << 20),
        cost_estimate=pl.CostEstimate(flops=flops, bytes_accessed=nbytes, transcendentals=0),
    )(*args)


def sds(shape, dtype=F32):
    return jax.ShapeDtypeStruct(shape, dtype)
CHIPS = 4
LANES = 128


def cp(src, dst, send, recv, dev):
    return pltpu.make_async_remote_copy(
        src_ref=src, dst_ref=dst, send_sem=send, recv_sem=recv, device_id=dev, device_id_type=pl.DeviceIdType.MESH
    )


def greet(devices):
    barrier = pltpu.get_barrier_semaphore()
    for dev in devices:
        pl.semaphore_signal(barrier, inc=1, device_id=dev, device_id_type=pl.DeviceIdType.MESH)
    pl.semaphore_wait(barrier, len(devices))


def head_place():
    me = lax.axis_index("head")
    chip, core = me // 2, me % 2
    seq = lax.axis_index("seq")

    def dev(step, flip=False):
        c = lax.rem(chip + step, CHIPS)
        return (seq, c * 2 + (1 - core if flip else core))

    return me, chip, core, dev


def head_peers():
    dev = head_place()[3]
    return [dev(0, True)] + [dev(d) for d in range(1, CHIPS)]


def gather_over_head(x, o, ssem, rsem, lsem):
    rows = x.shape[0]
    me, chip, core, dev = head_place()

    def at(step, flip=False):
        return o.at[pl.ds(pl.multiple_of(dev(step, flip)[1] * rows, rows), rows)]

    own = pltpu.make_async_copy(x, at(0), lsem)
    own.start()
    out = [cp(x, at(0), ssem.at[d], rsem.at[d], dev(d)) for d in (1, 3, 2)]
    out.append(cp(x, at(0), ssem.at[0], rsem.at[0], dev(0, True)))
    for s in out:
        s.start()
    for d in (1, 3, 2):
        cp(x, at(CHIPS - d), ssem.at[d], rsem.at[d], dev(d)).wait_recv()
        fwd = cp(at(CHIPS - d), at(CHIPS - d), ssem.at[CHIPS + d], rsem.at[CHIPS + d], dev(0, True))
        fwd.start()
        out.append(fwd)
    own.wait()
    cp(x, at(0, True), ssem.at[0], rsem.at[0], dev(0, True)).wait_recv()
    for d in range(1, CHIPS):
        cp(x, at(CHIPS - d, True), ssem.at[CHIPS + d], rsem.at[CHIPS + d], dev(0, True)).wait_recv()
    for s in out:
        s.wait_send()


def reduce_over_head(x, total, pair, got, mid, ssem, rsem):
    rows = total.shape[0]
    me, chip, core, dev = head_place()
    partner = dev(0, True)

    def at(step, flip=False):
        return x.at[pl.ds(pl.multiple_of(dev(step, flip)[1] * rows, rows), rows)]

    order = (2, 1, 3, 0)
    first = [cp(at(d, True), pair.at[d], ssem.at[d], rsem.at[d], partner) for d in order]
    for s in first:
        s.start()
    second = []
    for s, d in zip(first, order):
        s.wait_recv()
        both = at(d)[...].astype(F32) + pair[d].astype(F32)
        if d:
            mid[d] = both.astype(BF16)
            t = cp(mid.at[d], got.at[d], ssem.at[CHIPS + d], rsem.at[CHIPS + d], dev(d))
            t.start()
            second.append(t)
        else:
            total[...] = both
    for s in (second[1], second[2], second[0]):
        s.wait_recv()
    total[...] = total[...] + ((got[1].astype(F32) + got[3].astype(F32)) + got[2].astype(F32))
    for s in first + second:
        s.wait_send()


def mean_scale(v):
    return lax.rsqrt(jnp.mean(v * v, axis=1, keepdims=True) + 1e-05)


def norm_back(v, gain, d_norm):
    r = mean_scale(v)
    e = d_norm * gain
    d_v = r * e - v * (r * r * r * jnp.mean(e * v, axis=1, keepdims=True))
    return d_v, jnp.sum(d_norm * v * r, axis=0, keepdims=True)


def mid_forward(x, tokens, gain, all_o, hidden_o, total, block, pair, got, mid, s1, r1, s2, r2, ls):
    greet(head_peers())
    reduce_over_head(x, total, pair, got, mid, s1, r1)
    hidden = tokens[...].astype(F32) + total[...]
    hidden_o[...] = hidden
    block[...] = (hidden * mean_scale(hidden) * gain[...]).astype(BF16)
    gather_over_head(block, all_o, s2, r2, ls)


def mid_backward(x, hidden, cot, gain, all_o, d_hidden_o, d_gain_o, total, block, pair, got, mid, s1, r1, s2, r2, ls):
    greet(head_peers())
    reduce_over_head(x, total, pair, got, mid, s1, r1)
    d_norm, d_gain = norm_back(hidden[...], gain[...], total[...])
    d_hidden = cot[...].astype(F32) + d_norm
    d_hidden_o[...] = d_hidden
    d_gain_o[...] = d_gain
    block[...] = d_hidden.astype(BF16)
    gather_over_head(block, all_o, s2, r2, ls)


def last_backward(x, tokens, d_hidden, gain, d_tokens_o, d_gain_o, total, pair, got, mid, s1, r1):
    greet(head_peers())
    reduce_over_head(x, total, pair, got, mid, s1, r1)
    d_norm, d_gain = norm_back(tokens[...].astype(F32), gain[...], total[...])
    d_tokens_o[...] = d_hidden[...] + d_norm
    d_gain_o[...] = d_gain


def reach(kernel, outs, scratch, cid, limit, *args, anywhere=(), nbytes=12_000_000):
    return pl.pallas_call(
        kernel,
        out_shape=outs,
        in_specs=[pl.BlockSpec(memory_space=pl.ANY) if i in anywhere else VMEM for i in range(len(args))],
        out_specs=[VMEM for _ in outs],
        scratch_shapes=scratch,
        compiler_params=pltpu.CompilerParams(
            collective_id=cid, has_side_effects=True, vmem_limit_bytes=limit << 20
        ),
        cost_estimate=pl.CostEstimate(flops=0, bytes_accessed=nbytes, transcendentals=0),
    )(*args)


def sems(n):
    return pltpu.SemaphoreType.DMA((n,))


def reduce_scratch(rows, cols):
    return [pltpu.VMEM((CHIPS, rows, cols), BF16) for _ in range(3)] + [sems(2 * CHIPS), sems(2 * CHIPS)]


def gather_scratch():
    return [sems(2 * CHIPS), sems(2 * CHIPS), pltpu.SemaphoreType.DMA]


SIDE = 4


def seq_place():
    me = lax.axis_index("seq")
    z, y = me // SIDE, me % SIDE
    head = lax.axis_index("head")

    def dev(dz, dy):
        return (lax.rem(z + dz, SIDE) * SIDE + lax.rem(y + dy, SIDE), head)

    return me, z, y, dev


def side_peers():
    dev = seq_place()[3]
    return [dev(0, d) for d in range(1, SIDE)] + [dev(d, 0) for d in range(1, SIDE)]


def share(src, got, place, to, ssem, rsem):
    got[place] = src[...]
    out = [cp(src, got.at[place], ssem.at[d], rsem.at[d], to(d)) for d in range(1, SIDE)]
    for s in out:
        s.start()
    for d in range(1, SIDE):
        back = lax.rem(place + SIDE - d, SIDE)
        cp(src, got.at[back], ssem.at[d], rsem.at[d], to(d)).wait_recv()
    return out


def unit_top():
    return jnp.where(iota((DK + DV, DK), 0) == iota((DK + DV, DK), 1), 1.0, 0.0)


def add_low(pair, low):
    return jnp.concatenate([pair[:DK], pair[DK:] + low], axis=0)


def states_forward(ab, start_o, ga_o, ta_o, got1, tot, got2, s1, r1, s2, r2):
    me, z, y, dev = seq_place()
    heads = ab.shape[0]
    greet(side_peers())
    out = share(ab, got1, y, lambda d: dev(0, d), s1, r1)
    before = []
    for h in range(heads):
        whole = got1[0, h].astype(F32)
        prefix = jnp.where(y > 0, whole, unit_top())
        for j in range(1, SIDE):
            a, b = got1[j, h, :DK, :], got1[j, h, DK:, :].astype(F32)
            whole = add_low(dot_left2(whole, a), b)
            if j < SIDE - 1:
                prefix = jnp.where(y > j, whole, prefix)
        tot[h] = whole.astype(BF16)
        before.append(prefix)
        for j in range(SIDE):
            ga_o[j, h] = got1[j, h, :DK, :]
    out += share(tot, got2, z, lambda d: dev(d, 0), s2, r2)
    for h in range(heads):
        held = jnp.zeros((DV, DK), F32)
        for j in range(SIDE - 1):
            held = jnp.where(
                z > j, dot_left2(held, got2[j, h, :DK, :]) + got2[j, h, DK:, :].astype(F32), held
            )
        start_o[h] = dot3(held, before[h][:DK]) + before[h][DK:]
        for j in range(SIDE):
            ta_o[j, h] = got2[j, h, :DK, :]
    for s in out:
        s.wait_send()


def states_backward(inc, ga, ta, later_o, got1, tot, got2, s1, r1, s2, r2):
    me, z, y, dev = seq_place()
    heads = inc.shape[0]
    greet(side_peers())
    out = share(inc, got1, y, lambda d: dev(0, d), s1, r1)
    after = []
    for h in range(heads):
        whole = add_low(dot(unit_top(), ga[SIDE - 1, h], "nt"), got1[SIDE - 1, h].astype(F32))
        suffix = jnp.where(y < SIDE - 1, whole, unit_top())
        for j in range(SIDE - 2, -1, -1):
            whole = add_low(dot_left2(whole, ga[j, h], "nt"), got1[j, h].astype(F32))
            if j:
                suffix = jnp.where(y < j, whole, suffix)
        tot[h] = whole[DK:].astype(BF16)
        after.append(suffix)
    out += share(tot, got2, z, lambda d: dev(d, 0), s2, r2)
    for h in range(heads):
        held = jnp.zeros((DV, DK), F32)
        for j in range(SIDE - 1, 0, -1):
            held = jnp.where(z < j, dot_left2(held, ta[j, h], "nt") + got2[j, h].astype(F32), held)
        later_o[h] = dot3(held, after[h][:DK]) + after[h][DK:]
    for s in out:
        s.wait_send()


def reduce_over_seq(x, o, got1, mid, got2, own, ssem, rsem, lsem):
    half, rows, cols = o.shape
    me, z, y, dev = seq_place()
    greet(side_peers())
    ways = (lambda a, b: dev(b, a), lambda a, b: dev(a, b))

    def piece(i, a, b):
        owner = ways[i](a, b)[0]
        return x.at[pl.ds(pl.multiple_of(owner * rows, rows), rows), pl.ds(i * cols, cols)]

    sends, second, kept = [], [], {}
    for a in (2, 1, 3):
        for i in range(2):
            for b in (2, 1, 3, 0):
                k = (i * SIDE + a) * SIDE + b
                s = cp(piece(i, a, b), got1.at[i, a, b], ssem.at[k], rsem.at[k], ways[i](a, 0))
                s.start()
                sends.append(s)
    for i in range(2):
        for b in range(SIDE):
            kept[i, b] = pltpu.make_async_copy(piece(i, 0, b), own.at[i, b], lsem.at[i * SIDE + b])
            kept[i, b].start()
    for b in (2, 1, 3, 0):
        for i in range(2):
            kept[i, b].wait()
            for a in (1, 3, 2):
                k = (i * SIDE + a) * SIDE + b
                cp(piece(i, a, b), got1.at[i, a, b], ssem.at[k], rsem.at[k], ways[i](a, 0)).wait_recv()
            total = own[i, b].astype(F32) + (
                (got1[i, 1, b].astype(F32) + got1[i, 3, b].astype(F32)) + got1[i, 2, b].astype(F32)
            )
            if b:
                mid[i, b] = total.astype(BF16)
                k = 2 * SIDE * SIDE + i * SIDE + b
                s = cp(mid.at[i, b], got2.at[i, b], ssem.at[k], rsem.at[k], ways[i](0, b))
                s.start()
                second.append(s)
            else:
                o[i] = total
    for s in second:
        s.wait_recv()
    for i in range(2):
        o[i] = o[i] + ((got2[i, 1].astype(F32) + got2[i, 3].astype(F32)) + got2[i, 2].astype(F32))
    for s in sends + second:
        s.wait_send()


def small_sums(gains, convs, rate, gains_o, convs_o, rate_o, gbuf, sbuf, rbuf, s1, r1, s2, r2):
    me, z, y, dev = seq_place()
    head = lax.axis_index("head")
    heads, seqs = gbuf.shape[0], rbuf.shape[0]
    g = gains.shape[0]
    c = convs.shape[0]
    across = [(me, lax.rem(head + d, heads)) for d in range(1, heads)]
    along = [(lax.rem(me + d, seqs), head) for d in range(1, seqs)]
    greet(across + along)
    gbuf[head] = gains[...]
    out = [cp(gains, gbuf.at[head], s1.at[d], r1.at[d], across[d - 1]) for d in range(1, heads)]
    for s in out:
        s.start()
    for d in range(1, heads):
        cp(gains, gbuf.at[lax.rem(head + heads - d, heads)], s1.at[d], r1.at[d], across[d - 1]).wait_recv()
    total = gbuf[0]
    for i in range(1, heads):
        total = total + gbuf[i]
    for j in range(seqs):
        sbuf[j, :g] = total
        sbuf[j, g : g + c] = convs[...]
        sbuf[j, g + c :] = rate[j]
    rbuf[me] = sbuf[me]
    for d in range(1, seqs):
        s = cp(sbuf.at[lax.rem(me + d, seqs)], rbuf.at[me], s2.at[d], r2.at[d], along[d - 1])
        s.start()
        out.append(s)
    for d in range(1, seqs):
        cp(sbuf.at[0], rbuf.at[lax.rem(me + seqs - d, seqs)], s2.at[d], r2.at[d], along[d - 1]).wait_recv()
    total = rbuf[0]
    for i in range(1, seqs):
        total = total + rbuf[i]
    gains_o[...] = total[:g]
    convs_o[...] = total[g : g + c]
    rate_o[...] = total[g + c :]
    for s in out:
        s.wait_send()


def weight_grads(d_gu, middle, gated, n2, cot, d_mixed, o):
    a, b = d_gu.shape[0], middle.shape[0]
    for lo, left, right in ((0, d_gu, n2), (a, middle, cot), (a + b, gated, d_mixed)):
        out = dot(left[...], right[...]).astype(BF16)
        n = left.shape[0]
        o[0, lo : lo + n] = out[:, :LANES]
        o[1, lo : lo + n] = out[:, LANES:]


def passed_along(shard, axis, by):
    length = lax.axis_size(axis)
    pairs = [(i, i + by) for i in range(length) if 0 <= i + by < length]
    return lax.ppermute(shard, axis, pairs)


def rms_scale(values, gain):
    return values * lax.rsqrt(jnp.mean(values * values, axis=-1, keepdims=True) + 1e-05) * gain


def local(
    tokens, mixer_gain, mixer_weight, rate_weight, conv_weight, decay_log, decay_bias, head_gain,
    output_weight, feed_gain, gate_up_weight, down_weight, doc_starts, cotangent,
):
    resid = tokens.astype(F32)
    normed = rms_scale(resid, mixer_gain).astype(BF16)
    gathered = lax.all_gather(normed, "head", axis=0, tiled=True)
    heads = mixer_weight.shape[1]
    gathered, cot_own, mixer_flat = lax.optimization_barrier(
        (gathered, cotangent, mixer_weight.reshape(D, heads * MIXW))
    )
    cot_rows = lax.all_gather(cot_own, "head", axis=0, tiled=True)
    rows = gathered.shape[0]
    blocks = rows // BLK
    units = heads * blocks
    seq = lax.axis_size("seq")
    projected = jnp.dot(gathered, mixer_flat, preferred_element_type=F32)
    rate_proj = jnp.einsum("td,dgh->tgh", gathered, rate_weight, preferred_element_type=F32).reshape(rows, 2 * heads)
    rim = projected[rows - PAD :].reshape(PAD, heads, MIXW)[:, :, :CONVW].reshape(PAD, heads * CONVW).astype(BF16)
    halo = passed_along(rim, "seq", 1).astype(F32)
    convw = conv_weight.reshape(KCONV, heads * CONVW)
    info = jnp.concatenate(
        [doc_starts, jnp.stack([lax.axis_index("seq") * rows, lax.axis_index("seq")]).astype(jnp.int32)]
    )
    dlog, dbias = decay_log.reshape(1, heads), decay_bias.reshape(1, heads)
    gain = head_gain.reshape(1, DV)

    conv, dec, inv, wu, qe, ol, step, ab = call(
        fwd_prep,
        [
            sds((rows, heads * CONVW)), sds((units, BLK, BLK)), sds((units, BLK, BLK), BF16),
            sds((units, BLK, DK + DV)), sds((rows, heads * DK)), sds((rows, heads * DV)),
            sds((units, DK + DV, DK)), sds((heads, DK + DV, DK), BF16),
        ],
        [pltpu.VMEM((PAD + rows, CONVW), F32)],
        56, info, projected, halo, rate_proj, convw, dlog, dbias,
    )
    start, ga, ta = reach(
        states_forward,
        [sds((heads, DV, DK)), sds((SIDE, heads, DK, DK), BF16), sds((SIDE, heads, DK, DK), BF16)],
        [
            pltpu.VMEM((SIDE, heads, DK + DV, DK), BF16), pltpu.VMEM((heads, DK + DV, DK), BF16),
            pltpu.VMEM((SIDE, heads, DK + DV, DK), BF16), sems(SIDE), sems(SIDE), sems(SIDE), sems(SIDE),
        ],
        1, 40, ab,
    )
    states, head_out, gated = call(
        fwd_out,
        [sds((units, DV, DK)), sds((rows, heads * DV)), sds((rows, heads * DV), BF16)],
        [], 48, start, step, qe, ol, projected, gain,
    )
    out_flat = output_weight.reshape(heads * DV, D)
    own = tokens.shape[0]
    mixed = jnp.dot(gated, out_flat, preferred_element_type=F32).astype(BF16)
    feed_row = feed_gain.reshape(1, D)
    gathered_two, hidden = reach(
        mid_forward,
        [sds((rows, D), BF16), sds((own, D))],
        [pltpu.VMEM((own, D), F32), pltpu.VMEM((own, D), BF16)] + reduce_scratch(own, D) + gather_scratch(),
        2, 48, mixed, tokens, feed_row,
    )
    hid = down_weight.shape[0]
    gu_t = gate_up_weight.transpose(1, 2, 0).reshape(2 * hid, D)
    by_last = (((1,), (1,)), ((), ()))
    by_first = (((0,), (0,)), ((), ()))
    d_middle = lax.dot_general(down_weight, cot_rows, by_last, preferred_element_type=F32)
    gate_up = lax.dot_general(gu_t, gathered_two, by_last, preferred_element_type=F32)
    gate, up = gate_up[:hid], gate_up[hid:]
    s = jax.nn.sigmoid(gate)
    middle = (gate * s * up).astype(BF16)
    d_gate_up = jnp.concatenate([d_middle * up * (s * (1.0 + gate * (1.0 - s))), d_middle * gate * s]).astype(BF16)
    d_two = lax.dot_general(d_gate_up, gu_t, by_first, preferred_element_type=F32).astype(BF16)
    d_mixed, d_hidden, g_feed_gain = reach(
        mid_backward,
        [sds((rows, D), BF16), sds((own, D)), sds((1, D))],
        [pltpu.VMEM((own, D), F32), pltpu.VMEM((own, D), BF16)] + reduce_scratch(own, D) + gather_scratch(),
        3, 48, d_two, hidden, cotangent, feed_row,
    )
    d_mixed, middle = lax.optimization_barrier((d_mixed, middle))
    feed = lax.dot_general(middle, down_weight, by_first, preferred_element_type=F32).astype(BF16)
    feed_sum = lax.psum_scatter(feed, "head", scatter_dimension=0, tiled=True).astype(F32)
    layer_out = (hidden + feed_sum).astype(BF16)
    d_mixed, feed = lax.optimization_barrier((d_mixed, feed))
    wide = 3 * hid + heads * DV
    right = pl.BlockSpec((rows, 2 * LANES), lambda j: (0, j))

    def whole(a):
        return pl.BlockSpec(a.shape, lambda j: (0, 0))

    gated_t = gated.T
    grads = pl.pallas_call(
        weight_grads,
        grid=(seq // 2,),
        out_shape=sds((seq, wide, LANES), BF16),
        in_specs=[whole(d_gate_up), whole(middle), whole(gated_t), right, right, right],
        out_specs=pl.BlockSpec((2, wide, LANES), lambda j: (j, 0, 0)),
        compiler_params=pltpu.CompilerParams(vmem_limit_bytes=48 << 20),
        cost_estimate=pl.CostEstimate(flops=2 * wide * rows * D, bytes_accessed=24_000_000, transcendentals=0),
    )(d_gate_up, middle, gated_t, gathered_two, cot_rows, d_mixed)
    d_mixed, grads = lax.optimization_barrier((d_mixed, grads))
    grads = lax.psum_scatter(grads.reshape(seq * wide, LANES), "seq", scatter_dimension=0, tiled=True).astype(F32)
    grad_gate_up = grads[: 2 * hid].reshape(2, hid, LANES).transpose(2, 0, 1)
    grad_down = grads[2 * hid : 3 * hid]
    grad_output = grads[3 * hid :].reshape(heads, DV, LANES)
    d_gated = jnp.einsum("td,vd->tv", d_mixed, out_flat, preferred_element_type=F32)
    d_out, d_gate, g_head_gain, y, inc = call(
        bwd_head,
        [
            sds((rows, heads * DV)), sds((rows, heads * DV), BF16), sds((1, DV)),
            sds((units, DV, DK)), sds((heads, DV, DK), BF16),
        ],
        [], 48, d_gated, head_out, projected, gain, qe, step,
    )
    (later,) = reach(
        states_backward,
        [sds((heads, DV, DK))],
        [
            pltpu.VMEM((SIDE, heads, DV, DK), BF16), pltpu.VMEM((heads, DV, DK), BF16),
            pltpu.VMEM((SIDE, heads, DV, DK), BF16), sems(SIDE), sems(SIDE), sems(SIDE), sems(SIDE),
        ],
        4, 40, inc, ga, ta,
    )
    d_projected, d_tail, d_edge, d_rate, d_convw, d_decay = call(
        bwd_mix,
        [
            sds((rows, heads * MIXW), BF16), sds((PAD, heads * CONVW)), sds((PAD, heads * CONVW)),
            sds((rows, 2 * heads)), sds((KCONV, heads * CONVW)), sds((1, 2 * heads)),
        ],
        [
            pltpu.VMEM((PAD + rows, CONVW), F32), pltpu.VMEM((PAD + rows, CONVW), F32),
            pltpu.VMEM((units, DV, DK), F32), pltpu.VMEM((rows, DK), F32), pltpu.VMEM((rows, heads * CONVW), F32),
        ],
        60, info, later, conv, dec, inv, wu, states, step, y, d_out, d_gate, rate_proj, projected, halo, convw,
        dlog, dbias,
    )
    tail = (d_tail + passed_along(d_edge, "seq", -1)).astype(BF16)
    for h in range(heads):
        d_projected = lax.dynamic_update_slice(
            d_projected, tail[:, h * CONVW : (h + 1) * CONVW], (rows - PAD, h * MIXW)
        )
    d_rate_low = d_rate.astype(BF16)
    d_normed = (
        jnp.einsum("tw,dw->td", d_projected, mixer_flat, preferred_element_type=F32)
        + jnp.einsum("tg,dg->td", d_rate_low, rate_weight.reshape(D, 2 * heads), preferred_element_type=F32)
    ).astype(BF16)
    grad_rate = jnp.einsum("td,tg->dg", gathered, d_rate_low, preferred_element_type=F32)
    grad_tokens, g_mixer_gain = reach(
        last_backward,
        [sds((own, D)), sds((1, D))],
        [pltpu.VMEM((own, D), F32)] + reduce_scratch(own, D),
        5, 48, d_normed, tokens, d_hidden, mixer_gain.reshape(1, D),
    )
    grad_mixer = jnp.einsum("td,tw->dw", gathered, d_projected, preferred_element_type=F32).astype(BF16)
    half = heads * MIXW // 2
    part = D // seq
    (grad_mixer,) = reach(
        reduce_over_seq,
        [sds((2, part, half))],
        [
            pltpu.VMEM((2, SIDE, SIDE, part, half), BF16), pltpu.VMEM((2, SIDE, part, half), BF16),
            pltpu.VMEM((2, SIDE, part, half), BF16), pltpu.VMEM((2, SIDE, part, half), BF16),
            sems(2 * SIDE * SIDE + 2 * SIDE), sems(2 * SIDE * SIDE + 2 * SIDE), sems(2 * SIDE),
        ],
        6, 56, grad_mixer, anywhere=(0,), nbytes=40_000_000,
    )
    grad_mixer = grad_mixer.transpose(1, 0, 2)

    def packed(*arrays):
        flat = jnp.concatenate([a.reshape(-1) for a in arrays])
        size = -(-flat.size // (8 * LANES)) * 8 * LANES
        return jnp.pad(flat, (0, size - flat.size)).reshape(-1, LANES)

    gains = packed(g_mixer_gain, g_feed_gain, g_head_gain)
    convs = packed(d_convw, d_decay)
    rate_own = jnp.pad(grad_rate.reshape(seq, -1, LANES), ((0, 0), (0, 8 - 2 * heads), (0, 0)))
    n_gain, n_conv = gains.shape[0], convs.shape[0]
    gains, convs, rate_own = reach(
        small_sums,
        [sds((n_gain, LANES)), sds((n_conv, LANES)), sds((8, LANES))],
        [
            pltpu.VMEM((lax.axis_size("head"), n_gain, LANES), F32),
            pltpu.VMEM((seq, n_gain + n_conv + 8, LANES), F32), pltpu.VMEM((seq, n_gain + n_conv + 8, LANES), F32),
            sems(8), sems(8), sems(16), sems(16),
        ],
        7, 40, gains, convs, rate_own, nbytes=1_000_000,
    )
    gains, convs = gains.reshape(-1), convs.reshape(-1)
    grad_mixer_gain, grad_feed_gain, grad_head_gain = gains[:D], gains[D : 2 * D], gains[2 * D : 2 * D + DV]
    n = KCONV * heads * CONVW
    grad_conv = convs[:n].reshape(KCONV, heads, CONVW)
    grad_decay_log, grad_decay_bias = convs[n : n + heads], convs[n + heads : n + 2 * heads]
    grad_rate = rate_own[: 2 * heads].reshape(part, 2, heads)
    return (
        layer_out, grad_tokens, grad_mixer_gain, grad_mixer, grad_rate, grad_conv, grad_decay_log, grad_decay_bias,
        grad_head_gain, grad_output, grad_feed_gain, grad_gate_up, grad_down,
    )


def solution(mesh):
    rows = P(("seq", "head"), None)
    return jax.shard_map(
        local,
        mesh=mesh,
        in_specs=(
            rows, P(), P(None, "head", None), P(None, None, "head"), P(None, "head", None), P("head"), P("head"),
            P(), P("head", None, None), P(), P(None, None, "head"), P("head", None), P(), rows,
        ),
        out_specs=(
            rows, rows, P(), P("seq", "head", None), P("seq", None, "head"), P(None, "head", None), P("head"),
            P("head"), P(), P("head", None, "seq"), P(), P("seq", None, "head"), P("head", "seq"),
        ),
        check_vma=False,
    )
```

```python
import functools

import jax
import jax.numpy as jnp
from jax import lax
from jax.experimental import pallas as pl
from jax.experimental.pallas import tpu as pltpu
from jax.sharding import PartitionSpec as P

D = 2048
DK = 128
DV = 256
KCONV = 4
MIXW = 768
CONVW = 512
NB = 4
BLK = 256
PAD = 8
F32 = jnp.float32
BF16 = jnp.bfloat16

VMEM = pl.BlockSpec(memory_space=pltpu.VMEM)
SMEM = pl.BlockSpec(memory_space=pltpu.SMEM)


def dot(a, b, form="nn"):
    dims = {"nn": ((1,), (0,)), "nt": ((1,), (1,)), "tn": ((0,), (0,))}[form]
    return lax.dot_general(a.astype(BF16), b.astype(BF16), (dims, ((), ())), preferred_element_type=F32)


def halves(a):
    hi = a.astype(BF16)
    return hi, (a - hi.astype(F32)).astype(BF16)


def dot3(a, b, form="nn"):
    ah, al = halves(a)
    bh, bl = halves(b)
    return dot(ah, bh, form) + (dot(ah, bl, form) + dot(al, bh, form))


def dot_exact_left(a, b, form="nn"):
    b1, rest = halves(b)
    rest = b - b1.astype(F32)
    b2 = rest.astype(BF16)
    b3 = (rest - b2.astype(F32)).astype(BF16)
    return dot(a, b1, form) + (dot(a, b2, form) + dot(a, b3, form))


def iota(shape, axis):
    return lax.broadcasted_iota(jnp.int32, shape, axis)


def doc_of(info, pos):
    count = jnp.zeros(pos.shape, jnp.int32)
    for i in range(NB):
        count = count + jnp.where(pos >= info[i], 1, 0)
    return jnp.where(pos < 0, -1, count)


def sigmoid(v):
    return 1.0 / (1.0 + jnp.exp(-v))


def softplus(v):
    return jnp.maximum(v, 0.0) + jnp.log1p(jnp.exp(-jnp.abs(v)))


def unit_lower_inverse(low):
    n = low.shape[0]
    row, col = iota((n, n), 0), iota((n, n), 1)
    eye = jnp.where(row == col, 1.0, 0.0)

    def same(b):
        return row // b == col // b

    x = jnp.where(same(8), -low, 0.0)
    inv = eye + x
    x = dot3(x, x)
    inv = inv + dot3(inv, x)
    x = dot3(x, x)
    inv = inv + dot3(inv, x)
    b = 8
    while b < n:
        off = jnp.where(same(2 * b) & jnp.logical_not(same(b)), low, 0.0)
        inv = inv - dot3(inv, dot3(off, inv))
        b *= 2
    return inv


def valid_column(info, rows, back):
    pos = info[NB] + iota((rows, 1), 0)
    return jnp.where(doc_of(info, pos) == doc_of(info, pos - back), 1.0, 0.0)


def vectors(conv):
    act = conv * sigmoid(conv)
    qa, ka, va = act[:, :DK], act[:, DK : 2 * DK], act[:, 2 * DK :]
    rq = lax.rsqrt(jnp.sum(qa * qa, axis=1, keepdims=True) + 1e-06)
    rk = lax.rsqrt(jnp.sum(ka * ka, axis=1, keepdims=True) + 1e-06)
    return qa, ka, va, rq, rk


def rates(rate_ref, dlog_ref, dbias_ref):
    heads = dlog_ref.shape[1]
    pre = rate_ref[:, :heads] + dbias_ref[...]
    log_decay = -jnp.exp(dlog_ref[...]) * softplus(pre)
    return sigmoid(rate_ref[:, heads:]), log_decay, pre


def block_masks(info, c):
    row, col = iota((BLK, BLK), 0), iota((BLK, BLK), 1)
    base = info[NB] + c * BLK
    docs_r, docs_c = doc_of(info, base + row), doc_of(info, base + col)
    keep = (docs_r == docs_c) & (col <= row)
    column = doc_of(info, base + iota((BLK, 1), 0))
    first = jnp.where(column == doc_of(info, base - 1 + iota((BLK, 1), 0) * 0), 1.0, 0.0)
    last = jnp.where(column == doc_of(info, base + BLK - 1 + iota((BLK, 1), 0) * 0), 1.0, 0.0)
    tri = jnp.where(col <= row, 1.0, 0.0)
    strict = jnp.where(col < row, 1.0, 0.0)
    return keep, first, last, tri, strict


def decays(g, first, last, tri):
    cum = dot_exact_left(tri, jnp.broadcast_to(g, (BLK, DK)))[:, :1]
    carry = first * jnp.exp(cum)
    to_end = last * jnp.exp(cum[BLK - 1 :, :] - cum)
    return carry, to_end


def fwd_prep(info, proj, halo, rate, convw, dlog, dbias, conv_o, dec_o, inv_o, wu_o, qe_o, ol_o, step_o, ab_o, xpad):
    rows = proj.shape[0]
    heads = dlog.shape[1]
    blocks = rows // BLK
    strength, log_decay, _ = rates(rate, dlog, dbias)
    valid = [valid_column(info, rows, KCONV - 1 - j) for j in range(KCONV)]
    for h in range(heads):
        src, dst = pl.ds(h * MIXW, CONVW), pl.ds(h * CONVW, CONVW)
        xpad[:PAD, :] = halo[:, dst]
        xpad[PAD:, :] = proj[:, src].astype(BF16).astype(F32)
        conv = jnp.zeros((rows, CONVW), F32)
        for j in range(KCONV):
            lo = PAD - (KCONV - 1) + j
            conv = conv + convw[j : j + 1, dst].astype(F32) * xpad[lo : lo + rows, :] * valid[j]
        conv_o[:, dst] = conv
    for c in range(blocks):
        keep, first, last, tri, strict = block_masks(info, c)
        here = pl.ds(c * BLK, BLK)
        for h in range(heads):
            qa, ka, va, rq, rk = vectors(conv_o[here, pl.ds(h * CONVW, CONVW)])
            q, k = qa * (rq * DK**-0.5), ka * rk
            beta = strength[c * BLK : (c + 1) * BLK, h : h + 1]
            g = log_decay[c * BLK : (c + 1) * BLK, h : h + 1]
            spread = dot_exact_left(tri, g * strict)
            dec = jnp.where(keep, jnp.exp(jnp.where(keep, spread, 0.0)), 0.0)
            carry, to_end = decays(g, first, last, tri)
            low = strict * (beta * dec * dot(k, k, "nt"))
            inv = unit_lower_inverse(low)
            u = h * blocks + c
            dec_o[u] = dec
            inv_o[u] = inv.astype(BF16)
            rhs = jnp.concatenate([(beta * carry) * k, beta * va], axis=1)
            wu = dot(inv, rhs)
            wu_o[u] = wu
            out = dot(dec * dot(q, k, "nt"), wu)
            qe_o[here, pl.ds(h * DK, DK)] = carry * q - out[:, :DK]
            ol_o[here, pl.ds(h * DV, DV)] = out[:, DK:]
            step = dot(wu, to_end * k, "tn")
            eye = jnp.where(iota((DK, DK), 0) == iota((DK, DK), 1), 1.0, 0.0)
            step_o[u, :DK] = carry[BLK - 1 :, :] * eye - step[:DK]
            step_o[u, DK:] = step[DK:]
    for h in range(heads):
        ab = step_o[h * blocks]
        for c in range(1, blocks):
            nxt = step_o[h * blocks + c]
            ab = dot3(ab, nxt[:DK])
            ab_o_tail = nxt[DK:]
            ab = jnp.concatenate([ab[:DK], ab[DK:] + ab_o_tail], axis=0)
        ab_o[h] = ab.astype(ab_o.dtype)


def fwd_out(start, step, qe, ol, proj, gain, states_o, head_o, gated_o):
    rows = qe.shape[0]
    heads = start.shape[0]
    blocks = rows // BLK
    for h in range(heads):
        state = start[h]
        for c in range(blocks):
            u = h * blocks + c
            here = pl.ds(c * BLK, BLK)
            states_o[u] = state
            out = ol[here, pl.ds(h * DV, DV)] + dot(qe[here, pl.ds(h * DK, DK)], state, "nt")
            head_o[here, pl.ds(h * DV, DV)] = out
            gate = proj[here, pl.ds(h * MIXW + CONVW, DV)]
            scale = lax.rsqrt(jnp.mean(out * out, axis=1, keepdims=True) + 1e-05)
            gated_o[here, pl.ds(h * DV, DV)] = (out * scale * gain[...] * (gate * sigmoid(gate))).astype(BF16)
            if c + 1 < blocks:
                state = dot3(state, step[u, :DK, :]) + step[u, DK:, :]


def dot_left2(a, b, form="nn"):
    ah, al = halves(a)
    return dot(ah, b, form) + dot(al, b, form)


def bwd_head(d_gated, head_out, proj, gain, qe, step, d_out_o, d_gate_o, d_gain_o, y_o, inc_o):
    rows = qe.shape[0]
    blocks = rows // BLK
    heads = qe.shape[1] // DK
    total = jnp.zeros((1, DV), F32)
    for h in range(heads):
        cols = pl.ds(h * DV, DV)
        for c in range(blocks):
            here = pl.ds(c * BLK, BLK)
            dg, out = d_gated[here, cols], head_out[here, cols]
            gate = proj[here, pl.ds(h * MIXW + CONVW, DV)]
            s = sigmoid(gate)
            silu = gate * s
            scale = lax.rsqrt(jnp.mean(out * out, axis=1, keepdims=True) + 1e-05)
            n = out * scale
            dn = dg * n
            d_gate_o[here, cols] = (dn * gain[...] * (s * (1.0 + gate * (1.0 - s)))).astype(BF16)
            total = total + jnp.sum(dn * silu, axis=0, keepdims=True)
            f = dg * gain[...] * silu
            d_out = scale * f - out * (scale * scale * scale) * jnp.mean(f * out, axis=1, keepdims=True)
            d_out_o[here, cols] = d_out
            y_o[h * blocks + c] = dot(d_out, qe[here, pl.ds(h * DK, DK)], "tn")
        inc = y_o[h * blocks + blocks - 1]
        for c in range(blocks - 2, -1, -1):
            inc = y_o[h * blocks + c] + dot3(inc, step[h * blocks + c, :DK, :], "nt")
        inc_o[h] = inc.astype(inc_o.dtype)
    d_gain_o[...] = total


def bwd_mix(
    info, later, conv, dec, inv, wu, states, step, y, d_out, d_gate, rate, proj, halo, convw, dlog, dbias,
    d_proj_o, d_tail_o, d_edge_o, d_rate_o, d_convw_o, d_decay_o, xpad, dpad, dsend, cols_s, d_pre_o
):
    rows = d_out.shape[0]
    heads = later.shape[0]
    blocks = rows // BLK
    strength, log_decay, pre = rates(rate, dlog, dbias)
    valid = [valid_column(info, rows, KCONV - 1 - j) for j in range(KCONV)]
    for h in range(heads):
        grad = later[h]
        for c in range(blocks - 1, -1, -1):
            u = h * blocks + c
            dsend[u] = grad
            if c:
                grad = dot3(grad, step[u, :DK, :], "nt") + y[u]
    for c in range(blocks):
        keep, first, last, tri, strict = block_masks(info, c)
        here = pl.ds(c * BLK, BLK)
        for h in range(heads):
            u = h * blocks + c
            cv = conv[here, pl.ds(h * CONVW, CONVW)]
            sg = sigmoid(cv)
            qa, ka, va, rq, rk = vectors(cv)
            rqs = rq * DK**-0.5
            q, k = qa * rqs, ka * rk
            beta = strength[c * BLK : (c + 1) * BLK, h : h + 1]
            g = log_decay[c * BLK : (c + 1) * BLK, h : h + 1]
            carry, to_end = decays(g, first, last, tri)
            dm = dec[u]
            sc = dm * dot(q, k, "nt")
            gm = dm * dot(k, k, "nt") * strict
            state, d_end = states[u], dsend[u]
            do = d_out[here, pl.ds(h * DV, DV)]
            ks = dot(k, state, "nt")
            qs = dot(q, state, "nt")
            fresh = wu[u, :, DK:] - dot(wu[u, :, :DK], state, "nt")
            kd = to_end * k
            d_fresh = dot(sc, do, "tn") + dot(kd, d_end, "nt")
            d_rhs = dot(inv[u], d_fresh, "tn")
            d_low = -dot(d_rhs, fresh, "nt")
            d_sc = dot(do, fresh, "nt")
            d_val = beta * d_rhs
            ebar = d_low * gm
            d_beta = jnp.sum(d_rhs * (va - carry * ks), axis=1, keepdims=True) + jnp.sum(ebar, axis=1, keepdims=True)
            e = d_sc * sc + beta * ebar
            d_scd = d_sc * dm
            d_gm = (beta * d_low) * (dm * strict)
            d_kd = dot(fresh, d_end)
            d_q = dot(d_scd, k) + carry * dot(do, state)
            d_k = (
                dot(d_scd, q, "tn")
                - (beta * carry) * dot(d_rhs, state)
                + to_end * d_kd
                + dot(d_gm, k)
                + dot(d_gm, k, "tn")
            )
            hcol = carry * jnp.sum(do * qs - beta * d_rhs * ks, axis=1, keepdims=True)
            fcol = jnp.sum(kd * d_kd, axis=1, keepdims=True)
            tail = carry[BLK - 1 :, :] * jnp.sum(
                jnp.sum(state * d_end, axis=1, keepdims=True), axis=0, keepdims=True
            )
            lane = iota((BLK, DK), 1)
            d_g = (
                jnp.sum(dot_exact_left(tri, e, "tn") * strict, axis=1, keepdims=True)
                + dot_exact_left(tri, jnp.where(lane == 0, hcol, 0.0), "tn")[:, :1]
                + dot_exact_left(strict, jnp.where(lane == 0, fcol, 0.0))[:, :1]
                + tail
            )
            cols_s[here, h : h + 1] = d_g
            cols_s[here, heads + h : heads + h + 1] = d_beta
            d_qa = rqs * d_q - qa * (rqs * rq * rq * jnp.sum(d_q * qa, axis=1, keepdims=True))
            d_ka = rk * d_k - ka * (rk * rk * rk * jnp.sum(d_k * ka, axis=1, keepdims=True))
            d_act = jnp.concatenate([d_qa, d_ka, d_val], axis=1)
            d_pre_o[here, pl.ds(h * CONVW, CONVW)] = d_act * (sg * (1.0 + cv * (1.0 - sg)))
    d_g, d_beta = cols_s[:, :heads], cols_s[:, heads : 2 * heads]
    d_bias = -d_g * jnp.exp(dlog[...]) * sigmoid(pre)
    d_rate_o[:, :heads] = d_bias
    d_rate_o[:, heads:] = d_beta * strength * (1.0 - strength)
    d_decay_o[:, :heads] = jnp.sum(d_g * log_decay, axis=0, keepdims=True)
    d_decay_o[:, heads:] = jnp.sum(d_bias, axis=0, keepdims=True)
    for h in range(heads):
        src, dst = pl.ds(h * MIXW, CONVW), pl.ds(h * CONVW, CONVW)
        xpad[:PAD, :] = halo[:, dst]
        xpad[PAD:, :] = proj[:, src].astype(BF16).astype(F32)
        dpad[...] = jnp.zeros_like(dpad)
        d_conv = d_pre_o[:, dst]
        for j in range(KCONV):
            lo = PAD - (KCONV - 1) + j
            masked = d_conv * valid[j]
            d_convw_o[j : j + 1, dst] = jnp.sum(masked * xpad[lo : lo + rows, :], axis=0, keepdims=True)
            dpad[lo : lo + rows, :] += convw[j : j + 1, dst].astype(F32) * masked
        d_edge_o[:, dst] = dpad[:PAD, :]
        d_tail_o[:, dst] = dpad[rows - PAD :, :]
        d_proj_o[:, src] = dpad[PAD:, :].astype(BF16)
        d_proj_o[:, pl.ds(h * MIXW + CONVW, DV)] = d_gate[:, pl.ds(h * DV, DV)]


def call(kernel, outs, scratch, limit, *args, flops=2_000_000_000, nbytes=16_000_000):
    def spec(a):
        return SMEM if a.dtype == jnp.int32 else VMEM

    return pl.pallas_call(
        kernel,
        out_shape=outs,
        in_specs=[spec(a) for a in args],
        out_specs=[VMEM for _ in outs],
        scratch_shapes=scratch,
        compiler_params=pltpu.CompilerParams(vmem_limit_bytes=limit << 20),
        cost_estimate=pl.CostEstimate(flops=flops, bytes_accessed=nbytes, transcendentals=0),
    )(*args)


def sds(shape, dtype=F32):
    return jax.ShapeDtypeStruct(shape, dtype)
CHIPS = 4
LANES = 128


def cp(src, dst, send, recv, dev):
    return pltpu.make_async_remote_copy(
        src_ref=src, dst_ref=dst, send_sem=send, recv_sem=recv, device_id=dev, device_id_type=pl.DeviceIdType.MESH
    )


def greet(devices):
    barrier = pltpu.get_barrier_semaphore()
    for dev in devices:
        pl.semaphore_signal(barrier, inc=1, device_id=dev, device_id_type=pl.DeviceIdType.MESH)
    pl.semaphore_wait(barrier, len(devices))


def head_place():
    me = lax.axis_index("head")
    chip, core = me // 2, me % 2
    seq = lax.axis_index("seq")

    def dev(step, flip=False):
        c = lax.rem(chip + step, CHIPS)
        return (seq, c * 2 + (1 - core if flip else core))

    return me, chip, core, dev


def head_peers():
    dev = head_place()[3]
    return [dev(0, True)] + [dev(d) for d in range(1, CHIPS)]


def gather_over_head(x, o, ssem, rsem, lsem):
    rows = x.shape[0]
    me, chip, core, dev = head_place()

    def at(step, flip=False):
        return o.at[pl.ds(pl.multiple_of(dev(step, flip)[1] * rows, rows), rows)]

    own = pltpu.make_async_copy(x, at(0), lsem)
    own.start()
    out = [cp(x, at(0), ssem.at[d], rsem.at[d], dev(d)) for d in (1, 3, 2)]
    out.append(cp(x, at(0), ssem.at[0], rsem.at[0], dev(0, True)))
    for s in out:
        s.start()
    for d in (1, 3, 2):
        cp(x, at(CHIPS - d), ssem.at[d], rsem.at[d], dev(d)).wait_recv()
        fwd = cp(at(CHIPS - d), at(CHIPS - d), ssem.at[CHIPS + d], rsem.at[CHIPS + d], dev(0, True))
        fwd.start()
        out.append(fwd)
    own.wait()
    cp(x, at(0, True), ssem.at[0], rsem.at[0], dev(0, True)).wait_recv()
    for d in range(1, CHIPS):
        cp(x, at(CHIPS - d, True), ssem.at[CHIPS + d], rsem.at[CHIPS + d], dev(0, True)).wait_recv()
    for s in out:
        s.wait_send()


def reduce_over_head(x, total, pair, got, mid, ssem, rsem):
    rows = total.shape[0]
    me, chip, core, dev = head_place()
    partner = dev(0, True)

    def at(step, flip=False):
        return x.at[pl.ds(pl.multiple_of(dev(step, flip)[1] * rows, rows), rows)]

    order = (2, 1, 3, 0)
    first = [cp(at(d, True), pair.at[d], ssem.at[d], rsem.at[d], partner) for d in order]
    for s in first:
        s.start()
    second = []
    for s, d in zip(first, order):
        s.wait_recv()
        both = at(d)[...].astype(F32) + pair[d].astype(F32)
        if d:
            mid[d] = both.astype(BF16)
            t = cp(mid.at[d], got.at[d], ssem.at[CHIPS + d], rsem.at[CHIPS + d], dev(d))
            t.start()
            second.append(t)
        else:
            total[...] = both
    for s in (second[1], second[2], second[0]):
        s.wait_recv()
    total[...] = total[...] + ((got[1].astype(F32) + got[3].astype(F32)) + got[2].astype(F32))
    for s in first + second:
        s.wait_send()


def mean_scale(v):
    return lax.rsqrt(jnp.mean(v * v, axis=1, keepdims=True) + 1e-05)


def norm_back(v, gain, d_norm):
    r = mean_scale(v)
    e = d_norm * gain
    d_v = r * e - v * (r * r * r * jnp.mean(e * v, axis=1, keepdims=True))
    return d_v, jnp.sum(d_norm * v * r, axis=0, keepdims=True)


def mid_forward(x, tokens, gain, all_o, hidden_o, total, block, pair, got, mid, s1, r1, s2, r2, ls):
    greet(head_peers())
    reduce_over_head(x, total, pair, got, mid, s1, r1)
    hidden = tokens[...].astype(F32) + total[...]
    hidden_o[...] = hidden
    block[...] = (hidden * mean_scale(hidden) * gain[...]).astype(BF16)
    gather_over_head(block, all_o, s2, r2, ls)


def mid_backward(x, hidden, cot, gain, all_o, d_hidden_o, d_gain_o, total, block, pair, got, mid, s1, r1, s2, r2, ls):
    greet(head_peers())
    reduce_over_head(x, total, pair, got, mid, s1, r1)
    d_norm, d_gain = norm_back(hidden[...], gain[...], total[...])
    d_hidden = cot[...].astype(F32) + d_norm
    d_hidden_o[...] = d_hidden
    d_gain_o[...] = d_gain
    block[...] = d_hidden.astype(BF16)
    gather_over_head(block, all_o, s2, r2, ls)


def reach(kernel, outs, scratch, cid, limit, *args, anywhere=(), nbytes=12_000_000):
    return pl.pallas_call(
        kernel,
        out_shape=outs,
        in_specs=[pl.BlockSpec(memory_space=pl.ANY) if i in anywhere else VMEM for i in range(len(args))],
        out_specs=[VMEM for _ in outs],
        scratch_shapes=scratch,
        compiler_params=pltpu.CompilerParams(
            collective_id=cid, has_side_effects=True, vmem_limit_bytes=limit << 20
        ),
        cost_estimate=pl.CostEstimate(flops=0, bytes_accessed=nbytes, transcendentals=0),
    )(*args)


def sems(n):
    return pltpu.SemaphoreType.DMA((n,))


def reduce_scratch(rows, cols):
    return [pltpu.VMEM((CHIPS, rows, cols), BF16) for _ in range(3)] + [sems(2 * CHIPS), sems(2 * CHIPS)]


def gather_scratch():
    return [sems(2 * CHIPS), sems(2 * CHIPS), pltpu.SemaphoreType.DMA]


SIDE = 4


def seq_place():
    me = lax.axis_index("seq")
    z, y = me // SIDE, me % SIDE
    head = lax.axis_index("head")

    def dev(dz, dy):
        return (lax.rem(z + dz, SIDE) * SIDE + lax.rem(y + dy, SIDE), head)

    return me, z, y, dev


def side_peers():
    dev = seq_place()[3]
    return [dev(0, d) for d in range(1, SIDE)] + [dev(d, 0) for d in range(1, SIDE)]


def share(src, got, place, to, ssem, rsem):
    got[place] = src[...]
    out = [cp(src, got.at[place], ssem.at[d], rsem.at[d], to(d)) for d in range(1, SIDE)]
    for s in out:
        s.start()
    for d in range(1, SIDE):
        back = lax.rem(place + SIDE - d, SIDE)
        cp(src, got.at[back], ssem.at[d], rsem.at[d], to(d)).wait_recv()
    return out


def unit_top():
    return jnp.where(iota((DK + DV, DK), 0) == iota((DK + DV, DK), 1), 1.0, 0.0)


def add_low(pair, low):
    return jnp.concatenate([pair[:DK], pair[DK:] + low], axis=0)


def states_forward(ab, start_o, ga_o, ta_o, got1, tot, got2, s1, r1, s2, r2):
    me, z, y, dev = seq_place()
    heads = ab.shape[0]
    greet(side_peers())
    out = share(ab, got1, y, lambda d: dev(0, d), s1, r1)
    before = []
    for h in range(heads):
        whole = got1[0, h].astype(F32)
        prefix = jnp.where(y > 0, whole, unit_top())
        for j in range(1, SIDE):
            a, b = got1[j, h, :DK, :], got1[j, h, DK:, :].astype(F32)
            whole = add_low(dot_left2(whole, a), b)
            if j < SIDE - 1:
                prefix = jnp.where(y > j, whole, prefix)
        tot[h] = whole.astype(BF16)
        before.append(prefix)
        for j in range(SIDE):
            ga_o[j, h] = got1[j, h, :DK, :]
    out += share(tot, got2, z, lambda d: dev(d, 0), s2, r2)
    for h in range(heads):
        held = jnp.zeros((DV, DK), F32)
        for j in range(SIDE - 1):
            held = jnp.where(
                z > j, dot_left2(held, got2[j, h, :DK, :]) + got2[j, h, DK:, :].astype(F32), held
            )
        start_o[h] = dot3(held, before[h][:DK]) + before[h][DK:]
        for j in range(SIDE):
            ta_o[j, h] = got2[j, h, :DK, :]
    for s in out:
        s.wait_send()


def states_backward(inc, ga, ta, later_o, got1, tot, got2, s1, r1, s2, r2):
    me, z, y, dev = seq_place()
    heads = inc.shape[0]
    greet(side_peers())
    out = share(inc, got1, y, lambda d: dev(0, d), s1, r1)
    after = []
    for h in range(heads):
        whole = add_low(dot(unit_top(), ga[SIDE - 1, h], "nt"), got1[SIDE - 1, h].astype(F32))
        suffix = jnp.where(y < SIDE - 1, whole, unit_top())
        for j in range(SIDE - 2, -1, -1):
            whole = add_low(dot_left2(whole, ga[j, h], "nt"), got1[j, h].astype(F32))
            if j:
                suffix = jnp.where(y < j, whole, suffix)
        tot[h] = whole[DK:].astype(BF16)
        after.append(suffix)
    out += share(tot, got2, z, lambda d: dev(d, 0), s2, r2)
    for h in range(heads):
        held = jnp.zeros((DV, DK), F32)
        for j in range(SIDE - 1, 0, -1):
            held = jnp.where(z < j, dot_left2(held, ta[j, h], "nt") + got2[j, h].astype(F32), held)
        later_o[h] = dot3(held, after[h][:DK]) + after[h][DK:]
    for s in out:
        s.wait_send()


def pair_sends(x, pair, ssem, rsem, steps):
    rows = pair.shape[1]
    dev = head_place()[3]
    out = {}
    for d in steps:
        owner = dev(d, True)[1]
        src = x.at[pl.ds(pl.multiple_of(owner * rows, rows), rows)]
        out[d] = cp(src, pair.at[d], ssem.at[d], rsem.at[d], dev(0, True))
        out[d].start()
    return out


def chip_sends(x, first, total, pair, got, mid, ssem, rsem, steps):
    rows = pair.shape[1]
    dev = head_place()[3]
    out = {}
    for d in steps:
        first[d].wait_recv()
        owner = dev(d)[1]
        both = x[pl.ds(pl.multiple_of(owner * rows, rows), rows), :].astype(F32) + pair[d].astype(F32)
        if d:
            mid[d] = both.astype(BF16)
            out[d] = cp(mid.at[d], got.at[d], ssem.at[CHIPS + d], rsem.at[CHIPS + d], dev(d))
            out[d].start()
        else:
            total[...] = both
    return out


def chip_sum(second, total, got):
    for d in (1, 3, 2):
        second[d].wait_recv()
    return total[...] + ((got[1].astype(F32) + got[3].astype(F32)) + got[2].astype(F32))


FAR = (2, 1, 3, 0)


def finish(
    dproj, normed, w, d_rate, rate_w, d_tail, d_edge, feed, hidden, tokens, d_hidden, gain, convs, decay, g_feed, g_head,
    layer_o, d_tokens_o, g_mixer_o, gains_o, convs_o, rate_o,
    dp, wv, edge, g, got1, mid, got2, dn, ta, pa, ga, ma, tb, pb, gb, mb, gains, gbuf, sbuf, rbuf,
    es, er, ls, s1, r1, sa, ra, sb, rb, sg, rg, ss, rs
):
    me, z, y, dev = seq_place()
    head = lax.axis_index("head")
    heads, seqs = gbuf.shape[0], rbuf.shape[0]
    rows = dp.shape[0]
    part, half = g_mixer_o.shape[1], g_mixer_o.shape[2]
    across = [(me, lax.rem(head + d, heads)) for d in range(1, heads)]
    along = [(lax.rem(me + d, seqs), head) for d in range(1, seqs)]
    load_p = pltpu.make_async_copy(dproj, dp, ls.at[0])
    load_p.start()
    load_w = pltpu.make_async_copy(w, wv, ls.at[1])
    load_w.start()
    greet(across + along)
    back = cp(d_edge, edge, es, er, (lax.rem(me + seqs - 1, seqs), head))
    back.start()
    feed_one = pair_sends(feed, pa, sa, ra, FAR)
    load_p.wait()
    back.wait_recv()
    there = jnp.where(me < seqs - 1, edge[...], 0.0)
    tail = jnp.concatenate([d_tail[:PAD, :], d_tail[PAD:, :] + there], axis=0).astype(BF16)
    wide = half - DV
    for i in range(2):
        dp[rows - 2 * PAD :, pl.ds(i * half, wide)] = tail[:, i * wide : (i + 1) * wide]

    ways = (lambda a, b: dev(b, a), lambda a, b: dev(a, b))

    def piece(i, owner):
        return g.at[i, owner]

    first, second = {}, {}
    places = [(dz, dy) for dz in FAR for dy in FAR]
    for dz, dy in places:
        owner = dev(dz, dy)[0]
        left = normed[:, pl.ds(pl.multiple_of(owner * part, part), part)]
        for i in range(2):
            a, b = (dy, dz) if i == 0 else (dz, dy)
            g[i, owner] = dot(left, dp[:, i * half : (i + 1) * half], "tn").astype(BF16)
            if a:
                k = (i * SIDE + a) * SIDE + b
                first[i, a, b] = cp(piece(i, owner), got1.at[i, a, b], s1.at[k], r1.at[k], ways[i](a, 0))
                first[i, a, b].start()
    feed_two = chip_sends(feed, feed_one, ta, pa, ga, ma, sa, ra, FAR)
    rates_t = dot(d_rate[:, :PAD], normed[...], "tn")

    load_w.wait()
    low = rows // CHIPS
    hp = head_place()[3]
    dn_one = {}
    for d in FAR:
        chip = hp(d)[1] // 2
        here = pl.ds(pl.multiple_of(chip * low, low), low)
        dn[here, :] = (dot(dp[here, :], wv[...], "nt") + dot(d_rate[here, :], rate_w[...], "nt")).astype(BF16)
        dn_one.update(pair_sends(dn, pb, sb, rb, (d,)))
    dn_two = chip_sends(dn, dn_one, tb, pb, gb, mb, sb, rb, FAR)
    layer_o[...] = (hidden[...] + chip_sum(feed_two, ta, ga)).astype(BF16)
    d_norm, d_gain = norm_back(tokens[...].astype(F32), gain[...], chip_sum(dn_two, tb, gb))
    d_tokens_o[...] = d_hidden[...] + d_norm

    ng = gains.shape[0]
    n_row = D // LANES
    gains[...] = jnp.zeros_like(gains)
    for r in range(n_row):
        at = slice(r * LANES, (r + 1) * LANES)
        gains[r : r + 1, :] = d_gain[:, at]
        gains[n_row + r : n_row + r + 1, :] = g_feed[:, at]
    for r in range(DV // LANES):
        gains[2 * n_row + r : 2 * n_row + r + 1, :] = g_head[:, r * LANES : (r + 1) * LANES]
    gbuf[head] = gains[...]
    g_out = [cp(gains, gbuf.at[head], sg.at[d], rg.at[d], across[d - 1]) for d in range(1, heads)]
    for s in g_out:
        s.start()
    taps, wide_c = convs.shape
    c_row = wide_c // LANES
    nc = taps * c_row
    for j in range(seqs):
        for t in range(taps):
            for r in range(c_row):
                lo = ng + t * c_row + r
                if j == 0:
                    sbuf[0, lo : lo + 1, :] = convs[t : t + 1, r * LANES : (r + 1) * LANES]
        if j == 0:
            sbuf[0, ng + nc : ng + nc + PAD, :] = jnp.zeros((PAD, LANES), F32)
            sbuf[0, ng + nc : ng + nc + 1, :] = decay[...]
        else:
            sbuf[j, ng : ng + nc + PAD, :] = sbuf[0, ng : ng + nc + PAD, :]
        sbuf[j, ng + nc + PAD :, :] = rates_t[:, j * LANES : (j + 1) * LANES]
    for d in range(1, heads):
        cp(gains, gbuf.at[lax.rem(head + heads - d, heads)], sg.at[d], rg.at[d], across[d - 1]).wait_recv()
    total = gbuf[0]
    for i in range(1, heads):
        total = total + gbuf[i]
    for j in range(seqs):
        sbuf[j, :ng, :] = total
    rbuf[me] = sbuf[me]
    s_out = []
    for d in range(1, seqs):
        s = cp(sbuf.at[lax.rem(me + d, seqs)], rbuf.at[me], ss.at[d], rs.at[d], along[d - 1])
        s.start()
        s_out.append(s)

    for b in FAR:
        for i in range(2):
            for a in (1, 3, 2):
                first[i, a, b].wait_recv()
            mine = g[i, ways[i](0, b)[0]].astype(F32)
            both = mine + (
                (got1[i, 1, b].astype(F32) + got1[i, 3, b].astype(F32)) + got1[i, 2, b].astype(F32)
            )
            if b:
                mid[i, b] = both.astype(BF16)
                k = 2 * SIDE * SIDE + i * SIDE + b
                second[i, b] = cp(mid.at[i, b], got2.at[i, b], s1.at[k], r1.at[k], ways[i](0, b))
                second[i, b].start()
            else:
                g_mixer_o[i] = both
    for d in range(1, seqs):
        cp(sbuf.at[0], rbuf.at[lax.rem(me + seqs - d, seqs)], ss.at[d], rs.at[d], along[d - 1]).wait_recv()
    total = rbuf[0]
    for i in range(1, seqs):
        total = total + rbuf[i]
    gains_o[...] = total[:ng]
    convs_o[...] = total[ng : ng + nc + PAD]
    rate_o[...] = total[ng + nc + PAD :]
    for i in range(2):
        for b in (1, 3, 2):
            second[i, b].wait_recv()
        g_mixer_o[i] = g_mixer_o[i] + (
            (got2[i, 1].astype(F32) + got2[i, 3].astype(F32)) + got2[i, 2].astype(F32)
        )
    done = list(first.values()) + list(second.values()) + g_out + s_out + [back]
    done += list(feed_one.values()) + list(feed_two.values()) + list(dn_one.values()) + list(dn_two.values())
    for s in done:
        s.wait_send()


def weight_grads(d_gu, middle, gated, n2, cot, d_mixed, o):
    a, b = d_gu.shape[0], middle.shape[0]
    for lo, left, right in ((0, d_gu, n2), (a, middle, cot), (a + b, gated, d_mixed)):
        out = dot(left[...], right[...]).astype(BF16)
        n = left.shape[0]
        o[0, lo : lo + n] = out[:, :LANES]
        o[1, lo : lo + n] = out[:, LANES:]


def passed_along(shard, axis, by):
    length = lax.axis_size(axis)
    pairs = [(i, i + by) for i in range(length) if 0 <= i + by < length]
    return lax.ppermute(shard, axis, pairs)


def rms_scale(values, gain):
    return values * lax.rsqrt(jnp.mean(values * values, axis=-1, keepdims=True) + 1e-05) * gain


def local(
    tokens, mixer_gain, mixer_weight, rate_weight, conv_weight, decay_log, decay_bias, head_gain,
    output_weight, feed_gain, gate_up_weight, down_weight, doc_starts, cotangent,
):
    resid = tokens.astype(F32)
    normed = rms_scale(resid, mixer_gain).astype(BF16)
    gathered = lax.all_gather(normed, "head", axis=0, tiled=True)
    heads = mixer_weight.shape[1]
    gathered, cot_own, mixer_flat = lax.optimization_barrier(
        (gathered, cotangent, mixer_weight.reshape(D, heads * MIXW))
    )
    cot_rows = lax.all_gather(cot_own, "head", axis=0, tiled=True)
    rows = gathered.shape[0]
    blocks = rows // BLK
    units = heads * blocks
    seq = lax.axis_size("seq")
    projected = jnp.dot(gathered, mixer_flat, preferred_element_type=F32)
    rate_proj = jnp.einsum("td,dgh->tgh", gathered, rate_weight, preferred_element_type=F32).reshape(rows, 2 * heads)
    rim = projected[rows - PAD :].reshape(PAD, heads, MIXW)[:, :, :CONVW].reshape(PAD, heads * CONVW).astype(BF16)
    halo = passed_along(rim, "seq", 1).astype(F32)
    convw = conv_weight.reshape(KCONV, heads * CONVW)
    info = jnp.concatenate(
        [doc_starts, jnp.stack([lax.axis_index("seq") * rows, lax.axis_index("seq")]).astype(jnp.int32)]
    )
    dlog, dbias = decay_log.reshape(1, heads), decay_bias.reshape(1, heads)
    gain = head_gain.reshape(1, DV)

    conv, dec, inv, wu, qe, ol, step, ab = call(
        fwd_prep,
        [
            sds((rows, heads * CONVW)), sds((units, BLK, BLK)), sds((units, BLK, BLK), BF16),
            sds((units, BLK, DK + DV)), sds((rows, heads * DK)), sds((rows, heads * DV)),
            sds((units, DK + DV, DK)), sds((heads, DK + DV, DK), BF16),
        ],
        [pltpu.VMEM((PAD + rows, CONVW), F32)],
        56, info, projected, halo, rate_proj, convw, dlog, dbias,
    )
    start, ga, ta = reach(
        states_forward,
        [sds((heads, DV, DK)), sds((SIDE, heads, DK, DK), BF16), sds((SIDE, heads, DK, DK), BF16)],
        [
            pltpu.VMEM((SIDE, heads, DK + DV, DK), BF16), pltpu.VMEM((heads, DK + DV, DK), BF16),
            pltpu.VMEM((SIDE, heads, DK + DV, DK), BF16), sems(SIDE), sems(SIDE), sems(SIDE), sems(SIDE),
        ],
        1, 40, ab,
    )
    states, head_out, gated = call(
        fwd_out,
        [sds((units, DV, DK)), sds((rows, heads * DV)), sds((rows, heads * DV), BF16)],
        [], 48, start, step, qe, ol, projected, gain,
    )
    out_flat = output_weight.reshape(heads * DV, D)
    own = tokens.shape[0]
    mixed = jnp.dot(gated, out_flat, preferred_element_type=F32).astype(BF16)
    feed_row = feed_gain.reshape(1, D)
    gathered_two, hidden = reach(
        mid_forward,
        [sds((rows, D), BF16), sds((own, D))],
        [pltpu.VMEM((own, D), F32), pltpu.VMEM((own, D), BF16)] + reduce_scratch(own, D) + gather_scratch(),
        2, 48, mixed, tokens, feed_row,
    )
    hid = down_weight.shape[0]
    gu_t = gate_up_weight.transpose(1, 2, 0).reshape(2 * hid, D)
    by_last = (((1,), (1,)), ((), ()))
    by_first = (((0,), (0,)), ((), ()))
    d_middle = lax.dot_general(down_weight, cot_rows, by_last, preferred_element_type=F32)
    gate_up = lax.dot_general(gu_t, gathered_two, by_last, preferred_element_type=F32)
    gate, up = gate_up[:hid], gate_up[hid:]
    s = jax.nn.sigmoid(gate)
    middle = (gate * s * up).astype(BF16)
    d_gate_up = jnp.concatenate([d_middle * up * (s * (1.0 + gate * (1.0 - s))), d_middle * gate * s]).astype(BF16)
    d_two = lax.dot_general(d_gate_up, gu_t, by_first, preferred_element_type=F32).astype(BF16)
    d_mixed, d_hidden, g_feed_gain = reach(
        mid_backward,
        [sds((rows, D), BF16), sds((own, D)), sds((1, D))],
        [pltpu.VMEM((own, D), F32), pltpu.VMEM((own, D), BF16)] + reduce_scratch(own, D) + gather_scratch(),
        3, 48, d_two, hidden, cotangent, feed_row,
    )
    wide = 3 * hid + heads * DV
    right = pl.BlockSpec((rows, 2 * LANES), lambda j: (0, j))

    def whole(a):
        return pl.BlockSpec(a.shape, lambda j: (0, 0))

    gated_t = gated.T
    grads = pl.pallas_call(
        weight_grads,
        grid=(seq // 2,),
        out_shape=sds((seq, wide, LANES), BF16),
        in_specs=[whole(d_gate_up), whole(middle), whole(gated_t), right, right, right],
        out_specs=pl.BlockSpec((2, wide, LANES), lambda j: (j, 0, 0)),
        compiler_params=pltpu.CompilerParams(vmem_limit_bytes=48 << 20),
        cost_estimate=pl.CostEstimate(flops=2 * wide * rows * D, bytes_accessed=24_000_000, transcendentals=0),
    )(d_gate_up, middle, gated_t, gathered_two, cot_rows, d_mixed)
    d_mixed, grads, middle = lax.optimization_barrier((d_mixed, grads, middle))
    feed = lax.dot_general(middle, down_weight, by_first, preferred_element_type=F32).astype(BF16)
    grads = lax.psum_scatter(grads.reshape(seq * wide, LANES), "seq", scatter_dimension=0, tiled=True).astype(F32)
    grad_gate_up = grads[: 2 * hid].reshape(2, hid, LANES).transpose(2, 0, 1)
    grad_down = grads[2 * hid : 3 * hid]
    grad_output = grads[3 * hid :].reshape(heads, DV, LANES)
    d_gated = jnp.einsum("td,vd->tv", d_mixed, out_flat, preferred_element_type=F32)
    d_out, d_gate, g_head_gain, y, inc = call(
        bwd_head,
        [
            sds((rows, heads * DV)), sds((rows, heads * DV), BF16), sds((1, DV)),
            sds((units, DV, DK)), sds((heads, DV, DK), BF16),
        ],
        [], 48, d_gated, head_out, projected, gain, qe, step,
    )
    (later,) = reach(
        states_backward,
        [sds((heads, DV, DK))],
        [
            pltpu.VMEM((SIDE, heads, DV, DK), BF16), pltpu.VMEM((heads, DV, DK), BF16),
            pltpu.VMEM((SIDE, heads, DV, DK), BF16), sems(SIDE), sems(SIDE), sems(SIDE), sems(SIDE),
        ],
        4, 40, inc, ga, ta,
    )
    d_projected, d_tail, d_edge, d_rate, d_convw, d_decay = call(
        bwd_mix,
        [
            sds((rows, heads * MIXW), BF16), sds((2 * PAD, heads * CONVW)), sds((PAD, heads * CONVW)),
            sds((rows, 2 * heads)), sds((KCONV, heads * CONVW)), sds((1, 2 * heads)),
        ],
        [
            pltpu.VMEM((PAD + rows, CONVW), F32), pltpu.VMEM((PAD + rows, CONVW), F32),
            pltpu.VMEM((units, DV, DK), F32), pltpu.VMEM((rows, DK), F32), pltpu.VMEM((rows, heads * CONVW), F32),
        ],
        60, info, later, conv, dec, inv, wu, states, step, y, d_out, d_gate, rate_proj, projected, halo, convw,
        dlog, dbias,
    )
    part, half, n_head = D // seq, MIXW, lax.axis_size("head")
    d_rate_low = jnp.pad(d_rate.astype(BF16), ((0, 0), (0, LANES - 2 * heads)))
    rate_pad = jnp.pad(rate_weight.reshape(D, 2 * heads), ((0, 0), (0, LANES - 2 * heads)))
    d_decay = jnp.pad(d_decay, ((0, 0), (0, LANES - 2 * heads)))
    n_gain, n_conv = 40, KCONV * heads * CONVW // LANES + PAD
    small = n_gain + n_conv + PAD
    layer_out, grad_tokens, grad_mixer, gains, convs, rate_own = reach(
        finish,
        [
            sds((own, D), BF16), sds((own, D)), sds((2, part, half)), sds((n_gain, LANES)), sds((n_conv, LANES)),
            sds((PAD, LANES)),
        ],
        [
            pltpu.VMEM((rows, heads * MIXW), BF16), pltpu.VMEM((D, heads * MIXW), BF16),
            pltpu.VMEM((PAD, heads * CONVW), F32), pltpu.VMEM((2, seq, part, half), BF16),
            pltpu.VMEM((2, SIDE, SIDE, part, half), BF16), pltpu.VMEM((2, SIDE, part, half), BF16),
            pltpu.VMEM((2, SIDE, part, half), BF16), pltpu.VMEM((rows, D), BF16),
        ]
        + 2 * ([pltpu.VMEM((own, D), F32)] + [pltpu.VMEM((CHIPS, own, D), BF16) for _ in range(3)])
        + [
            pltpu.VMEM((n_gain, LANES), F32), pltpu.VMEM((n_head, n_gain, LANES), F32),
            pltpu.VMEM((seq, small, LANES), F32), pltpu.VMEM((seq, small, LANES), F32),
            pltpu.SemaphoreType.DMA, pltpu.SemaphoreType.DMA, sems(2),
            sems(2 * SIDE * SIDE + 2 * SIDE), sems(2 * SIDE * SIDE + 2 * SIDE),
            sems(2 * CHIPS), sems(2 * CHIPS), sems(2 * CHIPS), sems(2 * CHIPS),
            sems(n_head), sems(n_head), sems(seq), sems(seq),
        ],
        5, 62, d_projected, gathered, mixer_flat, d_rate_low, rate_pad, d_tail, d_edge, feed, hidden, tokens,
        d_hidden, mixer_gain.reshape(1, D), d_convw, d_decay, g_feed_gain, g_head_gain,
        anywhere=(0, 2), nbytes=40_000_000,
    )
    grad_mixer = grad_mixer.transpose(1, 0, 2)
    gains, convs = gains.reshape(-1), convs.reshape(-1)
    grad_mixer_gain, grad_feed_gain, grad_head_gain = gains[:D], gains[D : 2 * D], gains[2 * D : 2 * D + DV]
    n = KCONV * heads * CONVW
    grad_conv = convs[:n].reshape(KCONV, heads, CONVW)
    grad_decay_log, grad_decay_bias = convs[n : n + heads], convs[n + heads : n + 2 * heads]
    grad_rate = rate_own[: 2 * heads].reshape(2, heads, part).transpose(2, 0, 1)
    return (
        layer_out, grad_tokens, grad_mixer_gain, grad_mixer, grad_rate, grad_conv, grad_decay_log, grad_decay_bias,
        grad_head_gain, grad_output, grad_feed_gain, grad_gate_up, grad_down,
    )


def solution(mesh):
    rows = P(("seq", "head"), None)
    return jax.shard_map(
        local,
        mesh=mesh,
        in_specs=(
            rows, P(), P(None, "head", None), P(None, None, "head"), P(None, "head", None), P("head"), P("head"),
            P(), P("head", None, None), P(), P(None, None, "head"), P("head", None), P(), rows,
        ),
        out_specs=(
            rows, rows, P(), P("seq", "head", None), P("seq", None, "head"), P(None, "head", None), P("head"),
            P("head"), P(), P("head", None, "seq"), P(), P("seq", None, "head"), P("head", "seq"),
        ),
        check_vma=False,
    )
```

```python
import functools

import jax
import jax.numpy as jnp
from jax import lax
from jax.experimental import pallas as pl
from jax.experimental.pallas import tpu as pltpu
from jax.sharding import PartitionSpec as P

D = 2048
DK = 128
DV = 256
KCONV = 4
MIXW = 768
CONVW = 512
NB = 4
BLK = 256
PAD = 8
F32 = jnp.float32
BF16 = jnp.bfloat16

VMEM = pl.BlockSpec(memory_space=pltpu.VMEM)
SMEM = pl.BlockSpec(memory_space=pltpu.SMEM)


def dot(a, b, form="nn"):
    dims = {"nn": ((1,), (0,)), "nt": ((1,), (1,)), "tn": ((0,), (0,))}[form]
    return lax.dot_general(a.astype(BF16), b.astype(BF16), (dims, ((), ())), preferred_element_type=F32)


def halves(a):
    hi = a.astype(BF16)
    return hi, (a - hi.astype(F32)).astype(BF16)


def dot3(a, b, form="nn"):
    ah, al = halves(a)
    bh, bl = halves(b)
    return dot(ah, bh, form) + (dot(ah, bl, form) + dot(al, bh, form))


def dot_exact_left(a, b, form="nn"):
    b1, rest = halves(b)
    rest = b - b1.astype(F32)
    b2 = rest.astype(BF16)
    b3 = (rest - b2.astype(F32)).astype(BF16)
    return dot(a, b1, form) + (dot(a, b2, form) + dot(a, b3, form))


def iota(shape, axis):
    return lax.broadcasted_iota(jnp.int32, shape, axis)


def doc_of(info, pos):
    count = jnp.zeros(pos.shape, jnp.int32)
    for i in range(NB):
        count = count + jnp.where(pos >= info[i], 1, 0)
    return jnp.where(pos < 0, -1, count)


def sigmoid(v):
    return 1.0 / (1.0 + jnp.exp(-v))


def softplus(v):
    return jnp.maximum(v, 0.0) + jnp.log1p(jnp.exp(-jnp.abs(v)))


def unit_lower_inverse(low):
    n = low.shape[0]
    row, col = iota((n, n), 0), iota((n, n), 1)
    eye = jnp.where(row == col, 1.0, 0.0)

    def same(b):
        return row // b == col // b

    x = jnp.where(same(8), -low, 0.0)
    inv = eye + x
    x = dot3(x, x)
    inv = inv + dot3(inv, x)
    x = dot3(x, x)
    inv = inv + dot3(inv, x)
    b = 8
    while b < n:
        off = jnp.where(same(2 * b) & jnp.logical_not(same(b)), low, 0.0)
        inv = inv - dot3(inv, dot3(off, inv))
        b *= 2
    return inv


def valid_column(info, rows, back):
    pos = info[NB] + iota((rows, 1), 0)
    return jnp.where(doc_of(info, pos) == doc_of(info, pos - back), 1.0, 0.0)


def vectors(conv):
    act = conv * sigmoid(conv)
    qa, ka, va = act[:, :DK], act[:, DK : 2 * DK], act[:, 2 * DK :]
    rq = lax.rsqrt(jnp.sum(qa * qa, axis=1, keepdims=True) + 1e-06)
    rk = lax.rsqrt(jnp.sum(ka * ka, axis=1, keepdims=True) + 1e-06)
    return qa, ka, va, rq, rk


def rates(rate_ref, dlog_ref, dbias_ref):
    heads = dlog_ref.shape[1]
    pre = rate_ref[:, :heads] + dbias_ref[...]
    log_decay = -jnp.exp(dlog_ref[...]) * softplus(pre)
    return sigmoid(rate_ref[:, heads:]), log_decay, pre


def block_masks(info, c):
    row, col = iota((BLK, BLK), 0), iota((BLK, BLK), 1)
    base = info[NB] + c * BLK
    docs_r, docs_c = doc_of(info, base + row), doc_of(info, base + col)
    keep = (docs_r == docs_c) & (col <= row)
    column = doc_of(info, base + iota((BLK, 1), 0))
    first = jnp.where(column == doc_of(info, base - 1 + iota((BLK, 1), 0) * 0), 1.0, 0.0)
    last = jnp.where(column == doc_of(info, base + BLK - 1 + iota((BLK, 1), 0) * 0), 1.0, 0.0)
    tri = jnp.where(col <= row, 1.0, 0.0)
    strict = jnp.where(col < row, 1.0, 0.0)
    return keep, first, last, tri, strict


def decays(g, first, last, tri):
    cum = dot_exact_left(tri, jnp.broadcast_to(g, (BLK, DK)))[:, :1]
    carry = first * jnp.exp(cum)
    to_end = last * jnp.exp(cum[BLK - 1 :, :] - cum)
    return carry, to_end


def fwd_prep(info, proj, halo, rate, convw, dlog, dbias, conv_o, dec_o, inv_o, wu_o, qe_o, ol_o, step_o, ab_o, xpad):
    rows = proj.shape[0]
    heads = dlog.shape[1]
    blocks = rows // BLK
    strength, log_decay, _ = rates(rate, dlog, dbias)
    valid = [valid_column(info, rows, KCONV - 1 - j) for j in range(KCONV)]
    for h in range(heads):
        src, dst = pl.ds(h * MIXW, CONVW), pl.ds(h * CONVW, CONVW)
        xpad[:PAD, :] = halo[:, dst]
        xpad[PAD:, :] = proj[:, src].astype(BF16).astype(F32)
        conv = jnp.zeros((rows, CONVW), F32)
        for j in range(KCONV):
            lo = PAD - (KCONV - 1) + j
            conv = conv + convw[j : j + 1, dst].astype(F32) * xpad[lo : lo + rows, :] * valid[j]
        conv_o[:, dst] = conv
    for c in range(blocks):
        keep, first, last, tri, strict = block_masks(info, c)
        here = pl.ds(c * BLK, BLK)
        for h in range(heads):
            qa, ka, va, rq, rk = vectors(conv_o[here, pl.ds(h * CONVW, CONVW)])
            q, k = qa * (rq * DK**-0.5), ka * rk
            beta = strength[c * BLK : (c + 1) * BLK, h : h + 1]
            g = log_decay[c * BLK : (c + 1) * BLK, h : h + 1]
            spread = dot_exact_left(tri, g * strict)
            dec = jnp.where(keep, jnp.exp(jnp.where(keep, spread, 0.0)), 0.0)
            carry, to_end = decays(g, first, last, tri)
            low = strict * (beta * dec * dot(k, k, "nt"))
            inv = unit_lower_inverse(low)
            u = h * blocks + c
            dec_o[u] = dec
            inv_o[u] = inv.astype(BF16)
            rhs = jnp.concatenate([(beta * carry) * k, beta * va], axis=1)
            wu = dot(inv, rhs)
            wu_o[u] = wu
            out = dot(dec * dot(q, k, "nt"), wu)
            qe_o[here, pl.ds(h * DK, DK)] = carry * q - out[:, :DK]
            ol_o[here, pl.ds(h * DV, DV)] = out[:, DK:]
            step = dot(wu, to_end * k, "tn")
            eye = jnp.where(iota((DK, DK), 0) == iota((DK, DK), 1), 1.0, 0.0)
            step_o[u, :DK] = carry[BLK - 1 :, :] * eye - step[:DK]
            step_o[u, DK:] = step[DK:]
    for h in range(heads):
        ab = step_o[h * blocks]
        for c in range(1, blocks):
            nxt = step_o[h * blocks + c]
            ab = dot3(ab, nxt[:DK])
            ab_o_tail = nxt[DK:]
            ab = jnp.concatenate([ab[:DK], ab[DK:] + ab_o_tail], axis=0)
        ab_o[h] = ab.astype(ab_o.dtype)


def fwd_out(start, step, qe, ol, proj, gain, states_o, head_o, gated_o):
    rows = qe.shape[0]
    heads = start.shape[0]
    blocks = rows // BLK
    for h in range(heads):
        state = start[h]
        for c in range(blocks):
            u = h * blocks + c
            here = pl.ds(c * BLK, BLK)
            states_o[u] = state
            out = ol[here, pl.ds(h * DV, DV)] + dot(qe[here, pl.ds(h * DK, DK)], state, "nt")
            head_o[here, pl.ds(h * DV, DV)] = out
            gate = proj[here, pl.ds(h * MIXW + CONVW, DV)]
            scale = lax.rsqrt(jnp.mean(out * out, axis=1, keepdims=True) + 1e-05)
            gated_o[here, pl.ds(h * DV, DV)] = (out * scale * gain[...] * (gate * sigmoid(gate))).astype(BF16)
            if c + 1 < blocks:
                state = dot3(state, step[u, :DK, :]) + step[u, DK:, :]


def dot_left2(a, b, form="nn"):
    ah, al = halves(a)
    return dot(ah, b, form) + dot(al, b, form)


def bwd_head(d_gated, head_out, proj, gain, qe, step, d_out_o, d_gate_o, d_gain_o, y_o, inc_o):
    rows = qe.shape[0]
    blocks = rows // BLK
    heads = qe.shape[1] // DK
    total = jnp.zeros((1, DV), F32)
    for h in range(heads):
        cols = pl.ds(h * DV, DV)
        for c in range(blocks):
            here = pl.ds(c * BLK, BLK)
            dg, out = d_gated[here, cols], head_out[here, cols]
            gate = proj[here, pl.ds(h * MIXW + CONVW, DV)]
            s = sigmoid(gate)
            silu = gate * s
            scale = lax.rsqrt(jnp.mean(out * out, axis=1, keepdims=True) + 1e-05)
            n = out * scale
            dn = dg * n
            d_gate_o[here, cols] = (dn * gain[...] * (s * (1.0 + gate * (1.0 - s)))).astype(BF16)
            total = total + jnp.sum(dn * silu, axis=0, keepdims=True)
            f = dg * gain[...] * silu
            d_out = scale * f - out * (scale * scale * scale) * jnp.mean(f * out, axis=1, keepdims=True)
            d_out_o[here, cols] = d_out
            y_o[h * blocks + c] = dot(d_out, qe[here, pl.ds(h * DK, DK)], "tn")
        inc = y_o[h * blocks + blocks - 1]
        for c in range(blocks - 2, -1, -1):
            inc = y_o[h * blocks + c] + dot3(inc, step[h * blocks + c, :DK, :], "nt")
        inc_o[h] = inc.astype(inc_o.dtype)
    d_gain_o[...] = total


def bwd_mix(
    info, later, conv, dec, inv, wu, states, step, y, d_out, d_gate, rate, proj, halo, convw, dlog, dbias, g_down, g_out,
    d_proj_o, d_tail_o, d_edge_o, d_rate_o, d_convw_o, d_decay_o, s_down_o, s_out_o,
    xpad, dpad, dsend, cols_s, d_pre_o, relay_d, relay_o, got_d, got_o, s1, r1
):
    greet(side_peers())
    grads = (g_down, g_out)
    spread = Spread(
        lambda i, owner: grads[i].at[owner], lambda i, b: (relay_d, relay_o)[i].at[b],
        lambda i, s, b: (got_d, got_o)[i].at[s, b], s1, r1,
    )
    for place in PLACES:
        spread.ready(*place)
    rows = d_out.shape[0]
    heads = later.shape[0]
    blocks = rows // BLK
    strength, log_decay, pre = rates(rate, dlog, dbias)
    valid = [valid_column(info, rows, KCONV - 1 - j) for j in range(KCONV)]
    for h in range(heads):
        grad = later[h]
        for c in range(blocks - 1, -1, -1):
            u = h * blocks + c
            dsend[u] = grad
            if c:
                grad = dot3(grad, step[u, :DK, :], "nt") + y[u]
    for c in range(blocks):
        keep, first, last, tri, strict = block_masks(info, c)
        here = pl.ds(c * BLK, BLK)
        for h in range(heads):
            u = h * blocks + c
            cv = conv[here, pl.ds(h * CONVW, CONVW)]
            sg = sigmoid(cv)
            qa, ka, va, rq, rk = vectors(cv)
            rqs = rq * DK**-0.5
            q, k = qa * rqs, ka * rk
            beta = strength[c * BLK : (c + 1) * BLK, h : h + 1]
            g = log_decay[c * BLK : (c + 1) * BLK, h : h + 1]
            carry, to_end = decays(g, first, last, tri)
            dm = dec[u]
            sc = dm * dot(q, k, "nt")
            gm = dm * dot(k, k, "nt") * strict
            state, d_end = states[u], dsend[u]
            do = d_out[here, pl.ds(h * DV, DV)]
            ks = dot(k, state, "nt")
            qs = dot(q, state, "nt")
            fresh = wu[u, :, DK:] - dot(wu[u, :, :DK], state, "nt")
            kd = to_end * k
            d_fresh = dot(sc, do, "tn") + dot(kd, d_end, "nt")
            d_rhs = dot(inv[u], d_fresh, "tn")
            d_low = -dot(d_rhs, fresh, "nt")
            d_sc = dot(do, fresh, "nt")
            d_val = beta * d_rhs
            ebar = d_low * gm
            d_beta = jnp.sum(d_rhs * (va - carry * ks), axis=1, keepdims=True) + jnp.sum(ebar, axis=1, keepdims=True)
            e = d_sc * sc + beta * ebar
            d_scd = d_sc * dm
            d_gm = (beta * d_low) * (dm * strict)
            d_kd = dot(fresh, d_end)
            d_q = dot(d_scd, k) + carry * dot(do, state)
            d_k = (
                dot(d_scd, q, "tn")
                - (beta * carry) * dot(d_rhs, state)
                + to_end * d_kd
                + dot(d_gm, k)
                + dot(d_gm, k, "tn")
            )
            hcol = carry * jnp.sum(do * qs - beta * d_rhs * ks, axis=1, keepdims=True)
            fcol = jnp.sum(kd * d_kd, axis=1, keepdims=True)
            tail = carry[BLK - 1 :, :] * jnp.sum(
                jnp.sum(state * d_end, axis=1, keepdims=True), axis=0, keepdims=True
            )
            lane = iota((BLK, DK), 1)
            d_g = (
                jnp.sum(dot_exact_left(tri, e, "tn") * strict, axis=1, keepdims=True)
                + dot_exact_left(tri, jnp.where(lane == 0, hcol, 0.0), "tn")[:, :1]
                + dot_exact_left(strict, jnp.where(lane == 0, fcol, 0.0))[:, :1]
                + tail
            )
            cols_s[here, h : h + 1] = d_g
            cols_s[here, heads + h : heads + h + 1] = d_beta
            d_qa = rqs * d_q - qa * (rqs * rq * rq * jnp.sum(d_q * qa, axis=1, keepdims=True))
            d_ka = rk * d_k - ka * (rk * rk * rk * jnp.sum(d_k * ka, axis=1, keepdims=True))
            d_act = jnp.concatenate([d_qa, d_ka, d_val], axis=1)
            d_pre_o[here, pl.ds(h * CONVW, CONVW)] = d_act * (sg * (1.0 + cv * (1.0 - sg)))
            if h == 1:
                spread.relays(c)
    d_g, d_beta = cols_s[:, :heads], cols_s[:, heads : 2 * heads]
    d_bias = -d_g * jnp.exp(dlog[...]) * sigmoid(pre)
    d_rate_o[:, :heads] = d_bias
    d_rate_o[:, heads:] = d_beta * strength * (1.0 - strength)
    d_decay_o[:, :heads] = jnp.sum(d_g * log_decay, axis=0, keepdims=True)
    d_decay_o[:, heads:] = jnp.sum(d_bias, axis=0, keepdims=True)
    for h in range(heads):
        src, dst = pl.ds(h * MIXW, CONVW), pl.ds(h * CONVW, CONVW)
        xpad[:PAD, :] = halo[:, dst]
        xpad[PAD:, :] = proj[:, src].astype(BF16).astype(F32)
        dpad[...] = jnp.zeros_like(dpad)
        d_conv = d_pre_o[:, dst]
        for j in range(KCONV):
            lo = PAD - (KCONV - 1) + j
            masked = d_conv * valid[j]
            d_convw_o[j : j + 1, dst] = jnp.sum(masked * xpad[lo : lo + rows, :], axis=0, keepdims=True)
            dpad[lo : lo + rows, :] += convw[j : j + 1, dst].astype(F32) * masked
        d_edge_o[:, dst] = dpad[:PAD, :]
        d_tail_o[:, dst] = dpad[rows - PAD :, :]
        d_proj_o[:, src] = dpad[PAD:, :].astype(BF16)
        d_proj_o[:, pl.ds(h * MIXW + CONVW, DV)] = d_gate[:, pl.ds(h * DV, DV)]
    for i, o in ((0, s_down_o), (1, s_out_o)):
        for b in FAR:
            o[b] = spread.total(i, b).astype(BF16)
    spread.end()


def call(kernel, outs, scratch, limit, *args, flops=2_000_000_000, nbytes=16_000_000):
    def spec(a):
        return SMEM if a.dtype == jnp.int32 else VMEM

    return pl.pallas_call(
        kernel,
        out_shape=outs,
        in_specs=[spec(a) for a in args],
        out_specs=[VMEM for _ in outs],
        scratch_shapes=scratch,
        compiler_params=pltpu.CompilerParams(vmem_limit_bytes=limit << 20),
        cost_estimate=pl.CostEstimate(flops=flops, bytes_accessed=nbytes, transcendentals=0),
    )(*args)


def sds(shape, dtype=F32):
    return jax.ShapeDtypeStruct(shape, dtype)
CHIPS = 4
LANES = 128


def cp(src, dst, send, recv, dev):
    return pltpu.make_async_remote_copy(
        src_ref=src, dst_ref=dst, send_sem=send, recv_sem=recv, device_id=dev, device_id_type=pl.DeviceIdType.MESH
    )


def greet(devices):
    barrier = pltpu.get_barrier_semaphore()
    for dev in devices:
        pl.semaphore_signal(barrier, inc=1, device_id=dev, device_id_type=pl.DeviceIdType.MESH)
    pl.semaphore_wait(barrier, len(devices))


def head_place():
    me = lax.axis_index("head")
    chip, core = me // 2, me % 2
    seq = lax.axis_index("seq")

    def dev(step, flip=False):
        c = lax.rem(chip + step, CHIPS)
        return (seq, c * 2 + (1 - core if flip else core))

    return me, chip, core, dev


def head_peers():
    dev = head_place()[3]
    return [dev(0, True)] + [dev(d) for d in range(1, CHIPS)]


def head_rows(o, rows, step, flip=False):
    owner = head_place()[3](step, flip)[1]
    return o.at[pl.ds(pl.multiple_of(owner * rows, rows), rows)]


def gather_start(x, o, ssem, rsem, lsem):
    rows = x.shape[0]
    dev = head_place()[3]
    pltpu.make_async_copy(x, head_rows(o, rows, 0), lsem).start()
    out = [cp(x, head_rows(o, rows, 0), ssem.at[d], rsem.at[d], dev(d)) for d in (2, 1, 3)]
    out.append(cp(x, head_rows(o, rows, 0), ssem.at[0], rsem.at[0], dev(0, True)))
    for s in out:
        s.start()
    return out


def gather_forward(x, o, ssem, rsem):
    rows = x.shape[0]
    dev = head_place()[3]
    out = []
    for d in (1, 3, 2):
        there = head_rows(o, rows, CHIPS - d)
        cp(x, there, ssem.at[d], rsem.at[d], dev(d)).wait_recv()
        fwd = cp(there, there, ssem.at[CHIPS + d], rsem.at[CHIPS + d], dev(0, True))
        fwd.start()
        out.append(fwd)
    return out


def gather_end(x, o, ssem, rsem, lsem, sent):
    rows = x.shape[0]
    dev = head_place()[3]
    pltpu.make_async_copy(x, head_rows(o, rows, 0), lsem).wait()
    cp(x, head_rows(o, rows, 0, True), ssem.at[0], rsem.at[0], dev(0, True)).wait_recv()
    for d in range(1, CHIPS):
        there = head_rows(o, rows, CHIPS - d, True)
        cp(x, there, ssem.at[CHIPS + d], rsem.at[CHIPS + d], dev(0, True)).wait_recv()
    for s in sent:
        s.wait_send()


def gather_over_head(x, o, ssem, rsem, lsem):
    sent = gather_start(x, o, ssem, rsem, lsem)
    sent += gather_forward(x, o, ssem, rsem)
    gather_end(x, o, ssem, rsem, lsem, sent)


def reduce_over_head(x, total, pair, got, mid, ssem, rsem):
    rows = total.shape[0]
    me, chip, core, dev = head_place()
    partner = dev(0, True)

    def at(step, flip=False):
        return x.at[pl.ds(pl.multiple_of(dev(step, flip)[1] * rows, rows), rows)]

    order = (2, 1, 3, 0)
    first = [cp(at(d, True), pair.at[d], ssem.at[d], rsem.at[d], partner) for d in order]
    for s in first:
        s.start()
    second = []
    for s, d in zip(first, order):
        s.wait_recv()
        both = at(d)[...].astype(F32) + pair[d].astype(F32)
        if d:
            mid[d] = both.astype(BF16)
            t = cp(mid.at[d], got.at[d], ssem.at[CHIPS + d], rsem.at[CHIPS + d], dev(d))
            t.start()
            second.append(t)
        else:
            total[...] = both
    for s in (second[1], second[2], second[0]):
        s.wait_recv()
    total[...] = total[...] + ((got[1].astype(F32) + got[3].astype(F32)) + got[2].astype(F32))
    for s in first + second:
        s.wait_send()


def mean_scale(v):
    return lax.rsqrt(jnp.mean(v * v, axis=1, keepdims=True) + 1e-05)


def norm_back(v, gain, d_norm):
    r = mean_scale(v)
    e = d_norm * gain
    d_v = r * e - v * (r * r * r * jnp.mean(e * v, axis=1, keepdims=True))
    return d_v, jnp.sum(d_norm * v * r, axis=0, keepdims=True)


def mid_forward(x, tokens, gain, all_o, hidden_o, total, block, pair, got, mid, s1, r1, s2, r2, ls):
    greet(head_peers())
    reduce_over_head(x, total, pair, got, mid, s1, r1)
    hidden = tokens[...].astype(F32) + total[...]
    hidden_o[...] = hidden
    block[...] = (hidden * mean_scale(hidden) * gain[...]).astype(BF16)
    gather_over_head(block, all_o, s2, r2, ls)


def mid_backward(
    x, hidden, cot, gain, d_gu, n2, all_o, d_hidden_o, d_gain_o, grad_o,
    total, block, pair, got, mid, g, relay, seqs_got, part, last_got, s1, r1, s2, r2, ls, s3, r3, s4, r4
):
    greet(head_peers() + side_peers())
    one = pair_sends(x, pair, s1, r1, FAR)
    spread = Spread(
        lambda i, owner: g.at[owner, i], lambda i, b: relay.at[i, b], lambda i, s, b: seqs_got.at[i, s, b], s3, r3
    )
    settle = Settle(lambda i, b: last_got.at[i, b], s4, r4)
    dev = seq_place()[3]
    hid = g.shape[2]

    def make(place):
        owner = dev(*place)[0]
        cols = n2[:, pl.ds(pl.multiple_of(owner * LANES, LANES), LANES)]
        out = dot(d_gu[...], cols).astype(BF16)
        g[owner, 0] = out[:hid]
        g[owner, 1] = out[hid:]
        spread.ready(*place)

    for place in PLACES[:2]:
        make(place)
    two = chip_sends(x, one, total, pair, got, mid, s1, r1, FAR)
    for place in PLACES[2:]:
        make(place)
    spread.relays(0)
    d_norm, d_gain = norm_back(hidden[...], gain[...], chip_sum(two, total, got))
    d_hidden = cot[...].astype(F32) + d_norm
    d_hidden_o[...] = d_hidden
    d_gain_o[...] = d_gain
    block[...] = d_hidden.astype(BF16)
    ahead = gather_start(block, all_o, s2, r2, ls)
    spread.relays(1)
    ahead += gather_forward(block, all_o, s2, r2)
    for b in FAR:
        for i in range(2):
            both = spread.total(i, b)
            if b:
                part[i, b] = both.astype(BF16)
                settle.send(part.at[i, b], i, b)
            else:
                grad_o[i] = both
    gather_end(block, all_o, s2, r2, ls, ahead)
    for i in range(2):
        grad_o[i] = grad_o[i] + settle.others(i)
    spread.end()
    settle.end()
    for s in list(one.values()) + list(two.values()):
        s.wait_send()


def reach(kernel, outs, scratch, cid, limit, *args, anywhere=(), scalars=(), nbytes=12_000_000):
    return pl.pallas_call(
        kernel,
        out_shape=outs,
        in_specs=[
            pl.BlockSpec(memory_space=pl.ANY) if i in anywhere else SMEM if i in scalars else VMEM for i in range(len(args))
        ],
        out_specs=[VMEM for _ in outs],
        scratch_shapes=scratch,
        compiler_params=pltpu.CompilerParams(
            collective_id=cid, has_side_effects=True, vmem_limit_bytes=limit << 20
        ),
        cost_estimate=pl.CostEstimate(flops=0, bytes_accessed=nbytes, transcendentals=0),
    )(*args)


def sems(n):
    return pltpu.SemaphoreType.DMA((n,))


def reduce_scratch(rows, cols):
    return [pltpu.VMEM((CHIPS, rows, cols), BF16) for _ in range(3)] + [sems(2 * CHIPS), sems(2 * CHIPS)]


def gather_scratch():
    return [sems(2 * CHIPS), sems(2 * CHIPS), pltpu.SemaphoreType.DMA]


SIDE = 4


def seq_place():
    me = lax.axis_index("seq")
    z, y = me // SIDE, me % SIDE
    head = lax.axis_index("head")

    def dev(dz, dy):
        return (lax.rem(z + dz, SIDE) * SIDE + lax.rem(y + dy, SIDE), head)

    return me, z, y, dev


def side_peers():
    dev = seq_place()[3]
    return [dev(0, d) for d in range(1, SIDE)] + [dev(d, 0) for d in range(1, SIDE)]


FAR = (2, 1, 3, 0)
FIRST, OTHER = (2, 1), (3, 0)
PLACES = (
    (2, 2), (2, 1), (1, 2), (2, 3), (3, 2), (2, 0), (0, 2), (1, 3), (3, 1), (1, 0), (0, 3), (3, 3), (1, 1), (3, 0), (0, 1),
    (0, 0),
)


class Spread:
    def __init__(self, piece, relay, got, ssem, rsem):
        self.piece, self.relay, self.got, self.ssem, self.rsem = piece, relay, got, ssem, rsem
        self.dev = seq_place()[3]
        self.sent = []

    def way(self, i, a, b):
        return self.dev(b, a) if i == 0 else self.dev(a, b)

    def copy(self, i, a, b, owner):
        k = (i * SIDE + a) * SIDE + b
        if a == 2:
            dst, step = self.relay(i, b), 1 if b in FIRST else 3
        else:
            dst, step = self.got(i, 0 if a == 1 else 1, b), a
        return cp(self.piece(i, owner), dst, self.ssem.at[k], self.rsem.at[k], self.way(i, step, 0))

    def send(self, i, a, b, owner):
        s = self.copy(i, a, b, owner)
        s.start()
        self.sent.append(s)

    def late(self, a, b):
        return a == 1 and b in FIRST or a == 3 and b in OTHER

    def ready(self, dz, dy):
        owner = self.dev(dz, dy)[0]
        for i in range(2):
            a, b = (dy, dz) if i == 0 else (dz, dy)
            if a and not self.late(a, b):
                self.send(i, a, b, owner)

    def relays(self, part=None):
        for n, b in enumerate(FAR):
            if part is not None and n // 2 != part:
                continue
            for i in range(2):
                a = 1 if b in FIRST else 3
                owner = self.way(i, a, b)[0]
                self.copy(i, 2, b, owner).wait_recv()
                both = self.piece(i, owner)[...].astype(F32) + self.relay(i, b)[...].astype(F32)
                self.relay(i, b)[...] = both.astype(BF16)
                k = (i * SIDE + a) * SIDE + b
                s = cp(
                    self.relay(i, b), self.got(i, 0 if a == 1 else 1, b), self.ssem.at[k], self.rsem.at[k],
                    self.way(i, a, 0),
                )
                s.start()
                self.sent.append(s)

    def total(self, i, b):
        owner = self.way(i, 0, b)[0]
        for a in (1, 3):
            self.copy(i, a, b, owner).wait_recv()
        return self.piece(i, owner)[...].astype(F32) + (
            self.got(i, 0, b)[...].astype(F32) + self.got(i, 1, b)[...].astype(F32)
        )

    def end(self):
        for s in self.sent:
            s.wait_send()


class Settle:
    def __init__(self, got, ssem, rsem):
        self.got, self.ssem, self.rsem = got, ssem, rsem
        self.dev = seq_place()[3]
        self.sent = {}

    def send(self, src, i, b):
        k = i * SIDE + b
        dev = self.dev(b, 0) if i == 0 else self.dev(0, b)
        self.sent[i, b] = cp(src, self.got(i, b), self.ssem.at[k], self.rsem.at[k], dev)
        self.sent[i, b].start()

    def others(self, i):
        for b in (1, 3, 2):
            self.sent[i, b].wait_recv()
        return (self.got(i, 1)[...].astype(F32) + self.got(i, 3)[...].astype(F32)) + self.got(i, 2)[...].astype(F32)

    def end(self):
        for s in self.sent.values():
            s.wait_send()


def share_start(src, got, place, to, ssem, rsem):
    got[place] = src[...]
    out = [cp(src, got.at[place], ssem.at[d], rsem.at[d], to(d)) for d in (2, 1, 3)]
    for s in out:
        s.start()

    def wait():
        for d in (1, 3, 2):
            back = lax.rem(place + SIDE - d, SIDE)
            cp(src, got.at[back], ssem.at[d], rsem.at[d], to(d)).wait_recv()

    return out, wait


def share(src, got, place, to, ssem, rsem):
    out, wait = share_start(src, got, place, to, ssem, rsem)
    wait()
    return out


def unit_top():
    return jnp.where(iota((DK + DV, DK), 0) == iota((DK + DV, DK), 1), 1.0, 0.0)


def add_low(pair, low):
    return jnp.concatenate([pair[:DK], pair[DK:] + low], axis=0)


def states_forward(ab, start_o, ga_o, ta_o, got1, tot, got2, s1, r1, s2, r2):
    me, z, y, dev = seq_place()
    heads = ab.shape[0]
    greet(side_peers())
    out = share(ab, got1, y, lambda d: dev(0, d), s1, r1)
    before = []
    for h in range(heads):
        whole = got1[0, h].astype(F32)
        prefix = jnp.where(y > 0, whole, unit_top())
        for j in range(1, SIDE):
            a, b = got1[j, h, :DK, :], got1[j, h, DK:, :].astype(F32)
            whole = add_low(dot_left2(whole, a), b)
            if j < SIDE - 1:
                prefix = jnp.where(y > j, whole, prefix)
        tot[h] = whole.astype(BF16)
        before.append(prefix)
        for j in range(SIDE):
            ga_o[j, h] = got1[j, h, :DK, :]
    out += share(tot, got2, z, lambda d: dev(d, 0), s2, r2)
    for h in range(heads):
        held = jnp.zeros((DV, DK), F32)
        for j in range(SIDE - 1):
            held = jnp.where(
                z > j, dot_left2(held, got2[j, h, :DK, :]) + got2[j, h, DK:, :].astype(F32), held
            )
        start_o[h] = dot3(held, before[h][:DK]) + before[h][DK:]
        for j in range(SIDE):
            ta_o[j, h] = got2[j, h, :DK, :]
    for s in out:
        s.wait_send()


def states_backward(inc, ga, ta, middle, cot, gated_t, d_mixed, later_o, g_down_o, g_out_o, got1, tot, got2, s1, r1, s2, r2):
    me, z, y, dev = seq_place()
    heads = inc.shape[0]
    seqs = g_down_o.shape[0]

    def blocks(o, left, right, part):
        for j in range(part * seqs // 4, (part + 1) * seqs // 4):
            if j % 2 == 0:
                both = dot(left[...], right[:, j * LANES : (j + 2) * LANES]).astype(BF16)
                o[j], o[j + 1] = both[:, :LANES], both[:, LANES:]

    greet(side_peers())
    out, wait = share_start(inc, got1, y, lambda d: dev(0, d), s1, r1)
    blocks(g_down_o, middle, cot, 0)
    blocks(g_down_o, middle, cot, 1)
    wait()
    after = []
    for h in range(heads):
        whole = add_low(dot(unit_top(), ga[SIDE - 1, h], "nt"), got1[SIDE - 1, h].astype(F32))
        suffix = jnp.where(y < SIDE - 1, whole, unit_top())
        for j in range(SIDE - 2, -1, -1):
            whole = add_low(dot_left2(whole, ga[j, h], "nt"), got1[j, h].astype(F32))
            if j:
                suffix = jnp.where(y < j, whole, suffix)
        tot[h] = whole[DK:].astype(BF16)
        after.append(suffix)
    more, wait = share_start(tot, got2, z, lambda d: dev(d, 0), s2, r2)
    out += more
    blocks(g_down_o, middle, cot, 2)
    blocks(g_down_o, middle, cot, 3)
    for part in range(4):
        blocks(g_out_o, gated_t, d_mixed, part)
    wait()
    for h in range(heads):
        held = jnp.zeros((DV, DK), F32)
        for j in range(SIDE - 1, 0, -1):
            held = jnp.where(z < j, dot_left2(held, ta[j, h], "nt") + got2[j, h].astype(F32), held)
        later_o[h] = dot3(held, after[h][:DK]) + after[h][DK:]
    for s in out:
        s.wait_send()


def pair_sends(x, pair, ssem, rsem, steps):
    rows = pair.shape[1]
    dev = head_place()[3]
    out = {}
    for d in steps:
        owner = dev(d, True)[1]
        src = x.at[pl.ds(pl.multiple_of(owner * rows, rows), rows)]
        out[d] = cp(src, pair.at[d], ssem.at[d], rsem.at[d], dev(0, True))
        out[d].start()
    return out


def chip_sends(x, first, total, pair, got, mid, ssem, rsem, steps):
    rows = pair.shape[1]
    dev = head_place()[3]
    out = {}
    for d in steps:
        first[d].wait_recv()
        owner = dev(d)[1]
        both = x[pl.ds(pl.multiple_of(owner * rows, rows), rows), :].astype(F32) + pair[d].astype(F32)
        if d:
            mid[d] = both.astype(BF16)
            out[d] = cp(mid.at[d], got.at[d], ssem.at[CHIPS + d], rsem.at[CHIPS + d], dev(d))
            out[d].start()
        else:
            total[...] = both
    return out


def chip_sum(second, total, got):
    for d in (1, 3, 2):
        second[d].wait_recv()
    return total[...] + ((got[1].astype(F32) + got[3].astype(F32)) + got[2].astype(F32))


def finish(
    dproj, normed, w, d_rate, rate_w, d_tail, d_edge, feed, hidden, tokens, d_hidden, gain, convs, decay, g_feed, g_head,
    s_down, s_out,
    layer_o, d_tokens_o, g_mixer_o, gains_o, convs_o, rate_o, g_down_o, g_out_o,
    dp, wv, edge, g, relay, got1, mid, got2, dn, ta, pa, ga, ma, tb, pb, gb, mb, gains, gbuf, sbuf, rbuf, got_d, got_o,
    es, er, ls, s1, r1, s2, r2, sa, ra, sb, rb, sg, rg, ss, rs, s5, r5
):
    me, z, y, dev = seq_place()
    head = lax.axis_index("head")
    heads, seqs = gbuf.shape[0], rbuf.shape[0]
    rows = dp.shape[0]
    part, half = g_mixer_o.shape[1], g_mixer_o.shape[2]
    across = [(me, lax.rem(head + d, heads)) for d in range(1, heads)]
    along = [(lax.rem(me + d, seqs), head) for d in range(1, seqs)]
    load_p = pltpu.make_async_copy(dproj, dp, ls.at[0])
    load_p.start()
    load_w = pltpu.make_async_copy(w, wv, ls.at[1])
    load_w.start()
    greet(across + along)
    back = cp(d_edge, edge, es, er, (lax.rem(me + seqs - 1, seqs), head))
    back.start()
    feed_one = pair_sends(feed, pa, sa, ra, FAR)
    load_p.wait()
    back.wait_recv()
    there = jnp.where(me < seqs - 1, edge[...], 0.0)
    tail = jnp.concatenate([d_tail[:PAD, :], d_tail[PAD:, :] + there], axis=0).astype(BF16)
    wide = half - DV
    for i in range(2):
        dp[rows - 2 * PAD :, pl.ds(i * half, wide)] = tail[:, i * wide : (i + 1) * wide]

    sums = (s_down, s_out)
    settle = Settle(lambda i, b: (got_d, got_o)[i].at[b], s5, r5)
    for b in (2, 1, 3):
        for i in range(2):
            settle.send(sums[i].at[b], i, b)

    spread = Spread(
        lambda i, owner: g.at[i, owner], lambda i, b: relay.at[i, b], lambda i, s, b: got1.at[i, s, b], s1, r1
    )
    settle_two = Settle(lambda i, b: got2.at[i, b], s2, r2)
    for place in PLACES:
        owner = dev(*place)[0]
        left = normed[:, pl.ds(pl.multiple_of(owner * part, part), part)]
        both = dot(left, dp[...], "tn").astype(BF16)
        for i in range(2):
            g[i, owner] = both[:, i * half : (i + 1) * half]
        spread.ready(*place)
    feed_two = chip_sends(feed, feed_one, ta, pa, ga, ma, sa, ra, FAR)
    rates_t = dot(d_rate[:, :PAD], normed[...], "tn")

    load_w.wait()
    low = rows // CHIPS
    hp = head_place()[3]
    dn_one = {}
    for d in FAR:
        chip = hp(d)[1] // 2
        here = pl.ds(pl.multiple_of(chip * low, low), low)
        dn[here, :] = (dot(dp[here, :], wv[...], "nt") + dot(d_rate[here, :], rate_w[...], "nt")).astype(BF16)
        dn_one.update(pair_sends(dn, pb, sb, rb, (d,)))
    dn_two = chip_sends(dn, dn_one, tb, pb, gb, mb, sb, rb, FAR)
    spread.relays()
    layer_o[...] = (hidden[...] + chip_sum(feed_two, ta, ga)).astype(BF16)
    d_norm, d_gain = norm_back(tokens[...].astype(F32), gain[...], chip_sum(dn_two, tb, gb))
    d_tokens_o[...] = d_hidden[...] + d_norm

    ng = gains.shape[0]
    n_row = D // LANES
    gains[...] = jnp.zeros_like(gains)
    for r in range(n_row):
        at = slice(r * LANES, (r + 1) * LANES)
        gains[r : r + 1, :] = d_gain[:, at]
        gains[n_row + r : n_row + r + 1, :] = g_feed[:, at]
    for r in range(DV // LANES):
        gains[2 * n_row + r : 2 * n_row + r + 1, :] = g_head[:, r * LANES : (r + 1) * LANES]
    gbuf[head] = gains[...]
    g_out = [cp(gains, gbuf.at[head], sg.at[d], rg.at[d], across[d - 1]) for d in range(1, heads)]
    for s in g_out:
        s.start()
    taps, wide_c = convs.shape
    c_row = wide_c // LANES
    nc = taps * c_row
    for j in range(seqs):
        for t in range(taps):
            for r in range(c_row):
                lo = ng + t * c_row + r
                if j == 0:
                    sbuf[0, lo : lo + 1, :] = convs[t : t + 1, r * LANES : (r + 1) * LANES]
        if j == 0:
            sbuf[0, ng + nc : ng + nc + PAD, :] = jnp.zeros((PAD, LANES), F32)
            sbuf[0, ng + nc : ng + nc + 1, :] = decay[...]
        else:
            sbuf[j, ng : ng + nc + PAD, :] = sbuf[0, ng : ng + nc + PAD, :]
        sbuf[j, ng + nc + PAD :, :] = rates_t[:, j * LANES : (j + 1) * LANES]
    for d in range(1, heads):
        cp(gains, gbuf.at[lax.rem(head + heads - d, heads)], sg.at[d], rg.at[d], across[d - 1]).wait_recv()
    total = gbuf[0]
    for i in range(1, heads):
        total = total + gbuf[i]
    for j in range(seqs):
        sbuf[j, :ng, :] = total
    rbuf[me] = sbuf[me]
    s_out = []
    for d in range(1, seqs):
        s = cp(sbuf.at[lax.rem(me + d, seqs)], rbuf.at[me], ss.at[d], rs.at[d], along[d - 1])
        s.start()
        s_out.append(s)

    for i, o in ((0, g_down_o), (1, g_out_o)):
        o[...] = sums[i][0].astype(F32) + settle.others(i)

    for b in FAR:
        for i in range(2):
            both = spread.total(i, b)
            if b:
                mid[i, b] = both.astype(BF16)
                settle_two.send(mid.at[i, b], i, b)
            else:
                g_mixer_o[i] = both
    for d in range(1, seqs):
        cp(sbuf.at[0], rbuf.at[lax.rem(me + seqs - d, seqs)], ss.at[d], rs.at[d], along[d - 1]).wait_recv()
    total = rbuf[0]
    for i in range(1, seqs):
        total = total + rbuf[i]
    gains_o[...] = total[:ng]
    convs_o[...] = total[ng : ng + nc + PAD]
    rate_o[...] = total[ng + nc + PAD :]
    for i in range(2):
        g_mixer_o[i] = g_mixer_o[i] + settle_two.others(i)
    spread.end()
    settle.end()
    settle_two.end()
    done = g_out + s_out + [back]
    done += list(feed_one.values()) + list(feed_two.values()) + list(dn_one.values()) + list(dn_two.values())
    for s in done:
        s.wait_send()


def passed_along(shard, axis, by):
    length = lax.axis_size(axis)
    pairs = [(i, i + by) for i in range(length) if 0 <= i + by < length]
    return lax.ppermute(shard, axis, pairs)


def rms_scale(values, gain):
    return values * lax.rsqrt(jnp.mean(values * values, axis=-1, keepdims=True) + 1e-05) * gain


def local(
    tokens, mixer_gain, mixer_weight, rate_weight, conv_weight, decay_log, decay_bias, head_gain,
    output_weight, feed_gain, gate_up_weight, down_weight, doc_starts, cotangent,
):
    resid = tokens.astype(F32)
    normed = rms_scale(resid, mixer_gain).astype(BF16)
    gathered = lax.all_gather(normed, "head", axis=0, tiled=True)
    heads = mixer_weight.shape[1]
    gathered, cot_own, mixer_flat = lax.optimization_barrier(
        (gathered, cotangent, mixer_weight.reshape(D, heads * MIXW))
    )
    cot_rows = lax.all_gather(cot_own, "head", axis=0, tiled=True)
    rows = gathered.shape[0]
    blocks = rows // BLK
    units = heads * blocks
    seq = lax.axis_size("seq")
    projected = jnp.dot(gathered, mixer_flat, preferred_element_type=F32)
    rate_proj = jnp.einsum("td,dgh->tgh", gathered, rate_weight, preferred_element_type=F32).reshape(rows, 2 * heads)
    rim = projected[rows - PAD :].reshape(PAD, heads, MIXW)[:, :, :CONVW].reshape(PAD, heads * CONVW).astype(BF16)
    halo = passed_along(rim, "seq", 1).astype(F32)
    convw = conv_weight.reshape(KCONV, heads * CONVW)
    info = jnp.concatenate(
        [doc_starts, jnp.stack([lax.axis_index("seq") * rows, lax.axis_index("seq")]).astype(jnp.int32)]
    )
    dlog, dbias = decay_log.reshape(1, heads), decay_bias.reshape(1, heads)
    gain = head_gain.reshape(1, DV)

    conv, dec, inv, wu, qe, ol, step, ab = call(
        fwd_prep,
        [
            sds((rows, heads * CONVW)), sds((units, BLK, BLK)), sds((units, BLK, BLK), BF16),
            sds((units, BLK, DK + DV)), sds((rows, heads * DK)), sds((rows, heads * DV)),
            sds((units, DK + DV, DK)), sds((heads, DK + DV, DK), BF16),
        ],
        [pltpu.VMEM((PAD + rows, CONVW), F32)],
        56, info, projected, halo, rate_proj, convw, dlog, dbias,
    )
    start, ga, ta = reach(
        states_forward,
        [sds((heads, DV, DK)), sds((SIDE, heads, DK, DK), BF16), sds((SIDE, heads, DK, DK), BF16)],
        [
            pltpu.VMEM((SIDE, heads, DK + DV, DK), BF16), pltpu.VMEM((heads, DK + DV, DK), BF16),
            pltpu.VMEM((SIDE, heads, DK + DV, DK), BF16), sems(SIDE), sems(SIDE), sems(SIDE), sems(SIDE),
        ],
        1, 40, ab,
    )
    states, head_out, gated = call(
        fwd_out,
        [sds((units, DV, DK)), sds((rows, heads * DV)), sds((rows, heads * DV), BF16)],
        [], 48, start, step, qe, ol, projected, gain,
    )
    out_flat = output_weight.reshape(heads * DV, D)
    own = tokens.shape[0]
    mixed = jnp.dot(gated, out_flat, preferred_element_type=F32).astype(BF16)
    feed_row = feed_gain.reshape(1, D)
    gathered_two, hidden = reach(
        mid_forward,
        [sds((rows, D), BF16), sds((own, D))],
        [pltpu.VMEM((own, D), F32), pltpu.VMEM((own, D), BF16)] + reduce_scratch(own, D) + gather_scratch(),
        2, 48, mixed, tokens, feed_row,
    )
    hid = down_weight.shape[0]
    gu_t = gate_up_weight.transpose(1, 2, 0).reshape(2 * hid, D)
    by_last = (((1,), (1,)), ((), ()))
    by_first = (((0,), (0,)), ((), ()))
    d_middle = lax.dot_general(down_weight, cot_rows, by_last, preferred_element_type=F32)
    gate_up = lax.dot_general(gu_t, gathered_two, by_last, preferred_element_type=F32)
    gate, up = gate_up[:hid], gate_up[hid:]
    s = jax.nn.sigmoid(gate)
    middle = (gate * s * up).astype(BF16)
    d_gate_up = jnp.concatenate([d_middle * up * (s * (1.0 + gate * (1.0 - s))), d_middle * gate * s]).astype(BF16)
    d_two = lax.dot_general(d_gate_up, gu_t, by_first, preferred_element_type=F32).astype(BF16)
    part, half, n_head = D // seq, MIXW, lax.axis_size("head")
    d_mixed, d_hidden, g_feed_gain, grads = reach(
        mid_backward,
        [sds((rows, D), BF16), sds((own, D)), sds((1, D)), sds((2, hid, LANES))],
        [pltpu.VMEM((own, D), F32), pltpu.VMEM((own, D), BF16)]
        + [pltpu.VMEM((CHIPS, own, D), BF16) for _ in range(3)]
        + [
            pltpu.VMEM((seq, 2, hid, LANES), BF16), pltpu.VMEM((2, SIDE, hid, LANES), BF16),
            pltpu.VMEM((2, 2, SIDE, hid, LANES), BF16), pltpu.VMEM((2, SIDE, hid, LANES), BF16),
            pltpu.VMEM((2, SIDE, hid, LANES), BF16), sems(2 * CHIPS), sems(2 * CHIPS),
        ]
        + gather_scratch()
        + [sems(2 * SIDE * SIDE), sems(2 * SIDE * SIDE), sems(2 * SIDE), sems(2 * SIDE)],
        3, 60, d_two, hidden, cotangent, feed_row, d_gate_up, gathered_two, nbytes=30_000_000,
    )
    grad_gate_up = grads.transpose(2, 0, 1)
    d_mixed, middle = lax.optimization_barrier((d_mixed, middle))
    feed = lax.dot_general(middle, down_weight, by_first, preferred_element_type=F32).astype(BF16)
    gated_t = gated.T
    d_gated = jnp.einsum("td,vd->tv", d_mixed, out_flat, preferred_element_type=F32)
    d_out, d_gate, g_head_gain, y, inc = call(
        bwd_head,
        [
            sds((rows, heads * DV)), sds((rows, heads * DV), BF16), sds((1, DV)),
            sds((units, DV, DK)), sds((heads, DV, DK), BF16),
        ],
        [], 48, d_gated, head_out, projected, gain, qe, step,
    )
    later, g_down, g_out = reach(
        states_backward,
        [sds((heads, DV, DK)), sds((seq, hid, LANES), BF16), sds((seq, heads * DV, LANES), BF16)],
        [
            pltpu.VMEM((SIDE, heads, DV, DK), BF16), pltpu.VMEM((heads, DV, DK), BF16),
            pltpu.VMEM((SIDE, heads, DV, DK), BF16), sems(SIDE), sems(SIDE), sems(SIDE), sems(SIDE),
        ],
        4, 48, inc, ga, ta, middle, cot_rows, gated_t, d_mixed,
    )
    d_projected, d_tail, d_edge, d_rate, d_convw, d_decay, s_down, s_out = reach(
        bwd_mix,
        [
            sds((rows, heads * MIXW), BF16), sds((2 * PAD, heads * CONVW)), sds((PAD, heads * CONVW)),
            sds((rows, 2 * heads)), sds((KCONV, heads * CONVW)), sds((1, 2 * heads)),
            sds((SIDE, hid, LANES), BF16), sds((SIDE, heads * DV, LANES), BF16),
        ],
        [
            pltpu.VMEM((PAD + rows, CONVW), F32), pltpu.VMEM((PAD + rows, CONVW), F32),
            pltpu.VMEM((units, DV, DK), F32), pltpu.VMEM((rows, DK), F32), pltpu.VMEM((rows, heads * CONVW), F32),
            pltpu.VMEM((SIDE, hid, LANES), BF16), pltpu.VMEM((SIDE, heads * DV, LANES), BF16),
            pltpu.VMEM((2, SIDE, hid, LANES), BF16), pltpu.VMEM((2, SIDE, heads * DV, LANES), BF16),
            sems(2 * SIDE * SIDE), sems(2 * SIDE * SIDE),
        ],
        6, 62, info, later, conv, dec, inv, wu, states, step, y, d_out, d_gate, rate_proj, projected, halo, convw,
        dlog, dbias, g_down, g_out, scalars=(0,), nbytes=30_000_000,
    )
    d_rate_low = jnp.pad(d_rate.astype(BF16), ((0, 0), (0, LANES - 2 * heads)))
    rate_pad = jnp.pad(rate_weight.reshape(D, 2 * heads), ((0, 0), (0, LANES - 2 * heads)))
    d_decay = jnp.pad(d_decay, ((0, 0), (0, LANES - 2 * heads)))
    n_gain, n_conv = 40, KCONV * heads * CONVW // LANES + PAD
    small = n_gain + n_conv + PAD
    layer_out, grad_tokens, grad_mixer, gains, convs, rate_own, grad_down, grad_output = reach(
        finish,
        [
            sds((own, D), BF16), sds((own, D)), sds((2, part, half)), sds((n_gain, LANES)), sds((n_conv, LANES)),
            sds((PAD, LANES)), sds((hid, LANES)), sds((heads * DV, LANES)),
        ],
        [
            pltpu.VMEM((rows, heads * MIXW), BF16), pltpu.VMEM((D, heads * MIXW), BF16),
            pltpu.VMEM((PAD, heads * CONVW), F32), pltpu.VMEM((2, seq, part, half), BF16),
            pltpu.VMEM((2, SIDE, part, half), BF16), pltpu.VMEM((2, 2, SIDE, part, half), BF16),
            pltpu.VMEM((2, SIDE, part, half), BF16), pltpu.VMEM((2, SIDE, part, half), BF16), pltpu.VMEM((rows, D), BF16),
        ]
        + 2 * ([pltpu.VMEM((own, D), F32)] + [pltpu.VMEM((CHIPS, own, D), BF16) for _ in range(3)])
        + [
            pltpu.VMEM((n_gain, LANES), F32), pltpu.VMEM((n_head, n_gain, LANES), F32),
            pltpu.VMEM((seq, small, LANES), F32), pltpu.VMEM((seq, small, LANES), F32),
            pltpu.VMEM((SIDE, hid, LANES), BF16), pltpu.VMEM((SIDE, heads * DV, LANES), BF16),
            pltpu.SemaphoreType.DMA, pltpu.SemaphoreType.DMA, sems(2),
            sems(2 * SIDE * SIDE), sems(2 * SIDE * SIDE), sems(2 * SIDE), sems(2 * SIDE),
            sems(2 * CHIPS), sems(2 * CHIPS), sems(2 * CHIPS), sems(2 * CHIPS),
            sems(n_head), sems(n_head), sems(seq), sems(seq), sems(2 * SIDE), sems(2 * SIDE),
        ],
        5, 62, d_projected, gathered, mixer_flat, d_rate_low, rate_pad, d_tail, d_edge, feed, hidden, tokens,
        d_hidden, mixer_gain.reshape(1, D), d_convw, d_decay, g_feed_gain, g_head_gain, s_down, s_out,
        anywhere=(0, 2), nbytes=40_000_000,
    )
    grad_mixer = grad_mixer.transpose(1, 0, 2)
    grad_output = grad_output.reshape(heads, DV, LANES)
    gains, convs = gains.reshape(-1), convs.reshape(-1)
    grad_mixer_gain, grad_feed_gain, grad_head_gain = gains[:D], gains[D : 2 * D], gains[2 * D : 2 * D + DV]
    n = KCONV * heads * CONVW
    grad_conv = convs[:n].reshape(KCONV, heads, CONVW)
    grad_decay_log, grad_decay_bias = convs[n : n + heads], convs[n + heads : n + 2 * heads]
    grad_rate = rate_own[: 2 * heads].reshape(2, heads, part).transpose(2, 0, 1)
    return (
        layer_out, grad_tokens, grad_mixer_gain, grad_mixer, grad_rate, grad_conv, grad_decay_log, grad_decay_bias,
        grad_head_gain, grad_output, grad_feed_gain, grad_gate_up, grad_down,
    )


def solution(mesh):
    rows = P(("seq", "head"), None)
    return jax.shard_map(
        local,
        mesh=mesh,
        in_specs=(
            rows, P(), P(None, "head", None), P(None, None, "head"), P(None, "head", None), P("head"), P("head"),
            P(), P("head", None, None), P(), P(None, None, "head"), P("head", None), P(), rows,
        ),
        out_specs=(
            rows, rows, P(), P("seq", "head", None), P("seq", None, "head"), P(None, "head", None), P("head"),
            P("head"), P(), P("head", None, "seq"), P(), P("seq", None, "head"), P("head", "seq"),
        ),
        check_vma=False,
    )
```

```python
import functools

import jax
import jax.numpy as jnp
from jax import lax
from jax.experimental import pallas as pl
from jax.experimental.pallas import tpu as pltpu
from jax.sharding import PartitionSpec as P

D = 2048
DK = 128
DV = 256
KCONV = 4
MIXW = 768
CONVW = 512
NB = 4
BLK = 256
PAD = 8
F32 = jnp.float32
BF16 = jnp.bfloat16

VMEM = pl.BlockSpec(memory_space=pltpu.VMEM)
SMEM = pl.BlockSpec(memory_space=pltpu.SMEM)


def dot(a, b, form="nn"):
    dims = {"nn": ((1,), (0,)), "nt": ((1,), (1,)), "tn": ((0,), (0,))}[form]
    return lax.dot_general(a.astype(BF16), b.astype(BF16), (dims, ((), ())), preferred_element_type=F32)


def halves(a):
    hi = a.astype(BF16)
    return hi, (a - hi.astype(F32)).astype(BF16)


def dot3(a, b, form="nn"):
    ah, al = halves(a)
    bh, bl = halves(b)
    return dot(ah, bh, form) + (dot(ah, bl, form) + dot(al, bh, form))


def dot_exact_left(a, b, form="nn"):
    b1, rest = halves(b)
    rest = b - b1.astype(F32)
    b2 = rest.astype(BF16)
    b3 = (rest - b2.astype(F32)).astype(BF16)
    return dot(a, b1, form) + (dot(a, b2, form) + dot(a, b3, form))


def iota(shape, axis):
    return lax.broadcasted_iota(jnp.int32, shape, axis)


def doc_of(info, pos):
    count = jnp.zeros(pos.shape, jnp.int32)
    for i in range(NB):
        count = count + jnp.where(pos >= info[i], 1, 0)
    return jnp.where(pos < 0, -1, count)


def sigmoid(v):
    return 1.0 / (1.0 + jnp.exp(-v))


def softplus(v):
    return jnp.maximum(v, 0.0) + jnp.log1p(jnp.exp(-jnp.abs(v)))


def unit_lower_inverse(low):
    n = low.shape[0]
    row, col = iota((n, n), 0), iota((n, n), 1)
    eye = jnp.where(row == col, 1.0, 0.0)

    def same(b):
        return row // b == col // b

    x = jnp.where(same(8), -low, 0.0)
    inv = eye + x
    x = dot3(x, x)
    inv = inv + dot3(inv, x)
    x = dot3(x, x)
    inv = inv + dot3(inv, x)
    b = 8
    while b < n:
        off = jnp.where(same(2 * b) & jnp.logical_not(same(b)), low, 0.0)
        inv = inv - dot3(inv, dot3(off, inv))
        b *= 2
    return inv


def valid_column(info, rows, back):
    pos = info[NB] + iota((rows, 1), 0)
    return jnp.where(doc_of(info, pos) == doc_of(info, pos - back), 1.0, 0.0)


def vectors(conv):
    act = conv * sigmoid(conv)
    qa, ka, va = act[:, :DK], act[:, DK : 2 * DK], act[:, 2 * DK :]
    rq = lax.rsqrt(jnp.sum(qa * qa, axis=1, keepdims=True) + 1e-06)
    rk = lax.rsqrt(jnp.sum(ka * ka, axis=1, keepdims=True) + 1e-06)
    return qa, ka, va, rq, rk


def rates(rate_ref, dlog_ref, dbias_ref):
    heads = dlog_ref.shape[1]
    pre = rate_ref[:, :heads] + dbias_ref[...]
    log_decay = -jnp.exp(dlog_ref[...]) * softplus(pre)
    return sigmoid(rate_ref[:, heads:]), log_decay, pre


def block_masks(info, c):
    row, col = iota((BLK, BLK), 0), iota((BLK, BLK), 1)
    base = info[NB] + c * BLK
    docs_r, docs_c = doc_of(info, base + row), doc_of(info, base + col)
    keep = (docs_r == docs_c) & (col <= row)
    column = doc_of(info, base + iota((BLK, 1), 0))
    first = jnp.where(column == doc_of(info, base - 1 + iota((BLK, 1), 0) * 0), 1.0, 0.0)
    last = jnp.where(column == doc_of(info, base + BLK - 1 + iota((BLK, 1), 0) * 0), 1.0, 0.0)
    tri = jnp.where(col <= row, 1.0, 0.0)
    strict = jnp.where(col < row, 1.0, 0.0)
    return keep, first, last, tri, strict


def decays(g, first, last, tri):
    cum = dot_exact_left(tri, jnp.broadcast_to(g, (BLK, DK)))[:, :1]
    carry = first * jnp.exp(cum)
    to_end = last * jnp.exp(cum[BLK - 1 :, :] - cum)
    return carry, to_end


def fwd_prep(info, proj, halo, rate, convw, dlog, dbias, conv_o, dec_o, inv_o, wu_o, qe_o, ol_o, step_o, ab_o, xpad):
    rows = proj.shape[0]
    heads = dlog.shape[1]
    blocks = rows // BLK
    strength, log_decay, _ = rates(rate, dlog, dbias)
    valid = [valid_column(info, rows, KCONV - 1 - j) for j in range(KCONV)]
    for h in range(heads):
        src, dst = pl.ds(h * MIXW, CONVW), pl.ds(h * CONVW, CONVW)
        xpad[:PAD, :] = halo[:, dst]
        xpad[PAD:, :] = proj[:, src].astype(BF16).astype(F32)
        conv = jnp.zeros((rows, CONVW), F32)
        for j in range(KCONV):
            lo = PAD - (KCONV - 1) + j
            conv = conv + convw[j : j + 1, dst].astype(F32) * xpad[lo : lo + rows, :] * valid[j]
        conv_o[:, dst] = conv
    for c in range(blocks):
        keep, first, last, tri, strict = block_masks(info, c)
        here = pl.ds(c * BLK, BLK)
        for h in range(heads):
            qa, ka, va, rq, rk = vectors(conv_o[here, pl.ds(h * CONVW, CONVW)])
            q, k = qa * (rq * DK**-0.5), ka * rk
            beta = strength[c * BLK : (c + 1) * BLK, h : h + 1]
            g = log_decay[c * BLK : (c + 1) * BLK, h : h + 1]
            spread = dot_exact_left(tri, g * strict)
            dec = jnp.where(keep, jnp.exp(jnp.where(keep, spread, 0.0)), 0.0)
            carry, to_end = decays(g, first, last, tri)
            low = strict * (beta * dec * dot(k, k, "nt"))
            inv = unit_lower_inverse(low)
            u = h * blocks + c
            dec_o[u] = dec
            inv_o[u] = inv.astype(BF16)
            rhs = jnp.concatenate([(beta * carry) * k, beta * va], axis=1)
            wu = dot(inv, rhs)
            wu_o[u] = wu
            out = dot(dec * dot(q, k, "nt"), wu)
            qe_o[here, pl.ds(h * DK, DK)] = carry * q - out[:, :DK]
            ol_o[here, pl.ds(h * DV, DV)] = out[:, DK:]
            step = dot(wu, to_end * k, "tn")
            eye = jnp.where(iota((DK, DK), 0) == iota((DK, DK), 1), 1.0, 0.0)
            step_o[u, :DK] = carry[BLK - 1 :, :] * eye - step[:DK]
            step_o[u, DK:] = step[DK:]
    for h in range(heads):
        ab = step_o[h * blocks]
        for c in range(1, blocks):
            nxt = step_o[h * blocks + c]
            ab = dot3(ab, nxt[:DK])
            ab_o_tail = nxt[DK:]
            ab = jnp.concatenate([ab[:DK], ab[DK:] + ab_o_tail], axis=0)
        ab_o[h] = ab.astype(ab_o.dtype)


def fwd_out(start, step, qe, ol, proj, gain, states_o, head_o, gated_o):
    rows = qe.shape[0]
    heads = start.shape[0]
    blocks = rows // BLK
    for h in range(heads):
        state = start[h]
        for c in range(blocks):
            u = h * blocks + c
            here = pl.ds(c * BLK, BLK)
            states_o[u] = state
            out = ol[here, pl.ds(h * DV, DV)] + dot(qe[here, pl.ds(h * DK, DK)], state, "nt")
            head_o[here, pl.ds(h * DV, DV)] = out
            gate = proj[here, pl.ds(h * MIXW + CONVW, DV)]
            scale = lax.rsqrt(jnp.mean(out * out, axis=1, keepdims=True) + 1e-05)
            gated_o[here, pl.ds(h * DV, DV)] = (out * scale * gain[...] * (gate * sigmoid(gate))).astype(BF16)
            if c + 1 < blocks:
                state = dot3(state, step[u, :DK, :]) + step[u, DK:, :]


def dot_left2(a, b, form="nn"):
    ah, al = halves(a)
    return dot(ah, b, form) + dot(al, b, form)


def head_back(d_mixed, out_w, head_out, proj, gain, qe, step, d_out_o, d_gate_o, y_o, inc_o):
    rows = qe.shape[0]
    blocks = rows // BLK
    heads = qe.shape[1] // DK
    total = jnp.zeros((1, DV), F32)
    for h in range(heads):
        cols = pl.ds(h * DV, DV)
        for c in range(blocks):
            here = pl.ds(c * BLK, BLK)
            dg, out = dot(d_mixed[here, :], out_w[cols, :], "nt"), head_out[here, cols]
            gate = proj[here, pl.ds(h * MIXW + CONVW, DV)]
            s = sigmoid(gate)
            silu = gate * s
            scale = lax.rsqrt(jnp.mean(out * out, axis=1, keepdims=True) + 1e-05)
            dn = dg * (out * scale)
            d_gate_o[here, pl.ds(h * MIXW + CONVW, DV)] = (dn * gain[...] * (s * (1.0 + gate * (1.0 - s)))).astype(BF16)
            total = total + jnp.sum(dn * silu, axis=0, keepdims=True)
            f = dg * gain[...] * silu
            d_out = scale * f - out * (scale * scale * scale) * jnp.mean(f * out, axis=1, keepdims=True)
            d_out_o[here, cols] = d_out
            y_o[h * blocks + c] = dot(d_out, qe[here, pl.ds(h * DK, DK)], "tn")
        inc = y_o[h * blocks + blocks - 1]
        for c in range(blocks - 2, -1, -1):
            inc = y_o[h * blocks + c] + dot3(inc, step[h * blocks + c, :DK, :], "nt")
        inc_o[h] = inc.astype(inc_o.dtype)
    return total


def mixer_back(
    info, d_mixed, out_w, head_out, proj, gain, qe, step, ga, ta, middle, cot, gated_t, s_gu, conv, dec, inv, wu, states,
    rate, halo, convw, dlog, dbias,
    d_proj_o, d_tail_o, d_edge_o, d_rate_o, d_convw_o, d_decay_o, d_gain_o, s_down_o, s_out_o, g_gu_o,
    d_out, y, inc, later, got1, tot, got2, xpad, dpad, dsend, cols_s, d_pre_o,
    g_down, g_out, relay_d, relay_o, got_d, got_o, last_got, s1, r1, s2, r2, s3, r3, s4, r4
):
    greet(side_peers())
    settle = Settle(lambda i, b: last_got.at[i, b], s4, r4)
    for b in (2, 1, 3):
        for i in range(2):
            settle.send(s_gu.at[i, b], i, b)
    grads = (g_down, g_out)
    spread = Spread(
        lambda i, owner: grads[i].at[owner], lambda i, b: (relay_d, relay_o)[i].at[b],
        lambda i, s, b: (got_d, got_o)[i].at[s, b], s3, r3,
    )
    d_gain_o[...] = head_back(d_mixed, out_w, head_out, proj, gain, qe, step, d_out, d_proj_o, y, inc)

    def make(o, left, right):
        for j in range(0, o.shape[0], 2):
            both = dot(left[...], right[:, j * LANES : (j + 2) * LANES]).astype(BF16)
            o[j], o[j + 1] = both[:, :LANES], both[:, LANES:]

    def level_one():
        make(g_down, middle, cot)
        make(g_out, gated_t, d_mixed)

    def level_two():
        for place in PLACES:
            spread.ready(*place, (0,))

    swaps = states_backward(inc, ga, ta, later, got1, tot, got2, s1, r1, s2, r2, level_one, level_two)
    for place in PLACES:
        spread.ready(*place, (1,))
    rows = d_out.shape[0]
    heads = later.shape[0]
    blocks = rows // BLK
    strength, log_decay, pre = rates(rate, dlog, dbias)
    valid = [valid_column(info, rows, KCONV - 1 - j) for j in range(KCONV)]
    for h in range(heads):
        grad = later[h]
        for c in range(blocks - 1, -1, -1):
            u = h * blocks + c
            dsend[u] = grad
            if c:
                grad = dot3(grad, step[u, :DK, :], "nt") + y[u]
    for c in range(blocks):
        keep, first, last, tri, strict = block_masks(info, c)
        here = pl.ds(c * BLK, BLK)
        for h in range(heads):
            u = h * blocks + c
            cv = conv[here, pl.ds(h * CONVW, CONVW)]
            sg = sigmoid(cv)
            qa, ka, va, rq, rk = vectors(cv)
            rqs = rq * DK**-0.5
            q, k = qa * rqs, ka * rk
            beta = strength[c * BLK : (c + 1) * BLK, h : h + 1]
            g = log_decay[c * BLK : (c + 1) * BLK, h : h + 1]
            carry, to_end = decays(g, first, last, tri)
            dm = dec[u]
            sc = dm * dot(q, k, "nt")
            gm = dm * dot(k, k, "nt") * strict
            state, d_end = states[u], dsend[u]
            do = d_out[here, pl.ds(h * DV, DV)]
            ks = dot(k, state, "nt")
            qs = dot(q, state, "nt")
            fresh = wu[u, :, DK:] - dot(wu[u, :, :DK], state, "nt")
            kd = to_end * k
            d_fresh = dot(sc, do, "tn") + dot(kd, d_end, "nt")
            d_rhs = dot(inv[u], d_fresh, "tn")
            d_low = -dot(d_rhs, fresh, "nt")
            d_sc = dot(do, fresh, "nt")
            d_val = beta * d_rhs
            ebar = d_low * gm
            d_beta = jnp.sum(d_rhs * (va - carry * ks), axis=1, keepdims=True) + jnp.sum(ebar, axis=1, keepdims=True)
            e = d_sc * sc + beta * ebar
            d_scd = d_sc * dm
            d_gm = (beta * d_low) * (dm * strict)
            d_kd = dot(fresh, d_end)
            d_q = dot(d_scd, k) + carry * dot(do, state)
            d_k = (
                dot(d_scd, q, "tn")
                - (beta * carry) * dot(d_rhs, state)
                + to_end * d_kd
                + dot(d_gm, k)
                + dot(d_gm, k, "tn")
            )
            hcol = carry * jnp.sum(do * qs - beta * d_rhs * ks, axis=1, keepdims=True)
            fcol = jnp.sum(kd * d_kd, axis=1, keepdims=True)
            tail = carry[BLK - 1 :, :] * jnp.sum(
                jnp.sum(state * d_end, axis=1, keepdims=True), axis=0, keepdims=True
            )
            lane = iota((BLK, DK), 1)
            d_g = (
                jnp.sum(dot_exact_left(tri, e, "tn") * strict, axis=1, keepdims=True)
                + dot_exact_left(tri, jnp.where(lane == 0, hcol, 0.0), "tn")[:, :1]
                + dot_exact_left(strict, jnp.where(lane == 0, fcol, 0.0))[:, :1]
                + tail
            )
            cols_s[here, h : h + 1] = d_g
            cols_s[here, heads + h : heads + h + 1] = d_beta
            d_qa = rqs * d_q - qa * (rqs * rq * rq * jnp.sum(d_q * qa, axis=1, keepdims=True))
            d_ka = rk * d_k - ka * (rk * rk * rk * jnp.sum(d_k * ka, axis=1, keepdims=True))
            d_act = jnp.concatenate([d_qa, d_ka, d_val], axis=1)
            d_pre_o[here, pl.ds(h * CONVW, CONVW)] = d_act * (sg * (1.0 + cv * (1.0 - sg)))
            spread.relays(c * heads + h)
    d_g, d_beta = cols_s[:, :heads], cols_s[:, heads : 2 * heads]
    d_bias = -d_g * jnp.exp(dlog[...]) * sigmoid(pre)
    d_rate_o[:, :heads] = d_bias
    d_rate_o[:, heads:] = d_beta * strength * (1.0 - strength)
    d_decay_o[:, :heads] = jnp.sum(d_g * log_decay, axis=0, keepdims=True)
    d_decay_o[:, heads:] = jnp.sum(d_bias, axis=0, keepdims=True)
    for h in range(heads):
        src, dst = pl.ds(h * MIXW, CONVW), pl.ds(h * CONVW, CONVW)
        xpad[:PAD, :] = halo[:, dst]
        xpad[PAD:, :] = proj[:, src].astype(BF16).astype(F32)
        dpad[...] = jnp.zeros_like(dpad)
        d_conv = d_pre_o[:, dst]
        for j in range(KCONV):
            lo = PAD - (KCONV - 1) + j
            masked = d_conv * valid[j]
            d_convw_o[j : j + 1, dst] = jnp.sum(masked * xpad[lo : lo + rows, :], axis=0, keepdims=True)
            dpad[lo : lo + rows, :] += convw[j : j + 1, dst].astype(F32) * masked
        d_edge_o[:, dst] = dpad[:PAD, :]
        d_tail_o[:, dst] = dpad[rows - PAD :, :]
        d_proj_o[:, src] = dpad[PAD:, :].astype(BF16)
    for i in range(2):
        g_gu_o[i] = s_gu[i, 0].astype(F32) + settle.others(i)
    for i, o in ((0, s_down_o), (1, s_out_o)):
        for b in FAR:
            o[b] = spread.total(i, b).astype(BF16)
    spread.end()
    settle.end()
    for s in swaps:
        s.wait_send()


def call(kernel, outs, scratch, limit, *args, flops=2_000_000_000, nbytes=16_000_000):
    def spec(a):
        return SMEM if a.dtype == jnp.int32 else VMEM

    return pl.pallas_call(
        kernel,
        out_shape=outs,
        in_specs=[spec(a) for a in args],
        out_specs=[VMEM for _ in outs],
        scratch_shapes=scratch,
        compiler_params=pltpu.CompilerParams(vmem_limit_bytes=limit << 20),
        cost_estimate=pl.CostEstimate(flops=flops, bytes_accessed=nbytes, transcendentals=0),
    )(*args)


def sds(shape, dtype=F32):
    return jax.ShapeDtypeStruct(shape, dtype)
CHIPS = 4
LANES = 128


def cp(src, dst, send, recv, dev):
    return pltpu.make_async_remote_copy(
        src_ref=src, dst_ref=dst, send_sem=send, recv_sem=recv, device_id=dev, device_id_type=pl.DeviceIdType.MESH
    )


def greet(devices):
    barrier = pltpu.get_barrier_semaphore()
    for dev in devices:
        pl.semaphore_signal(barrier, inc=1, device_id=dev, device_id_type=pl.DeviceIdType.MESH)
    pl.semaphore_wait(barrier, len(devices))


def head_place():
    me = lax.axis_index("head")
    chip, core = me // 2, me % 2
    seq = lax.axis_index("seq")

    def dev(step, flip=False):
        c = lax.rem(chip + step, CHIPS)
        return (seq, c * 2 + (1 - core if flip else core))

    return me, chip, core, dev


def head_peers():
    dev = head_place()[3]
    return [dev(0, True)] + [dev(d) for d in range(1, CHIPS)]


def head_rows(o, rows, step, flip=False):
    owner = head_place()[3](step, flip)[1]
    return o.at[pl.ds(pl.multiple_of(owner * rows, rows), rows)]


def gather_start(x, o, ssem, rsem, lsem):
    rows = x.shape[0]
    dev = head_place()[3]
    pltpu.make_async_copy(x, head_rows(o, rows, 0), lsem).start()
    out = [cp(x, head_rows(o, rows, 0), ssem.at[d], rsem.at[d], dev(d)) for d in (2, 1, 3)]
    out.append(cp(x, head_rows(o, rows, 0), ssem.at[0], rsem.at[0], dev(0, True)))
    for s in out:
        s.start()
    return out


def gather_forward(x, o, ssem, rsem):
    rows = x.shape[0]
    dev = head_place()[3]
    out = []
    for d in (1, 3, 2):
        there = head_rows(o, rows, CHIPS - d)
        cp(x, there, ssem.at[d], rsem.at[d], dev(d)).wait_recv()
        fwd = cp(there, there, ssem.at[CHIPS + d], rsem.at[CHIPS + d], dev(0, True))
        fwd.start()
        out.append(fwd)
    return out


def gather_end(x, o, ssem, rsem, lsem, sent):
    rows = x.shape[0]
    dev = head_place()[3]
    pltpu.make_async_copy(x, head_rows(o, rows, 0), lsem).wait()
    cp(x, head_rows(o, rows, 0, True), ssem.at[0], rsem.at[0], dev(0, True)).wait_recv()
    for d in range(1, CHIPS):
        there = head_rows(o, rows, CHIPS - d, True)
        cp(x, there, ssem.at[CHIPS + d], rsem.at[CHIPS + d], dev(0, True)).wait_recv()
    for s in sent:
        s.wait_send()


def gather_over_head(x, o, ssem, rsem, lsem):
    sent = gather_start(x, o, ssem, rsem, lsem)
    sent += gather_forward(x, o, ssem, rsem)
    gather_end(x, o, ssem, rsem, lsem, sent)


def reduce_over_head(x, total, pair, got, mid, ssem, rsem):
    rows = total.shape[0]
    me, chip, core, dev = head_place()
    partner = dev(0, True)

    def at(step, flip=False):
        return x.at[pl.ds(pl.multiple_of(dev(step, flip)[1] * rows, rows), rows)]

    order = (2, 1, 3, 0)
    first = [cp(at(d, True), pair.at[d], ssem.at[d], rsem.at[d], partner) for d in order]
    for s in first:
        s.start()
    second = []
    for s, d in zip(first, order):
        s.wait_recv()
        both = at(d)[...].astype(F32) + pair[d].astype(F32)
        if d:
            mid[d] = both.astype(BF16)
            t = cp(mid.at[d], got.at[d], ssem.at[CHIPS + d], rsem.at[CHIPS + d], dev(d))
            t.start()
            second.append(t)
        else:
            total[...] = both
    for s in (second[1], second[2], second[0]):
        s.wait_recv()
    total[...] = total[...] + ((got[1].astype(F32) + got[3].astype(F32)) + got[2].astype(F32))
    for s in first + second:
        s.wait_send()


def mean_scale(v):
    return lax.rsqrt(jnp.mean(v * v, axis=1, keepdims=True) + 1e-05)


def norm_back(v, gain, d_norm):
    r = mean_scale(v)
    e = d_norm * gain
    d_v = r * e - v * (r * r * r * jnp.mean(e * v, axis=1, keepdims=True))
    return d_v, jnp.sum(d_norm * v * r, axis=0, keepdims=True)


def mid_forward(x, tokens, gain, all_o, hidden_o, total, block, pair, got, mid, s1, r1, s2, r2, ls):
    greet(head_peers())
    reduce_over_head(x, total, pair, got, mid, s1, r1)
    hidden = tokens[...].astype(F32) + total[...]
    hidden_o[...] = hidden
    block[...] = (hidden * mean_scale(hidden) * gain[...]).astype(BF16)
    gather_over_head(block, all_o, s2, r2, ls)


def mid_backward(
    x, hidden, cot, gain, d_gu, n2, all_o, d_hidden_o, d_gain_o, sums_o,
    total, block, pair, got, mid, g, relay, seqs_got, s1, r1, s2, r2, ls, s3, r3
):
    greet(head_peers() + side_peers())
    one = pair_sends(x, pair, s1, r1, FAR)
    spread = Spread(
        lambda i, owner: g.at[owner, i], lambda i, b: relay.at[i, b], lambda i, s, b: seqs_got.at[i, s, b], s3, r3
    )
    dev = seq_place()[3]
    hid = g.shape[2]

    def make(place):
        owner = dev(*place)[0]
        cols = n2[:, pl.ds(pl.multiple_of(owner * LANES, LANES), LANES)]
        out = dot(d_gu[...], cols).astype(BF16)
        g[owner, 0] = out[:hid]
        g[owner, 1] = out[hid:]
        spread.ready(*place)

    for place in PLACES[:3]:
        make(place)
    two = chip_sends(x, one, total, pair, got, mid, s1, r1, FAR)
    for place in PLACES[3:]:
        make(place)
    d_norm, d_gain = norm_back(hidden[...], gain[...], chip_sum(two, total, got))
    d_hidden = cot[...].astype(F32) + d_norm
    d_hidden_o[...] = d_hidden
    d_gain_o[...] = d_gain
    block[...] = d_hidden.astype(BF16)
    ahead = gather_start(block, all_o, s2, r2, ls)
    spread.relays()
    ahead += gather_forward(block, all_o, s2, r2)
    for b in FAR:
        for i in range(2):
            sums_o[i, b] = spread.total(i, b).astype(BF16)
    gather_end(block, all_o, s2, r2, ls, ahead)
    spread.end()
    for s in list(one.values()) + list(two.values()):
        s.wait_send()


def reach(kernel, outs, scratch, cid, limit, *args, anywhere=(), scalars=(), nbytes=12_000_000):
    return pl.pallas_call(
        kernel,
        out_shape=outs,
        in_specs=[
            pl.BlockSpec(memory_space=pl.ANY) if i in anywhere else SMEM if i in scalars else VMEM for i in range(len(args))
        ],
        out_specs=[VMEM for _ in outs],
        scratch_shapes=scratch,
        compiler_params=pltpu.CompilerParams(
            collective_id=cid, has_side_effects=True, vmem_limit_bytes=limit << 20
        ),
        cost_estimate=pl.CostEstimate(flops=0, bytes_accessed=nbytes, transcendentals=0),
    )(*args)


def sems(n):
    return pltpu.SemaphoreType.DMA((n,))


def reduce_scratch(rows, cols):
    return [pltpu.VMEM((CHIPS, rows, cols), BF16) for _ in range(3)] + [sems(2 * CHIPS), sems(2 * CHIPS)]


def gather_scratch():
    return [sems(2 * CHIPS), sems(2 * CHIPS), pltpu.SemaphoreType.DMA]


SIDE = 4


def seq_place():
    me = lax.axis_index("seq")
    z, y = me // SIDE, me % SIDE
    head = lax.axis_index("head")

    def dev(dz, dy):
        return (lax.rem(z + dz, SIDE) * SIDE + lax.rem(y + dy, SIDE), head)

    return me, z, y, dev


def side_peers():
    dev = seq_place()[3]
    return [dev(0, d) for d in range(1, SIDE)] + [dev(d, 0) for d in range(1, SIDE)]


FAR = (2, 1, 3, 0)
FIRST, OTHER = (2, 1), (3, 0)
PLACES = (
    (2, 2), (2, 1), (1, 2), (2, 3), (3, 2), (2, 0), (0, 2), (1, 3), (3, 1), (1, 0), (0, 3), (3, 3), (1, 1), (3, 0), (0, 1),
    (0, 0),
)


class Spread:
    def __init__(self, piece, relay, got, ssem, rsem):
        self.piece, self.relay, self.got, self.ssem, self.rsem = piece, relay, got, ssem, rsem
        self.dev = seq_place()[3]
        self.sent = []

    def way(self, i, a, b):
        return self.dev(b, a) if i == 0 else self.dev(a, b)

    def copy(self, i, a, b, owner):
        k = (i * SIDE + a) * SIDE + b
        if a == 2:
            dst, step = self.relay(i, b), 1 if b in FIRST else 3
        else:
            dst, step = self.got(i, 0 if a == 1 else 1, b), a
        return cp(self.piece(i, owner), dst, self.ssem.at[k], self.rsem.at[k], self.way(i, step, 0))

    def send(self, i, a, b, owner):
        s = self.copy(i, a, b, owner)
        s.start()
        self.sent.append(s)

    def late(self, a, b):
        return a == 1 and b in FIRST or a == 3 and b in OTHER

    def ready(self, dz, dy, halves_=(0, 1)):
        owner = self.dev(dz, dy)[0]
        for i in halves_:
            a, b = (dy, dz) if i == 0 else (dz, dy)
            if a and not self.late(a, b):
                self.send(i, a, b, owner)

    def relays(self, part=None):
        for n, b in enumerate(FAR):
            if part is not None and n != part:
                continue
            for i in range(2):
                a = 1 if b in FIRST else 3
                owner = self.way(i, a, b)[0]
                self.copy(i, 2, b, owner).wait_recv()
                both = self.piece(i, owner)[...].astype(F32) + self.relay(i, b)[...].astype(F32)
                self.relay(i, b)[...] = both.astype(BF16)
                k = (i * SIDE + a) * SIDE + b
                s = cp(
                    self.relay(i, b), self.got(i, 0 if a == 1 else 1, b), self.ssem.at[k], self.rsem.at[k],
                    self.way(i, a, 0),
                )
                s.start()
                self.sent.append(s)

    def total(self, i, b):
        owner = self.way(i, 0, b)[0]
        for a in (1, 3):
            self.copy(i, a, b, owner).wait_recv()
        return self.piece(i, owner)[...].astype(F32) + (
            self.got(i, 0, b)[...].astype(F32) + self.got(i, 1, b)[...].astype(F32)
        )

    def end(self):
        for s in self.sent:
            s.wait_send()


class Settle:
    def __init__(self, got, ssem, rsem):
        self.got, self.ssem, self.rsem = got, ssem, rsem
        self.dev = seq_place()[3]
        self.sent = {}

    def send(self, src, i, b):
        k = i * SIDE + b
        dev = self.dev(b, 0) if i == 0 else self.dev(0, b)
        self.sent[i, b] = cp(src, self.got(i, b), self.ssem.at[k], self.rsem.at[k], dev)
        self.sent[i, b].start()

    def others(self, i):
        for b in (1, 3, 2):
            self.sent[i, b].wait_recv()
        return (self.got(i, 1)[...].astype(F32) + self.got(i, 3)[...].astype(F32)) + self.got(i, 2)[...].astype(F32)

    def end(self):
        for s in self.sent.values():
            s.wait_send()


def share_start(src, got, place, to, ssem, rsem):
    got[place] = src[...]
    out = [cp(src, got.at[place], ssem.at[d], rsem.at[d], to(d)) for d in (2, 1, 3)]
    for s in out:
        s.start()

    def wait():
        for d in (1, 3, 2):
            back = lax.rem(place + SIDE - d, SIDE)
            cp(src, got.at[back], ssem.at[d], rsem.at[d], to(d)).wait_recv()

    return out, wait


def share(src, got, place, to, ssem, rsem):
    out, wait = share_start(src, got, place, to, ssem, rsem)
    wait()
    return out


def unit_top():
    return jnp.where(iota((DK + DV, DK), 0) == iota((DK + DV, DK), 1), 1.0, 0.0)


def add_low(pair, low):
    return jnp.concatenate([pair[:DK], pair[DK:] + low], axis=0)


def states_forward(ab, start_o, ga_o, ta_o, got1, tot, got2, s1, r1, s2, r2):
    me, z, y, dev = seq_place()
    heads = ab.shape[0]
    greet(side_peers())
    out = share(ab, got1, y, lambda d: dev(0, d), s1, r1)
    before = []
    for h in range(heads):
        whole = got1[0, h].astype(F32)
        prefix = jnp.where(y > 0, whole, unit_top())
        for j in range(1, SIDE):
            a, b = got1[j, h, :DK, :], got1[j, h, DK:, :].astype(F32)
            whole = add_low(dot_left2(whole, a), b)
            if j < SIDE - 1:
                prefix = jnp.where(y > j, whole, prefix)
        tot[h] = whole.astype(BF16)
        before.append(prefix)
        for j in range(SIDE):
            ga_o[j, h] = got1[j, h, :DK, :]
    out += share(tot, got2, z, lambda d: dev(d, 0), s2, r2)
    for h in range(heads):
        held = jnp.zeros((DV, DK), F32)
        for j in range(SIDE - 1):
            held = jnp.where(
                z > j, dot_left2(held, got2[j, h, :DK, :]) + got2[j, h, DK:, :].astype(F32), held
            )
        start_o[h] = dot3(held, before[h][:DK]) + before[h][DK:]
        for j in range(SIDE):
            ta_o[j, h] = got2[j, h, :DK, :]
    for s in out:
        s.wait_send()


def states_backward(inc, ga, ta, later_o, got1, tot, got2, s1, r1, s2, r2, level_one, level_two):
    me, z, y, dev = seq_place()
    heads = inc.shape[0]
    out, wait = share_start(inc, got1, y, lambda d: dev(0, d), s1, r1)
    level_one()
    wait()
    after = []
    for h in range(heads):
        whole = add_low(dot(unit_top(), ga[SIDE - 1, h], "nt"), got1[SIDE - 1, h].astype(F32))
        suffix = jnp.where(y < SIDE - 1, whole, unit_top())
        for j in range(SIDE - 2, -1, -1):
            whole = add_low(dot_left2(whole, ga[j, h], "nt"), got1[j, h].astype(F32))
            if j:
                suffix = jnp.where(y < j, whole, suffix)
        tot[h] = whole[DK:].astype(BF16)
        after.append(suffix)
    more, wait = share_start(tot, got2, z, lambda d: dev(d, 0), s2, r2)
    level_two()
    wait()
    for h in range(heads):
        held = jnp.zeros((DV, DK), F32)
        for j in range(SIDE - 1, 0, -1):
            held = jnp.where(z < j, dot_left2(held, ta[j, h], "nt") + got2[j, h].astype(F32), held)
        later_o[h] = dot3(held, after[h][:DK]) + after[h][DK:]
    return out + more


def pair_sends(x, pair, ssem, rsem, steps):
    rows = pair.shape[1]
    dev = head_place()[3]
    out = {}
    for d in steps:
        owner = dev(d, True)[1]
        src = x.at[pl.ds(pl.multiple_of(owner * rows, rows), rows)]
        out[d] = cp(src, pair.at[d], ssem.at[d], rsem.at[d], dev(0, True))
        out[d].start()
    return out


def chip_sends(x, first, total, pair, got, mid, ssem, rsem, steps):
    rows = pair.shape[1]
    dev = head_place()[3]
    out = {}
    for d in steps:
        first[d].wait_recv()
        owner = dev(d)[1]
        both = x[pl.ds(pl.multiple_of(owner * rows, rows), rows), :].astype(F32) + pair[d].astype(F32)
        if d:
            mid[d] = both.astype(BF16)
            out[d] = cp(mid.at[d], got.at[d], ssem.at[CHIPS + d], rsem.at[CHIPS + d], dev(d))
            out[d].start()
        else:
            total[...] = both
    return out


def chip_sum(second, total, got):
    for d in (1, 3, 2):
        second[d].wait_recv()
    return total[...] + ((got[1].astype(F32) + got[3].astype(F32)) + got[2].astype(F32))


def finish(
    dproj, normed, w, d_rate, rate_w, d_tail, d_edge, feed, hidden, tokens, d_hidden, gain, convs, decay, g_feed, g_head,
    s_down, s_out,
    layer_o, d_tokens_o, g_mixer_o, gains_o, convs_o, rate_o, g_down_o, g_out_o,
    dp, wv, edge, g, relay, got1, mid, got2, dn, ta, pa, ga, ma, tb, pb, gb, mb, gains, gbuf, sbuf, rbuf, got_d, got_o,
    es, er, ls, s1, r1, s2, r2, sa, ra, sb, rb, sg, rg, ss, rs, s5, r5
):
    me, z, y, dev = seq_place()
    head = lax.axis_index("head")
    heads, seqs = gbuf.shape[0], rbuf.shape[0]
    rows = dp.shape[0]
    part, half = g_mixer_o.shape[1], g_mixer_o.shape[2]
    across = [(me, lax.rem(head + d, heads)) for d in range(1, heads)]
    along = [(lax.rem(me + d, seqs), head) for d in range(1, seqs)]
    load_p = pltpu.make_async_copy(dproj, dp, ls.at[0])
    load_p.start()
    load_w = pltpu.make_async_copy(w, wv, ls.at[1])
    load_w.start()
    greet(across + along)
    back = cp(d_edge, edge, es, er, (lax.rem(me + seqs - 1, seqs), head))
    back.start()
    feed_one = pair_sends(feed, pa, sa, ra, FAR)
    load_p.wait()
    back.wait_recv()
    there = jnp.where(me < seqs - 1, edge[...], 0.0)
    tail = jnp.concatenate([d_tail[:PAD, :], d_tail[PAD:, :] + there], axis=0).astype(BF16)
    wide = half - DV
    for i in range(2):
        dp[rows - 2 * PAD :, pl.ds(i * half, wide)] = tail[:, i * wide : (i + 1) * wide]

    sums = (s_down, s_out)
    settle = Settle(lambda i, b: (got_d, got_o)[i].at[b], s5, r5)
    for b in (2, 1, 3):
        for i in range(2):
            settle.send(sums[i].at[b], i, b)

    spread = Spread(
        lambda i, owner: g.at[i, owner], lambda i, b: relay.at[i, b], lambda i, s, b: got1.at[i, s, b], s1, r1
    )
    settle_two = Settle(lambda i, b: got2.at[i, b], s2, r2)
    for place in PLACES:
        owner = dev(*place)[0]
        left = normed[:, pl.ds(pl.multiple_of(owner * part, part), part)]
        both = dot(left, dp[...], "tn").astype(BF16)
        for i in range(2):
            g[i, owner] = both[:, i * half : (i + 1) * half]
        spread.ready(*place)
    feed_two = chip_sends(feed, feed_one, ta, pa, ga, ma, sa, ra, FAR)
    rates_t = dot(d_rate[:, :PAD], normed[...], "tn")

    load_w.wait()
    low = rows // CHIPS
    hp = head_place()[3]
    dn_one = {}
    for d in FAR:
        chip = hp(d)[1] // 2
        here = pl.ds(pl.multiple_of(chip * low, low), low)
        dn[here, :] = (dot(dp[here, :], wv[...], "nt") + dot(d_rate[here, :], rate_w[...], "nt")).astype(BF16)
        dn_one.update(pair_sends(dn, pb, sb, rb, (d,)))
        spread.relays(FAR.index(d))
    dn_two = chip_sends(dn, dn_one, tb, pb, gb, mb, sb, rb, FAR)
    layer_o[...] = (hidden[...] + chip_sum(feed_two, ta, ga)).astype(BF16)
    d_norm, d_gain = norm_back(tokens[...].astype(F32), gain[...], chip_sum(dn_two, tb, gb))
    d_tokens_o[...] = d_hidden[...] + d_norm

    ng = gains.shape[0]
    n_row = D // LANES
    gains[...] = jnp.zeros_like(gains)
    for r in range(n_row):
        at = slice(r * LANES, (r + 1) * LANES)
        gains[r : r + 1, :] = d_gain[:, at]
        gains[n_row + r : n_row + r + 1, :] = g_feed[:, at]
    for r in range(DV // LANES):
        gains[2 * n_row + r : 2 * n_row + r + 1, :] = g_head[:, r * LANES : (r + 1) * LANES]
    gbuf[head] = gains[...]
    g_out = [cp(gains, gbuf.at[head], sg.at[d], rg.at[d], across[d - 1]) for d in range(1, heads)]
    for s in g_out:
        s.start()
    taps, wide_c = convs.shape
    c_row = wide_c // LANES
    nc = taps * c_row
    for j in range(seqs):
        for t in range(taps):
            for r in range(c_row):
                lo = ng + t * c_row + r
                if j == 0:
                    sbuf[0, lo : lo + 1, :] = convs[t : t + 1, r * LANES : (r + 1) * LANES]
        if j == 0:
            sbuf[0, ng + nc : ng + nc + PAD, :] = jnp.zeros((PAD, LANES), F32)
            sbuf[0, ng + nc : ng + nc + 1, :] = decay[...]
        else:
            sbuf[j, ng : ng + nc + PAD, :] = sbuf[0, ng : ng + nc + PAD, :]
        sbuf[j, ng + nc + PAD :, :] = rates_t[:, j * LANES : (j + 1) * LANES]
    for d in range(1, heads):
        cp(gains, gbuf.at[lax.rem(head + heads - d, heads)], sg.at[d], rg.at[d], across[d - 1]).wait_recv()
    total = gbuf[0]
    for i in range(1, heads):
        total = total + gbuf[i]
    for j in range(seqs):
        sbuf[j, :ng, :] = total
    rbuf[me] = sbuf[me]
    s_out = []
    for d in range(1, seqs):
        s = cp(sbuf.at[lax.rem(me + d, seqs)], rbuf.at[me], ss.at[d], rs.at[d], along[d - 1])
        s.start()
        s_out.append(s)

    for i, o in ((0, g_down_o), (1, g_out_o)):
        o[...] = sums[i][0].astype(F32) + settle.others(i)

    for b in FAR:
        for i in range(2):
            both = spread.total(i, b)
            if b:
                mid[i, b] = both.astype(BF16)
                settle_two.send(mid.at[i, b], i, b)
            else:
                g_mixer_o[i] = both
    for d in range(1, seqs):
        cp(sbuf.at[0], rbuf.at[lax.rem(me + seqs - d, seqs)], ss.at[d], rs.at[d], along[d - 1]).wait_recv()
    total = rbuf[0]
    for i in range(1, seqs):
        total = total + rbuf[i]
    gains_o[...] = total[:ng]
    convs_o[...] = total[ng : ng + nc + PAD]
    rate_o[...] = total[ng + nc + PAD :]
    for i in range(2):
        g_mixer_o[i] = g_mixer_o[i] + settle_two.others(i)
    spread.end()
    settle.end()
    settle_two.end()
    done = g_out + s_out + [back]
    done += list(feed_one.values()) + list(feed_two.values()) + list(dn_one.values()) + list(dn_two.values())
    for s in done:
        s.wait_send()


def passed_along(shard, axis, by):
    length = lax.axis_size(axis)
    pairs = [(i, i + by) for i in range(length) if 0 <= i + by < length]
    return lax.ppermute(shard, axis, pairs)


def rms_scale(values, gain):
    return values * lax.rsqrt(jnp.mean(values * values, axis=-1, keepdims=True) + 1e-05) * gain


def local(
    tokens, mixer_gain, mixer_weight, rate_weight, conv_weight, decay_log, decay_bias, head_gain,
    output_weight, feed_gain, gate_up_weight, down_weight, doc_starts, cotangent,
):
    resid = tokens.astype(F32)
    normed = rms_scale(resid, mixer_gain).astype(BF16)
    gathered = lax.all_gather(normed, "head", axis=0, tiled=True)
    heads = mixer_weight.shape[1]
    gathered, cot_own, mixer_flat = lax.optimization_barrier(
        (gathered, cotangent, mixer_weight.reshape(D, heads * MIXW))
    )
    cot_rows = lax.all_gather(cot_own, "head", axis=0, tiled=True)
    rows = gathered.shape[0]
    blocks = rows // BLK
    units = heads * blocks
    seq = lax.axis_size("seq")
    projected = jnp.dot(gathered, mixer_flat, preferred_element_type=F32)
    rate_proj = jnp.einsum("td,dgh->tgh", gathered, rate_weight, preferred_element_type=F32).reshape(rows, 2 * heads)
    rim = projected[rows - PAD :].reshape(PAD, heads, MIXW)[:, :, :CONVW].reshape(PAD, heads * CONVW).astype(BF16)
    halo = passed_along(rim, "seq", 1).astype(F32)
    convw = conv_weight.reshape(KCONV, heads * CONVW)
    info = jnp.concatenate(
        [doc_starts, jnp.stack([lax.axis_index("seq") * rows, lax.axis_index("seq")]).astype(jnp.int32)]
    )
    dlog, dbias = decay_log.reshape(1, heads), decay_bias.reshape(1, heads)
    gain = head_gain.reshape(1, DV)

    conv, dec, inv, wu, qe, ol, step, ab = call(
        fwd_prep,
        [
            sds((rows, heads * CONVW)), sds((units, BLK, BLK)), sds((units, BLK, BLK), BF16),
            sds((units, BLK, DK + DV)), sds((rows, heads * DK)), sds((rows, heads * DV)),
            sds((units, DK + DV, DK)), sds((heads, DK + DV, DK), BF16),
        ],
        [pltpu.VMEM((PAD + rows, CONVW), F32)],
        56, info, projected, halo, rate_proj, convw, dlog, dbias,
    )
    start, ga, ta = reach(
        states_forward,
        [sds((heads, DV, DK)), sds((SIDE, heads, DK, DK), BF16), sds((SIDE, heads, DK, DK), BF16)],
        [
            pltpu.VMEM((SIDE, heads, DK + DV, DK), BF16), pltpu.VMEM((heads, DK + DV, DK), BF16),
            pltpu.VMEM((SIDE, heads, DK + DV, DK), BF16), sems(SIDE), sems(SIDE), sems(SIDE), sems(SIDE),
        ],
        1, 40, ab,
    )
    states, head_out, gated = call(
        fwd_out,
        [sds((units, DV, DK)), sds((rows, heads * DV)), sds((rows, heads * DV), BF16)],
        [], 48, start, step, qe, ol, projected, gain,
    )
    out_flat = output_weight.reshape(heads * DV, D)
    own = tokens.shape[0]
    mixed = jnp.dot(gated, out_flat, preferred_element_type=F32).astype(BF16)
    feed_row = feed_gain.reshape(1, D)
    gathered_two, hidden = reach(
        mid_forward,
        [sds((rows, D), BF16), sds((own, D))],
        [pltpu.VMEM((own, D), F32), pltpu.VMEM((own, D), BF16)] + reduce_scratch(own, D) + gather_scratch(),
        2, 48, mixed, tokens, feed_row,
    )
    hid = down_weight.shape[0]
    gu_t = gate_up_weight.transpose(1, 2, 0).reshape(2 * hid, D)
    by_last = (((1,), (1,)), ((), ()))
    by_first = (((0,), (0,)), ((), ()))
    d_middle = lax.dot_general(down_weight, cot_rows, by_last, preferred_element_type=F32)
    gate_up = lax.dot_general(gu_t, gathered_two, by_last, preferred_element_type=F32)
    gate, up = gate_up[:hid], gate_up[hid:]
    s = jax.nn.sigmoid(gate)
    middle = (gate * s * up).astype(BF16)
    d_gate_up = jnp.concatenate([d_middle * up * (s * (1.0 + gate * (1.0 - s))), d_middle * gate * s]).astype(BF16)
    d_two = lax.dot_general(d_gate_up, gu_t, by_first, preferred_element_type=F32).astype(BF16)
    part, half, n_head = D // seq, MIXW, lax.axis_size("head")
    d_mixed, d_hidden, g_feed_gain, grads = reach(
        mid_backward,
        [sds((rows, D), BF16), sds((own, D)), sds((1, D)), sds((2, SIDE, hid, LANES), BF16)],
        [pltpu.VMEM((own, D), F32), pltpu.VMEM((own, D), BF16)]
        + [pltpu.VMEM((CHIPS, own, D), BF16) for _ in range(3)]
        + [
            pltpu.VMEM((seq, 2, hid, LANES), BF16), pltpu.VMEM((2, SIDE, hid, LANES), BF16),
            pltpu.VMEM((2, 2, SIDE, hid, LANES), BF16), sems(2 * CHIPS), sems(2 * CHIPS),
        ]
        + gather_scratch()
        + [sems(2 * SIDE * SIDE), sems(2 * SIDE * SIDE)],
        3, 60, d_two, hidden, cotangent, feed_row, d_gate_up, gathered_two, nbytes=30_000_000,
    )
    d_mixed, middle = lax.optimization_barrier((d_mixed, middle))
    feed = lax.dot_general(middle, down_weight, by_first, preferred_element_type=F32).astype(BF16)
    gated_t = gated.T
    d_projected, d_tail, d_edge, d_rate, d_convw, d_decay, g_head_gain, s_down, s_out, grad_gate_up = reach(
        mixer_back,
        [
            sds((rows, heads * MIXW), BF16), sds((2 * PAD, heads * CONVW)), sds((PAD, heads * CONVW)),
            sds((rows, 2 * heads)), sds((KCONV, heads * CONVW)), sds((1, 2 * heads)), sds((1, DV)),
            sds((SIDE, hid, LANES), BF16), sds((SIDE, heads * DV, LANES), BF16), sds((2, hid, LANES)),
        ],
        [
            pltpu.VMEM((rows, heads * DV), F32), pltpu.VMEM((units, DV, DK), F32),
            pltpu.VMEM((heads, DV, DK), BF16), pltpu.VMEM((heads, DV, DK), F32),
            pltpu.VMEM((SIDE, heads, DV, DK), BF16), pltpu.VMEM((heads, DV, DK), BF16),
            pltpu.VMEM((SIDE, heads, DV, DK), BF16),
            pltpu.VMEM((PAD + rows, CONVW), F32), pltpu.VMEM((PAD + rows, CONVW), F32),
            pltpu.VMEM((units, DV, DK), F32), pltpu.VMEM((rows, DK), F32), pltpu.VMEM((rows, heads * CONVW), F32),
            pltpu.VMEM((seq, hid, LANES), BF16), pltpu.VMEM((seq, heads * DV, LANES), BF16),
            pltpu.VMEM((SIDE, hid, LANES), BF16), pltpu.VMEM((SIDE, heads * DV, LANES), BF16),
            pltpu.VMEM((2, SIDE, hid, LANES), BF16), pltpu.VMEM((2, SIDE, heads * DV, LANES), BF16),
            pltpu.VMEM((2, SIDE, hid, LANES), BF16),
            sems(SIDE), sems(SIDE), sems(SIDE), sems(SIDE), sems(2 * SIDE * SIDE), sems(2 * SIDE * SIDE),
            sems(2 * SIDE), sems(2 * SIDE),
        ],
        4, 63, info, d_mixed, out_flat, head_out, projected, gain, qe, step, ga, ta, middle, cot_rows, gated_t, grads,
        conv, dec, inv, wu, states, rate_proj, halo, convw, dlog, dbias, scalars=(0,), nbytes=40_000_000,
    )
    grad_gate_up = grad_gate_up.transpose(2, 0, 1)
    d_rate_low = jnp.pad(d_rate.astype(BF16), ((0, 0), (0, LANES - 2 * heads)))
    rate_pad = jnp.pad(rate_weight.reshape(D, 2 * heads), ((0, 0), (0, LANES - 2 * heads)))
    d_decay = jnp.pad(d_decay, ((0, 0), (0, LANES - 2 * heads)))
    n_gain, n_conv = 40, KCONV * heads * CONVW // LANES + PAD
    small = n_gain + n_conv + PAD
    layer_out, grad_tokens, grad_mixer, gains, convs, rate_own, grad_down, grad_output = reach(
        finish,
        [
            sds((own, D), BF16), sds((own, D)), sds((2, part, half)), sds((n_gain, LANES)), sds((n_conv, LANES)),
            sds((PAD, LANES)), sds((hid, LANES)), sds((heads * DV, LANES)),
        ],
        [
            pltpu.VMEM((rows, heads * MIXW), BF16), pltpu.VMEM((D, heads * MIXW), BF16),
            pltpu.VMEM((PAD, heads * CONVW), F32), pltpu.VMEM((2, seq, part, half), BF16),
            pltpu.VMEM((2, SIDE, part, half), BF16), pltpu.VMEM((2, 2, SIDE, part, half), BF16),
            pltpu.VMEM((2, SIDE, part, half), BF16), pltpu.VMEM((2, SIDE, part, half), BF16), pltpu.VMEM((rows, D), BF16),
        ]
        + 2 * ([pltpu.VMEM((own, D), F32)] + [pltpu.VMEM((CHIPS, own, D), BF16) for _ in range(3)])
        + [
            pltpu.VMEM((n_gain, LANES), F32), pltpu.VMEM((n_head, n_gain, LANES), F32),
            pltpu.VMEM((seq, small, LANES), F32), pltpu.VMEM((seq, small, LANES), F32),
            pltpu.VMEM((SIDE, hid, LANES), BF16), pltpu.VMEM((SIDE, heads * DV, LANES), BF16),
            pltpu.SemaphoreType.DMA, pltpu.SemaphoreType.DMA, sems(2),
            sems(2 * SIDE * SIDE), sems(2 * SIDE * SIDE), sems(2 * SIDE), sems(2 * SIDE),
            sems(2 * CHIPS), sems(2 * CHIPS), sems(2 * CHIPS), sems(2 * CHIPS),
            sems(n_head), sems(n_head), sems(seq), sems(seq), sems(2 * SIDE), sems(2 * SIDE),
        ],
        5, 62, d_projected, gathered, mixer_flat, d_rate_low, rate_pad, d_tail, d_edge, feed, hidden, tokens,
        d_hidden, mixer_gain.reshape(1, D), d_convw, d_decay, g_feed_gain, g_head_gain, s_down, s_out,
        anywhere=(0, 2), nbytes=40_000_000,
    )
    grad_mixer = grad_mixer.transpose(1, 0, 2)
    grad_output = grad_output.reshape(heads, DV, LANES)
    gains, convs = gains.reshape(-1), convs.reshape(-1)
    grad_mixer_gain, grad_feed_gain, grad_head_gain = gains[:D], gains[D : 2 * D], gains[2 * D : 2 * D + DV]
    n = KCONV * heads * CONVW
    grad_conv = convs[:n].reshape(KCONV, heads, CONVW)
    grad_decay_log, grad_decay_bias = convs[n : n + heads], convs[n + heads : n + 2 * heads]
    grad_rate = rate_own[: 2 * heads].reshape(2, heads, part).transpose(2, 0, 1)
    return (
        layer_out, grad_tokens, grad_mixer_gain, grad_mixer, grad_rate, grad_conv, grad_decay_log, grad_decay_bias,
        grad_head_gain, grad_output, grad_feed_gain, grad_gate_up, grad_down,
    )


def solution(mesh):
    rows = P(("seq", "head"), None)
    return jax.shard_map(
        local,
        mesh=mesh,
        in_specs=(
            rows, P(), P(None, "head", None), P(None, None, "head"), P(None, "head", None), P("head"), P("head"),
            P(), P("head", None, None), P(), P(None, None, "head"), P("head", None), P(), rows,
        ),
        out_specs=(
            rows, rows, P(), P("seq", "head", None), P("seq", None, "head"), P(None, "head", None), P("head"),
            P("head"), P(), P("head", None, "seq"), P(), P("seq", None, "head"), P("head", "seq"),
        ),
        check_vma=False,
    )
```

```python
import functools

import jax
import jax.numpy as jnp
from jax import lax
from jax.experimental import pallas as pl
from jax.experimental.pallas import tpu as pltpu
from jax.sharding import PartitionSpec as P

D = 2048
DK = 128
DV = 256
KCONV = 4
MIXW = 768
CONVW = 512
NB = 4
BLK = 256
PAD = 8
F32 = jnp.float32
BF16 = jnp.bfloat16

VMEM = pl.BlockSpec(memory_space=pltpu.VMEM)
SMEM = pl.BlockSpec(memory_space=pltpu.SMEM)


def dot(a, b, form="nn"):
    dims = {"nn": ((1,), (0,)), "nt": ((1,), (1,)), "tn": ((0,), (0,))}[form]
    return lax.dot_general(a.astype(BF16), b.astype(BF16), (dims, ((), ())), preferred_element_type=F32)


def halves(a):
    hi = a.astype(BF16)
    return hi, (a - hi.astype(F32)).astype(BF16)


def dot3(a, b, form="nn"):
    ah, al = halves(a)
    bh, bl = halves(b)
    return dot(ah, bh, form) + (dot(ah, bl, form) + dot(al, bh, form))


def dot_exact_left(a, b, form="nn"):
    b1, rest = halves(b)
    rest = b - b1.astype(F32)
    b2 = rest.astype(BF16)
    b3 = (rest - b2.astype(F32)).astype(BF16)
    return dot(a, b1, form) + (dot(a, b2, form) + dot(a, b3, form))


def iota(shape, axis):
    return lax.broadcasted_iota(jnp.int32, shape, axis)


def doc_of(info, pos):
    count = jnp.zeros(pos.shape, jnp.int32)
    for i in range(NB):
        count = count + jnp.where(pos >= info[i], 1, 0)
    return jnp.where(pos < 0, -1, count)


def sigmoid(v):
    return 1.0 / (1.0 + jnp.exp(-v))


def softplus(v):
    return jnp.maximum(v, 0.0) + jnp.log1p(jnp.exp(-jnp.abs(v)))


def unit_lower_inverse(low):
    n = low.shape[0]
    row, col = iota((n, n), 0), iota((n, n), 1)
    eye = jnp.where(row == col, 1.0, 0.0)

    def same(b):
        return row // b == col // b

    x = jnp.where(same(8), -low, 0.0)
    inv = eye + x
    x = dot(x, x)
    inv = inv + dot(inv, x)
    x = dot(x, x)
    inv = inv + dot(inv, x)
    b = 8
    while b < n:
        off = jnp.where(same(2 * b) & jnp.logical_not(same(b)), low, 0.0)
        inv = inv - dot(inv, dot(off, inv))
        b *= 2
    return inv + dot(inv, eye - inv - dot3(low, inv))


def valid_column(info, rows, back):
    pos = info[NB] + iota((rows, 1), 0)
    return jnp.where(doc_of(info, pos) == doc_of(info, pos - back), 1.0, 0.0)


def vectors(conv):
    act = conv * sigmoid(conv)
    qa, ka, va = act[:, :DK], act[:, DK : 2 * DK], act[:, 2 * DK :]
    rq = lax.rsqrt(jnp.sum(qa * qa, axis=1, keepdims=True) + 1e-06)
    rk = lax.rsqrt(jnp.sum(ka * ka, axis=1, keepdims=True) + 1e-06)
    return qa, ka, va, rq, rk


def rates(rate_ref, dlog_ref, dbias_ref):
    heads = dlog_ref.shape[1]
    pre = rate_ref[:, :heads] + dbias_ref[...]
    log_decay = -jnp.exp(dlog_ref[...]) * softplus(pre)
    return sigmoid(rate_ref[:, heads:]), log_decay, pre


def block_masks(info, c):
    row, col = iota((BLK, BLK), 0), iota((BLK, BLK), 1)
    base = info[NB] + c * BLK
    docs_r, docs_c = doc_of(info, base + row), doc_of(info, base + col)
    keep = (docs_r == docs_c) & (col <= row)
    column = doc_of(info, base + iota((BLK, 1), 0))
    first = jnp.where(column == doc_of(info, base - 1 + iota((BLK, 1), 0) * 0), 1.0, 0.0)
    last = jnp.where(column == doc_of(info, base + BLK - 1 + iota((BLK, 1), 0) * 0), 1.0, 0.0)
    tri = jnp.where(col <= row, 1.0, 0.0)
    strict = jnp.where(col < row, 1.0, 0.0)
    return keep, first, last, tri, strict


def decays(g, first, last, tri):
    cum = dot_exact_left(tri, jnp.broadcast_to(g, (BLK, DK)))[:, :1]
    carry = first * jnp.exp(cum)
    to_end = last * jnp.exp(cum[BLK - 1 :, :] - cum)
    return carry, to_end


def fwd_prep(info, proj, halo, rate, convw, dlog, dbias, conv_o, dec_o, inv_o, wu_o, qe_o, ol_o, step_o, ab_o, xpad):
    rows = proj.shape[0]
    heads = dlog.shape[1]
    blocks = rows // BLK
    strength, log_decay, _ = rates(rate, dlog, dbias)
    valid = [valid_column(info, rows, KCONV - 1 - j) for j in range(KCONV)]
    for h in range(heads):
        src, dst = pl.ds(h * MIXW, CONVW), pl.ds(h * CONVW, CONVW)
        xpad[:PAD, :] = halo[:, dst]
        xpad[PAD:, :] = proj[:, src].astype(BF16).astype(F32)
        conv = jnp.zeros((rows, CONVW), F32)
        for j in range(KCONV):
            lo = PAD - (KCONV - 1) + j
            conv = conv + convw[j : j + 1, dst].astype(F32) * xpad[lo : lo + rows, :] * valid[j]
        conv_o[:, dst] = conv
    for c in range(blocks):
        keep, first, last, tri, strict = block_masks(info, c)
        here = pl.ds(c * BLK, BLK)
        for h in range(heads):
            qa, ka, va, rq, rk = vectors(conv_o[here, pl.ds(h * CONVW, CONVW)])
            q, k = qa * (rq * DK**-0.5), ka * rk
            beta = strength[c * BLK : (c + 1) * BLK, h : h + 1]
            g = log_decay[c * BLK : (c + 1) * BLK, h : h + 1]
            spread = dot_exact_left(tri, g * strict)
            dec = jnp.where(keep, jnp.exp(jnp.where(keep, spread, 0.0)), 0.0)
            carry, to_end = decays(g, first, last, tri)
            low = strict * (beta * dec * dot(k, k, "nt"))
            inv = unit_lower_inverse(low)
            u = h * blocks + c
            dec_o[u] = dec
            inv_o[u] = inv.astype(BF16)
            rhs = jnp.concatenate([(beta * carry) * k, beta * va], axis=1)
            wu = dot(inv, rhs)
            wu_o[u] = wu
            out = dot(dec * dot(q, k, "nt"), wu)
            qe_o[here, pl.ds(h * DK, DK)] = carry * q - out[:, :DK]
            ol_o[here, pl.ds(h * DV, DV)] = out[:, DK:]
            step = dot(wu, to_end * k, "tn")
            eye = jnp.where(iota((DK, DK), 0) == iota((DK, DK), 1), 1.0, 0.0)
            step_o[u, :DK] = carry[BLK - 1 :, :] * eye - step[:DK]
            step_o[u, DK:] = step[DK:]
    for h in range(heads):
        ab = step_o[h * blocks]
        for c in range(1, blocks):
            nxt = step_o[h * blocks + c]
            ab = dot3(ab, nxt[:DK])
            ab_o_tail = nxt[DK:]
            ab = jnp.concatenate([ab[:DK], ab[DK:] + ab_o_tail], axis=0)
        ab_o[h] = ab.astype(ab_o.dtype)


def fwd_out(start, step, qe, ol, proj, gain, states_o, head_o, gated_o):
    rows = qe.shape[0]
    heads = start.shape[0]
    blocks = rows // BLK
    for h in range(heads):
        state = start[h]
        for c in range(blocks):
            u = h * blocks + c
            here = pl.ds(c * BLK, BLK)
            states_o[u] = state
            out = ol[here, pl.ds(h * DV, DV)] + dot(qe[here, pl.ds(h * DK, DK)], state, "nt")
            head_o[here, pl.ds(h * DV, DV)] = out
            gate = proj[here, pl.ds(h * MIXW + CONVW, DV)]
            scale = lax.rsqrt(jnp.mean(out * out, axis=1, keepdims=True) + 1e-05)
            gated_o[here, pl.ds(h * DV, DV)] = (out * scale * gain[...] * (gate * sigmoid(gate))).astype(BF16)
            if c + 1 < blocks:
                state = dot3(state, step[u, :DK, :]) + step[u, DK:, :]


def dot_left2(a, b, form="nn"):
    ah, al = halves(a)
    return dot(ah, b, form) + dot(al, b, form)


def head_back(d_mixed, out_w, head_out, proj, gain, qe, step, d_out_o, d_gate_o, y_o, inc_o):
    rows = qe.shape[0]
    blocks = rows // BLK
    heads = qe.shape[1] // DK
    total = jnp.zeros((1, DV), F32)
    for h in range(heads):
        cols = pl.ds(h * DV, DV)
        for c in range(blocks):
            here = pl.ds(c * BLK, BLK)
            dg, out = dot(d_mixed[here, :], out_w[cols, :], "nt"), head_out[here, cols]
            gate = proj[here, pl.ds(h * MIXW + CONVW, DV)]
            s = sigmoid(gate)
            silu = gate * s
            scale = lax.rsqrt(jnp.mean(out * out, axis=1, keepdims=True) + 1e-05)
            dn = dg * (out * scale)
            d_gate_o[here, pl.ds(h * MIXW + CONVW, DV)] = (dn * gain[...] * (s * (1.0 + gate * (1.0 - s)))).astype(BF16)
            total = total + jnp.sum(dn * silu, axis=0, keepdims=True)
            f = dg * gain[...] * silu
            d_out = scale * f - out * (scale * scale * scale) * jnp.mean(f * out, axis=1, keepdims=True)
            d_out_o[here, cols] = d_out
            y_o[h * blocks + c] = dot(d_out, qe[here, pl.ds(h * DK, DK)], "tn")
        inc = y_o[h * blocks + blocks - 1]
        for c in range(blocks - 2, -1, -1):
            inc = y_o[h * blocks + c] + dot3(inc, step[h * blocks + c, :DK, :], "nt")
        inc_o[h] = inc.astype(inc_o.dtype)
    return total


def mixer_back(
    info, d_mixed, out_w, head_out, proj, gain, qe, step, ga, ta, middle, cot, gated_t, s_gu, conv, dec, inv, wu, states,
    rate, halo, convw, dlog, dbias,
    d_proj_o, d_tail_o, d_edge_o, d_rate_o, d_convw_o, d_decay_o, d_gain_o, s_down_o, s_out_o, g_gu_o,
    d_out, y, inc, later, got1, tot, got2, xpad, dpad, dsend, cols_s, d_pre_o,
    g_down, g_out, relay_d, relay_o, got_d, got_o, last_got, s1, r1, s2, r2, s3, r3, s4, r4
):
    greet(side_peers())
    settle = Settle(lambda i, b: last_got.at[i, b], s4, r4)
    for b in (2, 1, 3):
        for i in range(2):
            settle.send(s_gu.at[i, b], i, b)
    grads = (g_down, g_out)
    spread = Spread(
        lambda i, owner: grads[i].at[owner], lambda i, b: (relay_d, relay_o)[i].at[b],
        lambda i, s, b: (got_d, got_o)[i].at[s, b], s3, r3,
    )
    d_gain_o[...] = head_back(d_mixed, out_w, head_out, proj, gain, qe, step, d_out, d_proj_o, y, inc)

    def make(o, left, right):
        for j in range(0, o.shape[0], 2):
            both = dot(left[...], right[:, j * LANES : (j + 2) * LANES]).astype(BF16)
            o[j], o[j + 1] = both[:, :LANES], both[:, LANES:]

    def level_one():
        make(g_down, middle, cot)
        make(g_out, gated_t, d_mixed)

    def level_two():
        for place in PLACES:
            spread.ready(*place, (0,))

    swaps = states_backward(inc, ga, ta, later, got1, tot, got2, s1, r1, s2, r2, level_one, level_two)
    for place in PLACES:
        spread.ready(*place, (1,))
    rows = d_out.shape[0]
    heads = later.shape[0]
    blocks = rows // BLK
    strength, log_decay, pre = rates(rate, dlog, dbias)
    valid = [valid_column(info, rows, KCONV - 1 - j) for j in range(KCONV)]
    for h in range(heads):
        grad = later[h]
        for c in range(blocks - 1, -1, -1):
            u = h * blocks + c
            dsend[u] = grad
            if c:
                grad = dot3(grad, step[u, :DK, :], "nt") + y[u]
    for c in range(blocks):
        keep, first, last, tri, strict = block_masks(info, c)
        here = pl.ds(c * BLK, BLK)
        for h in range(heads):
            u = h * blocks + c
            cv = conv[here, pl.ds(h * CONVW, CONVW)]
            sg = sigmoid(cv)
            qa, ka, va, rq, rk = vectors(cv)
            rqs = rq * DK**-0.5
            q, k = qa * rqs, ka * rk
            beta = strength[c * BLK : (c + 1) * BLK, h : h + 1]
            g = log_decay[c * BLK : (c + 1) * BLK, h : h + 1]
            carry, to_end = decays(g, first, last, tri)
            dm = dec[u]
            sc = dm * dot(q, k, "nt")
            gm = dm * dot(k, k, "nt") * strict
            state, d_end = states[u], dsend[u]
            do = d_out[here, pl.ds(h * DV, DV)]
            ks = dot(k, state, "nt")
            qs = dot(q, state, "nt")
            fresh = wu[u, :, DK:] - dot(wu[u, :, :DK], state, "nt")
            kd = to_end * k
            d_fresh = dot(sc, do, "tn") + dot(kd, d_end, "nt")
            d_rhs = dot(inv[u], d_fresh, "tn")
            d_low = -dot(d_rhs, fresh, "nt")
            d_sc = dot(do, fresh, "nt")
            d_val = beta * d_rhs
            ebar = d_low * gm
            d_beta = jnp.sum(d_rhs * (va - carry * ks), axis=1, keepdims=True) + jnp.sum(ebar, axis=1, keepdims=True)
            e = d_sc * sc + beta * ebar
            d_scd = d_sc * dm
            d_gm = (beta * d_low) * (dm * strict)
            d_kd = dot(fresh, d_end)
            d_q = dot(d_scd, k) + carry * dot(do, state)
            d_k = (
                dot(d_scd, q, "tn")
                - (beta * carry) * dot(d_rhs, state)
                + to_end * d_kd
                + dot(d_gm, k)
                + dot(d_gm, k, "tn")
            )
            hcol = carry * jnp.sum(do * qs - beta * d_rhs * ks, axis=1, keepdims=True)
            fcol = jnp.sum(kd * d_kd, axis=1, keepdims=True)
            tail = carry[BLK - 1 :, :] * jnp.sum(
                jnp.sum(state * d_end, axis=1, keepdims=True), axis=0, keepdims=True
            )
            lane = iota((BLK, DK), 1)
            d_g = (
                jnp.sum(dot_exact_left(tri, e, "tn") * strict, axis=1, keepdims=True)
                + dot_exact_left(tri, jnp.where(lane == 0, hcol, 0.0), "tn")[:, :1]
                + dot_exact_left(strict, jnp.where(lane == 0, fcol, 0.0))[:, :1]
                + tail
            )
            cols_s[here, h : h + 1] = d_g
            cols_s[here, heads + h : heads + h + 1] = d_beta
            d_qa = rqs * d_q - qa * (rqs * rq * rq * jnp.sum(d_q * qa, axis=1, keepdims=True))
            d_ka = rk * d_k - ka * (rk * rk * rk * jnp.sum(d_k * ka, axis=1, keepdims=True))
            d_act = jnp.concatenate([d_qa, d_ka, d_val], axis=1)
            d_pre_o[here, pl.ds(h * CONVW, CONVW)] = d_act * (sg * (1.0 + cv * (1.0 - sg)))
            spread.relays(c * heads + h)
    d_g, d_beta = cols_s[:, :heads], cols_s[:, heads : 2 * heads]
    d_bias = -d_g * jnp.exp(dlog[...]) * sigmoid(pre)
    d_rate_o[:, :heads] = d_bias
    d_rate_o[:, heads:] = d_beta * strength * (1.0 - strength)
    d_decay_o[:, :heads] = jnp.sum(d_g * log_decay, axis=0, keepdims=True)
    d_decay_o[:, heads:] = jnp.sum(d_bias, axis=0, keepdims=True)
    for h in range(heads):
        src, dst = pl.ds(h * MIXW, CONVW), pl.ds(h * CONVW, CONVW)
        xpad[:PAD, :] = halo[:, dst]
        xpad[PAD:, :] = proj[:, src].astype(BF16).astype(F32)
        dpad[...] = jnp.zeros_like(dpad)
        d_conv = d_pre_o[:, dst]
        for j in range(KCONV):
            lo = PAD - (KCONV - 1) + j
            masked = d_conv * valid[j]
            d_convw_o[j : j + 1, dst] = jnp.sum(masked * xpad[lo : lo + rows, :], axis=0, keepdims=True)
            dpad[lo : lo + rows, :] += convw[j : j + 1, dst].astype(F32) * masked
        d_edge_o[:, dst] = dpad[:PAD, :]
        d_tail_o[:, dst] = dpad[rows - PAD :, :]
        d_proj_o[:, src] = dpad[PAD:, :].astype(BF16)
    for i in range(2):
        g_gu_o[i] = s_gu[i, 0].astype(F32) + settle.others(i)
    for i, o in ((0, s_down_o), (1, s_out_o)):
        for b in FAR:
            o[b] = spread.total(i, b).astype(BF16)
    spread.end()
    settle.end()
    for s in swaps:
        s.wait_send()


def call(kernel, outs, scratch, limit, *args, flops=2_000_000_000, nbytes=16_000_000):
    def spec(a):
        return SMEM if a.dtype == jnp.int32 else VMEM

    return pl.pallas_call(
        kernel,
        out_shape=outs,
        in_specs=[spec(a) for a in args],
        out_specs=[VMEM for _ in outs],
        scratch_shapes=scratch,
        compiler_params=pltpu.CompilerParams(vmem_limit_bytes=limit << 20),
        cost_estimate=pl.CostEstimate(flops=flops, bytes_accessed=nbytes, transcendentals=0),
    )(*args)


def sds(shape, dtype=F32):
    return jax.ShapeDtypeStruct(shape, dtype)
CHIPS = 4
LANES = 128


def cp(src, dst, send, recv, dev):
    return pltpu.make_async_remote_copy(
        src_ref=src, dst_ref=dst, send_sem=send, recv_sem=recv, device_id=dev, device_id_type=pl.DeviceIdType.MESH
    )


def greet(devices):
    barrier = pltpu.get_barrier_semaphore()
    for dev in devices:
        pl.semaphore_signal(barrier, inc=1, device_id=dev, device_id_type=pl.DeviceIdType.MESH)
    pl.semaphore_wait(barrier, len(devices))


def head_place():
    me = lax.axis_index("head")
    chip, core = me // 2, me % 2
    seq = lax.axis_index("seq")

    def dev(step, flip=False):
        c = lax.rem(chip + step, CHIPS)
        return (seq, c * 2 + (1 - core if flip else core))

    return me, chip, core, dev


def head_peers():
    dev = head_place()[3]
    return [dev(0, True)] + [dev(d) for d in range(1, CHIPS)]


def head_rows(o, rows, step, flip=False):
    owner = head_place()[3](step, flip)[1]
    return o.at[pl.ds(pl.multiple_of(owner * rows, rows), rows)]


def gather_start(x, o, ssem, rsem, lsem):
    rows = x.shape[0]
    dev = head_place()[3]
    pltpu.make_async_copy(x, head_rows(o, rows, 0), lsem).start()
    out = [cp(x, head_rows(o, rows, 0), ssem.at[d], rsem.at[d], dev(d)) for d in (2, 1, 3)]
    out.append(cp(x, head_rows(o, rows, 0), ssem.at[0], rsem.at[0], dev(0, True)))
    for s in out:
        s.start()
    return out


def gather_forward(x, o, ssem, rsem):
    rows = x.shape[0]
    dev = head_place()[3]
    out = []
    for d in (1, 3, 2):
        there = head_rows(o, rows, CHIPS - d)
        cp(x, there, ssem.at[d], rsem.at[d], dev(d)).wait_recv()
        fwd = cp(there, there, ssem.at[CHIPS + d], rsem.at[CHIPS + d], dev(0, True))
        fwd.start()
        out.append(fwd)
    return out


def gather_end(x, o, ssem, rsem, lsem, sent):
    rows = x.shape[0]
    dev = head_place()[3]
    pltpu.make_async_copy(x, head_rows(o, rows, 0), lsem).wait()
    cp(x, head_rows(o, rows, 0, True), ssem.at[0], rsem.at[0], dev(0, True)).wait_recv()
    for d in range(1, CHIPS):
        there = head_rows(o, rows, CHIPS - d, True)
        cp(x, there, ssem.at[CHIPS + d], rsem.at[CHIPS + d], dev(0, True)).wait_recv()
    for s in sent:
        s.wait_send()


def gather_over_head(x, o, ssem, rsem, lsem):
    sent = gather_start(x, o, ssem, rsem, lsem)
    sent += gather_forward(x, o, ssem, rsem)
    gather_end(x, o, ssem, rsem, lsem, sent)


def reduce_over_head(x, total, pair, got, mid, ssem, rsem):
    rows = total.shape[0]
    me, chip, core, dev = head_place()
    partner = dev(0, True)

    def at(step, flip=False):
        return x.at[pl.ds(pl.multiple_of(dev(step, flip)[1] * rows, rows), rows)]

    order = (2, 1, 3, 0)
    first = [cp(at(d, True), pair.at[d], ssem.at[d], rsem.at[d], partner) for d in order]
    for s in first:
        s.start()
    second = []
    for s, d in zip(first, order):
        s.wait_recv()
        both = at(d)[...].astype(F32) + pair[d].astype(F32)
        if d:
            mid[d] = both.astype(BF16)
            t = cp(mid.at[d], got.at[d], ssem.at[CHIPS + d], rsem.at[CHIPS + d], dev(d))
            t.start()
            second.append(t)
        else:
            total[...] = both
    for s in (second[1], second[2], second[0]):
        s.wait_recv()
    total[...] = total[...] + ((got[1].astype(F32) + got[3].astype(F32)) + got[2].astype(F32))
    for s in first + second:
        s.wait_send()


def mean_scale(v):
    return lax.rsqrt(jnp.mean(v * v, axis=1, keepdims=True) + 1e-05)


def norm_back(v, gain, d_norm):
    r = mean_scale(v)
    e = d_norm * gain
    d_v = r * e - v * (r * r * r * jnp.mean(e * v, axis=1, keepdims=True))
    return d_v, jnp.sum(d_norm * v * r, axis=0, keepdims=True)


def feed_forward(
    x, tokens, gain, cot, cot_all, gu, down,
    hidden_o, all_o, d_hidden_o, d_gain_o, sums_o, middle_o, feed_o,
    n2, guv, downv, d_middle, d_gu, d_two, block, ta, pa, ga, ma, tb, pb, gb, mb, g, relay, seqs_got,
    ls, sa, ra, sb, rb, s1, r1, l1, s2, r2, l2, s3, r3
):
    load_d = pltpu.make_async_copy(down, downv, ls.at[0])
    load_d.start()
    load_g = pltpu.make_async_copy(gu, guv, ls.at[1])
    load_g.start()
    greet(head_peers() + side_peers())
    one = pair_sends(x, pa, sa, ra, FAR)
    two = chip_sends(x, one, ta, pa, ga, ma, sa, ra, FAR)
    load_d.wait()
    d_middle[...] = dot(downv[...], cot_all[...], "nt")
    hidden = tokens[...].astype(F32) + chip_sum(two, ta, ga)
    hidden_o[...] = hidden
    block[...] = (hidden * mean_scale(hidden) * gain[...]).astype(BF16)
    ahead = gather_start(block, n2, s1, r1, l1)
    load_g.wait()
    ahead += gather_forward(block, n2, s1, r1)
    gather_end(block, n2, s1, r1, l1, ahead)
    hid = downv.shape[0]
    low = hid // 32 * 16
    for lo, hi in ((0, low), (low, hid)):
        gate = dot(guv[lo:hi, :], n2[...], "nt")
        up = dot(guv[hid + lo : hid + hi, :], n2[...], "nt")
        s = sigmoid(gate)
        silu = gate * s
        dm = d_middle[lo:hi, :]
        middle_o[lo:hi, :] = (silu * up).astype(BF16)
        d_gu[lo:hi, :] = (dm * up * (s * (1.0 + gate * (1.0 - s)))).astype(BF16)
        d_gu[hid + lo : hid + hi, :] = (dm * silu).astype(BF16)
    for j in range(0, D, 512):
        d_two[:, j : j + 512] = dot(d_gu[...], guv[:, j : j + 512], "tn").astype(BF16)
    one_b = pair_sends(d_two, pb, sb, rb, FAR)
    spread = Spread(
        lambda i, owner: g.at[owner, i], lambda i, b: relay.at[i, b], lambda i, s, b: seqs_got.at[i, s, b], s3, r3
    )
    dev = seq_place()[3]

    def make(place):
        owner = dev(*place)[0]
        cols = n2[:, pl.ds(pl.multiple_of(owner * LANES, LANES), LANES)]
        out = dot(d_gu[...], cols).astype(BF16)
        g[owner, 0] = out[:hid]
        g[owner, 1] = out[hid:]
        spread.ready(*place)

    for place in PLACES[:3]:
        make(place)
    two_b = chip_sends(d_two, one_b, tb, pb, gb, mb, sb, rb, FAR)
    for place in PLACES[3:]:
        make(place)
    d_norm, d_gain = norm_back(hidden_o[...], gain[...], chip_sum(two_b, tb, gb))
    d_hidden = cot[...].astype(F32) + d_norm
    d_hidden_o[...] = d_hidden
    d_gain_o[...] = d_gain
    block[...] = d_hidden.astype(BF16)
    ahead = gather_start(block, all_o, s2, r2, l2)
    spread.relays()
    for j in range(0, D, 512):
        feed_o[:, j : j + 512] = dot(middle_o[...], downv[:, j : j + 512], "tn").astype(BF16)
    ahead += gather_forward(block, all_o, s2, r2)
    for b in FAR:
        for i in range(2):
            sums_o[i, b] = spread.total(i, b).astype(BF16)
    gather_end(block, all_o, s2, r2, l2, ahead)
    spread.end()
    for sent in (one, two, one_b, two_b):
        for s in sent.values():
            s.wait_send()


def reach(kernel, outs, scratch, cid, limit, *args, anywhere=(), scalars=(), nbytes=12_000_000):
    return pl.pallas_call(
        kernel,
        out_shape=outs,
        in_specs=[
            pl.BlockSpec(memory_space=pl.ANY) if i in anywhere else SMEM if i in scalars else VMEM for i in range(len(args))
        ],
        out_specs=[VMEM for _ in outs],
        scratch_shapes=scratch,
        compiler_params=pltpu.CompilerParams(
            collective_id=cid, has_side_effects=True, vmem_limit_bytes=limit << 20
        ),
        cost_estimate=pl.CostEstimate(flops=0, bytes_accessed=nbytes, transcendentals=0),
    )(*args)


def sems(n):
    return pltpu.SemaphoreType.DMA((n,))


def reduce_scratch(rows, cols):
    return [pltpu.VMEM((CHIPS, rows, cols), BF16) for _ in range(3)] + [sems(2 * CHIPS), sems(2 * CHIPS)]


def gather_scratch():
    return [sems(2 * CHIPS), sems(2 * CHIPS), pltpu.SemaphoreType.DMA]


SIDE = 4


def seq_place():
    me = lax.axis_index("seq")
    z, y = me // SIDE, me % SIDE
    head = lax.axis_index("head")

    def dev(dz, dy):
        return (lax.rem(z + dz, SIDE) * SIDE + lax.rem(y + dy, SIDE), head)

    return me, z, y, dev


def side_peers():
    dev = seq_place()[3]
    return [dev(0, d) for d in range(1, SIDE)] + [dev(d, 0) for d in range(1, SIDE)]


FAR = (2, 1, 3, 0)
FIRST, OTHER = (2, 1), (3, 0)
PLACES = (
    (2, 2), (2, 1), (1, 2), (2, 3), (3, 2), (2, 0), (0, 2), (1, 3), (3, 1), (1, 0), (0, 1), (3, 3), (1, 1), (0, 3), (3, 0),
    (0, 0),
)


class Spread:
    def __init__(self, piece, relay, got, ssem, rsem):
        self.piece, self.relay, self.got, self.ssem, self.rsem = piece, relay, got, ssem, rsem
        self.dev = seq_place()[3]
        self.sent = []

    def way(self, i, a, b):
        return self.dev(b, a) if i == 0 else self.dev(a, b)

    def copy(self, i, a, b, owner):
        k = (i * SIDE + a) * SIDE + b
        if a == 2:
            dst, step = self.relay(i, b), 1 if b in FIRST else 3
        else:
            dst, step = self.got(i, 0 if a == 1 else 1, b), a
        return cp(self.piece(i, owner), dst, self.ssem.at[k], self.rsem.at[k], self.way(i, step, 0))

    def send(self, i, a, b, owner):
        s = self.copy(i, a, b, owner)
        s.start()
        self.sent.append(s)

    def late(self, a, b):
        return a == 1 and b in FIRST or a == 3 and b in OTHER

    def ready(self, dz, dy, halves_=(0, 1)):
        owner = self.dev(dz, dy)[0]
        for i in halves_:
            a, b = (dy, dz) if i == 0 else (dz, dy)
            if a and not self.late(a, b):
                self.send(i, a, b, owner)

    def relays(self, part=None):
        for n, b in enumerate(FAR):
            if part is not None and n != part:
                continue
            for i in range(2):
                a = 1 if b in FIRST else 3
                owner = self.way(i, a, b)[0]
                self.copy(i, 2, b, owner).wait_recv()
                both = self.piece(i, owner)[...].astype(F32) + self.relay(i, b)[...].astype(F32)
                self.relay(i, b)[...] = both.astype(BF16)
                k = (i * SIDE + a) * SIDE + b
                s = cp(
                    self.relay(i, b), self.got(i, 0 if a == 1 else 1, b), self.ssem.at[k], self.rsem.at[k],
                    self.way(i, a, 0),
                )
                s.start()
                self.sent.append(s)

    def total(self, i, b):
        owner = self.way(i, 0, b)[0]
        for a in (1, 3):
            self.copy(i, a, b, owner).wait_recv()
        return self.piece(i, owner)[...].astype(F32) + (
            self.got(i, 0, b)[...].astype(F32) + self.got(i, 1, b)[...].astype(F32)
        )

    def end(self):
        for s in self.sent:
            s.wait_send()


class Settle:
    def __init__(self, got, ssem, rsem):
        self.got, self.ssem, self.rsem = got, ssem, rsem
        self.dev = seq_place()[3]
        self.sent = {}

    def send(self, src, i, b):
        k = i * SIDE + b
        dev = self.dev(b, 0) if i == 0 else self.dev(0, b)
        self.sent[i, b] = cp(src, self.got(i, b), self.ssem.at[k], self.rsem.at[k], dev)
        self.sent[i, b].start()

    def others(self, i):
        for b in (1, 3, 2):
            self.sent[i, b].wait_recv()
        return (self.got(i, 1)[...].astype(F32) + self.got(i, 3)[...].astype(F32)) + self.got(i, 2)[...].astype(F32)

    def end(self):
        for s in self.sent.values():
            s.wait_send()


def share_start(src, got, place, to, ssem, rsem, size=SIDE, own=None):
    part = (lambda d: src) if own is None else (lambda d: src.at[lax.rem(place + d, size)])
    got[place] = src[...] if own is None else src[place]
    steps = (2, 1, 3) if size == SIDE else range(1, size)
    out = [cp(part(d), got.at[place], ssem.at[d], rsem.at[d], to(d)) for d in steps]
    for s in out:
        s.start()

    def wait():
        for d in steps:
            back = lax.rem(place + size - d, size)
            cp(part(d), got.at[back], ssem.at[d], rsem.at[d], to(d)).wait_recv()

    return out, wait


def in_order(got):
    total = got[0]
    for i in range(1, got.shape[0]):
        total = total + got[i]
    return total


def share(src, got, place, to, ssem, rsem):
    out, wait = share_start(src, got, place, to, ssem, rsem)
    wait()
    return out


def unit_top():
    return jnp.where(iota((DK + DV, DK), 0) == iota((DK + DV, DK), 1), 1.0, 0.0)


def add_low(pair, low):
    return jnp.concatenate([pair[:DK], pair[DK:] + low], axis=0)


def states_forward(ab, start_o, ga_o, ta_o, got1, tot, got2, s1, r1, s2, r2):
    me, z, y, dev = seq_place()
    heads = ab.shape[0]
    greet(side_peers())
    out = share(ab, got1, y, lambda d: dev(0, d), s1, r1)
    before = []
    for h in range(heads):
        whole = got1[0, h].astype(F32)
        prefix = jnp.where(y > 0, whole, unit_top())
        for j in range(1, SIDE):
            a, b = got1[j, h, :DK, :], got1[j, h, DK:, :].astype(F32)
            whole = add_low(dot_left2(whole, a), b)
            if j < SIDE - 1:
                prefix = jnp.where(y > j, whole, prefix)
        tot[h] = whole.astype(BF16)
        before.append(prefix)
        for j in range(SIDE):
            ga_o[j, h] = got1[j, h, :DK, :]
    out += share(tot, got2, z, lambda d: dev(d, 0), s2, r2)
    for h in range(heads):
        held = jnp.zeros((DV, DK), F32)
        for j in range(SIDE - 1):
            held = jnp.where(
                z > j, dot_left2(held, got2[j, h, :DK, :]) + got2[j, h, DK:, :].astype(F32), held
            )
        start_o[h] = dot3(held, before[h][:DK]) + before[h][DK:]
        for j in range(SIDE):
            ta_o[j, h] = got2[j, h, :DK, :]
    for s in out:
        s.wait_send()


def states_backward(inc, ga, ta, later_o, got1, tot, got2, s1, r1, s2, r2, level_one, level_two):
    me, z, y, dev = seq_place()
    heads = inc.shape[0]
    out, wait = share_start(inc, got1, y, lambda d: dev(0, d), s1, r1)
    level_one()
    wait()
    after = []
    for h in range(heads):
        whole = add_low(dot(unit_top(), ga[SIDE - 1, h], "nt"), got1[SIDE - 1, h].astype(F32))
        suffix = jnp.where(y < SIDE - 1, whole, unit_top())
        for j in range(SIDE - 2, -1, -1):
            whole = add_low(dot_left2(whole, ga[j, h], "nt"), got1[j, h].astype(F32))
            if j:
                suffix = jnp.where(y < j, whole, suffix)
        tot[h] = whole[DK:].astype(BF16)
        after.append(suffix)
    more, wait = share_start(tot, got2, z, lambda d: dev(d, 0), s2, r2)
    level_two()
    wait()
    for h in range(heads):
        held = jnp.zeros((DV, DK), F32)
        for j in range(SIDE - 1, 0, -1):
            held = jnp.where(z < j, dot_left2(held, ta[j, h], "nt") + got2[j, h].astype(F32), held)
        later_o[h] = dot3(held, after[h][:DK]) + after[h][DK:]
    return out + more


def pair_sends(x, pair, ssem, rsem, steps):
    rows = pair.shape[1]
    dev = head_place()[3]
    out = {}
    for d in steps:
        owner = dev(d, True)[1]
        src = x.at[pl.ds(pl.multiple_of(owner * rows, rows), rows)]
        out[d] = cp(src, pair.at[d], ssem.at[d], rsem.at[d], dev(0, True))
        out[d].start()
    return out


def chip_sends(x, first, total, pair, got, mid, ssem, rsem, steps):
    rows = pair.shape[1]
    dev = head_place()[3]
    out = {}
    for d in steps:
        first[d].wait_recv()
        owner = dev(d)[1]
        both = x[pl.ds(pl.multiple_of(owner * rows, rows), rows), :].astype(F32) + pair[d].astype(F32)
        if d:
            mid[d] = both.astype(BF16)
            out[d] = cp(mid.at[d], got.at[d], ssem.at[CHIPS + d], rsem.at[CHIPS + d], dev(d))
            out[d].start()
        else:
            total[...] = both
    return out


def chip_sum(second, total, got):
    for d in (1, 3, 2):
        second[d].wait_recv()
    return total[...] + ((got[1].astype(F32) + got[3].astype(F32)) + got[2].astype(F32))


def finish(
    dproj, normed, w, d_rate, rate_w, d_tail, d_edge, feed, hidden, tokens, d_hidden, gain, convs, decay, g_feed, g_head,
    s_down, s_out,
    layer_o, d_tokens_o, g_mixer_o, g_gain_o, g_feed_o, g_head_o, conv_o, dlog_o, dbias_o, rate_o, g_down_o, g_out_o,
    dp, wv, edge, g, relay, got1, mid, got2, dn, ta, pa, ga, ma, tb, pb, gb, mb, got_d, got_o,
    e0, eh, e1, ey, e2, ez, m0, mh, m1, my, m2, mz,
    es, er, ls, s1, r1, s2, r2, sa, ra, sb, rb, s5, r5, se, re, sm, rm
):
    me, z, y, dev = seq_place()
    head = lax.axis_index("head")
    heads, seqs = eh.shape[0], g.shape[1]
    rows = dp.shape[0]
    part, half = g_mixer_o.shape[1], g_mixer_o.shape[2]
    load_p = pltpu.make_async_copy(dproj, dp, ls.at[0])
    load_p.start()
    load_w = pltpu.make_async_copy(w, wv, ls.at[1])
    load_w.start()

    def across(d):
        return (me, lax.rem(head + d, heads))

    before, behind = (lax.rem(me + seqs - 1, seqs), head), (lax.rem(me + 1, seqs), head)
    greet([across(d) for d in range(1, heads)] + side_peers() + [before, behind])
    back = cp(d_edge, edge, es, er, before)
    back.start()
    feed_one = pair_sends(feed, pa, sa, ra, FAR)

    n_row, h_row = D // LANES, DV // LANES
    taps, wide_c = convs.shape
    c_row = wide_c // LANES
    ng, nc = e0.shape[0], taps * c_row + PAD
    for r in range(n_row):
        e0[r : r + 1, :] = g_feed[:, r * LANES : (r + 1) * LANES]
    e0[n_row:, :] = jnp.zeros((ng - n_row, LANES), F32)
    for r in range(h_row):
        e0[n_row + r : n_row + r + 1, :] = g_head[:, r * LANES : (r + 1) * LANES]
    small, wait_head = share_start(e0, eh, head, across, se.at[0], re.at[0], heads)
    for t in range(taps):
        for r in range(c_row):
            lo = ng + t * c_row + r
            e1[0, lo : lo + 1, :] = convs[t : t + 1, r * LANES : (r + 1) * LANES]
    e1[0, ng + nc - PAD : ng + nc, :] = jnp.zeros((PAD, LANES), F32)
    e1[0, ng + nc - PAD : ng + nc - PAD + 1, :] = decay[...]
    rates_t = dot(d_rate[:, :PAD], normed[...], "tn")
    for i in range(SIDE):
        if i:
            e1[i, ng : ng + nc, :] = e1[0, ng : ng + nc, :]
        for j in range(SIDE):
            at = (j * SIDE + i) * LANES
            e1[i, ng + nc + j * PAD : ng + nc + (j + 1) * PAD, :] = rates_t[:, at : at + LANES]

    sums = (s_down, s_out)
    settle = Settle(lambda i, b: (got_d, got_o)[i].at[b], s5, r5)
    for b in (2, 1, 3):
        for i in range(2):
            settle.send(sums[i].at[b], i, b)
    load_p.wait()
    back.wait_recv()
    there = jnp.where(me < seqs - 1, edge[...], 0.0)
    tail = jnp.concatenate([d_tail[:PAD, :], d_tail[PAD:, :] + there], axis=0).astype(BF16)
    wide = half - DV
    for i in range(2):
        dp[rows - 2 * PAD :, pl.ds(i * half, wide)] = tail[:, i * wide : (i + 1) * wide]

    spread = Spread(
        lambda i, owner: g.at[i, owner], lambda i, b: relay.at[i, b], lambda i, s, b: got1.at[i, s, b], s1, r1
    )
    settle_two = Settle(lambda i, b: got2.at[i, b], s2, r2)
    for n, place in enumerate(PLACES):
        owner = dev(*place)[0]
        left = normed[:, pl.ds(pl.multiple_of(owner * part, part), part)]
        both = dot(left, dp[...], "tn").astype(BF16)
        for i in range(2):
            g[i, owner] = both[:, i * half : (i + 1) * half]
        spread.ready(*place)
        if n == 2:
            wait_head()
            gains = in_order(eh)
            for i in range(SIDE):
                e1[i, :ng, :] = gains
            more, wait_y = share_start(e1, ey, y, lambda d: dev(0, d), se.at[1], re.at[1], SIDE, True)
            small += more
        if n == 9:
            wait_y()
            total = in_order(ey)
            for j in range(SIDE):
                e2[j, : ng + nc, :] = total[: ng + nc]
                e2[j, ng + nc :, :] = total[ng + nc + j * PAD : ng + nc + (j + 1) * PAD]
            more, wait_z = share_start(e2, ez, z, lambda d: dev(d, 0), se.at[2], re.at[2], SIDE, True)
            small += more
    feed_two = chip_sends(feed, feed_one, ta, pa, ga, ma, sa, ra, FAR)

    load_w.wait()
    low = rows // CHIPS
    hp = head_place()[3]
    dn_one = {}
    for d in FAR:
        chip = hp(d)[1] // 2
        here = pl.ds(pl.multiple_of(chip * low, low), low)
        dn[here, :] = (dot(dp[here, :], wv[...], "nt") + dot(d_rate[here, :], rate_w[...], "nt")).astype(BF16)
        dn_one.update(pair_sends(dn, pb, sb, rb, (d,)))
        spread.relays(FAR.index(d))
    dn_two = chip_sends(dn, dn_one, tb, pb, gb, mb, sb, rb, FAR)
    wait_z()
    total = in_order(ez)
    for r in range(n_row):
        g_feed_o[:, r * LANES : (r + 1) * LANES] = total[r : r + 1]
    for r in range(h_row):
        g_head_o[:, r * LANES : (r + 1) * LANES] = total[n_row + r : n_row + r + 1]
    own = conv_o.shape[1]
    for t in range(taps):
        for h in range(own):
            for r in range(c_row // own):
                lo = ng + t * c_row + h * (c_row // own) + r
                conv_o[t, h : h + 1, r * LANES : (r + 1) * LANES] = total[lo : lo + 1]
    dlog_o[...] = total[ng + nc - PAD : ng + nc - PAD + 1, :own]
    dbias_o[...] = total[ng + nc - PAD : ng + nc - PAD + 1, own : 2 * own]
    for i in range(2):
        rate_o[i] = total[ng + nc + i * own : ng + nc + (i + 1) * own]
    layer_o[...] = (hidden[...] + chip_sum(feed_two, ta, ga)).astype(BF16)
    d_norm, d_gain = norm_back(tokens[...].astype(F32), gain[...], chip_sum(dn_two, tb, gb))
    d_tokens_o[...] = d_hidden[...] + d_norm

    for r in range(n_row):
        m0[r : r + 1, :] = d_gain[:, r * LANES : (r + 1) * LANES]
    more, wait_head = share_start(m0, mh, head, across, sm.at[0], rm.at[0], heads)
    small += more

    def settle_mixer(b):
        for i in range(2):
            both = spread.total(i, b)
            if b:
                mid[i, b] = both.astype(BF16)
                settle_two.send(mid.at[i, b], i, b)
            else:
                g_mixer_o[i] = both

    settle_mixer(2)
    wait_head()
    m1[...] = in_order(mh)
    more, wait_y = share_start(m1, my, y, lambda d: dev(0, d), sm.at[1], rm.at[1])
    small += more
    settle_mixer(1)
    settle_mixer(3)
    wait_y()
    m2[...] = in_order(my)
    more, wait_z = share_start(m2, mz, z, lambda d: dev(d, 0), sm.at[2], rm.at[2])
    small += more
    settle_mixer(0)
    for i, o in ((0, g_down_o), (1, g_out_o)):
        o[...] = sums[i][0].astype(F32) + settle.others(i)
    wait_z()
    total = in_order(mz)
    for r in range(n_row):
        g_gain_o[:, r * LANES : (r + 1) * LANES] = total[r : r + 1]
    for i in range(2):
        g_mixer_o[i] = g_mixer_o[i] + settle_two.others(i)
    spread.end()
    settle.end()
    settle_two.end()
    done = small + [back]
    done += list(feed_one.values()) + list(feed_two.values()) + list(dn_one.values()) + list(dn_two.values())
    for s in done:
        s.wait_send()


def passed_along(shard, axis, by):
    length = lax.axis_size(axis)
    pairs = [(i, i + by) for i in range(length) if 0 <= i + by < length]
    return lax.ppermute(shard, axis, pairs)


def rms_scale(values, gain):
    return values * lax.rsqrt(jnp.mean(values * values, axis=-1, keepdims=True) + 1e-05) * gain


def local(
    tokens, mixer_gain, mixer_weight, rate_weight, conv_weight, decay_log, decay_bias, head_gain,
    output_weight, feed_gain, gate_up_weight, down_weight, doc_starts, cotangent,
):
    resid = tokens.astype(F32)
    normed = rms_scale(resid, mixer_gain).astype(BF16)
    gathered = lax.all_gather(normed, "head", axis=0, tiled=True)
    heads = mixer_weight.shape[1]
    gathered, cot_own, mixer_flat = lax.optimization_barrier(
        (gathered, cotangent, mixer_weight.reshape(D, heads * MIXW))
    )
    cot_rows = lax.all_gather(cot_own, "head", axis=0, tiled=True)
    rows = gathered.shape[0]
    blocks = rows // BLK
    units = heads * blocks
    seq = lax.axis_size("seq")
    projected = jnp.dot(gathered, mixer_flat, preferred_element_type=F32)
    rate_proj = jnp.einsum("td,dgh->tgh", gathered, rate_weight, preferred_element_type=F32).reshape(rows, 2 * heads)
    rim = projected[rows - PAD :].reshape(PAD, heads, MIXW)[:, :, :CONVW].reshape(PAD, heads * CONVW).astype(BF16)
    halo = passed_along(rim, "seq", 1).astype(F32)
    convw = conv_weight.reshape(KCONV, heads * CONVW)
    info = jnp.concatenate(
        [doc_starts, jnp.stack([lax.axis_index("seq") * rows, lax.axis_index("seq")]).astype(jnp.int32)]
    )
    dlog, dbias = decay_log.reshape(1, heads), decay_bias.reshape(1, heads)
    gain = head_gain.reshape(1, DV)

    conv, dec, inv, wu, qe, ol, step, ab = call(
        fwd_prep,
        [
            sds((rows, heads * CONVW)), sds((units, BLK, BLK)), sds((units, BLK, BLK), BF16),
            sds((units, BLK, DK + DV)), sds((rows, heads * DK)), sds((rows, heads * DV)),
            sds((units, DK + DV, DK)), sds((heads, DK + DV, DK), BF16),
        ],
        [pltpu.VMEM((PAD + rows, CONVW), F32)],
        56, info, projected, halo, rate_proj, convw, dlog, dbias,
    )
    start, ga, ta = reach(
        states_forward,
        [sds((heads, DV, DK)), sds((SIDE, heads, DK, DK), BF16), sds((SIDE, heads, DK, DK), BF16)],
        [
            pltpu.VMEM((SIDE, heads, DK + DV, DK), BF16), pltpu.VMEM((heads, DK + DV, DK), BF16),
            pltpu.VMEM((SIDE, heads, DK + DV, DK), BF16), sems(SIDE), sems(SIDE), sems(SIDE), sems(SIDE),
        ],
        1, 40, ab,
    )
    states, head_out, gated = call(
        fwd_out,
        [sds((units, DV, DK)), sds((rows, heads * DV)), sds((rows, heads * DV), BF16)],
        [], 48, start, step, qe, ol, projected, gain,
    )
    out_flat = output_weight.reshape(heads * DV, D)
    own = tokens.shape[0]
    mixed = jnp.dot(gated, out_flat, preferred_element_type=F32).astype(BF16)
    hid = down_weight.shape[0]
    part, half, n_head = D // seq, MIXW, lax.axis_size("head")
    gu_t = gate_up_weight.transpose(1, 2, 0).reshape(2 * hid, D)

    def sums_of_head():
        return [pltpu.VMEM((own, D), F32)] + [pltpu.VMEM((CHIPS, own, D), BF16) for _ in range(3)]

    hidden, d_mixed, d_hidden, g_feed_gain, grads, middle, feed = reach(
        feed_forward,
        [
            sds((own, D)), sds((rows, D), BF16), sds((own, D)), sds((1, D)), sds((2, SIDE, hid, LANES), BF16),
            sds((hid, rows), BF16), sds((rows, D), BF16),
        ],
        [
            pltpu.VMEM((rows, D), BF16), pltpu.VMEM((2 * hid, D), BF16), pltpu.VMEM((hid, D), BF16),
            pltpu.VMEM((hid, rows), F32), pltpu.VMEM((2 * hid, rows), BF16), pltpu.VMEM((rows, D), BF16),
            pltpu.VMEM((own, D), BF16),
        ]
        + sums_of_head()
        + sums_of_head()
        + [
            pltpu.VMEM((seq, 2, hid, LANES), BF16), pltpu.VMEM((2, SIDE, hid, LANES), BF16),
            pltpu.VMEM((2, 2, SIDE, hid, LANES), BF16), sems(2), sems(2 * CHIPS), sems(2 * CHIPS), sems(2 * CHIPS),
            sems(2 * CHIPS),
        ]
        + gather_scratch()
        + gather_scratch()
        + [sems(2 * SIDE * SIDE), sems(2 * SIDE * SIDE)],
        2, 63, mixed, tokens, feed_gain.reshape(1, D), cotangent, cot_rows, gu_t, down_weight,
        anywhere=(5, 6), nbytes=40_000_000,
    )
    gated_t = gated.T
    d_projected, d_tail, d_edge, d_rate, d_convw, d_decay, g_head_gain, s_down, s_out, grad_gate_up = reach(
        mixer_back,
        [
            sds((rows, heads * MIXW), BF16), sds((2 * PAD, heads * CONVW)), sds((PAD, heads * CONVW)),
            sds((rows, 2 * heads)), sds((KCONV, heads * CONVW)), sds((1, 2 * heads)), sds((1, DV)),
            sds((SIDE, hid, LANES), BF16), sds((SIDE, heads * DV, LANES), BF16), sds((2, hid, LANES)),
        ],
        [
            pltpu.VMEM((rows, heads * DV), F32), pltpu.VMEM((units, DV, DK), F32),
            pltpu.VMEM((heads, DV, DK), BF16), pltpu.VMEM((heads, DV, DK), F32),
            pltpu.VMEM((SIDE, heads, DV, DK), BF16), pltpu.VMEM((heads, DV, DK), BF16),
            pltpu.VMEM((SIDE, heads, DV, DK), BF16),
            pltpu.VMEM((PAD + rows, CONVW), F32), pltpu.VMEM((PAD + rows, CONVW), F32),
            pltpu.VMEM((units, DV, DK), F32), pltpu.VMEM((rows, DK), F32), pltpu.VMEM((rows, heads * CONVW), F32),
            pltpu.VMEM((seq, hid, LANES), BF16), pltpu.VMEM((seq, heads * DV, LANES), BF16),
            pltpu.VMEM((SIDE, hid, LANES), BF16), pltpu.VMEM((SIDE, heads * DV, LANES), BF16),
            pltpu.VMEM((2, SIDE, hid, LANES), BF16), pltpu.VMEM((2, SIDE, heads * DV, LANES), BF16),
            pltpu.VMEM((2, SIDE, hid, LANES), BF16),
            sems(SIDE), sems(SIDE), sems(SIDE), sems(SIDE), sems(2 * SIDE * SIDE), sems(2 * SIDE * SIDE),
            sems(2 * SIDE), sems(2 * SIDE),
        ],
        4, 63, info, d_mixed, out_flat, head_out, projected, gain, qe, step, ga, ta, middle, cot_rows, gated_t, grads,
        conv, dec, inv, wu, states, rate_proj, halo, convw, dlog, dbias, scalars=(0,), nbytes=40_000_000,
    )
    grad_gate_up = grad_gate_up.transpose(2, 0, 1)
    d_rate_low = jnp.pad(d_rate.astype(BF16), ((0, 0), (0, LANES - 2 * heads)))
    rate_pad = jnp.pad(rate_weight.reshape(D, 2 * heads), ((0, 0), (0, LANES - 2 * heads)))
    d_decay = jnp.pad(d_decay, ((0, 0), (0, LANES - 2 * heads)))
    n_gain, n_conv, n_last = D // LANES + PAD, KCONV * heads * CONVW // LANES + PAD, D // LANES
    n_y, n_z = n_gain + n_conv + SIDE * PAD, n_gain + n_conv + PAD

    def rows_of(*shape):
        return pltpu.VMEM(shape + (LANES,), F32)

    (
        layer_out, grad_tokens, grad_mixer, grad_mixer_gain, grad_feed_gain, grad_head_gain, grad_conv, grad_decay_log,
        grad_decay_bias, grad_rate, grad_down, grad_output,
    ) = reach(
        finish,
        [
            sds((own, D), BF16), sds((own, D)), sds((2, part, half)), sds((1, D)), sds((1, D)), sds((1, DV)),
            sds((KCONV, heads, CONVW)), sds((1, heads)), sds((1, heads)), sds((2, heads, LANES)), sds((hid, LANES)),
            sds((heads * DV, LANES)),
        ],
        [
            pltpu.VMEM((rows, heads * MIXW), BF16), pltpu.VMEM((D, heads * MIXW), BF16),
            pltpu.VMEM((PAD, heads * CONVW), F32), pltpu.VMEM((2, seq, part, half), BF16),
            pltpu.VMEM((2, SIDE, part, half), BF16), pltpu.VMEM((2, 2, SIDE, part, half), BF16),
            pltpu.VMEM((2, SIDE, part, half), BF16), pltpu.VMEM((2, SIDE, part, half), BF16), pltpu.VMEM((rows, D), BF16),
        ]
        + sums_of_head()
        + sums_of_head()
        + [
            pltpu.VMEM((SIDE, hid, LANES), BF16), pltpu.VMEM((SIDE, heads * DV, LANES), BF16),
            rows_of(n_gain), rows_of(n_head, n_gain), rows_of(SIDE, n_y), rows_of(SIDE, n_y), rows_of(SIDE, n_z),
            rows_of(SIDE, n_z), rows_of(n_last), rows_of(n_head, n_last), rows_of(n_last), rows_of(SIDE, n_last),
            rows_of(n_last), rows_of(SIDE, n_last),
            pltpu.SemaphoreType.DMA, pltpu.SemaphoreType.DMA, sems(2),
            sems(2 * SIDE * SIDE), sems(2 * SIDE * SIDE), sems(2 * SIDE), sems(2 * SIDE),
            sems(2 * CHIPS), sems(2 * CHIPS), sems(2 * CHIPS), sems(2 * CHIPS), sems(2 * SIDE), sems(2 * SIDE),
            pltpu.SemaphoreType.DMA((3, n_head)), pltpu.SemaphoreType.DMA((3, n_head)),
            pltpu.SemaphoreType.DMA((3, n_head)), pltpu.SemaphoreType.DMA((3, n_head)),
        ],
        5, 62, d_projected, gathered, mixer_flat, d_rate_low, rate_pad, d_tail, d_edge, feed, hidden, tokens,
        d_hidden, mixer_gain.reshape(1, D), d_convw, d_decay, g_feed_gain, g_head_gain, s_down, s_out,
        anywhere=(0, 2), nbytes=40_000_000,
    )
    grad_mixer = grad_mixer.transpose(1, 0, 2)
    grad_output = grad_output.reshape(heads, DV, LANES)
    grad_rate = grad_rate.transpose(2, 0, 1)
    grad_mixer_gain, grad_feed_gain, grad_head_gain = (
        v.reshape(-1) for v in (grad_mixer_gain, grad_feed_gain, grad_head_gain)
    )
    grad_decay_log, grad_decay_bias = grad_decay_log.reshape(-1), grad_decay_bias.reshape(-1)
    return (
        layer_out, grad_tokens, grad_mixer_gain, grad_mixer, grad_rate, grad_conv, grad_decay_log, grad_decay_bias,
        grad_head_gain, grad_output, grad_feed_gain, grad_gate_up, grad_down,
    )


def solution(mesh):
    rows = P(("seq", "head"), None)
    return jax.shard_map(
        local,
        mesh=mesh,
        in_specs=(
            rows, P(), P(None, "head", None), P(None, None, "head"), P(None, "head", None), P("head"), P("head"),
            P(), P("head", None, None), P(), P(None, None, "head"), P("head", None), P(), rows,
        ),
        out_specs=(
            rows, rows, P(), P("seq", "head", None), P("seq", None, "head"), P(None, "head", None), P("head"),
            P("head"), P(), P("head", None, "seq"), P(), P("seq", None, "head"), P("head", "seq"),
        ),
        check_vma=False,
    )
```

```python
import functools

import jax
import jax.numpy as jnp
from jax import lax
from jax.experimental import pallas as pl
from jax.experimental.pallas import tpu as pltpu
from jax.sharding import PartitionSpec as P

D = 2048
DK = 128
DV = 256
KCONV = 4
MIXW = 768
CONVW = 512
NB = 4
BLK = 256
PAD = 8
F32 = jnp.float32
BF16 = jnp.bfloat16

VMEM = pl.BlockSpec(memory_space=pltpu.VMEM)
SMEM = pl.BlockSpec(memory_space=pltpu.SMEM)


def dot(a, b, form="nn"):
    dims = {"nn": ((1,), (0,)), "nt": ((1,), (1,)), "tn": ((0,), (0,))}[form]
    return lax.dot_general(a.astype(BF16), b.astype(BF16), (dims, ((), ())), preferred_element_type=F32)


def halves(a):
    hi = a.astype(BF16)
    return hi, (a - hi.astype(F32)).astype(BF16)


def dot3(a, b, form="nn"):
    ah, al = halves(a)
    bh, bl = halves(b)
    return dot(ah, bh, form) + (dot(ah, bl, form) + dot(al, bh, form))


def dot_exact_left(a, b, form="nn"):
    b1, rest = halves(b)
    rest = b - b1.astype(F32)
    b2 = rest.astype(BF16)
    b3 = (rest - b2.astype(F32)).astype(BF16)
    return dot(a, b1, form) + (dot(a, b2, form) + dot(a, b3, form))


def iota(shape, axis):
    return lax.broadcasted_iota(jnp.int32, shape, axis)


def doc_of(info, pos):
    count = jnp.zeros(pos.shape, jnp.int32)
    for i in range(NB):
        count = count + jnp.where(pos >= info[i], 1, 0)
    return jnp.where(pos < 0, -1, count)


def sigmoid(v):
    return 1.0 / (1.0 + jnp.exp(-v))


def softplus(v):
    return jnp.maximum(v, 0.0) + jnp.log1p(jnp.exp(-jnp.abs(v)))


def unit_lower_inverse(low):
    n = low.shape[0]
    row, col = iota((n, n), 0), iota((n, n), 1)
    eye = jnp.where(row == col, 1.0, 0.0)

    def same(b):
        return row // b == col // b

    x = jnp.where(same(8), -low, 0.0)
    inv = eye + x
    x = dot(x, x)
    inv = inv + dot(inv, x)
    x = dot(x, x)
    inv = inv + dot(inv, x)
    b = 8
    while b < n:
        off = jnp.where(same(2 * b) & jnp.logical_not(same(b)), low, 0.0)
        inv = inv - dot(inv, dot(off, inv))
        b *= 2
    return inv + dot(inv, eye - inv - dot3(low, inv))


def valid_column(info, rows, back):
    pos = info[NB] + iota((rows, 1), 0)
    return jnp.where(doc_of(info, pos) == doc_of(info, pos - back), 1.0, 0.0)


def vectors(conv):
    act = conv * sigmoid(conv)
    qa, ka, va = act[:, :DK], act[:, DK : 2 * DK], act[:, 2 * DK :]
    rq = lax.rsqrt(jnp.sum(qa * qa, axis=1, keepdims=True) + 1e-06)
    rk = lax.rsqrt(jnp.sum(ka * ka, axis=1, keepdims=True) + 1e-06)
    return qa, ka, va, rq, rk


def rates(rate_ref, dlog_ref, dbias_ref):
    heads = dlog_ref.shape[1]
    pre = rate_ref[:, :heads] + dbias_ref[...]
    log_decay = -jnp.exp(dlog_ref[...]) * softplus(pre)
    return sigmoid(rate_ref[:, heads:]), log_decay, pre


def block_masks(info, c):
    row, col = iota((BLK, BLK), 0), iota((BLK, BLK), 1)
    base = info[NB] + c * BLK
    docs_r, docs_c = doc_of(info, base + row), doc_of(info, base + col)
    keep = (docs_r == docs_c) & (col <= row)
    column = doc_of(info, base + iota((BLK, 1), 0))
    first = jnp.where(column == doc_of(info, base - 1 + iota((BLK, 1), 0) * 0), 1.0, 0.0)
    last = jnp.where(column == doc_of(info, base + BLK - 1 + iota((BLK, 1), 0) * 0), 1.0, 0.0)
    tri = jnp.where(col <= row, 1.0, 0.0)
    strict = jnp.where(col < row, 1.0, 0.0)
    return keep, first, last, tri, strict


def decays(g, first, last, tri):
    cum = dot_exact_left(tri, jnp.broadcast_to(g, (BLK, DK)))[:, :1]
    carry = first * jnp.exp(cum)
    to_end = last * jnp.exp(cum[BLK - 1 :, :] - cum)
    return carry, to_end


def mixer_forward(
    info, proj, rate, convw, dlog, dbias, out_w, gain, cot,
    conv_o, dec_o, inv_o, wu_o, qe_o, step_o, states_o, head_o, gated_o, ga_o, ta_o, halo_o, mixed_o, cot_o,
    xpad, ol, gs, scores, ab, rim, rim_got, got1, tot, got2, hs, hr, s1, r1, s2, r2, sc, rc, lc
):
    rows = proj.shape[0]
    heads = dlog.shape[1]
    blocks = rows // BLK
    me, z, y, dev = seq_place()
    seqs, head = SIDE * SIDE, lax.axis_index("head")
    before, behind = (lax.rem(me + seqs - 1, seqs), head), (lax.rem(me + 1, seqs), head)
    greet(side_peers() + [before, behind] + head_peers())
    cot_sent = gather_start(cot, cot_o, sc, rc, lc)
    for h in range(heads):
        rim[:, pl.ds(h * CONVW, CONVW)] = proj[rows - PAD :, pl.ds(h * MIXW, CONVW)].astype(BF16).astype(F32)
    ahead = cp(rim, rim_got, hs, hr, behind)
    ahead.start()
    strength, log_decay, _ = rates(rate, dlog, dbias)
    valid = [valid_column(info, rows, KCONV - 1 - j) for j in range(KCONV)]
    ahead.wait_recv()
    halo_o[...] = jnp.where(me > 0, rim_got[...], 0.0)
    for h in range(heads):
        src, dst = pl.ds(h * MIXW, CONVW), pl.ds(h * CONVW, CONVW)
        xpad[:PAD, :] = halo_o[:, dst]
        xpad[PAD:, :] = proj[:, src].astype(BF16).astype(F32)
        conv = jnp.zeros((rows, CONVW), F32)
        for j in range(KCONV):
            lo = PAD - (KCONV - 1) + j
            conv = conv + convw[j : j + 1, dst].astype(F32) * xpad[lo : lo + rows, :] * valid[j]
        conv_o[:, dst] = conv
    for c in range(blocks):
        keep, first, last, tri, strict = block_masks(info, c)
        here = pl.ds(c * BLK, BLK)
        for h in range(heads):
            qa, ka, va, rq, rk = vectors(conv_o[here, pl.ds(h * CONVW, CONVW)])
            q, k = qa * (rq * DK**-0.5), ka * rk
            beta = strength[c * BLK : (c + 1) * BLK, h : h + 1]
            g = log_decay[c * BLK : (c + 1) * BLK, h : h + 1]
            spread = dot_exact_left(tri, g * strict)
            dec = jnp.where(keep, jnp.exp(jnp.where(keep, spread, 0.0)), 0.0)
            carry, to_end = decays(g, first, last, tri)
            low = strict * (beta * dec * dot(k, k, "nt"))
            inv = unit_lower_inverse(low)
            u = h * blocks + c
            dec_o[u] = dec
            inv_o[u] = inv.astype(BF16)
            rhs = jnp.concatenate([(beta * carry) * k, beta * va], axis=1)
            wu = dot(inv, rhs)
            wu_o[u] = wu
            scores[u] = (dec * dot(q, k, "nt")).astype(BF16)
            qe_o[here, pl.ds(h * DK, DK)] = carry * q
            step = dot(wu, to_end * k, "tn")
            eye = jnp.where(iota((DK, DK), 0) == iota((DK, DK), 1), 1.0, 0.0)
            step_o[u, :DK] = carry[BLK - 1 :, :] * eye - step[:DK]
            step_o[u, DK:] = step[DK:]
        if c == 0:
            cot_sent += gather_forward(cot, cot_o, sc, rc)
    for h in range(heads):
        whole = step_o[h * blocks]
        for c in range(1, blocks):
            nxt = step_o[h * blocks + c]
            whole = add_low(dot3(whole, nxt[:DK]), nxt[DK:])
        ab[h] = whole.astype(ab.dtype)

    out, wait = share_start(ab, got1, y, lambda d: dev(0, d), s1, r1)
    for h in range(heads):
        for c in range(blocks):
            u, here = h * blocks + c, pl.ds(c * BLK, BLK)
            block = dot(scores[u], wu_o[u])
            qe_o[here, pl.ds(h * DK, DK)] = qe_o[here, pl.ds(h * DK, DK)] - block[:, :DK]
            ol[here, pl.ds(h * DV, DV)] = block[:, DK:]
    wait()
    held_before = []
    for h in range(heads):
        whole = got1[0, h].astype(F32)
        prefix = jnp.where(y > 0, whole, unit_top())
        for j in range(1, SIDE):
            a, b = got1[j, h, :DK, :], got1[j, h, DK:, :].astype(F32)
            whole = add_low(dot_left2(whole, a), b)
            if j < SIDE - 1:
                prefix = jnp.where(y > j, whole, prefix)
        tot[h] = whole.astype(BF16)
        held_before.append(prefix)
        for j in range(SIDE):
            ga_o[j, h] = got1[j, h, :DK, :]
    more, wait = share_start(tot, got2, z, lambda d: dev(d, 0), s2, r2)
    for h in range(heads):
        gate = proj[:, pl.ds(h * MIXW + CONVW, DV)]
        gs[:, pl.ds(h * DV, DV)] = gain[...] * (gate * sigmoid(gate))
    wait()
    for h in range(heads):
        held = jnp.zeros((DV, DK), F32)
        for j in range(SIDE - 1):
            held = jnp.where(
                z > j, dot_left2(held, got2[j, h, :DK, :]) + got2[j, h, DK:, :].astype(F32), held
            )
        for j in range(SIDE):
            ta_o[j, h] = got2[j, h, :DK, :]
        state = dot3(held, held_before[h][:DK]) + held_before[h][DK:]
        for c in range(blocks):
            u = h * blocks + c
            here, cols = pl.ds(c * BLK, BLK), pl.ds(h * DV, DV)
            states_o[u] = state
            block = ol[here, cols] + dot(qe_o[here, pl.ds(h * DK, DK)], state, "nt")
            head_o[here, cols] = block
            gated_o[here, cols] = (block * mean_scale(block) * gs[here, cols]).astype(BF16)
            if c + 1 < blocks:
                state = dot3(state, step_o[u, :DK, :]) + step_o[u, DK:, :]
    for j in range(0, D, CONVW):
        mixed_o[:, j : j + CONVW] = dot(gated_o[...], out_w[:, j : j + CONVW]).astype(BF16)
    gather_end(cot, cot_o, sc, rc, lc, cot_sent)
    for s in out + more + [ahead]:
        s.wait_send()


def dot_left2(a, b, form="nn"):
    ah, al = halves(a)
    return dot(ah, b, form) + dot(al, b, form)


def head_back(d_mixed, out_w, head_out, proj, gain, qe, step, d_out_o, d_gate_o, y_o, inc_o):
    rows = qe.shape[0]
    blocks = rows // BLK
    heads = qe.shape[1] // DK
    total = jnp.zeros((1, DV), F32)
    for h in range(heads):
        cols = pl.ds(h * DV, DV)
        for c in range(blocks):
            here = pl.ds(c * BLK, BLK)
            dg, out = dot(d_mixed[here, :], out_w[cols, :], "nt"), head_out[here, cols]
            gate = proj[here, pl.ds(h * MIXW + CONVW, DV)]
            s = sigmoid(gate)
            silu = gate * s
            scale = lax.rsqrt(jnp.mean(out * out, axis=1, keepdims=True) + 1e-05)
            dn = dg * (out * scale)
            d_gate_o[here, pl.ds(h * MIXW + CONVW, DV)] = (dn * gain[...] * (s * (1.0 + gate * (1.0 - s)))).astype(BF16)
            total = total + jnp.sum(dn * silu, axis=0, keepdims=True)
            f = dg * gain[...] * silu
            d_out = scale * f - out * (scale * scale * scale) * jnp.mean(f * out, axis=1, keepdims=True)
            d_out_o[here, cols] = d_out
            y_o[h * blocks + c] = dot(d_out, qe[here, pl.ds(h * DK, DK)], "tn")
        inc = y_o[h * blocks + blocks - 1]
        for c in range(blocks - 2, -1, -1):
            inc = y_o[h * blocks + c] + dot3(inc, step[h * blocks + c, :DK, :], "nt")
        inc_o[h] = inc.astype(inc_o.dtype)
    return total


def mixer_back(
    info, d_mixed, out_w, head_out, proj, gain, qe, step, ga, ta, middle, cot, gated_t, s_gu, conv, dec, inv, wu, states,
    rate, halo, convw, dlog, dbias,
    d_proj_o, d_tail_o, d_edge_o, d_rate_o, d_convw_o, d_decay_o, d_gain_o, s_down_o, s_out_o, g_gu_o,
    d_out, y, inc, later, got1, tot, got2, xpad, dpad, dsend, cols_s, d_pre_o,
    g_down, g_out, relay_d, relay_o, got_d, got_o, last_got, s1, r1, s2, r2, s3, r3, s4, r4
):
    greet(side_peers())
    settle = Settle(lambda i, b: last_got.at[i, b], s4, r4)
    for b in (2, 1, 3):
        for i in range(2):
            settle.send(s_gu.at[i, b], i, b)
    grads = (g_down, g_out)
    spread = Spread(
        lambda i, owner: grads[i].at[owner], lambda i, b: (relay_d, relay_o)[i].at[b],
        lambda i, s, b: (got_d, got_o)[i].at[s, b], s3, r3,
    )
    d_gain_o[...] = head_back(d_mixed, out_w, head_out, proj, gain, qe, step, d_out, d_proj_o, y, inc)

    def make(o, left, right):
        for j in range(0, o.shape[0], 2):
            both = dot(left[...], right[:, j * LANES : (j + 2) * LANES]).astype(BF16)
            o[j], o[j + 1] = both[:, :LANES], both[:, LANES:]

    def level_one():
        make(g_down, middle, cot)
        make(g_out, gated_t, d_mixed)

    def level_two():
        for place in PLACES:
            spread.ready(*place, (0,))

    swaps = states_backward(inc, ga, ta, later, got1, tot, got2, s1, r1, s2, r2, level_one, level_two)
    for place in PLACES:
        spread.ready(*place, (1,))
    rows = d_out.shape[0]
    heads = later.shape[0]
    blocks = rows // BLK
    strength, log_decay, pre = rates(rate, dlog, dbias)
    valid = [valid_column(info, rows, KCONV - 1 - j) for j in range(KCONV)]
    for h in range(heads):
        grad = later[h]
        for c in range(blocks - 1, -1, -1):
            u = h * blocks + c
            dsend[u] = grad
            if c:
                grad = dot3(grad, step[u, :DK, :], "nt") + y[u]
    for c in range(blocks):
        keep, first, last, tri, strict = block_masks(info, c)
        here = pl.ds(c * BLK, BLK)
        for h in range(heads):
            u = h * blocks + c
            cv = conv[here, pl.ds(h * CONVW, CONVW)]
            sg = sigmoid(cv)
            qa, ka, va, rq, rk = vectors(cv)
            rqs = rq * DK**-0.5
            q, k = qa * rqs, ka * rk
            beta = strength[c * BLK : (c + 1) * BLK, h : h + 1]
            g = log_decay[c * BLK : (c + 1) * BLK, h : h + 1]
            carry, to_end = decays(g, first, last, tri)
            dm = dec[u]
            sc = dm * dot(q, k, "nt")
            gm = dm * dot(k, k, "nt") * strict
            state, d_end = states[u], dsend[u]
            do = d_out[here, pl.ds(h * DV, DV)]
            ks = dot(k, state, "nt")
            qs = dot(q, state, "nt")
            fresh = wu[u, :, DK:] - dot(wu[u, :, :DK], state, "nt")
            kd = to_end * k
            d_fresh = dot(sc, do, "tn") + dot(kd, d_end, "nt")
            d_rhs = dot(inv[u], d_fresh, "tn")
            d_low = -dot(d_rhs, fresh, "nt")
            d_sc = dot(do, fresh, "nt")
            d_val = beta * d_rhs
            ebar = d_low * gm
            d_beta = jnp.sum(d_rhs * (va - carry * ks), axis=1, keepdims=True) + jnp.sum(ebar, axis=1, keepdims=True)
            e = d_sc * sc + beta * ebar
            d_scd = d_sc * dm
            d_gm = (beta * d_low) * (dm * strict)
            d_kd = dot(fresh, d_end)
            d_q = dot(d_scd, k) + carry * dot(do, state)
            d_k = (
                dot(d_scd, q, "tn")
                - (beta * carry) * dot(d_rhs, state)
                + to_end * d_kd
                + dot(d_gm, k)
                + dot(d_gm, k, "tn")
            )
            hcol = carry * jnp.sum(do * qs - beta * d_rhs * ks, axis=1, keepdims=True)
            fcol = jnp.sum(kd * d_kd, axis=1, keepdims=True)
            tail = carry[BLK - 1 :, :] * jnp.sum(
                jnp.sum(state * d_end, axis=1, keepdims=True), axis=0, keepdims=True
            )
            lane = iota((BLK, DK), 1)
            d_g = (
                jnp.sum(dot_exact_left(tri, e, "tn") * strict, axis=1, keepdims=True)
                + dot_exact_left(tri, jnp.where(lane == 0, hcol, 0.0), "tn")[:, :1]
                + dot_exact_left(strict, jnp.where(lane == 0, fcol, 0.0))[:, :1]
                + tail
            )
            cols_s[here, h : h + 1] = d_g
            cols_s[here, heads + h : heads + h + 1] = d_beta
            d_qa = rqs * d_q - qa * (rqs * rq * rq * jnp.sum(d_q * qa, axis=1, keepdims=True))
            d_ka = rk * d_k - ka * (rk * rk * rk * jnp.sum(d_k * ka, axis=1, keepdims=True))
            d_act = jnp.concatenate([d_qa, d_ka, d_val], axis=1)
            d_pre_o[here, pl.ds(h * CONVW, CONVW)] = d_act * (sg * (1.0 + cv * (1.0 - sg)))
            spread.relays(c * heads + h)
    d_g, d_beta = cols_s[:, :heads], cols_s[:, heads : 2 * heads]
    d_bias = -d_g * jnp.exp(dlog[...]) * sigmoid(pre)
    d_rate_o[:, :heads] = d_bias
    d_rate_o[:, heads:] = d_beta * strength * (1.0 - strength)
    d_decay_o[:, :heads] = jnp.sum(d_g * log_decay, axis=0, keepdims=True)
    d_decay_o[:, heads:] = jnp.sum(d_bias, axis=0, keepdims=True)
    for h in range(heads):
        src, dst = pl.ds(h * MIXW, CONVW), pl.ds(h * CONVW, CONVW)
        xpad[:PAD, :] = halo[:, dst]
        xpad[PAD:, :] = proj[:, src].astype(BF16).astype(F32)
        dpad[...] = jnp.zeros_like(dpad)
        d_conv = d_pre_o[:, dst]
        for j in range(KCONV):
            lo = PAD - (KCONV - 1) + j
            masked = d_conv * valid[j]
            d_convw_o[j : j + 1, dst] = jnp.sum(masked * xpad[lo : lo + rows, :], axis=0, keepdims=True)
            dpad[lo : lo + rows, :] += convw[j : j + 1, dst].astype(F32) * masked
        d_edge_o[:, dst] = dpad[:PAD, :]
        d_tail_o[:, dst] = dpad[rows - PAD :, :]
        d_proj_o[:, src] = dpad[PAD:, :].astype(BF16)
    for i in range(2):
        g_gu_o[i] = s_gu[i, 0].astype(F32) + settle.others(i)
    for i, o in ((0, s_down_o), (1, s_out_o)):
        for b in FAR:
            o[b] = spread.total(i, b).astype(BF16)
    spread.end()
    settle.end()
    for s in swaps:
        s.wait_send()


def call(kernel, outs, scratch, limit, *args, flops=2_000_000_000, nbytes=16_000_000):
    def spec(a):
        return SMEM if a.dtype == jnp.int32 else VMEM

    return pl.pallas_call(
        kernel,
        out_shape=outs,
        in_specs=[spec(a) for a in args],
        out_specs=[VMEM for _ in outs],
        scratch_shapes=scratch,
        compiler_params=pltpu.CompilerParams(vmem_limit_bytes=limit << 20),
        cost_estimate=pl.CostEstimate(flops=flops, bytes_accessed=nbytes, transcendentals=0),
    )(*args)


def sds(shape, dtype=F32):
    return jax.ShapeDtypeStruct(shape, dtype)
CHIPS = 4
LANES = 128


def cp(src, dst, send, recv, dev):
    return pltpu.make_async_remote_copy(
        src_ref=src, dst_ref=dst, send_sem=send, recv_sem=recv, device_id=dev, device_id_type=pl.DeviceIdType.MESH
    )


def greet(devices):
    barrier = pltpu.get_barrier_semaphore()
    for dev in devices:
        pl.semaphore_signal(barrier, inc=1, device_id=dev, device_id_type=pl.DeviceIdType.MESH)
    pl.semaphore_wait(barrier, len(devices))


def head_place():
    me = lax.axis_index("head")
    chip, core = me // 2, me % 2
    seq = lax.axis_index("seq")

    def dev(step, flip=False):
        c = lax.rem(chip + step, CHIPS)
        return (seq, c * 2 + (1 - core if flip else core))

    return me, chip, core, dev


def head_peers():
    dev = head_place()[3]
    return [dev(0, True)] + [dev(d) for d in range(1, CHIPS)]


def head_rows(o, rows, step, flip=False, lo=0, size=None):
    owner = head_place()[3](step, flip)[1]
    size = size or rows
    return o.at[pl.ds(pl.multiple_of(owner * rows + lo, size), size)]


def gather_start(x, o, ssem, rsem, lsem):
    rows = x.shape[0]
    dev = head_place()[3]
    pltpu.make_async_copy(x, head_rows(o, rows, 0), lsem).start()
    out = [cp(x, head_rows(o, rows, 0), ssem.at[d], rsem.at[d], dev(d)) for d in (1, 3)]
    out.append(cp(x, head_rows(o, rows, 0), ssem.at[0], rsem.at[0], dev(0, True)))
    for s in out:
        s.start()
    return out


def opposite(rows):
    return ((0, 2, 6, 1), (rows // 2, 8, 9, 3))


def gather_forward(x, o, ssem, rsem):
    rows = x.shape[0]
    dev = head_place()[3]
    partner = dev(0, True)
    out = []

    def go(src, k, to):
        s = cp(src, src, ssem.at[k], rsem.at[k], to)
        s.start()
        out.append(s)

    for lo, relay, core, step in opposite(rows):
        there = head_rows(o, rows, CHIPS - step)
        cp(x, there, ssem.at[step], rsem.at[step], dev(step)).wait_recv()
        go(head_rows(o, rows, CHIPS - step, False, lo, rows // 2), relay, dev(step))
        go(there, CHIPS + step, partner)
    for lo, relay, core, step in opposite(rows):
        there = head_rows(o, rows, 2, False, lo, rows // 2)
        cp(there, there, ssem.at[relay], rsem.at[relay], dev(step)).wait_recv()
        go(there, core, partner)
    return out


def gather_end(x, o, ssem, rsem, lsem, sent):
    rows = x.shape[0]
    dev = head_place()[3]
    partner = dev(0, True)
    pltpu.make_async_copy(x, head_rows(o, rows, 0), lsem).wait()
    cp(x, head_rows(o, rows, 0, True), ssem.at[0], rsem.at[0], partner).wait_recv()
    for lo, relay, core, step in opposite(rows):
        k = CHIPS + step
        cp(x, head_rows(o, rows, CHIPS - step, True), ssem.at[k], rsem.at[k], partner).wait_recv()
        there = head_rows(o, rows, 2, True, lo, rows // 2)
        cp(there, there, ssem.at[core], rsem.at[core], partner).wait_recv()
    for s in sent:
        s.wait_send()


def mean_scale(v):
    return lax.rsqrt(jnp.mean(v * v, axis=1, keepdims=True) + 1e-05)


def first_norm(tokens, gain, all_o, block, ssem, rsem, lsem):
    greet(head_peers())
    v = tokens[...].astype(F32)
    block[...] = (v * mean_scale(v) * gain[...]).astype(BF16)
    sent = gather_start(block, all_o, ssem, rsem, lsem)
    sent += gather_forward(block, all_o, ssem, rsem)
    gather_end(block, all_o, ssem, rsem, lsem, sent)


def norm_back(v, gain, d_norm):
    r = mean_scale(v)
    e = d_norm * gain
    d_v = r * e - v * (r * r * r * jnp.mean(e * v, axis=1, keepdims=True))
    return d_v, jnp.sum(d_norm * v * r, axis=0, keepdims=True)


def feed_forward(
    x, tokens, gain, cot, cot_all, gu, down,
    hidden_o, all_o, d_hidden_o, d_gain_o, sums_o, middle_o, feed_o,
    n2, guv, downv, d_middle, d_gu, d_two, block, ta, pa, ga, ma, tb, pb, gb, mb, g, relay, seqs_got,
    ls, sa, ra, sb, rb, s1, r1, l1, s2, r2, l2, s3, r3
):
    load_d = pltpu.make_async_copy(down, downv, ls.at[0])
    load_d.start()
    load_g = pltpu.make_async_copy(gu, guv, ls.at[1])
    load_g.start()
    greet(head_peers() + side_peers())
    one = pair_sends(x, pa, sa, ra, FAR)
    two = ChipSum(x, one, ta, pa, ga, ma, sa, ra)
    load_d.wait()
    d_middle[...] = dot(downv[...], cot_all[...], "nt")
    two.relay()
    hidden = tokens[...].astype(F32) + two.result()
    hidden_o[...] = hidden
    block[...] = (hidden * mean_scale(hidden) * gain[...]).astype(BF16)
    ahead = gather_start(block, n2, s1, r1, l1)
    load_g.wait()
    ahead += gather_forward(block, n2, s1, r1)
    gather_end(block, n2, s1, r1, l1, ahead)
    hid = downv.shape[0]
    low = hid // 32 * 16
    for lo, hi in ((0, low), (low, hid)):
        gate = dot(guv[lo:hi, :], n2[...], "nt")
        up = dot(guv[hid + lo : hid + hi, :], n2[...], "nt")
        s = sigmoid(gate)
        silu = gate * s
        dm = d_middle[lo:hi, :]
        middle_o[lo:hi, :] = (silu * up).astype(BF16)
        d_gu[lo:hi, :] = (dm * up * (s * (1.0 + gate * (1.0 - s)))).astype(BF16)
        d_gu[hid + lo : hid + hi, :] = (dm * silu).astype(BF16)
    for j in range(0, D, 512):
        d_two[:, j : j + 512] = dot(d_gu[...], guv[:, j : j + 512], "tn").astype(BF16)
    one_b = pair_sends(d_two, pb, sb, rb, FAR)
    spread = Spread(
        lambda i, owner: g.at[owner, i], lambda i, b: relay.at[i, b], lambda i, s, b: seqs_got.at[i, s, b], s3, r3
    )
    dev = seq_place()[3]

    def make(place):
        owner = dev(*place)[0]
        cols = n2[:, pl.ds(pl.multiple_of(owner * LANES, LANES), LANES)]
        out = dot(d_gu[...], cols).astype(BF16)
        g[owner, 0] = out[:hid]
        g[owner, 1] = out[hid:]
        spread.ready(*place)

    for place in PLACES[:3]:
        make(place)
    two_b = ChipSum(d_two, one_b, tb, pb, gb, mb, sb, rb)
    for place in PLACES[3:9]:
        make(place)
    two_b.relay()
    for place in PLACES[9:]:
        make(place)
    d_norm, d_gain = norm_back(hidden_o[...], gain[...], two_b.result())
    d_hidden = cot[...].astype(F32) + d_norm
    d_hidden_o[...] = d_hidden
    d_gain_o[...] = d_gain
    block[...] = d_hidden.astype(BF16)
    ahead = gather_start(block, all_o, s2, r2, l2)
    spread.relays()
    for j in range(0, D, 512):
        feed_o[:, j : j + 512] = dot(middle_o[...], downv[:, j : j + 512], "tn").astype(BF16)
    ahead += gather_forward(block, all_o, s2, r2)
    for b in FAR:
        for i in range(2):
            sums_o[i, b] = spread.total(i, b).astype(BF16)
    gather_end(block, all_o, s2, r2, l2, ahead)
    spread.end()
    two.end()
    two_b.end()


def reach(kernel, outs, scratch, cid, limit, *args, anywhere=(), scalars=(), nbytes=12_000_000):
    return pl.pallas_call(
        kernel,
        out_shape=outs,
        in_specs=[
            pl.BlockSpec(memory_space=pl.ANY) if i in anywhere else SMEM if i in scalars else VMEM for i in range(len(args))
        ],
        out_specs=[VMEM for _ in outs],
        scratch_shapes=scratch,
        compiler_params=pltpu.CompilerParams(
            collective_id=cid, has_side_effects=True, vmem_limit_bytes=limit << 20
        ),
        cost_estimate=pl.CostEstimate(flops=0, bytes_accessed=nbytes, transcendentals=0),
    )(*args)


def sems(n):
    return pltpu.SemaphoreType.DMA((n,))


def gather_scratch():
    return [sems(10), sems(10), pltpu.SemaphoreType.DMA]


SIDE = 4


def seq_place():
    me = lax.axis_index("seq")
    z, y = me // SIDE, me % SIDE
    head = lax.axis_index("head")

    def dev(dz, dy):
        return (lax.rem(z + dz, SIDE) * SIDE + lax.rem(y + dy, SIDE), head)

    return me, z, y, dev


def side_peers():
    dev = seq_place()[3]
    return [dev(0, d) for d in range(1, SIDE)] + [dev(d, 0) for d in range(1, SIDE)]


FAR = (2, 1, 3, 0)
FIRST, OTHER = (2, 1), (3, 0)
PLACES = (
    (2, 2), (2, 1), (1, 2), (2, 3), (3, 2), (2, 0), (0, 2), (1, 3), (3, 1), (1, 0), (0, 1), (3, 3), (1, 1), (0, 3), (3, 0),
    (0, 0),
)


class Spread:
    def __init__(self, piece, relay, got, ssem, rsem):
        self.piece, self.relay, self.got, self.ssem, self.rsem = piece, relay, got, ssem, rsem
        self.dev = seq_place()[3]
        self.sent = []

    def way(self, i, a, b):
        return self.dev(b, a) if i == 0 else self.dev(a, b)

    def copy(self, i, a, b, owner):
        k = (i * SIDE + a) * SIDE + b
        if a == 2:
            dst, step = self.relay(i, b), 1 if b in FIRST else 3
        else:
            dst, step = self.got(i, 0 if a == 1 else 1, b), a
        return cp(self.piece(i, owner), dst, self.ssem.at[k], self.rsem.at[k], self.way(i, step, 0))

    def send(self, i, a, b, owner):
        s = self.copy(i, a, b, owner)
        s.start()
        self.sent.append(s)

    def late(self, a, b):
        return a == 1 and b in FIRST or a == 3 and b in OTHER

    def ready(self, dz, dy, halves_=(0, 1)):
        owner = self.dev(dz, dy)[0]
        for i in halves_:
            a, b = (dy, dz) if i == 0 else (dz, dy)
            if a and not self.late(a, b):
                self.send(i, a, b, owner)

    def relays(self, part=None):
        for n, b in enumerate(FAR):
            if part is not None and n != part:
                continue
            for i in range(2):
                a = 1 if b in FIRST else 3
                owner = self.way(i, a, b)[0]
                self.copy(i, 2, b, owner).wait_recv()
                both = self.piece(i, owner)[...].astype(F32) + self.relay(i, b)[...].astype(F32)
                self.relay(i, b)[...] = both.astype(BF16)
                k = (i * SIDE + a) * SIDE + b
                s = cp(
                    self.relay(i, b), self.got(i, 0 if a == 1 else 1, b), self.ssem.at[k], self.rsem.at[k],
                    self.way(i, a, 0),
                )
                s.start()
                self.sent.append(s)

    def total(self, i, b):
        owner = self.way(i, 0, b)[0]
        for a in (1, 3):
            self.copy(i, a, b, owner).wait_recv()
        return self.piece(i, owner)[...].astype(F32) + (
            self.got(i, 0, b)[...].astype(F32) + self.got(i, 1, b)[...].astype(F32)
        )

    def end(self):
        for s in self.sent:
            s.wait_send()


class Settle:
    def __init__(self, got, ssem, rsem):
        self.got, self.ssem, self.rsem = got, ssem, rsem
        self.dev = seq_place()[3]
        self.sent = {}

    def send(self, src, i, b):
        k = i * SIDE + b
        dev = self.dev(b, 0) if i == 0 else self.dev(0, b)
        self.sent[i, b] = cp(src, self.got(i, b), self.ssem.at[k], self.rsem.at[k], dev)
        self.sent[i, b].start()

    def others(self, i):
        for b in (1, 3, 2):
            self.sent[i, b].wait_recv()
        return (self.got(i, 1)[...].astype(F32) + self.got(i, 3)[...].astype(F32)) + self.got(i, 2)[...].astype(F32)

    def end(self):
        for s in self.sent.values():
            s.wait_send()


def share_start(src, got, place, to, ssem, rsem, size=SIDE, own=None):
    part = (lambda d: src) if own is None else (lambda d: src.at[lax.rem(place + d, size)])
    got[place] = src[...] if own is None else src[place]
    steps = (2, 1, 3) if size == SIDE else range(1, size)
    out = [cp(part(d), got.at[place], ssem.at[d], rsem.at[d], to(d)) for d in steps]
    for s in out:
        s.start()

    def wait():
        for d in steps:
            back = lax.rem(place + size - d, size)
            cp(part(d), got.at[back], ssem.at[d], rsem.at[d], to(d)).wait_recv()

    return out, wait


def in_order(got):
    total = got[0]
    for i in range(1, got.shape[0]):
        total = total + got[i]
    return total


def share(src, got, place, to, ssem, rsem):
    out, wait = share_start(src, got, place, to, ssem, rsem)
    wait()
    return out


def unit_top():
    return jnp.where(iota((DK + DV, DK), 0) == iota((DK + DV, DK), 1), 1.0, 0.0)


def add_low(pair, low):
    return jnp.concatenate([pair[:DK], pair[DK:] + low], axis=0)


def states_backward(inc, ga, ta, later_o, got1, tot, got2, s1, r1, s2, r2, level_one, level_two):
    me, z, y, dev = seq_place()
    heads = inc.shape[0]
    out, wait = share_start(inc, got1, y, lambda d: dev(0, d), s1, r1)
    level_one()
    wait()
    after = []
    for h in range(heads):
        whole = add_low(dot(unit_top(), ga[SIDE - 1, h], "nt"), got1[SIDE - 1, h].astype(F32))
        suffix = jnp.where(y < SIDE - 1, whole, unit_top())
        for j in range(SIDE - 2, -1, -1):
            whole = add_low(dot_left2(whole, ga[j, h], "nt"), got1[j, h].astype(F32))
            if j:
                suffix = jnp.where(y < j, whole, suffix)
        tot[h] = whole[DK:].astype(BF16)
        after.append(suffix)
    more, wait = share_start(tot, got2, z, lambda d: dev(d, 0), s2, r2)
    level_two()
    wait()
    for h in range(heads):
        held = jnp.zeros((DV, DK), F32)
        for j in range(SIDE - 1, 0, -1):
            held = jnp.where(z < j, dot_left2(held, ta[j, h], "nt") + got2[j, h].astype(F32), held)
        later_o[h] = dot3(held, after[h][:DK]) + after[h][DK:]
    return out + more


def pair_sends(x, pair, ssem, rsem, steps):
    rows = pair.shape[1]
    dev = head_place()[3]
    out = {}
    for d in steps:
        owner = dev(d, True)[1]
        src = x.at[pl.ds(pl.multiple_of(owner * rows, rows), rows)]
        out[d] = cp(src, pair.at[d], ssem.at[d], rsem.at[d], dev(0, True))
        out[d].start()
    return out


class ChipSum:
    def __init__(self, x, first, total, pair, got, mid, ssem, rsem):
        self.x, self.first, self.total, self.pair = x, first, total, pair
        self.got, self.mid, self.ssem, self.rsem = got, mid, ssem, rsem
        self.rows = pair.shape[1]
        self.dev = head_place()[3]
        half = self.rows // 2
        self.top, self.low = slice(0, half), slice(half, self.rows)
        self.sent = []
        self.mid[2] = self.both(2).astype(BF16)
        self.send(2, self.top, 0, 4, 1)
        self.send(2, self.low, 0, 5, 3)
        self.right = self.both(1)
        self.mid[1, self.low] = self.right[self.low].astype(BF16)
        self.send(1, self.low, 1, 6, 1)
        self.left = self.both(3)
        self.mid[3, self.top] = self.left[self.top].astype(BF16)
        self.send(3, self.top, 3, 7, 3)
        self.total[...] = self.both(0)

    def both(self, d):
        self.first[d].wait_recv()
        owner = self.dev(d)[1]
        mine = self.x[pl.ds(pl.multiple_of(owner * self.rows, self.rows), self.rows), :]
        return mine.astype(F32) + self.pair[d].astype(F32)

    def copy(self, d, part, slot, k, step):
        at = pl.ds(part.start, part.stop - part.start)
        return cp(self.mid.at[d, at], self.got.at[slot, at], self.ssem.at[k], self.rsem.at[k], self.dev(step))

    def send(self, *what):
        s = self.copy(*what)
        s.start()
        self.sent.append(s)

    def relay(self):
        self.copy(2, self.top, 0, 4, 1).wait_recv()
        self.mid[1, self.top] = (self.right[self.top] + self.got[0, self.top].astype(F32)).astype(BF16)
        self.send(1, self.top, 1, 8, 1)
        self.copy(2, self.low, 0, 5, 3).wait_recv()
        self.mid[3, self.low] = (self.left[self.low] + self.got[0, self.low].astype(F32)).astype(BF16)
        self.send(3, self.low, 3, 9, 3)

    def result(self):
        self.copy(1, self.low, 1, 6, 1).wait_recv()
        self.copy(3, self.top, 3, 7, 3).wait_recv()
        self.copy(1, self.top, 1, 8, 1).wait_recv()
        self.copy(3, self.low, 3, 9, 3).wait_recv()
        return self.total[...] + (self.got[1].astype(F32) + self.got[3].astype(F32))

    def end(self):
        for s in self.sent + list(self.first.values()):
            s.wait_send()


def finish(
    dproj, normed, w, d_rate, rate_w, d_tail, d_edge, feed, hidden, tokens, d_hidden, gain, convs, decay, g_feed, g_head,
    s_down, s_out,
    layer_o, d_tokens_o, g_mixer_o, g_gain_o, g_feed_o, g_head_o, conv_o, dlog_o, dbias_o, rate_o, g_down_o, g_out_o,
    dp, wv, edge, g, relay, got1, mid, got2, dn, ta, pa, ga, ma, tb, pb, gb, mb, got_d, got_o,
    e0, eh, e1, ey, e2, ez, m0, mh, m1, my, m2, mz,
    es, er, ls, s1, r1, s2, r2, sa, ra, sb, rb, s5, r5, se, re, sm, rm
):
    me, z, y, dev = seq_place()
    head = lax.axis_index("head")
    heads, seqs = eh.shape[0], g.shape[1]
    rows = dp.shape[0]
    part, half = g_mixer_o.shape[1], g_mixer_o.shape[2]
    load_p = pltpu.make_async_copy(dproj, dp, ls.at[0])
    load_p.start()
    load_w = pltpu.make_async_copy(w, wv, ls.at[1])
    load_w.start()

    def across(d):
        return (me, lax.rem(head + d, heads))

    before, behind = (lax.rem(me + seqs - 1, seqs), head), (lax.rem(me + 1, seqs), head)
    greet([across(d) for d in range(1, heads)] + side_peers() + [before, behind])
    back = cp(d_edge, edge, es, er, before)
    back.start()
    feed_one = pair_sends(feed, pa, sa, ra, FAR)

    n_row, h_row = D // LANES, DV // LANES
    taps, wide_c = convs.shape
    c_row = wide_c // LANES
    ng, nc = e0.shape[0], taps * c_row + PAD
    for r in range(n_row):
        e0[r : r + 1, :] = g_feed[:, r * LANES : (r + 1) * LANES]
    e0[n_row:, :] = jnp.zeros((ng - n_row, LANES), F32)
    for r in range(h_row):
        e0[n_row + r : n_row + r + 1, :] = g_head[:, r * LANES : (r + 1) * LANES]
    small, wait_head = share_start(e0, eh, head, across, se.at[0], re.at[0], heads)
    for t in range(taps):
        for r in range(c_row):
            lo = ng + t * c_row + r
            e1[0, lo : lo + 1, :] = convs[t : t + 1, r * LANES : (r + 1) * LANES]
    e1[0, ng + nc - PAD : ng + nc, :] = jnp.zeros((PAD, LANES), F32)
    e1[0, ng + nc - PAD : ng + nc - PAD + 1, :] = decay[...]
    rates_t = dot(d_rate[:, :PAD], normed[...], "tn")
    for i in range(SIDE):
        if i:
            e1[i, ng : ng + nc, :] = e1[0, ng : ng + nc, :]
        for j in range(SIDE):
            at = (j * SIDE + i) * LANES
            e1[i, ng + nc + j * PAD : ng + nc + (j + 1) * PAD, :] = rates_t[:, at : at + LANES]

    sums = (s_down, s_out)
    settle = Settle(lambda i, b: (got_d, got_o)[i].at[b], s5, r5)
    for b in (2, 1, 3):
        for i in range(2):
            settle.send(sums[i].at[b], i, b)
    load_p.wait()
    back.wait_recv()
    there = jnp.where(me < seqs - 1, edge[...], 0.0)
    tail = jnp.concatenate([d_tail[:PAD, :], d_tail[PAD:, :] + there], axis=0).astype(BF16)
    wide = half - DV
    for i in range(2):
        dp[rows - 2 * PAD :, pl.ds(i * half, wide)] = tail[:, i * wide : (i + 1) * wide]

    spread = Spread(
        lambda i, owner: g.at[i, owner], lambda i, b: relay.at[i, b], lambda i, s, b: got1.at[i, s, b], s1, r1
    )
    settle_two = Settle(lambda i, b: got2.at[i, b], s2, r2)
    for n, place in enumerate(PLACES):
        owner = dev(*place)[0]
        left = normed[:, pl.ds(pl.multiple_of(owner * part, part), part)]
        both = dot(left, dp[...], "tn").astype(BF16)
        for i in range(2):
            g[i, owner] = both[:, i * half : (i + 1) * half]
        spread.ready(*place)
        if n == 2:
            wait_head()
            gains = in_order(eh)
            for i in range(SIDE):
                e1[i, :ng, :] = gains
            more, wait_y = share_start(e1, ey, y, lambda d: dev(0, d), se.at[1], re.at[1], SIDE, True)
            small += more
        if n == 9:
            wait_y()
            total = in_order(ey)
            for j in range(SIDE):
                e2[j, : ng + nc, :] = total[: ng + nc]
                e2[j, ng + nc :, :] = total[ng + nc + j * PAD : ng + nc + (j + 1) * PAD]
            more, wait_z = share_start(e2, ez, z, lambda d: dev(d, 0), se.at[2], re.at[2], SIDE, True)
            small += more
    feed_two = ChipSum(feed, feed_one, ta, pa, ga, ma, sa, ra)

    load_w.wait()
    low = rows // CHIPS
    hp = head_place()[3]
    dn_one = {}
    for d in FAR:
        chip = hp(d)[1] // 2
        here = pl.ds(pl.multiple_of(chip * low, low), low)
        dn[here, :] = (dot(dp[here, :], wv[...], "nt") + dot(d_rate[here, :], rate_w[...], "nt")).astype(BF16)
        dn_one.update(pair_sends(dn, pb, sb, rb, (d,)))
        spread.relays(FAR.index(d))
    feed_two.relay()
    dn_two = ChipSum(dn, dn_one, tb, pb, gb, mb, sb, rb)
    wait_z()
    total = in_order(ez)
    for r in range(n_row):
        g_feed_o[:, r * LANES : (r + 1) * LANES] = total[r : r + 1]
    for r in range(h_row):
        g_head_o[:, r * LANES : (r + 1) * LANES] = total[n_row + r : n_row + r + 1]
    own = conv_o.shape[1]
    for t in range(taps):
        for h in range(own):
            for r in range(c_row // own):
                lo = ng + t * c_row + h * (c_row // own) + r
                conv_o[t, h : h + 1, r * LANES : (r + 1) * LANES] = total[lo : lo + 1]
    dlog_o[...] = total[ng + nc - PAD : ng + nc - PAD + 1, :own]
    dbias_o[...] = total[ng + nc - PAD : ng + nc - PAD + 1, own : 2 * own]
    for i in range(2):
        rate_o[i] = total[ng + nc + i * own : ng + nc + (i + 1) * own]
    dn_two.relay()
    layer_o[...] = (hidden[...] + feed_two.result()).astype(BF16)
    d_norm, d_gain = norm_back(tokens[...].astype(F32), gain[...], dn_two.result())
    d_tokens_o[...] = d_hidden[...] + d_norm

    for r in range(n_row):
        m0[r : r + 1, :] = d_gain[:, r * LANES : (r + 1) * LANES]
    more, wait_head = share_start(m0, mh, head, across, sm.at[0], rm.at[0], heads)
    small += more

    def settle_mixer(b):
        for i in range(2):
            both = spread.total(i, b)
            if b:
                mid[i, b] = both.astype(BF16)
                settle_two.send(mid.at[i, b], i, b)
            else:
                g_mixer_o[i] = both

    settle_mixer(2)
    wait_head()
    m1[...] = in_order(mh)
    more, wait_y = share_start(m1, my, y, lambda d: dev(0, d), sm.at[1], rm.at[1])
    small += more
    settle_mixer(1)
    settle_mixer(3)
    wait_y()
    m2[...] = in_order(my)
    more, wait_z = share_start(m2, mz, z, lambda d: dev(d, 0), sm.at[2], rm.at[2])
    small += more
    settle_mixer(0)
    for i, o in ((0, g_down_o), (1, g_out_o)):
        o[...] = sums[i][0].astype(F32) + settle.others(i)
    wait_z()
    total = in_order(mz)
    for r in range(n_row):
        g_gain_o[:, r * LANES : (r + 1) * LANES] = total[r : r + 1]
    for i in range(2):
        g_mixer_o[i] = g_mixer_o[i] + settle_two.others(i)
    spread.end()
    settle.end()
    settle_two.end()
    feed_two.end()
    dn_two.end()
    for s in small + [back]:
        s.wait_send()


def hand_over(*refs):
    n = len(refs) // 2
    for src, dst in zip(refs[:n], refs[n:]):
        if src.shape == dst.shape:
            dst[...] = src[...]
        else:
            for i in range(src.shape[0]):
                dst[:, i, :] = src[i]


def local(
    tokens, mixer_gain, mixer_weight, rate_weight, conv_weight, decay_log, decay_bias, head_gain,
    output_weight, feed_gain, gate_up_weight, down_weight, doc_starts, cotangent,
):
    own = tokens.shape[0]
    (gathered,) = reach(
        first_norm,
        [sds((own * lax.axis_size("head"), D), BF16)],
        [pltpu.VMEM((own, D), BF16)] + gather_scratch(),
        3, 32, tokens, mixer_gain.reshape(1, D),
    )
    heads = mixer_weight.shape[1]
    mixer_flat = mixer_weight.reshape(D, heads * MIXW)
    rows = gathered.shape[0]
    blocks = rows // BLK
    units = heads * blocks
    seq = lax.axis_size("seq")
    projected = jnp.dot(gathered, mixer_flat, preferred_element_type=F32)
    rate_proj = jnp.einsum("td,dgh->tgh", gathered, rate_weight, preferred_element_type=F32).reshape(rows, 2 * heads)
    convw = conv_weight.reshape(KCONV, heads * CONVW)
    info = jnp.concatenate(
        [doc_starts, jnp.stack([lax.axis_index("seq") * rows, lax.axis_index("seq")]).astype(jnp.int32)]
    )
    dlog, dbias = decay_log.reshape(1, heads), decay_bias.reshape(1, heads)
    gain = head_gain.reshape(1, DV)

    out_flat = output_weight.reshape(heads * DV, D)
    pairs = pltpu.VMEM((SIDE, heads, DK + DV, DK), BF16)
    conv, dec, inv, wu, qe, step, states, head_out, gated, ga, ta, halo, mixed, cot_rows = reach(
        mixer_forward,
        [
            sds((rows, heads * CONVW)), sds((units, BLK, BLK)), sds((units, BLK, BLK), BF16),
            sds((units, BLK, DK + DV)), sds((rows, heads * DK)), sds((units, DK + DV, DK)), sds((units, DV, DK)),
            sds((rows, heads * DV)), sds((rows, heads * DV), BF16), sds((SIDE, heads, DK, DK), BF16),
            sds((SIDE, heads, DK, DK), BF16), sds((PAD, heads * CONVW)), sds((rows, D), BF16), sds((rows, D), BF16),
        ],
        [
            pltpu.VMEM((PAD + rows, CONVW), F32), pltpu.VMEM((rows, heads * DV), F32),
            pltpu.VMEM((rows, heads * DV), F32), pltpu.VMEM((units, BLK, BLK), BF16),
            pltpu.VMEM((heads, DK + DV, DK), BF16), pltpu.VMEM((PAD, heads * CONVW), F32),
            pltpu.VMEM((PAD, heads * CONVW), F32), pairs, pltpu.VMEM((heads, DK + DV, DK), BF16), pairs,
            pltpu.SemaphoreType.DMA, pltpu.SemaphoreType.DMA, sems(SIDE), sems(SIDE), sems(SIDE), sems(SIDE),
        ]
        + gather_scratch(),
        1, 56, info, projected, rate_proj, convw, dlog, dbias, out_flat, gain, cotangent, scalars=(0,), nbytes=30_000_000,
    )
    hid = down_weight.shape[0]
    part, half, n_head = D // seq, MIXW, lax.axis_size("head")
    gu_t = gate_up_weight.transpose(1, 2, 0).reshape(2 * hid, D)

    def sums_of_head():
        return [pltpu.VMEM((own, D), F32)] + [pltpu.VMEM((CHIPS, own, D), BF16) for _ in range(3)]

    hidden, d_mixed, d_hidden, g_feed_gain, grads, middle, feed = reach(
        feed_forward,
        [
            sds((own, D)), sds((rows, D), BF16), sds((own, D)), sds((1, D)), sds((2, SIDE, hid, LANES), BF16),
            sds((hid, rows), BF16), sds((rows, D), BF16),
        ],
        [
            pltpu.VMEM((rows, D), BF16), pltpu.VMEM((2 * hid, D), BF16), pltpu.VMEM((hid, D), BF16),
            pltpu.VMEM((hid, rows), F32), pltpu.VMEM((2 * hid, rows), BF16), pltpu.VMEM((rows, D), BF16),
            pltpu.VMEM((own, D), BF16),
        ]
        + sums_of_head()
        + sums_of_head()
        + [
            pltpu.VMEM((seq, 2, hid, LANES), BF16), pltpu.VMEM((2, SIDE, hid, LANES), BF16),
            pltpu.VMEM((2, 2, SIDE, hid, LANES), BF16), sems(2), sems(10), sems(10), sems(10), sems(10),
        ]
        + gather_scratch()
        + gather_scratch()
        + [sems(2 * SIDE * SIDE), sems(2 * SIDE * SIDE)],
        2, 63, mixed, tokens, feed_gain.reshape(1, D), cotangent, cot_rows, gu_t, down_weight,
        anywhere=(5, 6), nbytes=40_000_000,
    )
    gated_t = gated.T
    d_projected, d_tail, d_edge, d_rate, d_convw, d_decay, g_head_gain, s_down, s_out, grad_gate_up = reach(
        mixer_back,
        [
            sds((rows, heads * MIXW), BF16), sds((2 * PAD, heads * CONVW)), sds((PAD, heads * CONVW)),
            sds((rows, 2 * heads)), sds((KCONV, heads * CONVW)), sds((1, 2 * heads)), sds((1, DV)),
            sds((SIDE, hid, LANES), BF16), sds((SIDE, heads * DV, LANES), BF16), sds((2, hid, LANES)),
        ],
        [
            pltpu.VMEM((rows, heads * DV), F32), pltpu.VMEM((units, DV, DK), F32),
            pltpu.VMEM((heads, DV, DK), BF16), pltpu.VMEM((heads, DV, DK), F32),
            pltpu.VMEM((SIDE, heads, DV, DK), BF16), pltpu.VMEM((heads, DV, DK), BF16),
            pltpu.VMEM((SIDE, heads, DV, DK), BF16),
            pltpu.VMEM((PAD + rows, CONVW), F32), pltpu.VMEM((PAD + rows, CONVW), F32),
            pltpu.VMEM((units, DV, DK), F32), pltpu.VMEM((rows, DK), F32), pltpu.VMEM((rows, heads * CONVW), F32),
            pltpu.VMEM((seq, hid, LANES), BF16), pltpu.VMEM((seq, heads * DV, LANES), BF16),
            pltpu.VMEM((SIDE, hid, LANES), BF16), pltpu.VMEM((SIDE, heads * DV, LANES), BF16),
            pltpu.VMEM((2, SIDE, hid, LANES), BF16), pltpu.VMEM((2, SIDE, heads * DV, LANES), BF16),
            pltpu.VMEM((2, SIDE, hid, LANES), BF16),
            sems(SIDE), sems(SIDE), sems(SIDE), sems(SIDE), sems(2 * SIDE * SIDE), sems(2 * SIDE * SIDE),
            sems(2 * SIDE), sems(2 * SIDE),
        ],
        4, 63, info, d_mixed, out_flat, head_out, projected, gain, qe, step, ga, ta, middle, cot_rows, gated_t, grads,
        conv, dec, inv, wu, states, rate_proj, halo, convw, dlog, dbias, scalars=(0,), nbytes=40_000_000,
    )
    d_rate_low = jnp.pad(d_rate.astype(BF16), ((0, 0), (0, LANES - 2 * heads)))
    rate_pad = jnp.pad(rate_weight.reshape(D, 2 * heads), ((0, 0), (0, LANES - 2 * heads)))
    d_decay = jnp.pad(d_decay, ((0, 0), (0, LANES - 2 * heads)))
    n_gain, n_conv, n_last = D // LANES + PAD, KCONV * heads * CONVW // LANES + PAD, D // LANES
    n_y, n_z = n_gain + n_conv + SIDE * PAD, n_gain + n_conv + PAD

    def rows_of(*shape):
        return pltpu.VMEM(shape + (LANES,), F32)

    (
        layer_out, grad_tokens, grad_mixer, grad_mixer_gain, grad_feed_gain, grad_head_gain, grad_conv, grad_decay_log,
        grad_decay_bias, grad_rate, grad_down, grad_output,
    ) = reach(
        finish,
        [
            sds((own, D), BF16), sds((own, D)), sds((2, part, half)), sds((1, D)), sds((1, D)), sds((1, DV)),
            sds((KCONV, heads, CONVW)), sds((1, heads)), sds((1, heads)), sds((2, heads, LANES)), sds((hid, LANES)),
            sds((heads * DV, LANES)),
        ],
        [
            pltpu.VMEM((rows, heads * MIXW), BF16), pltpu.VMEM((D, heads * MIXW), BF16),
            pltpu.VMEM((PAD, heads * CONVW), F32), pltpu.VMEM((2, seq, part, half), BF16),
            pltpu.VMEM((2, SIDE, part, half), BF16), pltpu.VMEM((2, 2, SIDE, part, half), BF16),
            pltpu.VMEM((2, SIDE, part, half), BF16), pltpu.VMEM((2, SIDE, part, half), BF16), pltpu.VMEM((rows, D), BF16),
        ]
        + sums_of_head()
        + sums_of_head()
        + [
            pltpu.VMEM((SIDE, hid, LANES), BF16), pltpu.VMEM((SIDE, heads * DV, LANES), BF16),
            rows_of(n_gain), rows_of(n_head, n_gain), rows_of(SIDE, n_y), rows_of(SIDE, n_y), rows_of(SIDE, n_z),
            rows_of(SIDE, n_z), rows_of(n_last), rows_of(n_head, n_last), rows_of(n_last), rows_of(SIDE, n_last),
            rows_of(n_last), rows_of(SIDE, n_last),
            pltpu.SemaphoreType.DMA, pltpu.SemaphoreType.DMA, sems(2),
            sems(2 * SIDE * SIDE), sems(2 * SIDE * SIDE), sems(2 * SIDE), sems(2 * SIDE),
            sems(10), sems(10), sems(10), sems(10), sems(2 * SIDE), sems(2 * SIDE),
            pltpu.SemaphoreType.DMA((3, n_head)), pltpu.SemaphoreType.DMA((3, n_head)),
            pltpu.SemaphoreType.DMA((3, n_head)), pltpu.SemaphoreType.DMA((3, n_head)),
        ],
        5, 62, d_projected, gathered, mixer_flat, d_rate_low, rate_pad, d_tail, d_edge, feed, hidden, tokens,
        d_hidden, mixer_gain.reshape(1, D), d_convw, d_decay, g_feed_gain, g_head_gain, s_down, s_out,
        anywhere=(0, 2), nbytes=40_000_000,
    )
    results = [
        layer_out, grad_tokens, grad_mixer_gain, grad_feed_gain, grad_head_gain, grad_conv, grad_decay_log,
        grad_decay_bias, grad_rate, grad_down, grad_output, grad_gate_up, grad_mixer,
    ]
    (
        layer_out, grad_tokens, grad_mixer_gain, grad_feed_gain, grad_head_gain, grad_conv, grad_decay_log,
        grad_decay_bias, grad_rate, grad_down, grad_output, grad_gate_up, grad_mixer,
    ) = call(
        hand_over, [sds(v.shape, v.dtype) for v in results[:-1]] + [sds((part, heads, half))], [], 32, *results,
        flops=0, nbytes=6_000_000,
    )
    grad_gate_up = grad_gate_up.transpose(2, 0, 1)
    grad_output = grad_output.reshape(heads, DV, LANES)
    grad_rate = grad_rate.transpose(2, 0, 1)
    grad_mixer_gain, grad_feed_gain, grad_head_gain = (
        v.reshape(-1) for v in (grad_mixer_gain, grad_feed_gain, grad_head_gain)
    )
    grad_decay_log, grad_decay_bias = grad_decay_log.reshape(-1), grad_decay_bias.reshape(-1)
    return (
        layer_out, grad_tokens, grad_mixer_gain, grad_mixer, grad_rate, grad_conv, grad_decay_log, grad_decay_bias,
        grad_head_gain, grad_output, grad_feed_gain, grad_gate_up, grad_down,
    )


def solution(mesh):
    rows = P(("seq", "head"), None)
    return jax.shard_map(
        local,
        mesh=mesh,
        in_specs=(
            rows, P(), P(None, "head", None), P(None, None, "head"), P(None, "head", None), P("head"), P("head"),
            P(), P("head", None, None), P(), P(None, None, "head"), P("head", None), P(), rows,
        ),
        out_specs=(
            rows, rows, P(), P("seq", "head", None), P("seq", None, "head"), P(None, "head", None), P("head"),
            P("head"), P(), P("head", None, "seq"), P(), P("seq", None, "head"), P("head", "seq"),
        ),
        check_vma=False,
    )
```

```python
import functools

import jax
import jax.numpy as jnp
from jax import lax
from jax.experimental import pallas as pl
from jax.experimental.pallas import tpu as pltpu
from jax.sharding import PartitionSpec as P

D = 2048
DK = 128
DV = 256
KCONV = 4
MIXW = 768
CONVW = 512
NB = 4
BLK = 256
PAD = 8
F32 = jnp.float32
BF16 = jnp.bfloat16

VMEM = pl.BlockSpec(memory_space=pltpu.VMEM)
SMEM = pl.BlockSpec(memory_space=pltpu.SMEM)


def dot(a, b, form="nn"):
    dims = {"nn": ((1,), (0,)), "nt": ((1,), (1,)), "tn": ((0,), (0,))}[form]
    return lax.dot_general(a.astype(BF16), b.astype(BF16), (dims, ((), ())), preferred_element_type=F32)


def halves(a):
    hi = a.astype(BF16)
    return hi, (a - hi.astype(F32)).astype(BF16)


def dot3(a, b, form="nn"):
    ah, al = halves(a)
    bh, bl = halves(b)
    return dot(ah, bh, form) + (dot(ah, bl, form) + dot(al, bh, form))


def dot_exact_left(a, b, form="nn"):
    b1, rest = halves(b)
    rest = b - b1.astype(F32)
    b2 = rest.astype(BF16)
    b3 = (rest - b2.astype(F32)).astype(BF16)
    return dot(a, b1, form) + (dot(a, b2, form) + dot(a, b3, form))


def iota(shape, axis):
    return lax.broadcasted_iota(jnp.int32, shape, axis)


def doc_of(info, pos):
    count = jnp.zeros(pos.shape, jnp.int32)
    for i in range(NB):
        count = count + jnp.where(pos >= info[i], 1, 0)
    return jnp.where(pos < 0, -1, count)


def sigmoid(v):
    return 1.0 / (1.0 + jnp.exp(-v))


def softplus(v):
    return jnp.maximum(v, 0.0) + jnp.log1p(jnp.exp(-jnp.abs(v)))


def unit_lower_inverse(low):
    n = low.shape[0]
    row, col = iota((n, n), 0), iota((n, n), 1)
    eye = jnp.where(row == col, 1.0, 0.0)

    def same(b):
        return row // b == col // b

    x = jnp.where(same(8), -low, 0.0)
    inv = eye + x
    x = dot(x, x)
    inv = inv + dot(inv, x)
    x = dot(x, x)
    inv = inv + dot(inv, x)
    b = 8
    while b < n:
        off = jnp.where(same(2 * b) & jnp.logical_not(same(b)), low, 0.0)
        inv = inv - dot(inv, dot(off, inv))
        b *= 2
    return inv + dot(inv, eye - inv - dot3(low, inv))


def valid_column(info, rows, back):
    pos = info[NB] + iota((rows, 1), 0)
    return jnp.where(doc_of(info, pos) == doc_of(info, pos - back), 1.0, 0.0)


def vectors(conv):
    act = conv * sigmoid(conv)
    qa, ka, va = act[:, :DK], act[:, DK : 2 * DK], act[:, 2 * DK :]
    rq = lax.rsqrt(jnp.sum(qa * qa, axis=1, keepdims=True) + 1e-06)
    rk = lax.rsqrt(jnp.sum(ka * ka, axis=1, keepdims=True) + 1e-06)
    return qa, ka, va, rq, rk


def rates(rate_ref, dlog_ref, dbias_ref):
    heads = dlog_ref.shape[1]
    pre = rate_ref[:, :heads] + dbias_ref[...]
    log_decay = -jnp.exp(dlog_ref[...]) * softplus(pre)
    return sigmoid(rate_ref[:, heads:]), log_decay, pre


def block_masks(info, c):
    row, col = iota((BLK, BLK), 0), iota((BLK, BLK), 1)
    base = info[NB] + c * BLK
    docs_r, docs_c = doc_of(info, base + row), doc_of(info, base + col)
    keep = (docs_r == docs_c) & (col <= row)
    column = doc_of(info, base + iota((BLK, 1), 0))
    first = jnp.where(column == doc_of(info, base - 1 + iota((BLK, 1), 0) * 0), 1.0, 0.0)
    last = jnp.where(column == doc_of(info, base + BLK - 1 + iota((BLK, 1), 0) * 0), 1.0, 0.0)
    tri = jnp.where(col <= row, 1.0, 0.0)
    strict = jnp.where(col < row, 1.0, 0.0)
    return keep, first, last, tri, strict


def decays(g, first, last, tri):
    cum = dot_exact_left(tri, jnp.broadcast_to(g, (BLK, DK)))[:, :1]
    carry = first * jnp.exp(cum)
    to_end = last * jnp.exp(cum[BLK - 1 :, :] - cum)
    return carry, to_end


def mixer_forward(
    info, proj, rate, convw, dlog, dbias, out_w, gain, cot,
    conv_o, dec_o, inv_o, wu_o, qe_o, step_o, states_o, head_o, gated_o, ga_o, ta_o, halo_o, mixed_o, cot_o,
    xpad, ol, gs, scores, ab, rim, rim_got, got1, tot, got2, hs, hr, s1, r1, s2, r2, sc, rc, lc
):
    rows = proj.shape[0]
    heads = dlog.shape[1]
    blocks = rows // BLK
    me, z, y, dev = seq_place()
    seqs, head = SIDE * SIDE, lax.axis_index("head")
    before, behind = (lax.rem(me + seqs - 1, seqs), head), (lax.rem(me + 1, seqs), head)
    greet(side_peers() + [before, behind] + head_peers())
    cot_sent = gather_start(cot, cot_o, sc, rc, lc)
    for h in range(heads):
        rim[:, pl.ds(h * CONVW, CONVW)] = proj[rows - PAD :, pl.ds(h * MIXW, CONVW)].astype(BF16).astype(F32)
    ahead = cp(rim, rim_got, hs, hr, behind)
    ahead.start()
    strength, log_decay, _ = rates(rate, dlog, dbias)
    valid = [valid_column(info, rows, KCONV - 1 - j) for j in range(KCONV)]
    ahead.wait_recv()
    halo_o[...] = jnp.where(me > 0, rim_got[...], 0.0)
    for h in range(heads):
        src, dst = pl.ds(h * MIXW, CONVW), pl.ds(h * CONVW, CONVW)
        xpad[:PAD, :] = halo_o[:, dst]
        xpad[PAD:, :] = proj[:, src].astype(BF16).astype(F32)
        conv = jnp.zeros((rows, CONVW), F32)
        for j in range(KCONV):
            lo = PAD - (KCONV - 1) + j
            conv = conv + convw[j : j + 1, dst].astype(F32) * xpad[lo : lo + rows, :] * valid[j]
        conv_o[:, dst] = conv
    for c in range(blocks):
        keep, first, last, tri, strict = block_masks(info, c)
        here = pl.ds(c * BLK, BLK)
        for h in range(heads):
            qa, ka, va, rq, rk = vectors(conv_o[here, pl.ds(h * CONVW, CONVW)])
            q, k = qa * (rq * DK**-0.5), ka * rk
            beta = strength[c * BLK : (c + 1) * BLK, h : h + 1]
            g = log_decay[c * BLK : (c + 1) * BLK, h : h + 1]
            spread = dot_exact_left(tri, g * strict)
            dec = jnp.where(keep, jnp.exp(jnp.where(keep, spread, 0.0)), 0.0)
            carry, to_end = decays(g, first, last, tri)
            low = strict * (beta * dec * dot(k, k, "nt"))
            inv = unit_lower_inverse(low)
            u = h * blocks + c
            dec_o[u] = dec
            inv_o[u] = inv.astype(BF16)
            rhs = jnp.concatenate([(beta * carry) * k, beta * va], axis=1)
            wu = dot(inv, rhs)
            wu_o[u] = wu
            scores[u] = (dec * dot(q, k, "nt")).astype(BF16)
            qe_o[here, pl.ds(h * DK, DK)] = carry * q
            step = dot(wu, to_end * k, "tn")
            eye = jnp.where(iota((DK, DK), 0) == iota((DK, DK), 1), 1.0, 0.0)
            step_o[u, :DK] = carry[BLK - 1 :, :] * eye - step[:DK]
            step_o[u, DK:] = step[DK:]
        if c == 0:
            cot_sent += gather_forward(cot, cot_o, sc, rc)
    for h in range(heads):
        whole = step_o[h * blocks]
        for c in range(1, blocks):
            nxt = step_o[h * blocks + c]
            whole = add_low(dot3(whole, nxt[:DK]), nxt[DK:])
        ab[h] = whole.astype(ab.dtype)

    out, wait = share_start(ab, got1, y, lambda d: dev(0, d), s1, r1)
    for h in range(heads):
        for c in range(blocks):
            u, here = h * blocks + c, pl.ds(c * BLK, BLK)
            block = dot(scores[u], wu_o[u])
            qe_o[here, pl.ds(h * DK, DK)] = qe_o[here, pl.ds(h * DK, DK)] - block[:, :DK]
            ol[here, pl.ds(h * DV, DV)] = block[:, DK:]
    wait()
    held_before = []
    for h in range(heads):
        whole = got1[0, h].astype(F32)
        prefix = jnp.where(y > 0, whole, unit_top())
        for j in range(1, SIDE):
            a, b = got1[j, h, :DK, :], got1[j, h, DK:, :].astype(F32)
            whole = add_low(dot_left2(whole, a), b)
            if j < SIDE - 1:
                prefix = jnp.where(y > j, whole, prefix)
        tot[h] = whole.astype(BF16)
        held_before.append(prefix)
        for j in range(SIDE):
            ga_o[j, h] = got1[j, h, :DK, :]
    more, wait = share_start(tot, got2, z, lambda d: dev(d, 0), s2, r2)
    for h in range(heads):
        gate = proj[:, pl.ds(h * MIXW + CONVW, DV)]
        gs[:, pl.ds(h * DV, DV)] = gain[...] * (gate * sigmoid(gate))
    wait()
    for h in range(heads):
        held = jnp.zeros((DV, DK), F32)
        for j in range(SIDE - 1):
            held = jnp.where(
                z > j, dot_left2(held, got2[j, h, :DK, :]) + got2[j, h, DK:, :].astype(F32), held
            )
        for j in range(SIDE):
            ta_o[j, h] = got2[j, h, :DK, :]
        state = dot3(held, held_before[h][:DK]) + held_before[h][DK:]
        for c in range(blocks):
            u = h * blocks + c
            here, cols = pl.ds(c * BLK, BLK), pl.ds(h * DV, DV)
            states_o[u] = state
            block = ol[here, cols] + dot(qe_o[here, pl.ds(h * DK, DK)], state, "nt")
            head_o[here, cols] = block
            gated_o[here, cols] = (block * mean_scale(block) * gs[here, cols]).astype(BF16)
            if c + 1 < blocks:
                state = dot3(state, step_o[u, :DK, :]) + step_o[u, DK:, :]
    for j in range(0, D, CONVW):
        mixed_o[:, j : j + CONVW] = dot(gated_o[...], out_w[:, j : j + CONVW]).astype(BF16)
    gather_end(cot, cot_o, sc, rc, lc, cot_sent)
    for s in out + more + [ahead]:
        s.wait_send()


def dot_left2(a, b, form="nn"):
    ah, al = halves(a)
    return dot(ah, b, form) + dot(al, b, form)


def head_back(d_mixed, out_w, head_out, proj, gain, qe, step, d_out_o, d_gate_o, y_o, inc_o):
    rows = qe.shape[0]
    blocks = rows // BLK
    heads = qe.shape[1] // DK
    total = jnp.zeros((1, DV), F32)
    for h in range(heads):
        cols = pl.ds(h * DV, DV)
        for c in range(blocks):
            here = pl.ds(c * BLK, BLK)
            dg, out = dot(d_mixed[here, :], out_w[cols, :], "nt"), head_out[here, cols]
            gate = proj[here, pl.ds(h * MIXW + CONVW, DV)]
            s = sigmoid(gate)
            silu = gate * s
            scale = lax.rsqrt(jnp.mean(out * out, axis=1, keepdims=True) + 1e-05)
            dn = dg * (out * scale)
            d_gate_o[here, pl.ds(h * MIXW + CONVW, DV)] = (dn * gain[...] * (s * (1.0 + gate * (1.0 - s)))).astype(BF16)
            total = total + jnp.sum(dn * silu, axis=0, keepdims=True)
            f = dg * gain[...] * silu
            d_out = scale * f - out * (scale * scale * scale) * jnp.mean(f * out, axis=1, keepdims=True)
            d_out_o[here, cols] = d_out
            y_o[h * blocks + c] = dot(d_out, qe[here, pl.ds(h * DK, DK)], "tn")
        inc = y_o[h * blocks + blocks - 1]
        for c in range(blocks - 2, -1, -1):
            inc = y_o[h * blocks + c] + dot3(inc, step[h * blocks + c, :DK, :], "nt")
        inc_o[h] = inc.astype(inc_o.dtype)
    return total


def mixer_back(
    info, d_mixed, out_w, head_out, proj, gain, qe, step, ga, ta, middle, cot, gated_t, s_gu, conv, dec, inv, wu, states,
    rate, halo, convw, dlog, dbias,
    d_proj_o, d_tail_o, d_edge_o, d_rate_o, d_convw_o, d_decay_o, d_gain_o, s_down_o, s_out_o, g_gu_o,
    d_out, y, inc, later, got1, tot, got2, xpad, dpad, dsend, cols_s, d_pre_o,
    g_down, g_out, relay_d, relay_o, got_d, got_o, last_got, s1, r1, s2, r2, s3, r3, s4, r4
):
    greet(side_peers())
    settle = Settle(lambda i, b: last_got.at[i, b], s4, r4)
    for b in (2, 1, 3):
        for i in range(2):
            settle.send(s_gu.at[i, b], i, b)
    grads = (g_down, g_out)
    spread = Spread(
        lambda i, owner: grads[i].at[owner], lambda i, b: (relay_d, relay_o)[i].at[b],
        lambda i, s, b: (got_d, got_o)[i].at[s, b], s3, r3,
    )
    d_gain_o[...] = head_back(d_mixed, out_w, head_out, proj, gain, qe, step, d_out, d_proj_o, y, inc)

    def make(o, left, right):
        for j in range(0, o.shape[0], 2):
            both = dot(left[...], right[:, j * LANES : (j + 2) * LANES]).astype(BF16)
            o[j], o[j + 1] = both[:, :LANES], both[:, LANES:]

    def level_one():
        make(g_down, middle, cot)
        make(g_out, gated_t, d_mixed)

    def level_two():
        for place in PLACES:
            spread.ready(*place, (0,))

    swaps = states_backward(inc, ga, ta, later, got1, tot, got2, s1, r1, s2, r2, level_one, level_two)
    for place in PLACES:
        spread.ready(*place, (1,))
    rows = d_out.shape[0]
    heads = later.shape[0]
    blocks = rows // BLK
    strength, log_decay, pre = rates(rate, dlog, dbias)
    valid = [valid_column(info, rows, KCONV - 1 - j) for j in range(KCONV)]
    for h in range(heads):
        grad = later[h]
        for c in range(blocks - 1, -1, -1):
            u = h * blocks + c
            dsend[u] = grad
            if c:
                grad = dot3(grad, step[u, :DK, :], "nt") + y[u]
    for c in range(blocks):
        keep, first, last, tri, strict = block_masks(info, c)
        here = pl.ds(c * BLK, BLK)
        for h in range(heads):
            u = h * blocks + c
            cv = conv[here, pl.ds(h * CONVW, CONVW)]
            sg = sigmoid(cv)
            qa, ka, va, rq, rk = vectors(cv)
            rqs = rq * DK**-0.5
            q, k = qa * rqs, ka * rk
            beta = strength[c * BLK : (c + 1) * BLK, h : h + 1]
            g = log_decay[c * BLK : (c + 1) * BLK, h : h + 1]
            carry, to_end = decays(g, first, last, tri)
            dm = dec[u]
            sc = dm * dot3(q, k, "nt")
            gm = dm * dot3(k, k, "nt") * strict
            state, d_end = states[u], dsend[u]
            do = d_out[here, pl.ds(h * DV, DV)]
            ks = dot3(k, state, "nt")
            qs = dot3(q, state, "nt")
            fresh = wu[u, :, DK:] - dot3(wu[u, :, :DK], state, "nt")
            kd = to_end * k
            d_fresh = dot(sc, do, "tn") + dot(kd, d_end, "nt")
            ah, al = halves(d_fresh)
            d_rhs = dot(inv[u], ah, "tn") + dot(inv[u], al, "tn")
            d_low = -dot3(d_rhs, fresh, "nt")
            d_sc = dot3(do, fresh, "nt")
            d_val = beta * d_rhs
            ebar = d_low * gm
            d_beta = jnp.sum(d_rhs * (va - carry * ks), axis=1, keepdims=True) + jnp.sum(ebar, axis=1, keepdims=True)
            e = d_sc * sc + beta * ebar
            d_scd = d_sc * dm
            d_gm = (beta * d_low) * (dm * strict)
            d_kd = dot(fresh, d_end)
            d_q = dot(d_scd, k) + carry * dot(do, state)
            d_k = (
                dot(d_scd, q, "tn")
                - (beta * carry) * dot(d_rhs, state)
                + to_end * d_kd
                + dot(d_gm, k)
                + dot(d_gm, k, "tn")
            )
            hcol = carry * jnp.sum(do * qs - beta * d_rhs * ks, axis=1, keepdims=True)
            fcol = jnp.sum(kd * d_kd, axis=1, keepdims=True)
            tail = carry[BLK - 1 :, :] * jnp.sum(
                jnp.sum(state * d_end, axis=1, keepdims=True), axis=0, keepdims=True
            )
            lane = iota((BLK, DK), 1)
            d_g = (
                jnp.sum(dot_exact_left(tri, e, "tn") * strict, axis=1, keepdims=True)
                + dot_exact_left(tri, jnp.where(lane == 0, hcol, 0.0), "tn")[:, :1]
                + dot_exact_left(strict, jnp.where(lane == 0, fcol, 0.0))[:, :1]
                + tail
            )
            cols_s[here, h : h + 1] = d_g
            cols_s[here, heads + h : heads + h + 1] = d_beta
            d_qa = rqs * d_q - qa * (rqs * rq * rq * jnp.sum(d_q * qa, axis=1, keepdims=True))
            d_ka = rk * d_k - ka * (rk * rk * rk * jnp.sum(d_k * ka, axis=1, keepdims=True))
            d_act = jnp.concatenate([d_qa, d_ka, d_val], axis=1)
            d_pre_o[here, pl.ds(h * CONVW, CONVW)] = d_act * (sg * (1.0 + cv * (1.0 - sg)))
            spread.relays(c * heads + h)
    d_g, d_beta = cols_s[:, :heads], cols_s[:, heads : 2 * heads]
    d_bias = -d_g * jnp.exp(dlog[...]) * sigmoid(pre)
    rest = jnp.zeros((rows, LANES - 2 * heads), F32)
    d_rate_o[...] = jnp.concatenate([d_bias, d_beta * strength * (1.0 - strength), rest], axis=1).astype(BF16)
    d_decay_o[...] = jnp.zeros_like(d_decay_o)
    d_decay_o[:, :heads] = jnp.sum(d_g * log_decay, axis=0, keepdims=True)
    d_decay_o[:, heads : 2 * heads] = jnp.sum(d_bias, axis=0, keepdims=True)
    for h in range(heads):
        src, dst = pl.ds(h * MIXW, CONVW), pl.ds(h * CONVW, CONVW)
        xpad[:PAD, :] = halo[:, dst]
        xpad[PAD:, :] = proj[:, src].astype(BF16).astype(F32)
        dpad[...] = jnp.zeros_like(dpad)
        d_conv = d_pre_o[:, dst]
        for j in range(KCONV):
            lo = PAD - (KCONV - 1) + j
            masked = d_conv * valid[j]
            d_convw_o[j : j + 1, dst] = jnp.sum(masked * xpad[lo : lo + rows, :], axis=0, keepdims=True)
            dpad[lo : lo + rows, :] += convw[j : j + 1, dst].astype(F32) * masked
        d_edge_o[:, dst] = dpad[:PAD, :]
        d_tail_o[:, dst] = dpad[rows - PAD :, :]
        d_proj_o[:, src] = dpad[PAD:, :].astype(BF16)
    for i in range(2):
        g_gu_o[i] = s_gu[i, 0].astype(F32) + settle.others(i)
    for i, o in ((0, s_down_o), (1, s_out_o)):
        for b in FAR:
            o[b] = spread.total(i, b).astype(BF16)
    spread.end()
    settle.end()
    for s in swaps:
        s.wait_send()


def call(kernel, outs, scratch, limit, *args, flops=2_000_000_000, nbytes=16_000_000):
    def spec(a):
        return SMEM if a.dtype == jnp.int32 else VMEM

    return pl.pallas_call(
        kernel,
        out_shape=outs,
        in_specs=[spec(a) for a in args],
        out_specs=[VMEM for _ in outs],
        scratch_shapes=scratch,
        compiler_params=pltpu.CompilerParams(vmem_limit_bytes=limit << 20),
        cost_estimate=pl.CostEstimate(flops=flops, bytes_accessed=nbytes, transcendentals=0),
    )(*args)


def sds(shape, dtype=F32):
    return jax.ShapeDtypeStruct(shape, dtype)
CHIPS = 4
LANES = 128


def cp(src, dst, send, recv, dev):
    return pltpu.make_async_remote_copy(
        src_ref=src, dst_ref=dst, send_sem=send, recv_sem=recv, device_id=dev, device_id_type=pl.DeviceIdType.MESH
    )


def greet(devices):
    barrier = pltpu.get_barrier_semaphore()
    for dev in devices:
        pl.semaphore_signal(barrier, inc=1, device_id=dev, device_id_type=pl.DeviceIdType.MESH)
    pl.semaphore_wait(barrier, len(devices))


def head_place():
    me = lax.axis_index("head")
    chip, core = me // 2, me % 2
    seq = lax.axis_index("seq")

    def dev(step, flip=False):
        c = lax.rem(chip + step, CHIPS)
        return (seq, c * 2 + (1 - core if flip else core))

    return me, chip, core, dev


def head_peers():
    dev = head_place()[3]
    return [dev(0, True)] + [dev(d) for d in range(1, CHIPS)]


def head_rows(o, rows, step, flip=False, lo=0, size=None):
    owner = head_place()[3](step, flip)[1]
    size = size or rows
    return o.at[pl.ds(pl.multiple_of(owner * rows + lo, size), size)]


def gather_start(x, o, ssem, rsem, lsem):
    rows = x.shape[0]
    dev = head_place()[3]
    pltpu.make_async_copy(x, head_rows(o, rows, 0), lsem).start()
    out = [cp(x, head_rows(o, rows, 0), ssem.at[d], rsem.at[d], dev(d)) for d in (1, 3)]
    out.append(cp(x, head_rows(o, rows, 0), ssem.at[0], rsem.at[0], dev(0, True)))
    for s in out:
        s.start()
    return out


def opposite(rows):
    return ((0, 2, 6, 1), (rows // 2, 8, 9, 3))


def gather_forward(x, o, ssem, rsem):
    rows = x.shape[0]
    dev = head_place()[3]
    partner = dev(0, True)
    out = []

    def go(src, k, to):
        s = cp(src, src, ssem.at[k], rsem.at[k], to)
        s.start()
        out.append(s)

    for lo, relay, core, step in opposite(rows):
        there = head_rows(o, rows, CHIPS - step)
        cp(x, there, ssem.at[step], rsem.at[step], dev(step)).wait_recv()
        go(head_rows(o, rows, CHIPS - step, False, lo, rows // 2), relay, dev(step))
        go(there, CHIPS + step, partner)
    for lo, relay, core, step in opposite(rows):
        there = head_rows(o, rows, 2, False, lo, rows // 2)
        cp(there, there, ssem.at[relay], rsem.at[relay], dev(step)).wait_recv()
        go(there, core, partner)
    return out


def gather_end(x, o, ssem, rsem, lsem, sent):
    rows = x.shape[0]
    dev = head_place()[3]
    partner = dev(0, True)
    pltpu.make_async_copy(x, head_rows(o, rows, 0), lsem).wait()
    cp(x, head_rows(o, rows, 0, True), ssem.at[0], rsem.at[0], partner).wait_recv()
    for lo, relay, core, step in opposite(rows):
        k = CHIPS + step
        cp(x, head_rows(o, rows, CHIPS - step, True), ssem.at[k], rsem.at[k], partner).wait_recv()
        there = head_rows(o, rows, 2, True, lo, rows // 2)
        cp(there, there, ssem.at[core], rsem.at[core], partner).wait_recv()
    for s in sent:
        s.wait_send()


def mean_scale(v):
    return lax.rsqrt(jnp.mean(v * v, axis=1, keepdims=True) + 1e-05)


def first_norm(tokens, gain, all_o, block, ssem, rsem, lsem):
    greet(head_peers())
    v = tokens[...].astype(F32)
    block[...] = (v * mean_scale(v) * gain[...]).astype(BF16)
    sent = gather_start(block, all_o, ssem, rsem, lsem)
    sent += gather_forward(block, all_o, ssem, rsem)
    gather_end(block, all_o, ssem, rsem, lsem, sent)


def norm_back(v, gain, d_norm):
    r = mean_scale(v)
    e = d_norm * gain
    d_v = r * e - v * (r * r * r * jnp.mean(e * v, axis=1, keepdims=True))
    return d_v, jnp.sum(d_norm * v * r, axis=0, keepdims=True)


def feed_forward(
    x, tokens, gain, cot, cot_all, gu, down,
    hidden_o, all_o, d_hidden_o, d_gain_o, sums_o, middle_o, feed_o,
    n2, guv, downv, d_middle, d_gu, d_two, block, ta, pa, ga, ma, tb, pb, gb, mb, g, relay, seqs_got,
    ls, sa, ra, sb, rb, s1, r1, l1, s2, r2, l2, s3, r3
):
    load_d = pltpu.make_async_copy(down, downv, ls.at[0])
    load_d.start()
    load_g = pltpu.make_async_copy(gu, guv, ls.at[1])
    load_g.start()
    greet(head_peers() + side_peers())
    one = pair_sends(x, pa, sa, ra, FAR)
    two = ChipSum(x, one, ta, pa, ga, ma, sa, ra)
    load_d.wait()
    d_middle[...] = dot(downv[...], cot_all[...], "nt")
    two.relay()
    hidden = tokens[...].astype(F32) + two.result()
    hidden_o[...] = hidden
    block[...] = (hidden * mean_scale(hidden) * gain[...]).astype(BF16)
    ahead = gather_start(block, n2, s1, r1, l1)
    load_g.wait()
    ahead += gather_forward(block, n2, s1, r1)
    gather_end(block, n2, s1, r1, l1, ahead)
    hid = downv.shape[0]
    low = hid // 32 * 16
    for lo, hi in ((0, low), (low, hid)):
        gate = dot(guv[lo:hi, :], n2[...], "nt")
        up = dot(guv[hid + lo : hid + hi, :], n2[...], "nt")
        s = sigmoid(gate)
        silu = gate * s
        dm = d_middle[lo:hi, :]
        middle_o[lo:hi, :] = (silu * up).astype(BF16)
        d_gu[lo:hi, :] = (dm * up * (s * (1.0 + gate * (1.0 - s)))).astype(BF16)
        d_gu[hid + lo : hid + hi, :] = (dm * silu).astype(BF16)
    for j in range(0, D, 512):
        d_two[:, j : j + 512] = dot(d_gu[...], guv[:, j : j + 512], "tn").astype(BF16)
    one_b = pair_sends(d_two, pb, sb, rb, FAR)
    spread = Spread(
        lambda i, owner: g.at[owner, i], lambda i, b: relay.at[i, b], lambda i, s, b: seqs_got.at[i, s, b], s3, r3
    )
    dev = seq_place()[3]

    def make(place):
        owner = dev(*place)[0]
        cols = n2[:, pl.ds(pl.multiple_of(owner * LANES, LANES), LANES)]
        out = dot(d_gu[...], cols).astype(BF16)
        g[owner, 0] = out[:hid]
        g[owner, 1] = out[hid:]
        spread.ready(*place)

    for place in PLACES[:3]:
        make(place)
    two_b = ChipSum(d_two, one_b, tb, pb, gb, mb, sb, rb)
    for place in PLACES[3:9]:
        make(place)
    two_b.relay()
    for place in PLACES[9:]:
        make(place)
    d_norm, d_gain = norm_back(hidden_o[...], gain[...], two_b.result())
    d_hidden = cot[...].astype(F32) + d_norm
    d_hidden_o[...] = d_hidden
    d_gain_o[...] = d_gain
    block[...] = d_hidden.astype(BF16)
    ahead = gather_start(block, all_o, s2, r2, l2)
    spread.relays()
    for j in range(0, D, 512):
        feed_o[:, j : j + 512] = dot(middle_o[...], downv[:, j : j + 512], "tn").astype(BF16)
    ahead += gather_forward(block, all_o, s2, r2)
    for b in FAR:
        for i in range(2):
            sums_o[i, b] = spread.total(i, b).astype(BF16)
    gather_end(block, all_o, s2, r2, l2, ahead)
    spread.end()
    two.end()
    two_b.end()


def reach(kernel, outs, scratch, cid, limit, *args, anywhere=(), scalars=(), nbytes=12_000_000):
    return pl.pallas_call(
        kernel,
        out_shape=outs,
        in_specs=[
            pl.BlockSpec(memory_space=pl.ANY) if i in anywhere else SMEM if i in scalars else VMEM for i in range(len(args))
        ],
        out_specs=[VMEM for _ in outs],
        scratch_shapes=scratch,
        compiler_params=pltpu.CompilerParams(
            collective_id=cid, has_side_effects=True, vmem_limit_bytes=limit << 20
        ),
        cost_estimate=pl.CostEstimate(flops=0, bytes_accessed=nbytes, transcendentals=0),
    )(*args)


def sems(n):
    return pltpu.SemaphoreType.DMA((n,))


def gather_scratch():
    return [sems(10), sems(10), pltpu.SemaphoreType.DMA]


SIDE = 4


def seq_place():
    me = lax.axis_index("seq")
    z, y = me // SIDE, me % SIDE
    head = lax.axis_index("head")

    def dev(dz, dy):
        return (lax.rem(z + dz, SIDE) * SIDE + lax.rem(y + dy, SIDE), head)

    return me, z, y, dev


def side_peers():
    dev = seq_place()[3]
    return [dev(0, d) for d in range(1, SIDE)] + [dev(d, 0) for d in range(1, SIDE)]


FAR = (2, 1, 3, 0)
FIRST, OTHER = (2, 1), (3, 0)
PLACES = (
    (2, 2), (2, 1), (1, 2), (2, 3), (3, 2), (2, 0), (0, 2), (1, 3), (3, 1), (1, 0), (0, 1), (3, 3), (1, 1), (0, 3), (3, 0),
    (0, 0),
)


class Spread:
    def __init__(self, piece, relay, got, ssem, rsem):
        self.piece, self.relay, self.got, self.ssem, self.rsem = piece, relay, got, ssem, rsem
        self.dev = seq_place()[3]
        self.sent = []

    def way(self, i, a, b):
        return self.dev(b, a) if i == 0 else self.dev(a, b)

    def copy(self, i, a, b, owner):
        k = (i * SIDE + a) * SIDE + b
        if a == 2:
            dst, step = self.relay(i, b), 1 if b in FIRST else 3
        else:
            dst, step = self.got(i, 0 if a == 1 else 1, b), a
        return cp(self.piece(i, owner), dst, self.ssem.at[k], self.rsem.at[k], self.way(i, step, 0))

    def send(self, i, a, b, owner):
        s = self.copy(i, a, b, owner)
        s.start()
        self.sent.append(s)

    def late(self, a, b):
        return a == 1 and b in FIRST or a == 3 and b in OTHER

    def ready(self, dz, dy, halves_=(0, 1)):
        owner = self.dev(dz, dy)[0]
        for i in halves_:
            a, b = (dy, dz) if i == 0 else (dz, dy)
            if a and not self.late(a, b):
                self.send(i, a, b, owner)

    def relays(self, part=None):
        for n, b in enumerate(FAR):
            if part is not None and n != part:
                continue
            for i in range(2):
                a = 1 if b in FIRST else 3
                owner = self.way(i, a, b)[0]
                self.copy(i, 2, b, owner).wait_recv()
                both = self.piece(i, owner)[...].astype(F32) + self.relay(i, b)[...].astype(F32)
                self.relay(i, b)[...] = both.astype(BF16)
                k = (i * SIDE + a) * SIDE + b
                s = cp(
                    self.relay(i, b), self.got(i, 0 if a == 1 else 1, b), self.ssem.at[k], self.rsem.at[k],
                    self.way(i, a, 0),
                )
                s.start()
                self.sent.append(s)

    def total(self, i, b):
        owner = self.way(i, 0, b)[0]
        for a in (1, 3):
            self.copy(i, a, b, owner).wait_recv()
        return self.piece(i, owner)[...].astype(F32) + (
            self.got(i, 0, b)[...].astype(F32) + self.got(i, 1, b)[...].astype(F32)
        )

    def end(self):
        for s in self.sent:
            s.wait_send()


class Settle:
    def __init__(self, got, ssem, rsem):
        self.got, self.ssem, self.rsem = got, ssem, rsem
        self.dev = seq_place()[3]
        self.sent = {}

    def send(self, src, i, b):
        k = i * SIDE + b
        dev = self.dev(b, 0) if i == 0 else self.dev(0, b)
        self.sent[i, b] = cp(src, self.got(i, b), self.ssem.at[k], self.rsem.at[k], dev)
        self.sent[i, b].start()

    def others(self, i):
        for b in (1, 3, 2):
            self.sent[i, b].wait_recv()
        return (self.got(i, 1)[...].astype(F32) + self.got(i, 3)[...].astype(F32)) + self.got(i, 2)[...].astype(F32)

    def end(self):
        for s in self.sent.values():
            s.wait_send()


def share_start(src, got, place, to, ssem, rsem, size=SIDE, own=None):
    part = (lambda d: src) if own is None else (lambda d: src.at[lax.rem(place + d, size)])
    got[place] = src[...] if own is None else src[place]
    steps = (2, 1, 3) if size == SIDE else range(1, size)
    out = [cp(part(d), got.at[place], ssem.at[d], rsem.at[d], to(d)) for d in steps]
    for s in out:
        s.start()

    def wait():
        for d in steps:
            back = lax.rem(place + size - d, size)
            cp(part(d), got.at[back], ssem.at[d], rsem.at[d], to(d)).wait_recv()

    return out, wait


def in_order(got):
    total = got[0]
    for i in range(1, got.shape[0]):
        total = total + got[i]
    return total


def share(src, got, place, to, ssem, rsem):
    out, wait = share_start(src, got, place, to, ssem, rsem)
    wait()
    return out


def unit_top():
    return jnp.where(iota((DK + DV, DK), 0) == iota((DK + DV, DK), 1), 1.0, 0.0)


def add_low(pair, low):
    return jnp.concatenate([pair[:DK], pair[DK:] + low], axis=0)


def states_backward(inc, ga, ta, later_o, got1, tot, got2, s1, r1, s2, r2, level_one, level_two):
    me, z, y, dev = seq_place()
    heads = inc.shape[0]
    out, wait = share_start(inc, got1, y, lambda d: dev(0, d), s1, r1)
    level_one()
    wait()
    after = []
    for h in range(heads):
        whole = add_low(dot(unit_top(), ga[SIDE - 1, h], "nt"), got1[SIDE - 1, h].astype(F32))
        suffix = jnp.where(y < SIDE - 1, whole, unit_top())
        for j in range(SIDE - 2, -1, -1):
            whole = add_low(dot_left2(whole, ga[j, h], "nt"), got1[j, h].astype(F32))
            if j:
                suffix = jnp.where(y < j, whole, suffix)
        tot[h] = whole[DK:].astype(BF16)
        after.append(suffix)
    more, wait = share_start(tot, got2, z, lambda d: dev(d, 0), s2, r2)
    level_two()
    wait()
    for h in range(heads):
        held = jnp.zeros((DV, DK), F32)
        for j in range(SIDE - 1, 0, -1):
            held = jnp.where(z < j, dot_left2(held, ta[j, h], "nt") + got2[j, h].astype(F32), held)
        later_o[h] = dot3(held, after[h][:DK]) + after[h][DK:]
    return out + more


def pair_sends(x, pair, ssem, rsem, steps):
    rows = pair.shape[1]
    dev = head_place()[3]
    out = {}
    for d in steps:
        owner = dev(d, True)[1]
        src = x.at[pl.ds(pl.multiple_of(owner * rows, rows), rows)]
        out[d] = cp(src, pair.at[d], ssem.at[d], rsem.at[d], dev(0, True))
        out[d].start()
    return out


class ChipSum:
    def __init__(self, x, first, total, pair, got, mid, ssem, rsem):
        self.x, self.first, self.total, self.pair = x, first, total, pair
        self.got, self.mid, self.ssem, self.rsem = got, mid, ssem, rsem
        self.rows = pair.shape[1]
        self.dev = head_place()[3]
        half = self.rows // 2
        self.top, self.low = slice(0, half), slice(half, self.rows)
        self.sent = []
        self.mid[2] = self.both(2).astype(BF16)
        self.send(2, self.top, 0, 4, 1)
        self.send(2, self.low, 0, 5, 3)
        self.right = self.both(1)
        self.mid[1, self.low] = self.right[self.low].astype(BF16)
        self.send(1, self.low, 1, 6, 1)
        self.left = self.both(3)
        self.mid[3, self.top] = self.left[self.top].astype(BF16)
        self.send(3, self.top, 3, 7, 3)
        self.total[...] = self.both(0)

    def both(self, d):
        self.first[d].wait_recv()
        owner = self.dev(d)[1]
        mine = self.x[pl.ds(pl.multiple_of(owner * self.rows, self.rows), self.rows), :]
        return mine.astype(F32) + self.pair[d].astype(F32)

    def copy(self, d, part, slot, k, step):
        at = pl.ds(part.start, part.stop - part.start)
        return cp(self.mid.at[d, at], self.got.at[slot, at], self.ssem.at[k], self.rsem.at[k], self.dev(step))

    def send(self, *what):
        s = self.copy(*what)
        s.start()
        self.sent.append(s)

    def relay(self):
        self.copy(2, self.top, 0, 4, 1).wait_recv()
        self.mid[1, self.top] = (self.right[self.top] + self.got[0, self.top].astype(F32)).astype(BF16)
        self.send(1, self.top, 1, 8, 1)
        self.copy(2, self.low, 0, 5, 3).wait_recv()
        self.mid[3, self.low] = (self.left[self.low] + self.got[0, self.low].astype(F32)).astype(BF16)
        self.send(3, self.low, 3, 9, 3)

    def result(self):
        self.copy(1, self.low, 1, 6, 1).wait_recv()
        self.copy(3, self.top, 3, 7, 3).wait_recv()
        self.copy(1, self.top, 1, 8, 1).wait_recv()
        self.copy(3, self.low, 3, 9, 3).wait_recv()
        return self.total[...] + (self.got[1].astype(F32) + self.got[3].astype(F32))

    def end(self):
        for s in self.sent + list(self.first.values()):
            s.wait_send()


def finish(
    dproj, normed, w, d_rate, rate_w, d_tail, d_edge, feed, hidden, tokens, d_hidden, gain, convs, decay, g_feed, g_head,
    s_down, s_out,
    layer_o, d_tokens_o, g_mixer_o, g_gain_o, g_feed_o, g_head_o, conv_o, dlog_o, dbias_o, rate_o, g_down_o, g_out_o,
    dp, wv, edge, g, relay, got1, mid, got2, dn, ta, pa, ga, ma, tb, pb, gb, mb, got_d, got_o,
    e0, eh, e1, ey, e2, ez, m0, mh, m1, my, m2, mz,
    es, er, ls, s1, r1, s2, r2, sa, ra, sb, rb, s5, r5, se, re, sm, rm
):
    me, z, y, dev = seq_place()
    head = lax.axis_index("head")
    heads, seqs = eh.shape[0], g.shape[1]
    rows = dp.shape[0]
    part, half = g_mixer_o.shape[1], g_mixer_o.shape[2]
    load_p = pltpu.make_async_copy(dproj, dp, ls.at[0])
    load_p.start()
    load_w = pltpu.make_async_copy(w, wv, ls.at[1])
    load_w.start()

    def across(d):
        return (me, lax.rem(head + d, heads))

    before, behind = (lax.rem(me + seqs - 1, seqs), head), (lax.rem(me + 1, seqs), head)
    greet([across(d) for d in range(1, heads)] + side_peers() + [before, behind])
    back = cp(d_edge, edge, es, er, before)
    back.start()
    feed_one = pair_sends(feed, pa, sa, ra, FAR)

    n_row, h_row = D // LANES, DV // LANES
    taps, wide_c = convs.shape
    c_row = wide_c // LANES
    ng, nc = e0.shape[0], taps * c_row + PAD
    for r in range(n_row):
        e0[r : r + 1, :] = g_feed[:, r * LANES : (r + 1) * LANES]
    e0[n_row:, :] = jnp.zeros((ng - n_row, LANES), F32)
    for r in range(h_row):
        e0[n_row + r : n_row + r + 1, :] = g_head[:, r * LANES : (r + 1) * LANES]
    small, wait_head = share_start(e0, eh, head, across, se.at[0], re.at[0], heads)
    for t in range(taps):
        for r in range(c_row):
            lo = ng + t * c_row + r
            e1[0, lo : lo + 1, :] = convs[t : t + 1, r * LANES : (r + 1) * LANES]
    e1[0, ng + nc - PAD : ng + nc, :] = jnp.zeros((PAD, LANES), F32)
    e1[0, ng + nc - PAD : ng + nc - PAD + 1, :] = decay[...]
    rates_t = dot(d_rate[:, :PAD], normed[...], "tn")
    for i in range(SIDE):
        if i:
            e1[i, ng : ng + nc, :] = e1[0, ng : ng + nc, :]
        for j in range(SIDE):
            at = (j * SIDE + i) * LANES
            e1[i, ng + nc + j * PAD : ng + nc + (j + 1) * PAD, :] = rates_t[:, at : at + LANES]

    sums = (s_down, s_out)
    settle = Settle(lambda i, b: (got_d, got_o)[i].at[b], s5, r5)
    for b in (2, 1, 3):
        for i in range(2):
            settle.send(sums[i].at[b], i, b)
    load_p.wait()
    back.wait_recv()
    there = jnp.where(me < seqs - 1, edge[...], 0.0)
    tail = jnp.concatenate([d_tail[:PAD, :], d_tail[PAD:, :] + there], axis=0).astype(BF16)
    wide = half - DV
    for i in range(2):
        dp[rows - 2 * PAD :, pl.ds(i * half, wide)] = tail[:, i * wide : (i + 1) * wide]

    spread = Spread(
        lambda i, owner: g.at[i, owner], lambda i, b: relay.at[i, b], lambda i, s, b: got1.at[i, s, b], s1, r1
    )
    settle_two = Settle(lambda i, b: got2.at[i, b], s2, r2)
    for n, place in enumerate(PLACES):
        owner = dev(*place)[0]
        left = normed[:, pl.ds(pl.multiple_of(owner * part, part), part)]
        both = dot(left, dp[...], "tn").astype(BF16)
        for i in range(2):
            g[i, owner] = both[:, i * half : (i + 1) * half]
        spread.ready(*place)
        if n == 2:
            wait_head()
            gains = in_order(eh)
            for i in range(SIDE):
                e1[i, :ng, :] = gains
            more, wait_y = share_start(e1, ey, y, lambda d: dev(0, d), se.at[1], re.at[1], SIDE, True)
            small += more
        if n == 9:
            wait_y()
            total = in_order(ey)
            for j in range(SIDE):
                e2[j, : ng + nc, :] = total[: ng + nc]
                e2[j, ng + nc :, :] = total[ng + nc + j * PAD : ng + nc + (j + 1) * PAD]
            more, wait_z = share_start(e2, ez, z, lambda d: dev(d, 0), se.at[2], re.at[2], SIDE, True)
            small += more
    feed_two = ChipSum(feed, feed_one, ta, pa, ga, ma, sa, ra)

    load_w.wait()
    low = rows // CHIPS
    hp = head_place()[3]
    dn_one = {}
    for d in FAR:
        chip = hp(d)[1] // 2
        here = pl.ds(pl.multiple_of(chip * low, low), low)
        dn[here, :] = (dot(dp[here, :], wv[...], "nt") + dot(d_rate[here, :], rate_w[...], "nt")).astype(BF16)
        dn_one.update(pair_sends(dn, pb, sb, rb, (d,)))
        spread.relays(FAR.index(d))
    feed_two.relay()
    dn_two = ChipSum(dn, dn_one, tb, pb, gb, mb, sb, rb)
    wait_z()
    total = in_order(ez)
    for r in range(n_row):
        g_feed_o[:, r * LANES : (r + 1) * LANES] = total[r : r + 1]
    for r in range(h_row):
        g_head_o[:, r * LANES : (r + 1) * LANES] = total[n_row + r : n_row + r + 1]
    own = conv_o.shape[1]
    for t in range(taps):
        for h in range(own):
            for r in range(c_row // own):
                lo = ng + t * c_row + h * (c_row // own) + r
                conv_o[t, h : h + 1, r * LANES : (r + 1) * LANES] = total[lo : lo + 1]
    dlog_o[...] = total[ng + nc - PAD : ng + nc - PAD + 1, :own]
    dbias_o[...] = total[ng + nc - PAD : ng + nc - PAD + 1, own : 2 * own]
    for i in range(2):
        rate_o[i] = total[ng + nc + i * own : ng + nc + (i + 1) * own]
    dn_two.relay()
    layer_o[...] = (hidden[...] + feed_two.result()).astype(BF16)
    d_norm, d_gain = norm_back(tokens[...].astype(F32), gain[...], dn_two.result())
    d_tokens_o[...] = d_hidden[...] + d_norm

    for r in range(n_row):
        m0[r : r + 1, :] = d_gain[:, r * LANES : (r + 1) * LANES]
    more, wait_head = share_start(m0, mh, head, across, sm.at[0], rm.at[0], heads)
    small += more

    def settle_mixer(b):
        for i in range(2):
            both = spread.total(i, b)
            if b:
                mid[i, b] = both.astype(BF16)
                settle_two.send(mid.at[i, b], i, b)
            else:
                g_mixer_o[i] = both

    settle_mixer(2)
    wait_head()
    m1[...] = in_order(mh)
    more, wait_y = share_start(m1, my, y, lambda d: dev(0, d), sm.at[1], rm.at[1])
    small += more
    settle_mixer(1)
    settle_mixer(3)
    wait_y()
    m2[...] = in_order(my)
    more, wait_z = share_start(m2, mz, z, lambda d: dev(d, 0), sm.at[2], rm.at[2])
    small += more
    settle_mixer(0)
    for i, o in ((0, g_down_o), (1, g_out_o)):
        o[...] = sums[i][0].astype(F32) + settle.others(i)
    wait_z()
    total = in_order(mz)
    for r in range(n_row):
        g_gain_o[:, r * LANES : (r + 1) * LANES] = total[r : r + 1]
    for i in range(2):
        g_mixer_o[i] = g_mixer_o[i] + settle_two.others(i)
    spread.end()
    settle.end()
    settle_two.end()
    feed_two.end()
    dn_two.end()
    for s in small + [back]:
        s.wait_send()


def hand_over(*refs):
    n = (len(refs) - 2) // 2
    srcs, dsts, (held, done) = refs[:n], refs[n : 2 * n], refs[2 * n :]
    copies = [
        pltpu.make_async_copy(srcs[i], dsts[i] if i < n - 1 else held, done.at[i]) for i in range(n - 1, -1, -1)
    ]
    for s in copies:
        s.start()
    copies[0].wait()
    for i in range(held.shape[0]):
        dsts[-1][:, i, :] = held[i]
    for s in copies[1:]:
        s.wait()


def local(
    tokens, mixer_gain, mixer_weight, rate_weight, conv_weight, decay_log, decay_bias, head_gain,
    output_weight, feed_gain, gate_up_weight, down_weight, doc_starts, cotangent,
):
    own = tokens.shape[0]
    (gathered,) = reach(
        first_norm,
        [sds((own * lax.axis_size("head"), D), BF16)],
        [pltpu.VMEM((own, D), BF16)] + gather_scratch(),
        3, 32, tokens, mixer_gain.reshape(1, D),
    )
    heads = mixer_weight.shape[1]
    mixer_flat = mixer_weight.reshape(D, heads * MIXW)
    rows = gathered.shape[0]
    blocks = rows // BLK
    units = heads * blocks
    seq = lax.axis_size("seq")
    projected = jnp.dot(gathered, mixer_flat, preferred_element_type=F32)
    rate_proj = jnp.einsum("td,dgh->tgh", gathered, rate_weight, preferred_element_type=F32).reshape(rows, 2 * heads)
    convw = conv_weight.reshape(KCONV, heads * CONVW)
    info = jnp.concatenate(
        [doc_starts, jnp.stack([lax.axis_index("seq") * rows, lax.axis_index("seq")]).astype(jnp.int32)]
    )
    dlog, dbias = decay_log.reshape(1, heads), decay_bias.reshape(1, heads)
    gain = head_gain.reshape(1, DV)

    out_flat = output_weight.reshape(heads * DV, D)
    pairs = pltpu.VMEM((SIDE, heads, DK + DV, DK), BF16)
    conv, dec, inv, wu, qe, step, states, head_out, gated, ga, ta, halo, mixed, cot_rows = reach(
        mixer_forward,
        [
            sds((rows, heads * CONVW)), sds((units, BLK, BLK)), sds((units, BLK, BLK), BF16),
            sds((units, BLK, DK + DV)), sds((rows, heads * DK)), sds((units, DK + DV, DK)), sds((units, DV, DK)),
            sds((rows, heads * DV)), sds((rows, heads * DV), BF16), sds((SIDE, heads, DK, DK), BF16),
            sds((SIDE, heads, DK, DK), BF16), sds((PAD, heads * CONVW)), sds((rows, D), BF16), sds((rows, D), BF16),
        ],
        [
            pltpu.VMEM((PAD + rows, CONVW), F32), pltpu.VMEM((rows, heads * DV), F32),
            pltpu.VMEM((rows, heads * DV), F32), pltpu.VMEM((units, BLK, BLK), BF16),
            pltpu.VMEM((heads, DK + DV, DK), BF16), pltpu.VMEM((PAD, heads * CONVW), F32),
            pltpu.VMEM((PAD, heads * CONVW), F32), pairs, pltpu.VMEM((heads, DK + DV, DK), BF16), pairs,
            pltpu.SemaphoreType.DMA, pltpu.SemaphoreType.DMA, sems(SIDE), sems(SIDE), sems(SIDE), sems(SIDE),
        ]
        + gather_scratch(),
        1, 56, info, projected, rate_proj, convw, dlog, dbias, out_flat, gain, cotangent, scalars=(0,), nbytes=30_000_000,
    )
    hid = down_weight.shape[0]
    part, half, n_head = D // seq, MIXW, lax.axis_size("head")
    gu_t = gate_up_weight.transpose(1, 2, 0).reshape(2 * hid, D)

    def sums_of_head():
        return [pltpu.VMEM((own, D), F32)] + [pltpu.VMEM((CHIPS, own, D), BF16) for _ in range(3)]

    hidden, d_mixed, d_hidden, g_feed_gain, grads, middle, feed = reach(
        feed_forward,
        [
            sds((own, D)), sds((rows, D), BF16), sds((own, D)), sds((1, D)), sds((2, SIDE, hid, LANES), BF16),
            sds((hid, rows), BF16), sds((rows, D), BF16),
        ],
        [
            pltpu.VMEM((rows, D), BF16), pltpu.VMEM((2 * hid, D), BF16), pltpu.VMEM((hid, D), BF16),
            pltpu.VMEM((hid, rows), F32), pltpu.VMEM((2 * hid, rows), BF16), pltpu.VMEM((rows, D), BF16),
            pltpu.VMEM((own, D), BF16),
        ]
        + sums_of_head()
        + sums_of_head()
        + [
            pltpu.VMEM((seq, 2, hid, LANES), BF16), pltpu.VMEM((2, SIDE, hid, LANES), BF16),
            pltpu.VMEM((2, 2, SIDE, hid, LANES), BF16), sems(2), sems(10), sems(10), sems(10), sems(10),
        ]
        + gather_scratch()
        + gather_scratch()
        + [sems(2 * SIDE * SIDE), sems(2 * SIDE * SIDE)],
        2, 63, mixed, tokens, feed_gain.reshape(1, D), cotangent, cot_rows, gu_t, down_weight,
        anywhere=(5, 6), nbytes=40_000_000,
    )
    gated_t = gated.T
    d_projected, d_tail, d_edge, d_rate, d_convw, d_decay, g_head_gain, s_down, s_out, grad_gate_up = reach(
        mixer_back,
        [
            sds((rows, heads * MIXW), BF16), sds((2 * PAD, heads * CONVW)), sds((PAD, heads * CONVW)),
            sds((rows, LANES), BF16), sds((KCONV, heads * CONVW)), sds((1, LANES)), sds((1, DV)),
            sds((SIDE, hid, LANES), BF16), sds((SIDE, heads * DV, LANES), BF16), sds((2, hid, LANES)),
        ],
        [
            pltpu.VMEM((rows, heads * DV), F32), pltpu.VMEM((units, DV, DK), F32),
            pltpu.VMEM((heads, DV, DK), BF16), pltpu.VMEM((heads, DV, DK), F32),
            pltpu.VMEM((SIDE, heads, DV, DK), BF16), pltpu.VMEM((heads, DV, DK), BF16),
            pltpu.VMEM((SIDE, heads, DV, DK), BF16),
            pltpu.VMEM((PAD + rows, CONVW), F32), pltpu.VMEM((PAD + rows, CONVW), F32),
            pltpu.VMEM((units, DV, DK), F32), pltpu.VMEM((rows, DK), F32), pltpu.VMEM((rows, heads * CONVW), F32),
            pltpu.VMEM((seq, hid, LANES), BF16), pltpu.VMEM((seq, heads * DV, LANES), BF16),
            pltpu.VMEM((SIDE, hid, LANES), BF16), pltpu.VMEM((SIDE, heads * DV, LANES), BF16),
            pltpu.VMEM((2, SIDE, hid, LANES), BF16), pltpu.VMEM((2, SIDE, heads * DV, LANES), BF16),
            pltpu.VMEM((2, SIDE, hid, LANES), BF16),
            sems(SIDE), sems(SIDE), sems(SIDE), sems(SIDE), sems(2 * SIDE * SIDE), sems(2 * SIDE * SIDE),
            sems(2 * SIDE), sems(2 * SIDE),
        ],
        4, 63, info, d_mixed, out_flat, head_out, projected, gain, qe, step, ga, ta, middle, cot_rows, gated_t, grads,
        conv, dec, inv, wu, states, rate_proj, halo, convw, dlog, dbias, scalars=(0,), nbytes=40_000_000,
    )
    rate_pad = jnp.pad(rate_weight.reshape(D, 2 * heads), ((0, 0), (0, LANES - 2 * heads)))
    n_gain, n_conv, n_last = D // LANES + PAD, KCONV * heads * CONVW // LANES + PAD, D // LANES
    n_y, n_z = n_gain + n_conv + SIDE * PAD, n_gain + n_conv + PAD

    def rows_of(*shape):
        return pltpu.VMEM(shape + (LANES,), F32)

    (
        layer_out, grad_tokens, grad_mixer, grad_mixer_gain, grad_feed_gain, grad_head_gain, grad_conv, grad_decay_log,
        grad_decay_bias, grad_rate, grad_down, grad_output,
    ) = reach(
        finish,
        [
            sds((own, D), BF16), sds((own, D)), sds((2, part, half)), sds((1, D)), sds((1, D)), sds((1, DV)),
            sds((KCONV, heads, CONVW)), sds((1, heads)), sds((1, heads)), sds((2, heads, LANES)), sds((hid, LANES)),
            sds((heads * DV, LANES)),
        ],
        [
            pltpu.VMEM((rows, heads * MIXW), BF16), pltpu.VMEM((D, heads * MIXW), BF16),
            pltpu.VMEM((PAD, heads * CONVW), F32), pltpu.VMEM((2, seq, part, half), BF16),
            pltpu.VMEM((2, SIDE, part, half), BF16), pltpu.VMEM((2, 2, SIDE, part, half), BF16),
            pltpu.VMEM((2, SIDE, part, half), BF16), pltpu.VMEM((2, SIDE, part, half), BF16), pltpu.VMEM((rows, D), BF16),
        ]
        + sums_of_head()
        + sums_of_head()
        + [
            pltpu.VMEM((SIDE, hid, LANES), BF16), pltpu.VMEM((SIDE, heads * DV, LANES), BF16),
            rows_of(n_gain), rows_of(n_head, n_gain), rows_of(SIDE, n_y), rows_of(SIDE, n_y), rows_of(SIDE, n_z),
            rows_of(SIDE, n_z), rows_of(n_last), rows_of(n_head, n_last), rows_of(n_last), rows_of(SIDE, n_last),
            rows_of(n_last), rows_of(SIDE, n_last),
            pltpu.SemaphoreType.DMA, pltpu.SemaphoreType.DMA, sems(2),
            sems(2 * SIDE * SIDE), sems(2 * SIDE * SIDE), sems(2 * SIDE), sems(2 * SIDE),
            sems(10), sems(10), sems(10), sems(10), sems(2 * SIDE), sems(2 * SIDE),
            pltpu.SemaphoreType.DMA((3, n_head)), pltpu.SemaphoreType.DMA((3, n_head)),
            pltpu.SemaphoreType.DMA((3, n_head)), pltpu.SemaphoreType.DMA((3, n_head)),
        ],
        5, 62, d_projected, gathered, mixer_flat, d_rate, rate_pad, d_tail, d_edge, feed, hidden, tokens,
        d_hidden, mixer_gain.reshape(1, D), d_convw, d_decay, g_feed_gain, g_head_gain, s_down, s_out,
        anywhere=(0, 2), nbytes=40_000_000,
    )
    results = [
        layer_out, grad_tokens, grad_mixer_gain, grad_feed_gain, grad_head_gain, grad_conv, grad_decay_log,
        grad_decay_bias, grad_rate, grad_down, grad_output, grad_gate_up, grad_mixer,
    ]
    (
        layer_out, grad_tokens, grad_mixer_gain, grad_feed_gain, grad_head_gain, grad_conv, grad_decay_log,
        grad_decay_bias, grad_rate, grad_down, grad_output, grad_gate_up, grad_mixer,
    ) = pl.pallas_call(
        hand_over,
        out_shape=[sds(v.shape, v.dtype) for v in results[:-1]] + [sds((part, heads, half))],
        in_specs=[pl.BlockSpec(memory_space=pl.ANY) for _ in results],
        out_specs=[pl.BlockSpec(memory_space=pl.ANY) for _ in results[:-1]] + [VMEM],
        scratch_shapes=[pltpu.VMEM((heads, part, half), F32), sems(len(results))],
        compiler_params=pltpu.CompilerParams(vmem_limit_bytes=60 << 20),
        cost_estimate=pl.CostEstimate(flops=0, bytes_accessed=6_000_000, transcendentals=0),
    )(*results)
    grad_gate_up = grad_gate_up.transpose(2, 0, 1)
    grad_output = grad_output.reshape(heads, DV, LANES)
    grad_rate = grad_rate.transpose(2, 0, 1)
    grad_mixer_gain, grad_feed_gain, grad_head_gain = (
        v.reshape(-1) for v in (grad_mixer_gain, grad_feed_gain, grad_head_gain)
    )
    grad_decay_log, grad_decay_bias = grad_decay_log.reshape(-1), grad_decay_bias.reshape(-1)
    return (
        layer_out, grad_tokens, grad_mixer_gain, grad_mixer, grad_rate, grad_conv, grad_decay_log, grad_decay_bias,
        grad_head_gain, grad_output, grad_feed_gain, grad_gate_up, grad_down,
    )


def solution(mesh):
    rows = P(("seq", "head"), None)
    return jax.shard_map(
        local,
        mesh=mesh,
        in_specs=(
            rows, P(), P(None, "head", None), P(None, None, "head"), P(None, "head", None), P("head"), P("head"),
            P(), P("head", None, None), P(), P(None, None, "head"), P("head", None), P(), rows,
        ),
        out_specs=(
            rows, rows, P(), P("seq", "head", None), P("seq", None, "head"), P(None, "head", None), P("head"),
            P("head"), P(), P("head", None, "seq"), P(), P("seq", None, "head"), P("head", "seq"),
        ),
        check_vma=False,
    )
```

```python
import functools

import jax
import jax.numpy as jnp
from jax import lax
from jax.experimental import pallas as pl
from jax.experimental.pallas import tpu as pltpu
from jax.sharding import PartitionSpec as P

D = 2048
DK = 128
DV = 256
KCONV = 4
MIXW = 768
CONVW = 512
NB = 4
BLK = 256
PAD = 8
F32 = jnp.float32
BF16 = jnp.bfloat16

VMEM = pl.BlockSpec(memory_space=pltpu.VMEM)
SMEM = pl.BlockSpec(memory_space=pltpu.SMEM)


def dot(a, b, form="nn"):
    dims = {"nn": ((1,), (0,)), "nt": ((1,), (1,)), "tn": ((0,), (0,))}[form]
    return lax.dot_general(a.astype(BF16), b.astype(BF16), (dims, ((), ())), preferred_element_type=F32)


def halves(a):
    hi = a.astype(BF16)
    return hi, (a - hi.astype(F32)).astype(BF16)


def dot3(a, b, form="nn"):
    ah, al = halves(a)
    bh, bl = halves(b)
    return dot(ah, bh, form) + (dot(ah, bl, form) + dot(al, bh, form))


def dot_exact_left(a, b, form="nn"):
    b1, rest = halves(b)
    rest = b - b1.astype(F32)
    b2 = rest.astype(BF16)
    b3 = (rest - b2.astype(F32)).astype(BF16)
    return dot(a, b1, form) + (dot(a, b2, form) + dot(a, b3, form))


def iota(shape, axis):
    return lax.broadcasted_iota(jnp.int32, shape, axis)


def doc_of(info, pos):
    count = jnp.zeros(pos.shape, jnp.int32)
    for i in range(NB):
        count = count + jnp.where(pos >= info[i], 1, 0)
    return jnp.where(pos < 0, -1, count)


def sigmoid(v):
    return 1.0 / (1.0 + jnp.exp(-v))


def softplus(v):
    return jnp.maximum(v, 0.0) + jnp.log1p(jnp.exp(-jnp.abs(v)))


def unit_lower_inverse(low):
    n = low.shape[0]
    row, col = iota((n, n), 0), iota((n, n), 1)
    eye = jnp.where(row == col, 1.0, 0.0)

    def same(b):
        return row // b == col // b

    x = jnp.where(same(8), -low, 0.0)
    inv = eye + x
    x = dot(x, x)
    inv = inv + dot(inv, x)
    x = dot(x, x)
    inv = inv + dot(inv, x)
    b = 8
    while b < n:
        off = jnp.where(same(2 * b) & jnp.logical_not(same(b)), low, 0.0)
        inv = inv - dot(inv, dot(off, inv))
        b *= 2
    return inv + dot(inv, eye - inv - dot3(low, inv))


def valid_column(info, rows, back):
    pos = info[NB] + iota((rows, 1), 0)
    return jnp.where(doc_of(info, pos) == doc_of(info, pos - back), 1.0, 0.0)


def vectors(conv):
    act = conv * sigmoid(conv)
    qa, ka, va = act[:, :DK], act[:, DK : 2 * DK], act[:, 2 * DK :]
    rq = lax.rsqrt(jnp.sum(qa * qa, axis=1, keepdims=True) + 1e-06)
    rk = lax.rsqrt(jnp.sum(ka * ka, axis=1, keepdims=True) + 1e-06)
    return qa, ka, va, rq, rk


def rates(rate_ref, dlog_ref, dbias_ref):
    heads = dlog_ref.shape[1]
    pre = rate_ref[:, :heads] + dbias_ref[...]
    log_decay = -jnp.exp(dlog_ref[...]) * softplus(pre)
    return sigmoid(rate_ref[:, heads:]), log_decay, pre


def block_masks(info, c):
    row, col = iota((BLK, BLK), 0), iota((BLK, BLK), 1)
    base = info[NB] + c * BLK
    docs_r, docs_c = doc_of(info, base + row), doc_of(info, base + col)
    keep = (docs_r == docs_c) & (col <= row)
    column = doc_of(info, base + iota((BLK, 1), 0))
    first = jnp.where(column == doc_of(info, base - 1 + iota((BLK, 1), 0) * 0), 1.0, 0.0)
    last = jnp.where(column == doc_of(info, base + BLK - 1 + iota((BLK, 1), 0) * 0), 1.0, 0.0)
    tri = jnp.where(col <= row, 1.0, 0.0)
    strict = jnp.where(col < row, 1.0, 0.0)
    return keep, first, last, tri, strict


def decays(g, first, last, tri):
    cum = dot_exact_left(tri, jnp.broadcast_to(g, (BLK, DK)))[:, :1]
    carry = first * jnp.exp(cum)
    to_end = last * jnp.exp(cum[BLK - 1 :, :] - cum)
    return carry, to_end


def mixer_forward(
    info, proj, rate, convw, dlog, dbias, out_w, gain, cot,
    conv_o, dec_o, inv_o, wu_o, qe_o, step_o, states_o, head_o, gated_o, ga_o, ta_o, halo_o, mixed_o, cot_o,
    xpad, ol, gs, scores, ab, rim, rim_got, got1, tot, got2, hs, hr, s1, r1, s2, r2, sc, rc, lc
):
    rows = proj.shape[0]
    heads = dlog.shape[1]
    blocks = rows // BLK
    me, z, y, dev = seq_place()
    seqs, head = SIDE * SIDE, lax.axis_index("head")
    before, behind = (lax.rem(me + seqs - 1, seqs), head), (lax.rem(me + 1, seqs), head)
    greet(side_peers() + [before, behind] + head_peers())
    cot_sent = gather_start(cot, cot_o, sc, rc, lc)
    for h in range(heads):
        rim[:, pl.ds(h * CONVW, CONVW)] = proj[rows - PAD :, pl.ds(h * MIXW, CONVW)].astype(BF16).astype(F32)
    ahead = cp(rim, rim_got, hs, hr, behind)
    ahead.start()
    strength, log_decay, _ = rates(rate, dlog, dbias)
    valid = [valid_column(info, rows, KCONV - 1 - j) for j in range(KCONV)]
    ahead.wait_recv()
    halo_o[...] = jnp.where(me > 0, rim_got[...], 0.0)
    for h in range(heads):
        src, dst = pl.ds(h * MIXW, CONVW), pl.ds(h * CONVW, CONVW)
        xpad[:PAD, :] = halo_o[:, dst]
        xpad[PAD:, :] = proj[:, src].astype(BF16).astype(F32)
        conv = jnp.zeros((rows, CONVW), F32)
        for j in range(KCONV):
            lo = PAD - (KCONV - 1) + j
            conv = conv + convw[j : j + 1, dst].astype(F32) * xpad[lo : lo + rows, :] * valid[j]
        conv_o[:, dst] = conv
    for c in range(blocks):
        keep, first, last, tri, strict = block_masks(info, c)
        here = pl.ds(c * BLK, BLK)
        for h in range(heads):
            qa, ka, va, rq, rk = vectors(conv_o[here, pl.ds(h * CONVW, CONVW)])
            q, k = qa * (rq * DK**-0.5), ka * rk
            beta = strength[c * BLK : (c + 1) * BLK, h : h + 1]
            g = log_decay[c * BLK : (c + 1) * BLK, h : h + 1]
            spread = dot_exact_left(tri, g * strict)
            dec = jnp.where(keep, jnp.exp(jnp.where(keep, spread, 0.0)), 0.0)
            carry, to_end = decays(g, first, last, tri)
            low = strict * (beta * dec * dot(k, k, "nt"))
            inv = unit_lower_inverse(low)
            u = h * blocks + c
            dec_o[u] = dec
            inv_o[u] = inv.astype(BF16)
            rhs = jnp.concatenate([(beta * carry) * k, beta * va], axis=1)
            wu = dot(inv, rhs)
            wu_o[u] = wu
            scores[u] = (dec * dot(q, k, "nt")).astype(BF16)
            qe_o[here, pl.ds(h * DK, DK)] = carry * q
            step = dot(wu, to_end * k, "tn")
            eye = jnp.where(iota((DK, DK), 0) == iota((DK, DK), 1), 1.0, 0.0)
            step_o[u, :DK] = carry[BLK - 1 :, :] * eye - step[:DK]
            step_o[u, DK:] = step[DK:]
        if c == 0:
            cot_sent += gather_forward(cot, cot_o, sc, rc)
    for h in range(heads):
        whole = step_o[h * blocks]
        for c in range(1, blocks):
            nxt = step_o[h * blocks + c]
            whole = add_low(dot3(whole, nxt[:DK]), nxt[DK:])
        ab[h] = whole.astype(ab.dtype)

    out, wait = share_start(ab, got1, y, lambda d: dev(0, d), s1, r1)
    for h in range(heads):
        for c in range(blocks):
            u, here = h * blocks + c, pl.ds(c * BLK, BLK)
            block = dot(scores[u], wu_o[u])
            qe_o[here, pl.ds(h * DK, DK)] = qe_o[here, pl.ds(h * DK, DK)] - block[:, :DK]
            ol[here, pl.ds(h * DV, DV)] = block[:, DK:]
    wait()
    held_before = []
    for h in range(heads):
        whole = got1[0, h].astype(F32)
        prefix = jnp.where(y > 0, whole, unit_top())
        for j in range(1, SIDE):
            a, b = got1[j, h, :DK, :], got1[j, h, DK:, :].astype(F32)
            whole = add_low(dot_left2(whole, a), b)
            if j < SIDE - 1:
                prefix = jnp.where(y > j, whole, prefix)
        tot[h] = whole.astype(BF16)
        held_before.append(prefix)
        for j in range(SIDE):
            ga_o[j, h] = got1[j, h, :DK, :]
    more, wait = share_start(tot, got2, z, lambda d: dev(d, 0), s2, r2)
    for h in range(heads):
        gate = proj[:, pl.ds(h * MIXW + CONVW, DV)]
        gs[:, pl.ds(h * DV, DV)] = gain[...] * (gate * sigmoid(gate))
    wait()
    for h in range(heads):
        held = jnp.zeros((DV, DK), F32)
        for j in range(SIDE - 1):
            held = jnp.where(
                z > j, dot_left2(held, got2[j, h, :DK, :]) + got2[j, h, DK:, :].astype(F32), held
            )
        for j in range(SIDE):
            ta_o[j, h] = got2[j, h, :DK, :]
        state = dot3(held, held_before[h][:DK]) + held_before[h][DK:]
        for c in range(blocks):
            u = h * blocks + c
            here, cols = pl.ds(c * BLK, BLK), pl.ds(h * DV, DV)
            states_o[u] = state
            block = ol[here, cols] + dot(qe_o[here, pl.ds(h * DK, DK)], state, "nt")
            head_o[here, cols] = block
            gated_o[here, cols] = (block * mean_scale(block) * gs[here, cols]).astype(BF16)
            if c + 1 < blocks:
                state = dot3(state, step_o[u, :DK, :]) + step_o[u, DK:, :]
    for j in range(0, D, CONVW):
        mixed_o[:, j : j + CONVW] = dot(gated_o[...], out_w[:, j : j + CONVW]).astype(BF16)
    gather_end(cot, cot_o, sc, rc, lc, cot_sent)
    for s in out + more + [ahead]:
        s.wait_send()


def dot_left2(a, b, form="nn"):
    ah, al = halves(a)
    return dot(ah, b, form) + dot(al, b, form)


def head_back(d_mixed, out_w, head_out, proj, gain, qe, step, d_out_o, d_gate_o, y_o, inc_o):
    rows = qe.shape[0]
    blocks = rows // BLK
    heads = qe.shape[1] // DK
    total = jnp.zeros((1, DV), F32)
    for h in range(heads):
        cols = pl.ds(h * DV, DV)
        for c in range(blocks):
            here = pl.ds(c * BLK, BLK)
            dg, out = dot(d_mixed[here, :], out_w[cols, :], "nt"), head_out[here, cols]
            gate = proj[here, pl.ds(h * MIXW + CONVW, DV)]
            s = sigmoid(gate)
            silu = gate * s
            scale = lax.rsqrt(jnp.mean(out * out, axis=1, keepdims=True) + 1e-05)
            dn = dg * (out * scale)
            d_gate_o[here, pl.ds(h * MIXW + CONVW, DV)] = (dn * gain[...] * (s * (1.0 + gate * (1.0 - s)))).astype(BF16)
            total = total + jnp.sum(dn * silu, axis=0, keepdims=True)
            f = dg * gain[...] * silu
            d_out = scale * f - out * (scale * scale * scale) * jnp.mean(f * out, axis=1, keepdims=True)
            d_out_o[here, cols] = d_out
            y_o[h * blocks + c] = dot(d_out, qe[here, pl.ds(h * DK, DK)], "tn")
        inc = y_o[h * blocks + blocks - 1]
        for c in range(blocks - 2, -1, -1):
            inc = y_o[h * blocks + c] + dot3(inc, step[h * blocks + c, :DK, :], "nt")
        inc_o[h] = inc.astype(inc_o.dtype)
    return total


def mixer_back(
    info, d_mixed, out_w, head_out, proj, gain, qe, step, ga, ta, middle, cot, gated_t, s_gu, conv, dec, inv, wu, states,
    rate, halo, convw, dlog, dbias,
    d_proj_o, d_tail_o, d_edge_o, d_rate_o, d_convw_o, d_decay_o, d_gain_o, s_down_o, s_out_o, g_gu_o,
    d_out, y, inc, later, got1, tot, got2, xpad, dpad, dsend, cols_s, d_pre_o,
    gm_s, e_s, fresh_s, ks_s, d_fresh_s, dq_s, dk_s, cols_u,
    g_down, g_out, relay_d, relay_o, got_d, got_o, last_got, s1, r1, s2, r2, s3, r3, s4, r4
):
    greet(side_peers())
    settle = Settle(lambda i, b: last_got.at[i, b], s4, r4)
    for b in (2, 1, 3):
        for i in range(2):
            settle.send(s_gu.at[i, b], i, b)
    grads = (g_down, g_out)
    spread = Spread(
        lambda i, owner: grads[i].at[owner], lambda i, b: (relay_d, relay_o)[i].at[b],
        lambda i, s, b: (got_d, got_o)[i].at[s, b], s3, r3,
    )
    d_gain_o[...] = head_back(d_mixed, out_w, head_out, proj, gain, qe, step, d_out, d_proj_o, y, inc)

    rows = d_out.shape[0]
    heads = later.shape[0]
    blocks = rows // BLK
    strength, log_decay, pre = rates(rate, dlog, dbias)
    valid = [valid_column(info, rows, KCONV - 1 - j) for j in range(KCONV)]

    def early(c):
        keep, first, last, tri, strict = block_masks(info, c)
        here = pl.ds(c * BLK, BLK)
        for h in range(heads):
            u = h * blocks + c
            qa, ka, va, rq, rk = vectors(conv[here, pl.ds(h * CONVW, CONVW)])
            q, k = qa * (rq * DK**-0.5), ka * rk
            g = log_decay[c * BLK : (c + 1) * BLK, h : h + 1]
            carry, to_end = decays(g, first, last, tri)
            dm = dec[u]
            sc = dm * dot3(q, k, "nt")
            gm_s[u] = dm * dot3(k, k, "nt") * strict
            state = states[u]
            do = d_out[here, pl.ds(h * DV, DV)]
            ks_s[u] = dot3(k, state, "nt")
            fresh = wu[u, :, DK:] - dot3(wu[u, :, :DK], state, "nt")
            fresh_s[u] = fresh
            d_fresh_s[u] = dot(sc, do, "tn")
            d_sc = dot3(do, fresh, "nt")
            e_s[u] = d_sc * sc
            d_scd = d_sc * dm
            dq_s[u] = dot(d_scd, k) + carry * dot(do, state)
            dk_s[u] = dot(d_scd, q, "tn")
            cols_u[u, :, 0:1] = carry
            cols_u[u, :, 1:2] = to_end
            cols_u[u, :, 2:3] = jnp.sum(do * dot3(q, state, "nt"), axis=1, keepdims=True)

    def make(o, left, right):
        for j in range(0, o.shape[0], 2):
            both = dot(left[...], right[:, j * LANES : (j + 2) * LANES]).astype(BF16)
            o[j], o[j + 1] = both[:, :LANES], both[:, LANES:]

    def level_one():
        make(g_down, middle, cot)
        make(g_out, gated_t, d_mixed)
        early(0)

    def level_two():
        for place in PLACES:
            spread.ready(*place, (0,))
        for c in range(1, blocks):
            early(c)

    swaps = states_backward(inc, ga, ta, later, got1, tot, got2, s1, r1, s2, r2, level_one, level_two)
    for place in PLACES:
        spread.ready(*place, (1,))
    for h in range(heads):
        grad = later[h]
        for c in range(blocks - 1, -1, -1):
            u = h * blocks + c
            dsend[u] = grad
            if c:
                grad = dot3(grad, step[u, :DK, :], "nt") + y[u]
    for c in range(blocks):
        tri, strict = block_masks(info, c)[3:]
        here = pl.ds(c * BLK, BLK)
        for h in range(heads):
            u = h * blocks + c
            cv = conv[here, pl.ds(h * CONVW, CONVW)]
            sg = sigmoid(cv)
            qa, ka, va, rq, rk = vectors(cv)
            rqs = rq * DK**-0.5
            k = ka * rk
            beta = strength[c * BLK : (c + 1) * BLK, h : h + 1]
            carry, to_end, hq = cols_u[u, :, 0:1], cols_u[u, :, 1:2], cols_u[u, :, 2:3]
            dm = dec[u]
            gm, fresh, ks = gm_s[u], fresh_s[u], ks_s[u]
            state, d_end = states[u], dsend[u]
            kd = to_end * k
            ah, al = halves(d_fresh_s[u] + dot(kd, d_end, "nt"))
            d_rhs = dot(inv[u], ah, "tn") + dot(inv[u], al, "tn")
            d_low = -dot3(d_rhs, fresh, "nt")
            d_val = beta * d_rhs
            ebar = d_low * gm
            d_beta = jnp.sum(d_rhs * (va - carry * ks), axis=1, keepdims=True) + jnp.sum(ebar, axis=1, keepdims=True)
            e = e_s[u] + beta * ebar
            d_gm = (beta * d_low) * (dm * strict)
            d_kd = dot(fresh, d_end)
            d_q = dq_s[u]
            d_k = (
                dk_s[u]
                - (beta * carry) * dot(d_rhs, state)
                + to_end * d_kd
                + dot(d_gm, k)
                + dot(d_gm, k, "tn")
            )
            hcol = carry * (hq - jnp.sum(beta * d_rhs * ks, axis=1, keepdims=True))
            fcol = jnp.sum(kd * d_kd, axis=1, keepdims=True)
            tail = carry[BLK - 1 :, :] * jnp.sum(
                jnp.sum(state * d_end, axis=1, keepdims=True), axis=0, keepdims=True
            )
            lane = iota((BLK, DK), 1)
            d_g = (
                jnp.sum(dot_exact_left(tri, e, "tn") * strict, axis=1, keepdims=True)
                + dot_exact_left(tri, jnp.where(lane == 0, hcol, 0.0), "tn")[:, :1]
                + dot_exact_left(strict, jnp.where(lane == 0, fcol, 0.0))[:, :1]
                + tail
            )
            cols_s[here, h : h + 1] = d_g
            cols_s[here, heads + h : heads + h + 1] = d_beta
            d_qa = rqs * d_q - qa * (rqs * rq * rq * jnp.sum(d_q * qa, axis=1, keepdims=True))
            d_ka = rk * d_k - ka * (rk * rk * rk * jnp.sum(d_k * ka, axis=1, keepdims=True))
            d_act = jnp.concatenate([d_qa, d_ka, d_val], axis=1)
            d_pre_o[here, pl.ds(h * CONVW, CONVW)] = d_act * (sg * (1.0 + cv * (1.0 - sg)))
            spread.relays(c * heads + h)
    d_g, d_beta = cols_s[:, :heads], cols_s[:, heads : 2 * heads]
    d_bias = -d_g * jnp.exp(dlog[...]) * sigmoid(pre)
    rest = jnp.zeros((rows, LANES - 2 * heads), F32)
    d_rate_o[...] = jnp.concatenate([d_bias, d_beta * strength * (1.0 - strength), rest], axis=1).astype(BF16)
    d_decay_o[...] = jnp.zeros_like(d_decay_o)
    d_decay_o[:, :heads] = jnp.sum(d_g * log_decay, axis=0, keepdims=True)
    d_decay_o[:, heads : 2 * heads] = jnp.sum(d_bias, axis=0, keepdims=True)
    for h in range(heads):
        src, dst = pl.ds(h * MIXW, CONVW), pl.ds(h * CONVW, CONVW)
        xpad[:PAD, :] = halo[:, dst]
        xpad[PAD:, :] = proj[:, src].astype(BF16).astype(F32)
        dpad[...] = jnp.zeros_like(dpad)
        d_conv = d_pre_o[:, dst]
        for j in range(KCONV):
            lo = PAD - (KCONV - 1) + j
            masked = d_conv * valid[j]
            d_convw_o[j : j + 1, dst] = jnp.sum(masked * xpad[lo : lo + rows, :], axis=0, keepdims=True)
            dpad[lo : lo + rows, :] += convw[j : j + 1, dst].astype(F32) * masked
        d_edge_o[:, dst] = dpad[:PAD, :]
        d_tail_o[:, dst] = dpad[rows - PAD :, :]
        d_proj_o[:, src] = dpad[PAD:, :].astype(BF16)
    for i in range(2):
        g_gu_o[i] = s_gu[i, 0].astype(F32) + settle.others(i)
    for i, o in ((0, s_down_o), (1, s_out_o)):
        for b in FAR:
            o[b] = spread.total(i, b).astype(BF16)
    spread.end()
    settle.end()
    for s in swaps:
        s.wait_send()


def call(kernel, outs, scratch, limit, *args, flops=2_000_000_000, nbytes=16_000_000):
    def spec(a):
        return SMEM if a.dtype == jnp.int32 else VMEM

    return pl.pallas_call(
        kernel,
        out_shape=outs,
        in_specs=[spec(a) for a in args],
        out_specs=[VMEM for _ in outs],
        scratch_shapes=scratch,
        compiler_params=pltpu.CompilerParams(vmem_limit_bytes=limit << 20),
        cost_estimate=pl.CostEstimate(flops=flops, bytes_accessed=nbytes, transcendentals=0),
    )(*args)


def sds(shape, dtype=F32):
    return jax.ShapeDtypeStruct(shape, dtype)
CHIPS = 4
LANES = 128


def cp(src, dst, send, recv, dev):
    return pltpu.make_async_remote_copy(
        src_ref=src, dst_ref=dst, send_sem=send, recv_sem=recv, device_id=dev, device_id_type=pl.DeviceIdType.MESH
    )


def greet(devices):
    barrier = pltpu.get_barrier_semaphore()
    for dev in devices:
        pl.semaphore_signal(barrier, inc=1, device_id=dev, device_id_type=pl.DeviceIdType.MESH)
    pl.semaphore_wait(barrier, len(devices))


def head_place():
    me = lax.axis_index("head")
    chip, core = me // 2, me % 2
    seq = lax.axis_index("seq")

    def dev(step, flip=False):
        c = lax.rem(chip + step, CHIPS)
        return (seq, c * 2 + (1 - core if flip else core))

    return me, chip, core, dev


def head_peers():
    dev = head_place()[3]
    return [dev(0, True)] + [dev(d) for d in range(1, CHIPS)]


def head_rows(o, rows, step, flip=False, lo=0, size=None):
    owner = head_place()[3](step, flip)[1]
    size = size or rows
    return o.at[pl.ds(pl.multiple_of(owner * rows + lo, size), size)]


def gather_start(x, o, ssem, rsem, lsem):
    rows = x.shape[0]
    dev = head_place()[3]
    pltpu.make_async_copy(x, head_rows(o, rows, 0), lsem).start()
    out = [cp(x, head_rows(o, rows, 0), ssem.at[d], rsem.at[d], dev(d)) for d in (1, 3)]
    out.append(cp(x, head_rows(o, rows, 0), ssem.at[0], rsem.at[0], dev(0, True)))
    for s in out:
        s.start()
    return out


def opposite(rows):
    return ((0, 2, 6, 1), (rows // 2, 8, 9, 3))


def gather_forward(x, o, ssem, rsem):
    rows = x.shape[0]
    dev = head_place()[3]
    partner = dev(0, True)
    out = []

    def go(src, k, to):
        s = cp(src, src, ssem.at[k], rsem.at[k], to)
        s.start()
        out.append(s)

    for lo, relay, core, step in opposite(rows):
        there = head_rows(o, rows, CHIPS - step)
        cp(x, there, ssem.at[step], rsem.at[step], dev(step)).wait_recv()
        go(head_rows(o, rows, CHIPS - step, False, lo, rows // 2), relay, dev(step))
        go(there, CHIPS + step, partner)
    for lo, relay, core, step in opposite(rows):
        there = head_rows(o, rows, 2, False, lo, rows // 2)
        cp(there, there, ssem.at[relay], rsem.at[relay], dev(step)).wait_recv()
        go(there, core, partner)
    return out


def gather_end(x, o, ssem, rsem, lsem, sent):
    rows = x.shape[0]
    dev = head_place()[3]
    partner = dev(0, True)
    pltpu.make_async_copy(x, head_rows(o, rows, 0), lsem).wait()
    cp(x, head_rows(o, rows, 0, True), ssem.at[0], rsem.at[0], partner).wait_recv()
    for lo, relay, core, step in opposite(rows):
        k = CHIPS + step
        cp(x, head_rows(o, rows, CHIPS - step, True), ssem.at[k], rsem.at[k], partner).wait_recv()
        there = head_rows(o, rows, 2, True, lo, rows // 2)
        cp(there, there, ssem.at[core], rsem.at[core], partner).wait_recv()
    for s in sent:
        s.wait_send()


def mean_scale(v):
    return lax.rsqrt(jnp.mean(v * v, axis=1, keepdims=True) + 1e-05)


def first_norm(tokens, gain, all_o, block, ssem, rsem, lsem):
    greet(head_peers())
    v = tokens[...].astype(F32)
    block[...] = (v * mean_scale(v) * gain[...]).astype(BF16)
    sent = gather_start(block, all_o, ssem, rsem, lsem)
    sent += gather_forward(block, all_o, ssem, rsem)
    gather_end(block, all_o, ssem, rsem, lsem, sent)


def norm_back(v, gain, d_norm):
    r = mean_scale(v)
    e = d_norm * gain
    d_v = r * e - v * (r * r * r * jnp.mean(e * v, axis=1, keepdims=True))
    return d_v, jnp.sum(d_norm * v * r, axis=0, keepdims=True)


def feed_forward(
    x, tokens, gain, cot, cot_all, gu, down,
    hidden_o, all_o, d_hidden_o, d_gain_o, sums_o, middle_o, feed_o,
    n2, guv, downv, d_middle, d_gu, d_two, block, ta, pa, ga, ma, tb, pb, gb, mb, g, relay, seqs_got,
    ls, sa, ra, sb, rb, s1, r1, l1, s2, r2, l2, s3, r3
):
    load_d = pltpu.make_async_copy(down, downv, ls.at[0])
    load_d.start()
    load_g = pltpu.make_async_copy(gu, guv, ls.at[1])
    load_g.start()
    greet(head_peers() + side_peers())
    one = pair_sends(x, pa, sa, ra, FAR)
    two = ChipSum(x, one, ta, pa, ga, ma, sa, ra)
    load_d.wait()
    d_middle[...] = dot(downv[...], cot_all[...], "nt")
    two.relay()
    hidden = tokens[...].astype(F32) + two.result()
    hidden_o[...] = hidden
    block[...] = (hidden * mean_scale(hidden) * gain[...]).astype(BF16)
    ahead = gather_start(block, n2, s1, r1, l1)
    load_g.wait()
    ahead += gather_forward(block, n2, s1, r1)
    gather_end(block, n2, s1, r1, l1, ahead)
    hid = downv.shape[0]
    low = hid // 32 * 16
    for lo, hi in ((0, low), (low, hid)):
        gate = dot(guv[lo:hi, :], n2[...], "nt")
        up = dot(guv[hid + lo : hid + hi, :], n2[...], "nt")
        s = sigmoid(gate)
        silu = gate * s
        dm = d_middle[lo:hi, :]
        middle_o[lo:hi, :] = (silu * up).astype(BF16)
        d_gu[lo:hi, :] = (dm * up * (s * (1.0 + gate * (1.0 - s)))).astype(BF16)
        d_gu[hid + lo : hid + hi, :] = (dm * silu).astype(BF16)
    for j in range(0, D, 512):
        d_two[:, j : j + 512] = dot(d_gu[...], guv[:, j : j + 512], "tn").astype(BF16)
    one_b = pair_sends(d_two, pb, sb, rb, FAR)
    spread = Spread(
        lambda i, owner: g.at[owner, i], lambda i, b: relay.at[i, b], lambda i, s, b: seqs_got.at[i, s, b], s3, r3
    )
    dev = seq_place()[3]

    def make(place):
        owner = dev(*place)[0]
        cols = n2[:, pl.ds(pl.multiple_of(owner * LANES, LANES), LANES)]
        out = dot(d_gu[...], cols).astype(BF16)
        g[owner, 0] = out[:hid]
        g[owner, 1] = out[hid:]
        spread.ready(*place)

    for place in PLACES[:3]:
        make(place)
    two_b = ChipSum(d_two, one_b, tb, pb, gb, mb, sb, rb)
    for place in PLACES[3:9]:
        make(place)
    two_b.relay()
    for place in PLACES[9:]:
        make(place)
    d_norm, d_gain = norm_back(hidden_o[...], gain[...], two_b.result())
    d_hidden = cot[...].astype(F32) + d_norm
    d_hidden_o[...] = d_hidden
    d_gain_o[...] = d_gain
    block[...] = d_hidden.astype(BF16)
    ahead = gather_start(block, all_o, s2, r2, l2)
    spread.relays()
    for j in range(0, D, 512):
        feed_o[:, j : j + 512] = dot(middle_o[...], downv[:, j : j + 512], "tn").astype(BF16)
    ahead += gather_forward(block, all_o, s2, r2)
    for b in FAR:
        for i in range(2):
            sums_o[i, b] = spread.total(i, b).astype(BF16)
    gather_end(block, all_o, s2, r2, l2, ahead)
    spread.end()
    two.end()
    two_b.end()


def reach(kernel, outs, scratch, cid, limit, *args, anywhere=(), scalars=(), nbytes=12_000_000):
    return pl.pallas_call(
        kernel,
        out_shape=outs,
        in_specs=[
            pl.BlockSpec(memory_space=pl.ANY) if i in anywhere else SMEM if i in scalars else VMEM for i in range(len(args))
        ],
        out_specs=[VMEM for _ in outs],
        scratch_shapes=scratch,
        compiler_params=pltpu.CompilerParams(
            collective_id=cid, has_side_effects=True, vmem_limit_bytes=limit << 20
        ),
        cost_estimate=pl.CostEstimate(flops=0, bytes_accessed=nbytes, transcendentals=0),
    )(*args)


def sems(n):
    return pltpu.SemaphoreType.DMA((n,))


def gather_scratch():
    return [sems(10), sems(10), pltpu.SemaphoreType.DMA]


SIDE = 4


def seq_place():
    me = lax.axis_index("seq")
    z, y = me // SIDE, me % SIDE
    head = lax.axis_index("head")

    def dev(dz, dy):
        return (lax.rem(z + dz, SIDE) * SIDE + lax.rem(y + dy, SIDE), head)

    return me, z, y, dev


def side_peers():
    dev = seq_place()[3]
    return [dev(0, d) for d in range(1, SIDE)] + [dev(d, 0) for d in range(1, SIDE)]


FAR = (2, 1, 3, 0)
FIRST, OTHER = (2, 1), (3, 0)
PLACES = (
    (2, 2), (2, 1), (1, 2), (2, 3), (3, 2), (2, 0), (0, 2), (1, 3), (3, 1), (1, 0), (0, 1), (3, 3), (1, 1), (0, 3), (3, 0),
    (0, 0),
)


class Spread:
    def __init__(self, piece, relay, got, ssem, rsem):
        self.piece, self.relay, self.got, self.ssem, self.rsem = piece, relay, got, ssem, rsem
        self.dev = seq_place()[3]
        self.sent = []

    def way(self, i, a, b):
        return self.dev(b, a) if i == 0 else self.dev(a, b)

    def copy(self, i, a, b, owner):
        k = (i * SIDE + a) * SIDE + b
        if a == 2:
            dst, step = self.relay(i, b), 1 if b in FIRST else 3
        else:
            dst, step = self.got(i, 0 if a == 1 else 1, b), a
        return cp(self.piece(i, owner), dst, self.ssem.at[k], self.rsem.at[k], self.way(i, step, 0))

    def send(self, i, a, b, owner):
        s = self.copy(i, a, b, owner)
        s.start()
        self.sent.append(s)

    def late(self, a, b):
        return a == 1 and b in FIRST or a == 3 and b in OTHER

    def ready(self, dz, dy, halves_=(0, 1)):
        owner = self.dev(dz, dy)[0]
        for i in halves_:
            a, b = (dy, dz) if i == 0 else (dz, dy)
            if a and not self.late(a, b):
                self.send(i, a, b, owner)

    def relays(self, part=None):
        for n, b in enumerate(FAR):
            if part is not None and n != part:
                continue
            for i in range(2):
                a = 1 if b in FIRST else 3
                owner = self.way(i, a, b)[0]
                self.copy(i, 2, b, owner).wait_recv()
                both = self.piece(i, owner)[...].astype(F32) + self.relay(i, b)[...].astype(F32)
                self.relay(i, b)[...] = both.astype(BF16)
                k = (i * SIDE + a) * SIDE + b
                s = cp(
                    self.relay(i, b), self.got(i, 0 if a == 1 else 1, b), self.ssem.at[k], self.rsem.at[k],
                    self.way(i, a, 0),
                )
                s.start()
                self.sent.append(s)

    def total(self, i, b):
        owner = self.way(i, 0, b)[0]
        for a in (1, 3):
            self.copy(i, a, b, owner).wait_recv()
        return self.piece(i, owner)[...].astype(F32) + (
            self.got(i, 0, b)[...].astype(F32) + self.got(i, 1, b)[...].astype(F32)
        )

    def end(self):
        for s in self.sent:
            s.wait_send()


class Settle:
    def __init__(self, got, ssem, rsem):
        self.got, self.ssem, self.rsem = got, ssem, rsem
        self.dev = seq_place()[3]
        self.sent = {}

    def send(self, src, i, b):
        k = i * SIDE + b
        dev = self.dev(b, 0) if i == 0 else self.dev(0, b)
        self.sent[i, b] = cp(src, self.got(i, b), self.ssem.at[k], self.rsem.at[k], dev)
        self.sent[i, b].start()

    def others(self, i):
        for b in (1, 3, 2):
            self.sent[i, b].wait_recv()
        return (self.got(i, 1)[...].astype(F32) + self.got(i, 3)[...].astype(F32)) + self.got(i, 2)[...].astype(F32)

    def end(self):
        for s in self.sent.values():
            s.wait_send()


def share_start(src, got, place, to, ssem, rsem, size=SIDE, own=None):
    part = (lambda d: src) if own is None else (lambda d: src.at[lax.rem(place + d, size)])
    got[place] = src[...] if own is None else src[place]
    steps = (2, 1, 3) if size == SIDE else range(1, size)
    out = [cp(part(d), got.at[place], ssem.at[d], rsem.at[d], to(d)) for d in steps]
    for s in out:
        s.start()

    def wait():
        for d in steps:
            back = lax.rem(place + size - d, size)
            cp(part(d), got.at[back], ssem.at[d], rsem.at[d], to(d)).wait_recv()

    return out, wait


def in_order(got):
    total = got[0]
    for i in range(1, got.shape[0]):
        total = total + got[i]
    return total


def share(src, got, place, to, ssem, rsem):
    out, wait = share_start(src, got, place, to, ssem, rsem)
    wait()
    return out


def unit_top():
    return jnp.where(iota((DK + DV, DK), 0) == iota((DK + DV, DK), 1), 1.0, 0.0)


def add_low(pair, low):
    return jnp.concatenate([pair[:DK], pair[DK:] + low], axis=0)


def states_backward(inc, ga, ta, later_o, got1, tot, got2, s1, r1, s2, r2, level_one, level_two):
    me, z, y, dev = seq_place()
    heads = inc.shape[0]
    out, wait = share_start(inc, got1, y, lambda d: dev(0, d), s1, r1)
    level_one()
    wait()
    after = []
    for h in range(heads):
        whole = add_low(dot(unit_top(), ga[SIDE - 1, h], "nt"), got1[SIDE - 1, h].astype(F32))
        suffix = jnp.where(y < SIDE - 1, whole, unit_top())
        for j in range(SIDE - 2, -1, -1):
            whole = add_low(dot_left2(whole, ga[j, h], "nt"), got1[j, h].astype(F32))
            if j:
                suffix = jnp.where(y < j, whole, suffix)
        tot[h] = whole[DK:].astype(BF16)
        after.append(suffix)
    more, wait = share_start(tot, got2, z, lambda d: dev(d, 0), s2, r2)
    level_two()
    wait()
    for h in range(heads):
        held = jnp.zeros((DV, DK), F32)
        for j in range(SIDE - 1, 0, -1):
            held = jnp.where(z < j, dot_left2(held, ta[j, h], "nt") + got2[j, h].astype(F32), held)
        later_o[h] = dot3(held, after[h][:DK]) + after[h][DK:]
    return out + more


def pair_sends(x, pair, ssem, rsem, steps):
    rows = pair.shape[1]
    dev = head_place()[3]
    out = {}
    for d in steps:
        owner = dev(d, True)[1]
        src = x.at[pl.ds(pl.multiple_of(owner * rows, rows), rows)]
        out[d] = cp(src, pair.at[d], ssem.at[d], rsem.at[d], dev(0, True))
        out[d].start()
    return out


class ChipSum:
    def __init__(self, x, first, total, pair, got, mid, ssem, rsem):
        self.x, self.first, self.total, self.pair = x, first, total, pair
        self.got, self.mid, self.ssem, self.rsem = got, mid, ssem, rsem
        self.rows = pair.shape[1]
        self.dev = head_place()[3]
        half = self.rows // 2
        self.top, self.low = slice(0, half), slice(half, self.rows)
        self.sent = []
        self.mid[2] = self.both(2).astype(BF16)
        self.send(2, self.top, 0, 4, 1)
        self.send(2, self.low, 0, 5, 3)
        self.right = self.both(1)
        self.mid[1, self.low] = self.right[self.low].astype(BF16)
        self.send(1, self.low, 1, 6, 1)
        self.left = self.both(3)
        self.mid[3, self.top] = self.left[self.top].astype(BF16)
        self.send(3, self.top, 3, 7, 3)
        self.total[...] = self.both(0)

    def both(self, d):
        self.first[d].wait_recv()
        owner = self.dev(d)[1]
        mine = self.x[pl.ds(pl.multiple_of(owner * self.rows, self.rows), self.rows), :]
        return mine.astype(F32) + self.pair[d].astype(F32)

    def copy(self, d, part, slot, k, step):
        at = pl.ds(part.start, part.stop - part.start)
        return cp(self.mid.at[d, at], self.got.at[slot, at], self.ssem.at[k], self.rsem.at[k], self.dev(step))

    def send(self, *what):
        s = self.copy(*what)
        s.start()
        self.sent.append(s)

    def relay(self):
        self.copy(2, self.top, 0, 4, 1).wait_recv()
        self.mid[1, self.top] = (self.right[self.top] + self.got[0, self.top].astype(F32)).astype(BF16)
        self.send(1, self.top, 1, 8, 1)
        self.copy(2, self.low, 0, 5, 3).wait_recv()
        self.mid[3, self.low] = (self.left[self.low] + self.got[0, self.low].astype(F32)).astype(BF16)
        self.send(3, self.low, 3, 9, 3)

    def result(self):
        self.copy(1, self.low, 1, 6, 1).wait_recv()
        self.copy(3, self.top, 3, 7, 3).wait_recv()
        self.copy(1, self.top, 1, 8, 1).wait_recv()
        self.copy(3, self.low, 3, 9, 3).wait_recv()
        return self.total[...] + (self.got[1].astype(F32) + self.got[3].astype(F32))

    def end(self):
        for s in self.sent + list(self.first.values()):
            s.wait_send()


def finish(
    dproj, normed, w, d_rate, rate_w, d_tail, d_edge, feed, hidden, tokens, d_hidden, gain, convs, decay, g_feed, g_head,
    s_down, s_out,
    layer_o, d_tokens_o, g_mixer_o, g_gain_o, g_feed_o, g_head_o, conv_o, dlog_o, dbias_o, rate_o, g_down_o, g_out_o,
    dp, wv, edge, g, relay, got1, mid, got2, dn, ta, pa, ga, ma, tb, pb, gb, mb, got_d, got_o,
    e0, eh, e1, ey, e2, ez, m0, mh, m1, my, m2, mz,
    es, er, ls, s1, r1, s2, r2, sa, ra, sb, rb, s5, r5, se, re, sm, rm
):
    me, z, y, dev = seq_place()
    head = lax.axis_index("head")
    heads, seqs = eh.shape[0], g.shape[1]
    rows = dp.shape[0]
    part, half = g_mixer_o.shape[1], g_mixer_o.shape[2]
    load_p = pltpu.make_async_copy(dproj, dp, ls.at[0])
    load_p.start()
    load_w = pltpu.make_async_copy(w, wv, ls.at[1])
    load_w.start()

    def across(d):
        return (me, lax.rem(head + d, heads))

    before, behind = (lax.rem(me + seqs - 1, seqs), head), (lax.rem(me + 1, seqs), head)
    greet([across(d) for d in range(1, heads)] + side_peers() + [before, behind])
    back = cp(d_edge, edge, es, er, before)
    back.start()
    feed_one = pair_sends(feed, pa, sa, ra, FAR)

    n_row, h_row = D // LANES, DV // LANES
    taps, wide_c = convs.shape
    c_row = wide_c // LANES
    ng, nc = e0.shape[0], taps * c_row + PAD
    for r in range(n_row):
        e0[r : r + 1, :] = g_feed[:, r * LANES : (r + 1) * LANES]
    e0[n_row:, :] = jnp.zeros((ng - n_row, LANES), F32)
    for r in range(h_row):
        e0[n_row + r : n_row + r + 1, :] = g_head[:, r * LANES : (r + 1) * LANES]
    small, wait_head = share_start(e0, eh, head, across, se.at[0], re.at[0], heads)
    for t in range(taps):
        for r in range(c_row):
            lo = ng + t * c_row + r
            e1[0, lo : lo + 1, :] = convs[t : t + 1, r * LANES : (r + 1) * LANES]
    e1[0, ng + nc - PAD : ng + nc, :] = jnp.zeros((PAD, LANES), F32)
    e1[0, ng + nc - PAD : ng + nc - PAD + 1, :] = decay[...]
    rates_t = dot(d_rate[:, :PAD], normed[...], "tn")
    for i in range(SIDE):
        if i:
            e1[i, ng : ng + nc, :] = e1[0, ng : ng + nc, :]
        for j in range(SIDE):
            at = (j * SIDE + i) * LANES
            e1[i, ng + nc + j * PAD : ng + nc + (j + 1) * PAD, :] = rates_t[:, at : at + LANES]

    sums = (s_down, s_out)
    settle = Settle(lambda i, b: (got_d, got_o)[i].at[b], s5, r5)
    for b in (2, 1, 3):
        for i in range(2):
            settle.send(sums[i].at[b], i, b)
    load_p.wait()
    back.wait_recv()
    there = jnp.where(me < seqs - 1, edge[...], 0.0)
    tail = jnp.concatenate([d_tail[:PAD, :], d_tail[PAD:, :] + there], axis=0).astype(BF16)
    wide = half - DV
    for i in range(2):
        dp[rows - 2 * PAD :, pl.ds(i * half, wide)] = tail[:, i * wide : (i + 1) * wide]

    spread = Spread(
        lambda i, owner: g.at[i, owner], lambda i, b: relay.at[i, b], lambda i, s, b: got1.at[i, s, b], s1, r1
    )
    settle_two = Settle(lambda i, b: got2.at[i, b], s2, r2)
    for n, place in enumerate(PLACES):
        owner = dev(*place)[0]
        left = normed[:, pl.ds(pl.multiple_of(owner * part, part), part)]
        both = dot(left, dp[...], "tn").astype(BF16)
        for i in range(2):
            g[i, owner] = both[:, i * half : (i + 1) * half]
        spread.ready(*place)
        if n == 2:
            wait_head()
            gains = in_order(eh)
            for i in range(SIDE):
                e1[i, :ng, :] = gains
            more, wait_y = share_start(e1, ey, y, lambda d: dev(0, d), se.at[1], re.at[1], SIDE, True)
            small += more
        if n == 9:
            wait_y()
            total = in_order(ey)
            for j in range(SIDE):
                e2[j, : ng + nc, :] = total[: ng + nc]
                e2[j, ng + nc :, :] = total[ng + nc + j * PAD : ng + nc + (j + 1) * PAD]
            more, wait_z = share_start(e2, ez, z, lambda d: dev(d, 0), se.at[2], re.at[2], SIDE, True)
            small += more
    feed_two = ChipSum(feed, feed_one, ta, pa, ga, ma, sa, ra)

    load_w.wait()
    low = rows // CHIPS
    hp = head_place()[3]
    dn_one = {}
    for d in FAR:
        chip = hp(d)[1] // 2
        here = pl.ds(pl.multiple_of(chip * low, low), low)
        dn[here, :] = (dot(dp[here, :], wv[...], "nt") + dot(d_rate[here, :], rate_w[...], "nt")).astype(BF16)
        dn_one.update(pair_sends(dn, pb, sb, rb, (d,)))
        spread.relays(FAR.index(d))
    feed_two.relay()
    dn_two = ChipSum(dn, dn_one, tb, pb, gb, mb, sb, rb)
    wait_z()
    total = in_order(ez)
    for r in range(n_row):
        g_feed_o[:, r * LANES : (r + 1) * LANES] = total[r : r + 1]
    for r in range(h_row):
        g_head_o[:, r * LANES : (r + 1) * LANES] = total[n_row + r : n_row + r + 1]
    own = conv_o.shape[1]
    for t in range(taps):
        for h in range(own):
            for r in range(c_row // own):
                lo = ng + t * c_row + h * (c_row // own) + r
                conv_o[t, h : h + 1, r * LANES : (r + 1) * LANES] = total[lo : lo + 1]
    dlog_o[...] = total[ng + nc - PAD : ng + nc - PAD + 1, :own]
    dbias_o[...] = total[ng + nc - PAD : ng + nc - PAD + 1, own : 2 * own]
    for i in range(2):
        rate_o[i] = total[ng + nc + i * own : ng + nc + (i + 1) * own]
    dn_two.relay()
    layer_o[...] = (hidden[...] + feed_two.result()).astype(BF16)
    d_norm, d_gain = norm_back(tokens[...].astype(F32), gain[...], dn_two.result())
    d_tokens_o[...] = d_hidden[...] + d_norm

    for r in range(n_row):
        m0[r : r + 1, :] = d_gain[:, r * LANES : (r + 1) * LANES]
    more, wait_head = share_start(m0, mh, head, across, sm.at[0], rm.at[0], heads)
    small += more

    def settle_mixer(b):
        for i in range(2):
            both = spread.total(i, b)
            if b:
                mid[i, b] = both.astype(BF16)
                settle_two.send(mid.at[i, b], i, b)
            else:
                g_mixer_o[i] = both

    settle_mixer(2)
    wait_head()
    m1[...] = in_order(mh)
    more, wait_y = share_start(m1, my, y, lambda d: dev(0, d), sm.at[1], rm.at[1])
    small += more
    settle_mixer(1)
    settle_mixer(3)
    wait_y()
    m2[...] = in_order(my)
    more, wait_z = share_start(m2, mz, z, lambda d: dev(d, 0), sm.at[2], rm.at[2])
    small += more
    settle_mixer(0)
    for i, o in ((0, g_down_o), (1, g_out_o)):
        o[...] = sums[i][0].astype(F32) + settle.others(i)
    wait_z()
    total = in_order(mz)
    for r in range(n_row):
        g_gain_o[:, r * LANES : (r + 1) * LANES] = total[r : r + 1]
    for i in range(2):
        g_mixer_o[i] = g_mixer_o[i] + settle_two.others(i)
    spread.end()
    settle.end()
    settle_two.end()
    feed_two.end()
    dn_two.end()
    for s in small + [back]:
        s.wait_send()


def hand_over(*refs):
    n = (len(refs) - 2) // 2
    srcs, dsts, (held, done) = refs[:n], refs[n : 2 * n], refs[2 * n :]
    copies = [
        pltpu.make_async_copy(srcs[i], dsts[i] if i < n - 1 else held, done.at[i]) for i in range(n - 1, -1, -1)
    ]
    for s in copies:
        s.start()
    copies[0].wait()
    for i in range(held.shape[0]):
        dsts[-1][:, i, :] = held[i]
    for s in copies[1:]:
        s.wait()


def local(
    tokens, mixer_gain, mixer_weight, rate_weight, conv_weight, decay_log, decay_bias, head_gain,
    output_weight, feed_gain, gate_up_weight, down_weight, doc_starts, cotangent,
):
    own = tokens.shape[0]
    (gathered,) = reach(
        first_norm,
        [sds((own * lax.axis_size("head"), D), BF16)],
        [pltpu.VMEM((own, D), BF16)] + gather_scratch(),
        3, 32, tokens, mixer_gain.reshape(1, D),
    )
    heads = mixer_weight.shape[1]
    mixer_flat = mixer_weight.reshape(D, heads * MIXW)
    rows = gathered.shape[0]
    blocks = rows // BLK
    units = heads * blocks
    seq = lax.axis_size("seq")
    projected = jnp.dot(gathered, mixer_flat, preferred_element_type=F32)
    rate_proj = jnp.einsum("td,dgh->tgh", gathered, rate_weight, preferred_element_type=F32).reshape(rows, 2 * heads)
    convw = conv_weight.reshape(KCONV, heads * CONVW)
    info = jnp.concatenate(
        [doc_starts, jnp.stack([lax.axis_index("seq") * rows, lax.axis_index("seq")]).astype(jnp.int32)]
    )
    dlog, dbias = decay_log.reshape(1, heads), decay_bias.reshape(1, heads)
    gain = head_gain.reshape(1, DV)

    out_flat = output_weight.reshape(heads * DV, D)
    pairs = pltpu.VMEM((SIDE, heads, DK + DV, DK), BF16)
    conv, dec, inv, wu, qe, step, states, head_out, gated, ga, ta, halo, mixed, cot_rows = reach(
        mixer_forward,
        [
            sds((rows, heads * CONVW)), sds((units, BLK, BLK)), sds((units, BLK, BLK), BF16),
            sds((units, BLK, DK + DV)), sds((rows, heads * DK)), sds((units, DK + DV, DK)), sds((units, DV, DK)),
            sds((rows, heads * DV)), sds((rows, heads * DV), BF16), sds((SIDE, heads, DK, DK), BF16),
            sds((SIDE, heads, DK, DK), BF16), sds((PAD, heads * CONVW)), sds((rows, D), BF16), sds((rows, D), BF16),
        ],
        [
            pltpu.VMEM((PAD + rows, CONVW), F32), pltpu.VMEM((rows, heads * DV), F32),
            pltpu.VMEM((rows, heads * DV), F32), pltpu.VMEM((units, BLK, BLK), BF16),
            pltpu.VMEM((heads, DK + DV, DK), BF16), pltpu.VMEM((PAD, heads * CONVW), F32),
            pltpu.VMEM((PAD, heads * CONVW), F32), pairs, pltpu.VMEM((heads, DK + DV, DK), BF16), pairs,
            pltpu.SemaphoreType.DMA, pltpu.SemaphoreType.DMA, sems(SIDE), sems(SIDE), sems(SIDE), sems(SIDE),
        ]
        + gather_scratch(),
        1, 56, info, projected, rate_proj, convw, dlog, dbias, out_flat, gain, cotangent, scalars=(0,), nbytes=30_000_000,
    )
    hid = down_weight.shape[0]
    part, half, n_head = D // seq, MIXW, lax.axis_size("head")
    gu_t = gate_up_weight.transpose(1, 2, 0).reshape(2 * hid, D)

    def sums_of_head():
        return [pltpu.VMEM((own, D), F32)] + [pltpu.VMEM((CHIPS, own, D), BF16) for _ in range(3)]

    hidden, d_mixed, d_hidden, g_feed_gain, grads, middle, feed = reach(
        feed_forward,
        [
            sds((own, D)), sds((rows, D), BF16), sds((own, D)), sds((1, D)), sds((2, SIDE, hid, LANES), BF16),
            sds((hid, rows), BF16), sds((rows, D), BF16),
        ],
        [
            pltpu.VMEM((rows, D), BF16), pltpu.VMEM((2 * hid, D), BF16), pltpu.VMEM((hid, D), BF16),
            pltpu.VMEM((hid, rows), F32), pltpu.VMEM((2 * hid, rows), BF16), pltpu.VMEM((rows, D), BF16),
            pltpu.VMEM((own, D), BF16),
        ]
        + sums_of_head()
        + sums_of_head()
        + [
            pltpu.VMEM((seq, 2, hid, LANES), BF16), pltpu.VMEM((2, SIDE, hid, LANES), BF16),
            pltpu.VMEM((2, 2, SIDE, hid, LANES), BF16), sems(2), sems(10), sems(10), sems(10), sems(10),
        ]
        + gather_scratch()
        + gather_scratch()
        + [sems(2 * SIDE * SIDE), sems(2 * SIDE * SIDE)],
        2, 63, mixed, tokens, feed_gain.reshape(1, D), cotangent, cot_rows, gu_t, down_weight,
        anywhere=(5, 6), nbytes=40_000_000,
    )
    gated_t = gated.T
    d_projected, d_tail, d_edge, d_rate, d_convw, d_decay, g_head_gain, s_down, s_out, grad_gate_up = reach(
        mixer_back,
        [
            sds((rows, heads * MIXW), BF16), sds((2 * PAD, heads * CONVW)), sds((PAD, heads * CONVW)),
            sds((rows, LANES), BF16), sds((KCONV, heads * CONVW)), sds((1, LANES)), sds((1, DV)),
            sds((SIDE, hid, LANES), BF16), sds((SIDE, heads * DV, LANES), BF16), sds((2, hid, LANES)),
        ],
        [
            pltpu.VMEM((rows, heads * DV), F32), pltpu.VMEM((units, DV, DK), F32),
            pltpu.VMEM((heads, DV, DK), BF16), pltpu.VMEM((heads, DV, DK), F32),
            pltpu.VMEM((SIDE, heads, DV, DK), BF16), pltpu.VMEM((heads, DV, DK), BF16),
            pltpu.VMEM((SIDE, heads, DV, DK), BF16),
            pltpu.VMEM((PAD + rows, CONVW), F32), pltpu.VMEM((PAD + rows, CONVW), F32),
            pltpu.VMEM((units, DV, DK), F32), pltpu.VMEM((rows, DK), F32), pltpu.VMEM((rows, heads * CONVW), F32),
            pltpu.VMEM((units, BLK, BLK), F32), pltpu.VMEM((units, BLK, BLK), F32), pltpu.VMEM((units, BLK, DV), F32),
            pltpu.VMEM((units, BLK, DV), F32), pltpu.VMEM((units, BLK, DV), F32), pltpu.VMEM((units, BLK, DK), F32),
            pltpu.VMEM((units, BLK, DK), F32), pltpu.VMEM((units, BLK, LANES), F32),
            pltpu.VMEM((seq, hid, LANES), BF16), pltpu.VMEM((seq, heads * DV, LANES), BF16),
            pltpu.VMEM((SIDE, hid, LANES), BF16), pltpu.VMEM((SIDE, heads * DV, LANES), BF16),
            pltpu.VMEM((2, SIDE, hid, LANES), BF16), pltpu.VMEM((2, SIDE, heads * DV, LANES), BF16),
            pltpu.VMEM((2, SIDE, hid, LANES), BF16),
            sems(SIDE), sems(SIDE), sems(SIDE), sems(SIDE), sems(2 * SIDE * SIDE), sems(2 * SIDE * SIDE),
            sems(2 * SIDE), sems(2 * SIDE),
        ],
        4, 63, info, d_mixed, out_flat, head_out, projected, gain, qe, step, ga, ta, middle, cot_rows, gated_t, grads,
        conv, dec, inv, wu, states, rate_proj, halo, convw, dlog, dbias, scalars=(0,), nbytes=40_000_000,
    )
    rate_pad = jnp.pad(rate_weight.reshape(D, 2 * heads), ((0, 0), (0, LANES - 2 * heads)))
    n_gain, n_conv, n_last = D // LANES + PAD, KCONV * heads * CONVW // LANES + PAD, D // LANES
    n_y, n_z = n_gain + n_conv + SIDE * PAD, n_gain + n_conv + PAD

    def rows_of(*shape):
        return pltpu.VMEM(shape + (LANES,), F32)

    (
        layer_out, grad_tokens, grad_mixer, grad_mixer_gain, grad_feed_gain, grad_head_gain, grad_conv, grad_decay_log,
        grad_decay_bias, grad_rate, grad_down, grad_output,
    ) = reach(
        finish,
        [
            sds((own, D), BF16), sds((own, D)), sds((2, part, half)), sds((1, D)), sds((1, D)), sds((1, DV)),
            sds((KCONV, heads, CONVW)), sds((1, heads)), sds((1, heads)), sds((2, heads, LANES)), sds((hid, LANES)),
            sds((heads * DV, LANES)),
        ],
        [
            pltpu.VMEM((rows, heads * MIXW), BF16), pltpu.VMEM((D, heads * MIXW), BF16),
            pltpu.VMEM((PAD, heads * CONVW), F32), pltpu.VMEM((2, seq, part, half), BF16),
            pltpu.VMEM((2, SIDE, part, half), BF16), pltpu.VMEM((2, 2, SIDE, part, half), BF16),
            pltpu.VMEM((2, SIDE, part, half), BF16), pltpu.VMEM((2, SIDE, part, half), BF16), pltpu.VMEM((rows, D), BF16),
        ]
        + sums_of_head()
        + sums_of_head()
        + [
            pltpu.VMEM((SIDE, hid, LANES), BF16), pltpu.VMEM((SIDE, heads * DV, LANES), BF16),
            rows_of(n_gain), rows_of(n_head, n_gain), rows_of(SIDE, n_y), rows_of(SIDE, n_y), rows_of(SIDE, n_z),
            rows_of(SIDE, n_z), rows_of(n_last), rows_of(n_head, n_last), rows_of(n_last), rows_of(SIDE, n_last),
            rows_of(n_last), rows_of(SIDE, n_last),
            pltpu.SemaphoreType.DMA, pltpu.SemaphoreType.DMA, sems(2),
            sems(2 * SIDE * SIDE), sems(2 * SIDE * SIDE), sems(2 * SIDE), sems(2 * SIDE),
            sems(10), sems(10), sems(10), sems(10), sems(2 * SIDE), sems(2 * SIDE),
            pltpu.SemaphoreType.DMA((3, n_head)), pltpu.SemaphoreType.DMA((3, n_head)),
            pltpu.SemaphoreType.DMA((3, n_head)), pltpu.SemaphoreType.DMA((3, n_head)),
        ],
        5, 62, d_projected, gathered, mixer_flat, d_rate, rate_pad, d_tail, d_edge, feed, hidden, tokens,
        d_hidden, mixer_gain.reshape(1, D), d_convw, d_decay, g_feed_gain, g_head_gain, s_down, s_out,
        anywhere=(0, 2), nbytes=40_000_000,
    )
    results = [
        layer_out, grad_tokens, grad_mixer_gain, grad_feed_gain, grad_head_gain, grad_conv, grad_decay_log,
        grad_decay_bias, grad_rate, grad_down, grad_output, grad_gate_up, grad_mixer,
    ]
    (
        layer_out, grad_tokens, grad_mixer_gain, grad_feed_gain, grad_head_gain, grad_conv, grad_decay_log,
        grad_decay_bias, grad_rate, grad_down, grad_output, grad_gate_up, grad_mixer,
    ) = pl.pallas_call(
        hand_over,
        out_shape=[sds(v.shape, v.dtype) for v in results[:-1]] + [sds((part, heads, half))],
        in_specs=[pl.BlockSpec(memory_space=pl.ANY) for _ in results],
        out_specs=[VMEM for _ in results],
        scratch_shapes=[pltpu.VMEM((heads, part, half), F32), sems(len(results))],
        compiler_params=pltpu.CompilerParams(vmem_limit_bytes=60 << 20),
        cost_estimate=pl.CostEstimate(flops=0, bytes_accessed=6_000_000, transcendentals=0),
    )(*results)
    grad_gate_up = grad_gate_up.transpose(2, 0, 1)
    grad_output = grad_output.reshape(heads, DV, LANES)
    grad_rate = grad_rate.transpose(2, 0, 1)
    grad_mixer_gain, grad_feed_gain, grad_head_gain = (
        v.reshape(-1) for v in (grad_mixer_gain, grad_feed_gain, grad_head_gain)
    )
    grad_decay_log, grad_decay_bias = grad_decay_log.reshape(-1), grad_decay_bias.reshape(-1)
    return (
        layer_out, grad_tokens, grad_mixer_gain, grad_mixer, grad_rate, grad_conv, grad_decay_log, grad_decay_bias,
        grad_head_gain, grad_output, grad_feed_gain, grad_gate_up, grad_down,
    )


def solution(mesh):
    rows = P(("seq", "head"), None)
    return jax.shard_map(
        local,
        mesh=mesh,
        in_specs=(
            rows, P(), P(None, "head", None), P(None, None, "head"), P(None, "head", None), P("head"), P("head"),
            P(), P("head", None, None), P(), P(None, None, "head"), P("head", None), P(), rows,
        ),
        out_specs=(
            rows, rows, P(), P("seq", "head", None), P("seq", None, "head"), P(None, "head", None), P("head"),
            P("head"), P(), P("head", None, "seq"), P(), P("seq", None, "head"), P("head", "seq"),
        ),
        check_vma=False,
    )
```

```python
import functools

import jax
import jax.numpy as jnp
from jax import lax
from jax.experimental import pallas as pl
from jax.experimental.pallas import tpu as pltpu
from jax.sharding import PartitionSpec as P

D = 2048
DK = 128
DV = 256
KCONV = 4
MIXW = 768
CONVW = 512
NB = 4
BLK = 256
PAD = 8
F32 = jnp.float32
BF16 = jnp.bfloat16

VMEM = pl.BlockSpec(memory_space=pltpu.VMEM)
SMEM = pl.BlockSpec(memory_space=pltpu.SMEM)


def dot(a, b, form="nn"):
    dims = {"nn": ((1,), (0,)), "nt": ((1,), (1,)), "tn": ((0,), (0,))}[form]
    return lax.dot_general(a.astype(BF16), b.astype(BF16), (dims, ((), ())), preferred_element_type=F32)


def halves(a):
    hi = a.astype(BF16)
    return hi, (a - hi.astype(F32)).astype(BF16)


def dot3(a, b, form="nn"):
    ah, al = halves(a)
    bh, bl = halves(b)
    return dot(ah, bh, form) + (dot(ah, bl, form) + dot(al, bh, form))


def dot_exact_left(a, b, form="nn"):
    b1, rest = halves(b)
    rest = b - b1.astype(F32)
    b2 = rest.astype(BF16)
    b3 = (rest - b2.astype(F32)).astype(BF16)
    return dot(a, b1, form) + (dot(a, b2, form) + dot(a, b3, form))


def iota(shape, axis):
    return lax.broadcasted_iota(jnp.int32, shape, axis)


def doc_of(info, pos):
    count = jnp.zeros(pos.shape, jnp.int32)
    for i in range(NB):
        count = count + jnp.where(pos >= info[i], 1, 0)
    return jnp.where(pos < 0, -1, count)


def sigmoid(v):
    return 1.0 / (1.0 + jnp.exp(-v))


def softplus(v):
    return jnp.maximum(v, 0.0) + jnp.log1p(jnp.exp(-jnp.abs(v)))


def unit_lower_inverse(low):
    n = low.shape[0]
    row, col = iota((n, n), 0), iota((n, n), 1)
    eye = jnp.where(row == col, 1.0, 0.0)

    def same(b):
        return row // b == col // b

    x = jnp.where(same(8), -low, 0.0)
    inv = eye + x
    x = dot(x, x)
    inv = inv + dot(inv, x)
    x = dot(x, x)
    inv = inv + dot(inv, x)
    b = 8
    while b < n:
        off = jnp.where(same(2 * b) & jnp.logical_not(same(b)), low, 0.0)
        inv = inv - dot(inv, dot(off, inv))
        b *= 2
    return inv + dot(inv, eye - inv - dot3(low, inv))


def valid_column(info, rows, back):
    pos = info[NB] + iota((rows, 1), 0)
    return jnp.where(doc_of(info, pos) == doc_of(info, pos - back), 1.0, 0.0)


def vectors(conv):
    act = conv * sigmoid(conv)
    qa, ka, va = act[:, :DK], act[:, DK : 2 * DK], act[:, 2 * DK :]
    rq = lax.rsqrt(jnp.sum(qa * qa, axis=1, keepdims=True) + 1e-06)
    rk = lax.rsqrt(jnp.sum(ka * ka, axis=1, keepdims=True) + 1e-06)
    return qa, ka, va, rq, rk


def rates(rate_ref, dlog_ref, dbias_ref):
    heads = dlog_ref.shape[1]
    pre = rate_ref[:, :heads] + dbias_ref[...]
    log_decay = -jnp.exp(dlog_ref[...]) * softplus(pre)
    return sigmoid(rate_ref[:, heads:]), log_decay, pre


def block_masks(info, c):
    row, col = iota((BLK, BLK), 0), iota((BLK, BLK), 1)
    base = info[NB] + c * BLK
    docs_r, docs_c = doc_of(info, base + row), doc_of(info, base + col)
    keep = (docs_r == docs_c) & (col <= row)
    column = doc_of(info, base + iota((BLK, 1), 0))
    first = jnp.where(column == doc_of(info, base - 1 + iota((BLK, 1), 0) * 0), 1.0, 0.0)
    last = jnp.where(column == doc_of(info, base + BLK - 1 + iota((BLK, 1), 0) * 0), 1.0, 0.0)
    tri = jnp.where(col <= row, 1.0, 0.0)
    strict = jnp.where(col < row, 1.0, 0.0)
    return keep, first, last, tri, strict


def decays(g, first, last, tri):
    cum = dot_exact_left(tri, jnp.broadcast_to(g, (BLK, DK)))[:, :1]
    carry = first * jnp.exp(cum)
    to_end = last * jnp.exp(cum[BLK - 1 :, :] - cum)
    return carry, to_end


def mixer_forward(
    info, proj, rate, convw, dlog, dbias, out_w, gain, cot,
    conv_o, dec_o, inv_o, wu_o, qe_o, step_o, states_o, head_o, gated_o, ga_o, ta_o, halo_o, mixed_o, cot_o,
    xpad, ol, gs, scores, ab, rim, rim_got, got1, tot, got2, hs, hr, s1, r1, s2, r2, sc, rc, lc
):
    rows = proj.shape[0]
    heads = dlog.shape[1]
    blocks = rows // BLK
    me, z, y, dev = seq_place()
    seqs, head = SIDE * SIDE, lax.axis_index("head")
    before, behind = (lax.rem(me + seqs - 1, seqs), head), (lax.rem(me + 1, seqs), head)
    greet(side_peers() + [before, behind] + head_peers())
    cot_sent = gather_start(cot, cot_o, sc, rc, lc)
    for h in range(heads):
        rim[:, pl.ds(h * CONVW, CONVW)] = proj[rows - PAD :, pl.ds(h * MIXW, CONVW)].astype(BF16).astype(F32)
    ahead = cp(rim, rim_got, hs, hr, behind)
    ahead.start()
    strength, log_decay, _ = rates(rate, dlog, dbias)
    valid = [valid_column(info, rows, KCONV - 1 - j) for j in range(KCONV)]
    ahead.wait_recv()
    halo_o[...] = jnp.where(me > 0, rim_got[...], 0.0)
    for h in range(heads):
        src, dst = pl.ds(h * MIXW, CONVW), pl.ds(h * CONVW, CONVW)
        xpad[:PAD, :] = halo_o[:, dst]
        xpad[PAD:, :] = proj[:, src].astype(BF16).astype(F32)
        conv = jnp.zeros((rows, CONVW), F32)
        for j in range(KCONV):
            lo = PAD - (KCONV - 1) + j
            conv = conv + convw[j : j + 1, dst].astype(F32) * xpad[lo : lo + rows, :] * valid[j]
        conv_o[:, dst] = conv
    for c in range(blocks):
        keep, first, last, tri, strict = block_masks(info, c)
        here = pl.ds(c * BLK, BLK)
        for h in range(heads):
            qa, ka, va, rq, rk = vectors(conv_o[here, pl.ds(h * CONVW, CONVW)])
            q, k = qa * (rq * DK**-0.5), ka * rk
            beta = strength[c * BLK : (c + 1) * BLK, h : h + 1]
            g = log_decay[c * BLK : (c + 1) * BLK, h : h + 1]
            spread = dot_exact_left(tri, g * strict)
            dec = jnp.where(keep, jnp.exp(jnp.where(keep, spread, 0.0)), 0.0)
            carry, to_end = decays(g, first, last, tri)
            low = strict * (beta * dec * dot(k, k, "nt"))
            inv = unit_lower_inverse(low)
            u = h * blocks + c
            dec_o[u] = dec
            inv_o[u] = inv.astype(BF16)
            rhs = jnp.concatenate([(beta * carry) * k, beta * va], axis=1)
            wu = dot(inv, rhs)
            wu_o[u] = wu
            scores[u] = (dec * dot(q, k, "nt")).astype(BF16)
            qe_o[here, pl.ds(h * DK, DK)] = carry * q
            step = dot(wu, to_end * k, "tn")
            eye = jnp.where(iota((DK, DK), 0) == iota((DK, DK), 1), 1.0, 0.0)
            step_o[u, :DK] = carry[BLK - 1 :, :] * eye - step[:DK]
            step_o[u, DK:] = step[DK:]
        if c == 0:
            cot_sent += gather_forward(cot, cot_o, sc, rc)
    for h in range(heads):
        whole = step_o[h * blocks]
        for c in range(1, blocks):
            nxt = step_o[h * blocks + c]
            whole = add_low(dot3(whole, nxt[:DK]), nxt[DK:])
        ab[h] = whole.astype(ab.dtype)

    out, wait = share_start(ab, got1, y, lambda d: dev(0, d), s1, r1)
    for h in range(heads):
        for c in range(blocks):
            u, here = h * blocks + c, pl.ds(c * BLK, BLK)
            block = dot(scores[u], wu_o[u])
            qe_o[here, pl.ds(h * DK, DK)] = qe_o[here, pl.ds(h * DK, DK)] - block[:, :DK]
            ol[here, pl.ds(h * DV, DV)] = block[:, DK:]
    wait()
    held_before = []
    for h in range(heads):
        whole = got1[0, h].astype(F32)
        prefix = jnp.where(y > 0, whole, unit_top())
        for j in range(1, SIDE):
            a, b = got1[j, h, :DK, :], got1[j, h, DK:, :].astype(F32)
            whole = add_low(dot_left2(whole, a), b)
            if j < SIDE - 1:
                prefix = jnp.where(y > j, whole, prefix)
        tot[h] = whole.astype(BF16)
        held_before.append(prefix)
        for j in range(SIDE):
            ga_o[j, h] = got1[j, h, :DK, :]
    more, wait = share_start(tot, got2, z, lambda d: dev(d, 0), s2, r2)
    for h in range(heads):
        gate = proj[:, pl.ds(h * MIXW + CONVW, DV)]
        gs[:, pl.ds(h * DV, DV)] = gain[...] * (gate * sigmoid(gate))
    wait()
    for h in range(heads):
        held = jnp.zeros((DV, DK), F32)
        for j in range(SIDE - 1):
            held = jnp.where(
                z > j, dot_left2(held, got2[j, h, :DK, :]) + got2[j, h, DK:, :].astype(F32), held
            )
        for j in range(SIDE):
            ta_o[j, h] = got2[j, h, :DK, :]
        state = dot3(held, held_before[h][:DK]) + held_before[h][DK:]
        for c in range(blocks):
            u = h * blocks + c
            here, cols = pl.ds(c * BLK, BLK), pl.ds(h * DV, DV)
            states_o[u] = state
            block = ol[here, cols] + dot(qe_o[here, pl.ds(h * DK, DK)], state, "nt")
            head_o[here, cols] = block
            gated_o[here, cols] = (block * mean_scale(block) * gs[here, cols]).astype(BF16)
            if c + 1 < blocks:
                state = dot3(state, step_o[u, :DK, :]) + step_o[u, DK:, :]
    for j in range(0, D, CONVW):
        mixed_o[:, j : j + CONVW] = dot(gated_o[...], out_w[:, j : j + CONVW]).astype(BF16)
    gather_end(cot, cot_o, sc, rc, lc, cot_sent)
    for s in out + more + [ahead]:
        s.wait_send()


def dot_left2(a, b, form="nn"):
    ah, al = halves(a)
    return dot(ah, b, form) + dot(al, b, form)


def head_back(d_mixed, out_w, head_out, proj, gain, qe, step, d_out_o, d_gate_o, y_o, inc_o):
    rows = qe.shape[0]
    blocks = rows // BLK
    heads = qe.shape[1] // DK
    total = jnp.zeros((1, DV), F32)
    for h in range(heads):
        cols = pl.ds(h * DV, DV)
        for c in range(blocks):
            here = pl.ds(c * BLK, BLK)
            dg, out = dot(d_mixed[here, :], out_w[cols, :], "nt"), head_out[here, cols]
            gate = proj[here, pl.ds(h * MIXW + CONVW, DV)]
            s = sigmoid(gate)
            silu = gate * s
            scale = lax.rsqrt(jnp.mean(out * out, axis=1, keepdims=True) + 1e-05)
            dn = dg * (out * scale)
            d_gate_o[here, pl.ds(h * MIXW + CONVW, DV)] = (dn * gain[...] * (s * (1.0 + gate * (1.0 - s)))).astype(BF16)
            total = total + jnp.sum(dn * silu, axis=0, keepdims=True)
            f = dg * gain[...] * silu
            d_out = scale * f - out * (scale * scale * scale) * jnp.mean(f * out, axis=1, keepdims=True)
            d_out_o[here, cols] = d_out
            y_o[h * blocks + c] = dot(d_out, qe[here, pl.ds(h * DK, DK)], "tn")
        inc = y_o[h * blocks + blocks - 1]
        for c in range(blocks - 2, -1, -1):
            inc = y_o[h * blocks + c] + dot3(inc, step[h * blocks + c, :DK, :], "nt")
        inc_o[h] = inc.astype(inc_o.dtype)
    return total


def mixer_back(
    info, d_mixed, out_w, head_out, proj, gain, qe, step, ga, ta, middle, cot, gated_t, s_gu, conv, dec, inv, wu, states,
    rate, halo, convw, dlog, dbias,
    d_proj_o, d_tail_o, d_edge_o, d_rate_o, d_convw_o, d_decay_o, d_gain_o, s_down_o, s_out_o, g_gu_o,
    d_out, y, inc, later, got1, tot, got2, xpad, dpad, dsend, cols_s, d_pre_o,
    gm_s, e_s, fresh_s, ks_s, d_fresh_s, dq_s, dk_s, cols_u,
    g_down, g_out, relay_d, relay_o, got_d, got_o, last_got, s1, r1, s2, r2, s3, r3, s4, r4
):
    greet(side_peers())
    settle = Settle(lambda i, b: last_got.at[i, b], s4, r4)
    for b in (2, 1, 3):
        for i in range(2):
            settle.send(s_gu.at[i, b], i, b)
    grads = (g_out, g_down)
    spread = Spread(
        lambda i, owner: grads[i].at[owner], lambda i, b: (relay_o, relay_d)[i].at[b],
        lambda i, s, b: (got_o, got_d)[i].at[s, b], s3, r3,
    )
    def make(o, left, right):
        for j in range(0, o.shape[0], 2):
            both = dot(left[...], right[:, j * LANES : (j + 2) * LANES]).astype(BF16)
            o[j], o[j + 1] = both[:, :LANES], both[:, LANES:]

    make(g_down, middle, cot)
    for place in PLACES:
        spread.ready(*place, (1,))
    d_gain_o[...] = head_back(d_mixed, out_w, head_out, proj, gain, qe, step, d_out, d_proj_o, y, inc)

    rows = d_out.shape[0]
    heads = later.shape[0]
    blocks = rows // BLK
    strength, log_decay, pre = rates(rate, dlog, dbias)
    valid = [valid_column(info, rows, KCONV - 1 - j) for j in range(KCONV)]

    def early(c):
        keep, first, last, tri, strict = block_masks(info, c)
        here = pl.ds(c * BLK, BLK)
        for h in range(heads):
            u = h * blocks + c
            qa, ka, va, rq, rk = vectors(conv[here, pl.ds(h * CONVW, CONVW)])
            q, k = qa * (rq * DK**-0.5), ka * rk
            g = log_decay[c * BLK : (c + 1) * BLK, h : h + 1]
            carry, to_end = decays(g, first, last, tri)
            dm = dec[u]
            sc = dm * dot3(q, k, "nt")
            gm_s[u] = dm * dot3(k, k, "nt") * strict
            state = states[u]
            do = d_out[here, pl.ds(h * DV, DV)]
            ks_s[u] = dot3(k, state, "nt")
            fresh = wu[u, :, DK:] - dot3(wu[u, :, :DK], state, "nt")
            fresh_s[u] = fresh
            d_fresh_s[u] = dot(sc, do, "tn")
            d_sc = dot3(do, fresh, "nt")
            e_s[u] = d_sc * sc
            d_scd = d_sc * dm
            dq_s[u] = dot(d_scd, k) + carry * dot(do, state)
            dk_s[u] = dot(d_scd, q, "tn")
            cols_u[u, :, 0:1] = carry
            cols_u[u, :, 1:2] = to_end
            cols_u[u, :, 2:3] = jnp.sum(do * dot3(q, state, "nt"), axis=1, keepdims=True)

    def level_one():
        make(g_out, gated_t, d_mixed)
        early(0)

    def level_two():
        for place in PLACES:
            spread.ready(*place, (0,))
        for c in range(1, blocks):
            early(c)

    swaps = states_backward(inc, ga, ta, later, got1, tot, got2, s1, r1, s2, r2, level_one, level_two)
    spread.relays(None, (1,))
    for h in range(heads):
        grad = later[h]
        for c in range(blocks - 1, -1, -1):
            u = h * blocks + c
            dsend[u] = grad
            if c:
                grad = dot3(grad, step[u, :DK, :], "nt") + y[u]
    for c in range(blocks):
        tri, strict = block_masks(info, c)[3:]
        here = pl.ds(c * BLK, BLK)
        for h in range(heads):
            u = h * blocks + c
            cv = conv[here, pl.ds(h * CONVW, CONVW)]
            sg = sigmoid(cv)
            qa, ka, va, rq, rk = vectors(cv)
            rqs = rq * DK**-0.5
            k = ka * rk
            beta = strength[c * BLK : (c + 1) * BLK, h : h + 1]
            carry, to_end, hq = cols_u[u, :, 0:1], cols_u[u, :, 1:2], cols_u[u, :, 2:3]
            dm = dec[u]
            gm, fresh, ks = gm_s[u], fresh_s[u], ks_s[u]
            state, d_end = states[u], dsend[u]
            kd = to_end * k
            ah, al = halves(d_fresh_s[u] + dot(kd, d_end, "nt"))
            d_rhs = dot(inv[u], ah, "tn") + dot(inv[u], al, "tn")
            d_low = -dot3(d_rhs, fresh, "nt")
            d_val = beta * d_rhs
            ebar = d_low * gm
            d_beta = jnp.sum(d_rhs * (va - carry * ks), axis=1, keepdims=True) + jnp.sum(ebar, axis=1, keepdims=True)
            e = e_s[u] + beta * ebar
            d_gm = (beta * d_low) * (dm * strict)
            d_kd = dot(fresh, d_end)
            d_q = dq_s[u]
            d_k = (
                dk_s[u]
                - (beta * carry) * dot(d_rhs, state)
                + to_end * d_kd
                + dot(d_gm, k)
                + dot(d_gm, k, "tn")
            )
            hcol = carry * (hq - jnp.sum(beta * d_rhs * ks, axis=1, keepdims=True))
            fcol = jnp.sum(kd * d_kd, axis=1, keepdims=True)
            tail = carry[BLK - 1 :, :] * jnp.sum(
                jnp.sum(state * d_end, axis=1, keepdims=True), axis=0, keepdims=True
            )
            lane = iota((BLK, DK), 1)
            d_g = (
                jnp.sum(dot_exact_left(tri, e, "tn") * strict, axis=1, keepdims=True)
                + dot_exact_left(tri, jnp.where(lane == 0, hcol, 0.0), "tn")[:, :1]
                + dot_exact_left(strict, jnp.where(lane == 0, fcol, 0.0))[:, :1]
                + tail
            )
            cols_s[here, h : h + 1] = d_g
            cols_s[here, heads + h : heads + h + 1] = d_beta
            d_qa = rqs * d_q - qa * (rqs * rq * rq * jnp.sum(d_q * qa, axis=1, keepdims=True))
            d_ka = rk * d_k - ka * (rk * rk * rk * jnp.sum(d_k * ka, axis=1, keepdims=True))
            d_act = jnp.concatenate([d_qa, d_ka, d_val], axis=1)
            d_pre_o[here, pl.ds(h * CONVW, CONVW)] = d_act * (sg * (1.0 + cv * (1.0 - sg)))
            spread.relays(c * heads + h, (0,))
    d_g, d_beta = cols_s[:, :heads], cols_s[:, heads : 2 * heads]
    d_bias = -d_g * jnp.exp(dlog[...]) * sigmoid(pre)
    rest = jnp.zeros((rows, LANES - 2 * heads), F32)
    d_rate_o[...] = jnp.concatenate([d_bias, d_beta * strength * (1.0 - strength), rest], axis=1).astype(BF16)
    d_decay_o[...] = jnp.zeros_like(d_decay_o)
    d_decay_o[:, :heads] = jnp.sum(d_g * log_decay, axis=0, keepdims=True)
    d_decay_o[:, heads : 2 * heads] = jnp.sum(d_bias, axis=0, keepdims=True)
    for h in range(heads):
        src, dst = pl.ds(h * MIXW, CONVW), pl.ds(h * CONVW, CONVW)
        xpad[:PAD, :] = halo[:, dst]
        xpad[PAD:, :] = proj[:, src].astype(BF16).astype(F32)
        dpad[...] = jnp.zeros_like(dpad)
        d_conv = d_pre_o[:, dst]
        for j in range(KCONV):
            lo = PAD - (KCONV - 1) + j
            masked = d_conv * valid[j]
            d_convw_o[j : j + 1, dst] = jnp.sum(masked * xpad[lo : lo + rows, :], axis=0, keepdims=True)
            dpad[lo : lo + rows, :] += convw[j : j + 1, dst].astype(F32) * masked
        d_edge_o[:, dst] = dpad[:PAD, :]
        d_tail_o[:, dst] = dpad[rows - PAD :, :]
        d_proj_o[:, src] = dpad[PAD:, :].astype(BF16)
    for i in range(2):
        g_gu_o[i] = s_gu[i, 0].astype(F32) + settle.others(i)
    for i, o in ((1, s_down_o), (0, s_out_o)):
        for b in FAR:
            o[b] = spread.total(i, b).astype(BF16)
    spread.end()
    settle.end()
    for s in swaps:
        s.wait_send()


def call(kernel, outs, scratch, limit, *args, flops=2_000_000_000, nbytes=16_000_000):
    def spec(a):
        return SMEM if a.dtype == jnp.int32 else VMEM

    return pl.pallas_call(
        kernel,
        out_shape=outs,
        in_specs=[spec(a) for a in args],
        out_specs=[VMEM for _ in outs],
        scratch_shapes=scratch,
        compiler_params=pltpu.CompilerParams(vmem_limit_bytes=limit << 20),
        cost_estimate=pl.CostEstimate(flops=flops, bytes_accessed=nbytes, transcendentals=0),
    )(*args)


def sds(shape, dtype=F32):
    return jax.ShapeDtypeStruct(shape, dtype)
CHIPS = 4
LANES = 128


def cp(src, dst, send, recv, dev):
    return pltpu.make_async_remote_copy(
        src_ref=src, dst_ref=dst, send_sem=send, recv_sem=recv, device_id=dev, device_id_type=pl.DeviceIdType.MESH
    )


def greet(devices):
    barrier = pltpu.get_barrier_semaphore()
    for dev in devices:
        pl.semaphore_signal(barrier, inc=1, device_id=dev, device_id_type=pl.DeviceIdType.MESH)
    pl.semaphore_wait(barrier, len(devices))


def head_place():
    me = lax.axis_index("head")
    chip, core = me // 2, me % 2
    seq = lax.axis_index("seq")

    def dev(step, flip=False):
        c = lax.rem(chip + step, CHIPS)
        return (seq, c * 2 + (1 - core if flip else core))

    return me, chip, core, dev


def head_peers():
    dev = head_place()[3]
    return [dev(0, True)] + [dev(d) for d in range(1, CHIPS)]


def head_rows(o, rows, step, flip=False, lo=0, size=None):
    owner = head_place()[3](step, flip)[1]
    size = size or rows
    return o.at[pl.ds(pl.multiple_of(owner * rows + lo, size), size)]


def gather_start(x, o, ssem, rsem, lsem):
    rows = x.shape[0]
    dev = head_place()[3]
    pltpu.make_async_copy(x, head_rows(o, rows, 0), lsem).start()
    out = [cp(x, head_rows(o, rows, 0), ssem.at[d], rsem.at[d], dev(d)) for d in (1, 3)]
    out.append(cp(x, head_rows(o, rows, 0), ssem.at[0], rsem.at[0], dev(0, True)))
    for s in out:
        s.start()
    return out


def opposite(rows):
    return ((0, 2, 6, 1), (rows // 2, 8, 9, 3))


def gather_forward(x, o, ssem, rsem):
    rows = x.shape[0]
    dev = head_place()[3]
    partner = dev(0, True)
    out = []

    def go(src, k, to):
        s = cp(src, src, ssem.at[k], rsem.at[k], to)
        s.start()
        out.append(s)

    for lo, relay, core, step in opposite(rows):
        there = head_rows(o, rows, CHIPS - step)
        cp(x, there, ssem.at[step], rsem.at[step], dev(step)).wait_recv()
        go(head_rows(o, rows, CHIPS - step, False, lo, rows // 2), relay, dev(step))
        go(there, CHIPS + step, partner)
    for lo, relay, core, step in opposite(rows):
        there = head_rows(o, rows, 2, False, lo, rows // 2)
        cp(there, there, ssem.at[relay], rsem.at[relay], dev(step)).wait_recv()
        go(there, core, partner)
    return out


def gather_end(x, o, ssem, rsem, lsem, sent):
    rows = x.shape[0]
    dev = head_place()[3]
    partner = dev(0, True)
    pltpu.make_async_copy(x, head_rows(o, rows, 0), lsem).wait()
    cp(x, head_rows(o, rows, 0, True), ssem.at[0], rsem.at[0], partner).wait_recv()
    for lo, relay, core, step in opposite(rows):
        k = CHIPS + step
        cp(x, head_rows(o, rows, CHIPS - step, True), ssem.at[k], rsem.at[k], partner).wait_recv()
        there = head_rows(o, rows, 2, True, lo, rows // 2)
        cp(there, there, ssem.at[core], rsem.at[core], partner).wait_recv()
    for s in sent:
        s.wait_send()


def mean_scale(v):
    return lax.rsqrt(jnp.mean(v * v, axis=1, keepdims=True) + 1e-05)


def first_norm(tokens, gain, all_o, block, ssem, rsem, lsem):
    greet(head_peers())
    v = tokens[...].astype(F32)
    block[...] = (v * mean_scale(v) * gain[...]).astype(BF16)
    sent = gather_start(block, all_o, ssem, rsem, lsem)
    sent += gather_forward(block, all_o, ssem, rsem)
    gather_end(block, all_o, ssem, rsem, lsem, sent)


def norm_back(v, gain, d_norm):
    r = mean_scale(v)
    e = d_norm * gain
    d_v = r * e - v * (r * r * r * jnp.mean(e * v, axis=1, keepdims=True))
    return d_v, jnp.sum(d_norm * v * r, axis=0, keepdims=True)


def feed_forward(
    x, tokens, gain, cot, cot_all, gu, down,
    hidden_o, all_o, d_hidden_o, d_gain_o, sums_o, middle_o, feed_o,
    n2, guv, downv, d_middle, d_gu, d_two, block, ta, pa, ga, ma, tb, pb, gb, mb, g, relay, seqs_got,
    ls, sa, ra, sb, rb, s1, r1, l1, s2, r2, l2, s3, r3
):
    load_d = pltpu.make_async_copy(down, downv, ls.at[0])
    load_d.start()
    load_g = pltpu.make_async_copy(gu, guv, ls.at[1])
    load_g.start()
    greet(head_peers() + side_peers())
    one = pair_sends(x, pa, sa, ra, FAR)
    two = ChipSum(x, one, ta, pa, ga, ma, sa, ra)
    load_d.wait()
    d_middle[...] = dot(downv[...], cot_all[...], "nt")
    two.relay()
    hidden = tokens[...].astype(F32) + two.result()
    hidden_o[...] = hidden
    block[...] = (hidden * mean_scale(hidden) * gain[...]).astype(BF16)
    ahead = gather_start(block, n2, s1, r1, l1)
    load_g.wait()
    ahead += gather_forward(block, n2, s1, r1)
    gather_end(block, n2, s1, r1, l1, ahead)
    hid = downv.shape[0]
    low = hid // 32 * 16
    for lo, hi in ((0, low), (low, hid)):
        gate = dot(guv[lo:hi, :], n2[...], "nt")
        up = dot(guv[hid + lo : hid + hi, :], n2[...], "nt")
        s = sigmoid(gate)
        silu = gate * s
        dm = d_middle[lo:hi, :]
        middle_o[lo:hi, :] = (silu * up).astype(BF16)
        d_gu[lo:hi, :] = (dm * up * (s * (1.0 + gate * (1.0 - s)))).astype(BF16)
        d_gu[hid + lo : hid + hi, :] = (dm * silu).astype(BF16)
    for j in range(0, D, 512):
        d_two[:, j : j + 512] = dot(d_gu[...], guv[:, j : j + 512], "tn").astype(BF16)
    one_b = pair_sends(d_two, pb, sb, rb, FAR)
    spread = Spread(
        lambda i, owner: g.at[owner, i], lambda i, b: relay.at[i, b], lambda i, s, b: seqs_got.at[i, s, b], s3, r3
    )
    dev = seq_place()[3]

    def make(place):
        owner = dev(*place)[0]
        cols = n2[:, pl.ds(pl.multiple_of(owner * LANES, LANES), LANES)]
        out = dot(d_gu[...], cols).astype(BF16)
        g[owner, 0] = out[:hid]
        g[owner, 1] = out[hid:]
        spread.ready(*place)

    for place in PLACES[:3]:
        make(place)
    two_b = ChipSum(d_two, one_b, tb, pb, gb, mb, sb, rb)
    for place in PLACES[3:9]:
        make(place)
    two_b.relay()
    for place in PLACES[9:]:
        make(place)
    d_norm, d_gain = norm_back(hidden_o[...], gain[...], two_b.result())
    d_hidden = cot[...].astype(F32) + d_norm
    d_hidden_o[...] = d_hidden
    d_gain_o[...] = d_gain
    block[...] = d_hidden.astype(BF16)
    ahead = gather_start(block, all_o, s2, r2, l2)
    spread.relays()
    for j in range(0, D, 512):
        feed_o[:, j : j + 512] = dot(middle_o[...], downv[:, j : j + 512], "tn").astype(BF16)
    ahead += gather_forward(block, all_o, s2, r2)
    for b in FAR:
        for i in range(2):
            sums_o[i, b] = spread.total(i, b).astype(BF16)
    gather_end(block, all_o, s2, r2, l2, ahead)
    spread.end()
    two.end()
    two_b.end()


def reach(kernel, outs, scratch, cid, limit, *args, anywhere=(), scalars=(), nbytes=12_000_000):
    return pl.pallas_call(
        kernel,
        out_shape=outs,
        in_specs=[
            pl.BlockSpec(memory_space=pl.ANY) if i in anywhere else SMEM if i in scalars else VMEM for i in range(len(args))
        ],
        out_specs=[VMEM for _ in outs],
        scratch_shapes=scratch,
        compiler_params=pltpu.CompilerParams(
            collective_id=cid, has_side_effects=True, vmem_limit_bytes=limit << 20
        ),
        cost_estimate=pl.CostEstimate(flops=0, bytes_accessed=nbytes, transcendentals=0),
    )(*args)


def sems(n):
    return pltpu.SemaphoreType.DMA((n,))


def gather_scratch():
    return [sems(10), sems(10), pltpu.SemaphoreType.DMA]


SIDE = 4


def seq_place():
    me = lax.axis_index("seq")
    z, y = me // SIDE, me % SIDE
    head = lax.axis_index("head")

    def dev(dz, dy):
        return (lax.rem(z + dz, SIDE) * SIDE + lax.rem(y + dy, SIDE), head)

    return me, z, y, dev


def side_peers():
    dev = seq_place()[3]
    return [dev(0, d) for d in range(1, SIDE)] + [dev(d, 0) for d in range(1, SIDE)]


FAR = (2, 1, 3, 0)
FIRST, OTHER = (2, 1), (3, 0)
PLACES = (
    (2, 2), (2, 1), (1, 2), (2, 3), (3, 2), (2, 0), (0, 2), (1, 3), (3, 1), (1, 0), (0, 1), (3, 3), (1, 1), (0, 3), (3, 0),
    (0, 0),
)


class Spread:
    def __init__(self, piece, relay, got, ssem, rsem):
        self.piece, self.relay, self.got, self.ssem, self.rsem = piece, relay, got, ssem, rsem
        self.dev = seq_place()[3]
        self.sent = []

    def way(self, i, a, b):
        return self.dev(b, a) if i == 0 else self.dev(a, b)

    def copy(self, i, a, b, owner):
        k = (i * SIDE + a) * SIDE + b
        if a == 2:
            dst, step = self.relay(i, b), 1 if b in FIRST else 3
        else:
            dst, step = self.got(i, 0 if a == 1 else 1, b), a
        return cp(self.piece(i, owner), dst, self.ssem.at[k], self.rsem.at[k], self.way(i, step, 0))

    def send(self, i, a, b, owner):
        s = self.copy(i, a, b, owner)
        s.start()
        self.sent.append(s)

    def late(self, a, b):
        return a == 1 and b in FIRST or a == 3 and b in OTHER

    def ready(self, dz, dy, halves_=(0, 1)):
        owner = self.dev(dz, dy)[0]
        for i in halves_:
            a, b = (dy, dz) if i == 0 else (dz, dy)
            if a and not self.late(a, b):
                self.send(i, a, b, owner)

    def relays(self, part=None, halves_=(0, 1)):
        for n, b in enumerate(FAR):
            if part is not None and n != part:
                continue
            for i in halves_:
                a = 1 if b in FIRST else 3
                owner = self.way(i, a, b)[0]
                self.copy(i, 2, b, owner).wait_recv()
                both = self.piece(i, owner)[...].astype(F32) + self.relay(i, b)[...].astype(F32)
                self.relay(i, b)[...] = both.astype(BF16)
                k = (i * SIDE + a) * SIDE + b
                s = cp(
                    self.relay(i, b), self.got(i, 0 if a == 1 else 1, b), self.ssem.at[k], self.rsem.at[k],
                    self.way(i, a, 0),
                )
                s.start()
                self.sent.append(s)

    def total(self, i, b):
        owner = self.way(i, 0, b)[0]
        for a in (1, 3):
            self.copy(i, a, b, owner).wait_recv()
        return self.piece(i, owner)[...].astype(F32) + (
            self.got(i, 0, b)[...].astype(F32) + self.got(i, 1, b)[...].astype(F32)
        )

    def end(self):
        for s in self.sent:
            s.wait_send()


class Settle:
    def __init__(self, got, ssem, rsem):
        self.got, self.ssem, self.rsem = got, ssem, rsem
        self.dev = seq_place()[3]
        self.sent = {}

    def send(self, src, i, b):
        k = i * SIDE + b
        dev = self.dev(b, 0) if i == 0 else self.dev(0, b)
        self.sent[i, b] = cp(src, self.got(i, b), self.ssem.at[k], self.rsem.at[k], dev)
        self.sent[i, b].start()

    def others(self, i):
        for b in (1, 3, 2):
            self.sent[i, b].wait_recv()
        return (self.got(i, 1)[...].astype(F32) + self.got(i, 3)[...].astype(F32)) + self.got(i, 2)[...].astype(F32)

    def end(self):
        for s in self.sent.values():
            s.wait_send()


def share_start(src, got, place, to, ssem, rsem, size=SIDE, own=None):
    part = (lambda d: src) if own is None else (lambda d: src.at[lax.rem(place + d, size)])
    got[place] = src[...] if own is None else src[place]
    steps = (2, 1, 3) if size == SIDE else range(1, size)
    out = [cp(part(d), got.at[place], ssem.at[d], rsem.at[d], to(d)) for d in steps]
    for s in out:
        s.start()

    def wait():
        for d in steps:
            back = lax.rem(place + size - d, size)
            cp(part(d), got.at[back], ssem.at[d], rsem.at[d], to(d)).wait_recv()

    return out, wait


def in_order(got):
    total = got[0]
    for i in range(1, got.shape[0]):
        total = total + got[i]
    return total


def share(src, got, place, to, ssem, rsem):
    out, wait = share_start(src, got, place, to, ssem, rsem)
    wait()
    return out


def unit_top():
    return jnp.where(iota((DK + DV, DK), 0) == iota((DK + DV, DK), 1), 1.0, 0.0)


def add_low(pair, low):
    return jnp.concatenate([pair[:DK], pair[DK:] + low], axis=0)


def states_backward(inc, ga, ta, later_o, got1, tot, got2, s1, r1, s2, r2, level_one, level_two):
    me, z, y, dev = seq_place()
    heads = inc.shape[0]
    out, wait = share_start(inc, got1, y, lambda d: dev(0, d), s1, r1)
    level_one()
    wait()
    after = []
    for h in range(heads):
        whole = add_low(dot(unit_top(), ga[SIDE - 1, h], "nt"), got1[SIDE - 1, h].astype(F32))
        suffix = jnp.where(y < SIDE - 1, whole, unit_top())
        for j in range(SIDE - 2, -1, -1):
            whole = add_low(dot_left2(whole, ga[j, h], "nt"), got1[j, h].astype(F32))
            if j:
                suffix = jnp.where(y < j, whole, suffix)
        tot[h] = whole[DK:].astype(BF16)
        after.append(suffix)
    more, wait = share_start(tot, got2, z, lambda d: dev(d, 0), s2, r2)
    level_two()
    wait()
    for h in range(heads):
        held = jnp.zeros((DV, DK), F32)
        for j in range(SIDE - 1, 0, -1):
            held = jnp.where(z < j, dot_left2(held, ta[j, h], "nt") + got2[j, h].astype(F32), held)
        later_o[h] = dot3(held, after[h][:DK]) + after[h][DK:]
    return out + more


def pair_sends(x, pair, ssem, rsem, steps):
    rows = pair.shape[1]
    dev = head_place()[3]
    out = {}
    for d in steps:
        owner = dev(d, True)[1]
        src = x.at[pl.ds(pl.multiple_of(owner * rows, rows), rows)]
        out[d] = cp(src, pair.at[d], ssem.at[d], rsem.at[d], dev(0, True))
        out[d].start()
    return out


class ChipSum:
    def __init__(self, x, first, total, pair, got, mid, ssem, rsem):
        self.x, self.first, self.total, self.pair = x, first, total, pair
        self.got, self.mid, self.ssem, self.rsem = got, mid, ssem, rsem
        self.rows = pair.shape[1]
        self.dev = head_place()[3]
        half = self.rows // 2
        self.top, self.low = slice(0, half), slice(half, self.rows)
        self.sent = []
        self.mid[2] = self.both(2).astype(BF16)
        self.send(2, self.top, 0, 4, 1)
        self.send(2, self.low, 0, 5, 3)
        self.right = self.both(1)
        self.mid[1, self.low] = self.right[self.low].astype(BF16)
        self.send(1, self.low, 1, 6, 1)
        self.left = self.both(3)
        self.mid[3, self.top] = self.left[self.top].astype(BF16)
        self.send(3, self.top, 3, 7, 3)
        self.total[...] = self.both(0)

    def both(self, d):
        self.first[d].wait_recv()
        owner = self.dev(d)[1]
        mine = self.x[pl.ds(pl.multiple_of(owner * self.rows, self.rows), self.rows), :]
        return mine.astype(F32) + self.pair[d].astype(F32)

    def copy(self, d, part, slot, k, step):
        at = pl.ds(part.start, part.stop - part.start)
        return cp(self.mid.at[d, at], self.got.at[slot, at], self.ssem.at[k], self.rsem.at[k], self.dev(step))

    def send(self, *what):
        s = self.copy(*what)
        s.start()
        self.sent.append(s)

    def relay(self):
        self.copy(2, self.top, 0, 4, 1).wait_recv()
        self.mid[1, self.top] = (self.right[self.top] + self.got[0, self.top].astype(F32)).astype(BF16)
        self.send(1, self.top, 1, 8, 1)
        self.copy(2, self.low, 0, 5, 3).wait_recv()
        self.mid[3, self.low] = (self.left[self.low] + self.got[0, self.low].astype(F32)).astype(BF16)
        self.send(3, self.low, 3, 9, 3)

    def result(self):
        self.copy(1, self.low, 1, 6, 1).wait_recv()
        self.copy(3, self.top, 3, 7, 3).wait_recv()
        self.copy(1, self.top, 1, 8, 1).wait_recv()
        self.copy(3, self.low, 3, 9, 3).wait_recv()
        return self.total[...] + (self.got[1].astype(F32) + self.got[3].astype(F32))

    def end(self):
        for s in self.sent + list(self.first.values()):
            s.wait_send()


def finish(
    dproj, normed, w, d_rate, rate_w, d_tail, d_edge, feed, hidden, tokens, d_hidden, gain, convs, decay, g_feed, g_head,
    s_down, s_out,
    layer_o, d_tokens_o, g_mixer_o, g_gain_o, g_feed_o, g_head_o, conv_o, dlog_o, dbias_o, rate_o, g_down_o, g_out_o,
    dp, wv, edge, g, relay, got1, mid, got2, dn, ta, pa, ga, ma, tb, pb, gb, mb, got_d, got_o,
    e0, eh, e1, ey, e2, ez, m0, mh, m1, my, m2, mz,
    es, er, ls, s1, r1, s2, r2, sa, ra, sb, rb, s5, r5, se, re, sm, rm
):
    me, z, y, dev = seq_place()
    head = lax.axis_index("head")
    heads, seqs = eh.shape[0], g.shape[1]
    rows = dp.shape[0]
    part, half = g_mixer_o.shape[1], g_mixer_o.shape[2]
    load_p = pltpu.make_async_copy(dproj, dp, ls.at[0])
    load_p.start()
    load_w = pltpu.make_async_copy(w, wv, ls.at[1])
    load_w.start()

    def across(d):
        return (me, lax.rem(head + d, heads))

    before, behind = (lax.rem(me + seqs - 1, seqs), head), (lax.rem(me + 1, seqs), head)
    greet([across(d) for d in range(1, heads)] + side_peers() + [before, behind])
    back = cp(d_edge, edge, es, er, before)
    back.start()
    feed_one = pair_sends(feed, pa, sa, ra, FAR)

    n_row, h_row = D // LANES, DV // LANES
    taps, wide_c = convs.shape
    c_row = wide_c // LANES
    ng, nc = e0.shape[0], taps * c_row + PAD
    for r in range(n_row):
        e0[r : r + 1, :] = g_feed[:, r * LANES : (r + 1) * LANES]
    e0[n_row:, :] = jnp.zeros((ng - n_row, LANES), F32)
    for r in range(h_row):
        e0[n_row + r : n_row + r + 1, :] = g_head[:, r * LANES : (r + 1) * LANES]
    small, wait_head = share_start(e0, eh, head, across, se.at[0], re.at[0], heads)
    for t in range(taps):
        for r in range(c_row):
            lo = ng + t * c_row + r
            e1[0, lo : lo + 1, :] = convs[t : t + 1, r * LANES : (r + 1) * LANES]
    e1[0, ng + nc - PAD : ng + nc, :] = jnp.zeros((PAD, LANES), F32)
    e1[0, ng + nc - PAD : ng + nc - PAD + 1, :] = decay[...]
    rates_t = dot(d_rate[:, :PAD], normed[...], "tn")
    for i in range(SIDE):
        if i:
            e1[i, ng : ng + nc, :] = e1[0, ng : ng + nc, :]
        for j in range(SIDE):
            at = (j * SIDE + i) * LANES
            e1[i, ng + nc + j * PAD : ng + nc + (j + 1) * PAD, :] = rates_t[:, at : at + LANES]

    sums = (s_out, s_down)
    settle = Settle(lambda i, b: (got_o, got_d)[i].at[b], s5, r5)
    for b in (2, 1, 3):
        for i in range(2):
            settle.send(sums[i].at[b], i, b)
    load_p.wait()
    back.wait_recv()
    there = jnp.where(me < seqs - 1, edge[...], 0.0)
    tail = jnp.concatenate([d_tail[:PAD, :], d_tail[PAD:, :] + there], axis=0).astype(BF16)
    wide = half - DV
    for i in range(2):
        dp[rows - 2 * PAD :, pl.ds(i * half, wide)] = tail[:, i * wide : (i + 1) * wide]

    spread = Spread(
        lambda i, owner: g.at[i, owner], lambda i, b: relay.at[i, b], lambda i, s, b: got1.at[i, s, b], s1, r1
    )
    settle_two = Settle(lambda i, b: got2.at[i, b], s2, r2)
    for n, place in enumerate(PLACES):
        owner = dev(*place)[0]
        left = normed[:, pl.ds(pl.multiple_of(owner * part, part), part)]
        both = dot(left, dp[...], "tn").astype(BF16)
        for i in range(2):
            g[i, owner] = both[:, i * half : (i + 1) * half]
        spread.ready(*place)
        if n == 2:
            wait_head()
            gains = in_order(eh)
            for i in range(SIDE):
                e1[i, :ng, :] = gains
            more, wait_y = share_start(e1, ey, y, lambda d: dev(0, d), se.at[1], re.at[1], SIDE, True)
            small += more
        if n == 9:
            wait_y()
            total = in_order(ey)
            for j in range(SIDE):
                e2[j, : ng + nc, :] = total[: ng + nc]
                e2[j, ng + nc :, :] = total[ng + nc + j * PAD : ng + nc + (j + 1) * PAD]
            more, wait_z = share_start(e2, ez, z, lambda d: dev(d, 0), se.at[2], re.at[2], SIDE, True)
            small += more
    feed_two = ChipSum(feed, feed_one, ta, pa, ga, ma, sa, ra)

    load_w.wait()
    low = rows // CHIPS
    hp = head_place()[3]
    dn_one = {}
    for d in FAR:
        chip = hp(d)[1] // 2
        here = pl.ds(pl.multiple_of(chip * low, low), low)
        dn[here, :] = (dot(dp[here, :], wv[...], "nt") + dot(d_rate[here, :], rate_w[...], "nt")).astype(BF16)
        dn_one.update(pair_sends(dn, pb, sb, rb, (d,)))
        spread.relays(FAR.index(d))
    feed_two.relay()
    dn_two = ChipSum(dn, dn_one, tb, pb, gb, mb, sb, rb)
    wait_z()
    total = in_order(ez)
    for r in range(n_row):
        g_feed_o[:, r * LANES : (r + 1) * LANES] = total[r : r + 1]
    for r in range(h_row):
        g_head_o[:, r * LANES : (r + 1) * LANES] = total[n_row + r : n_row + r + 1]
    own = conv_o.shape[1]
    for t in range(taps):
        for h in range(own):
            for r in range(c_row // own):
                lo = ng + t * c_row + h * (c_row // own) + r
                conv_o[t, h : h + 1, r * LANES : (r + 1) * LANES] = total[lo : lo + 1]
    dlog_o[...] = total[ng + nc - PAD : ng + nc - PAD + 1, :own]
    dbias_o[...] = total[ng + nc - PAD : ng + nc - PAD + 1, own : 2 * own]
    for i in range(2):
        rate_o[i] = total[ng + nc + i * own : ng + nc + (i + 1) * own]
    dn_two.relay()
    layer_o[...] = (hidden[...] + feed_two.result()).astype(BF16)
    d_norm, d_gain = norm_back(tokens[...].astype(F32), gain[...], dn_two.result())
    d_tokens_o[...] = d_hidden[...] + d_norm

    for r in range(n_row):
        m0[r : r + 1, :] = d_gain[:, r * LANES : (r + 1) * LANES]
    more, wait_head = share_start(m0, mh, head, across, sm.at[0], rm.at[0], heads)
    small += more

    def settle_mixer(b):
        for i in range(2):
            both = spread.total(i, b)
            if b:
                mid[i, b] = both.astype(BF16)
                settle_two.send(mid.at[i, b], i, b)
            else:
                g_mixer_o[i] = both

    settle_mixer(2)
    wait_head()
    m1[...] = in_order(mh)
    more, wait_y = share_start(m1, my, y, lambda d: dev(0, d), sm.at[1], rm.at[1])
    small += more
    settle_mixer(1)
    settle_mixer(3)
    wait_y()
    m2[...] = in_order(my)
    more, wait_z = share_start(m2, mz, z, lambda d: dev(d, 0), sm.at[2], rm.at[2])
    small += more
    settle_mixer(0)
    for i, o in ((1, g_down_o), (0, g_out_o)):
        o[...] = sums[i][0].astype(F32) + settle.others(i)
    wait_z()
    total = in_order(mz)
    for r in range(n_row):
        g_gain_o[:, r * LANES : (r + 1) * LANES] = total[r : r + 1]
    for i in range(2):
        g_mixer_o[i] = g_mixer_o[i] + settle_two.others(i)
    spread.end()
    settle.end()
    settle_two.end()
    feed_two.end()
    dn_two.end()
    for s in small + [back]:
        s.wait_send()


def hand_over(*refs):
    n = (len(refs) - 2) // 2
    srcs, dsts, (held, done) = refs[:n], refs[n : 2 * n], refs[2 * n :]
    copies = [
        pltpu.make_async_copy(srcs[i], dsts[i] if i < n - 1 else held, done.at[i]) for i in range(n - 1, -1, -1)
    ]
    for s in copies:
        s.start()
    copies[0].wait()
    for i in range(held.shape[0]):
        dsts[-1][:, i, :] = held[i]
    for s in copies[1:]:
        s.wait()


def local(
    tokens, mixer_gain, mixer_weight, rate_weight, conv_weight, decay_log, decay_bias, head_gain,
    output_weight, feed_gain, gate_up_weight, down_weight, doc_starts, cotangent,
):
    own = tokens.shape[0]
    (gathered,) = reach(
        first_norm,
        [sds((own * lax.axis_size("head"), D), BF16)],
        [pltpu.VMEM((own, D), BF16)] + gather_scratch(),
        3, 32, tokens, mixer_gain.reshape(1, D),
    )
    heads = mixer_weight.shape[1]
    mixer_flat = mixer_weight.reshape(D, heads * MIXW)
    rows = gathered.shape[0]
    blocks = rows // BLK
    units = heads * blocks
    seq = lax.axis_size("seq")
    projected = jnp.dot(gathered, mixer_flat, preferred_element_type=F32)
    rate_proj = jnp.einsum("td,dgh->tgh", gathered, rate_weight, preferred_element_type=F32).reshape(rows, 2 * heads)
    convw = conv_weight.reshape(KCONV, heads * CONVW)
    info = jnp.concatenate(
        [doc_starts, jnp.stack([lax.axis_index("seq") * rows, lax.axis_index("seq")]).astype(jnp.int32)]
    )
    dlog, dbias = decay_log.reshape(1, heads), decay_bias.reshape(1, heads)
    gain = head_gain.reshape(1, DV)

    out_flat = output_weight.reshape(heads * DV, D)
    pairs = pltpu.VMEM((SIDE, heads, DK + DV, DK), BF16)
    conv, dec, inv, wu, qe, step, states, head_out, gated, ga, ta, halo, mixed, cot_rows = reach(
        mixer_forward,
        [
            sds((rows, heads * CONVW)), sds((units, BLK, BLK)), sds((units, BLK, BLK), BF16),
            sds((units, BLK, DK + DV)), sds((rows, heads * DK)), sds((units, DK + DV, DK)), sds((units, DV, DK)),
            sds((rows, heads * DV)), sds((rows, heads * DV), BF16), sds((SIDE, heads, DK, DK), BF16),
            sds((SIDE, heads, DK, DK), BF16), sds((PAD, heads * CONVW)), sds((rows, D), BF16), sds((rows, D), BF16),
        ],
        [
            pltpu.VMEM((PAD + rows, CONVW), F32), pltpu.VMEM((rows, heads * DV), F32),
            pltpu.VMEM((rows, heads * DV), F32), pltpu.VMEM((units, BLK, BLK), BF16),
            pltpu.VMEM((heads, DK + DV, DK), BF16), pltpu.VMEM((PAD, heads * CONVW), F32),
            pltpu.VMEM((PAD, heads * CONVW), F32), pairs, pltpu.VMEM((heads, DK + DV, DK), BF16), pairs,
            pltpu.SemaphoreType.DMA, pltpu.SemaphoreType.DMA, sems(SIDE), sems(SIDE), sems(SIDE), sems(SIDE),
        ]
        + gather_scratch(),
        1, 56, info, projected, rate_proj, convw, dlog, dbias, out_flat, gain, cotangent, scalars=(0,), nbytes=30_000_000,
    )
    hid = down_weight.shape[0]
    part, half, n_head = D // seq, MIXW, lax.axis_size("head")
    gu_t = gate_up_weight.transpose(1, 2, 0).reshape(2 * hid, D)

    def sums_of_head():
        return [pltpu.VMEM((own, D), F32)] + [pltpu.VMEM((CHIPS, own, D), BF16) for _ in range(3)]

    hidden, d_mixed, d_hidden, g_feed_gain, grads, middle, feed = reach(
        feed_forward,
        [
            sds((own, D)), sds((rows, D), BF16), sds((own, D)), sds((1, D)), sds((2, SIDE, hid, LANES), BF16),
            sds((hid, rows), BF16), sds((rows, D), BF16),
        ],
        [
            pltpu.VMEM((rows, D), BF16), pltpu.VMEM((2 * hid, D), BF16), pltpu.VMEM((hid, D), BF16),
            pltpu.VMEM((hid, rows), F32), pltpu.VMEM((2 * hid, rows), BF16), pltpu.VMEM((rows, D), BF16),
            pltpu.VMEM((own, D), BF16),
        ]
        + sums_of_head()
        + sums_of_head()
        + [
            pltpu.VMEM((seq, 2, hid, LANES), BF16), pltpu.VMEM((2, SIDE, hid, LANES), BF16),
            pltpu.VMEM((2, 2, SIDE, hid, LANES), BF16), sems(2), sems(10), sems(10), sems(10), sems(10),
        ]
        + gather_scratch()
        + gather_scratch()
        + [sems(2 * SIDE * SIDE), sems(2 * SIDE * SIDE)],
        2, 63, mixed, tokens, feed_gain.reshape(1, D), cotangent, cot_rows, gu_t, down_weight,
        anywhere=(5, 6), nbytes=40_000_000,
    )
    gated_t = gated.T
    d_projected, d_tail, d_edge, d_rate, d_convw, d_decay, g_head_gain, s_down, s_out, grad_gate_up = reach(
        mixer_back,
        [
            sds((rows, heads * MIXW), BF16), sds((2 * PAD, heads * CONVW)), sds((PAD, heads * CONVW)),
            sds((rows, LANES), BF16), sds((KCONV, heads * CONVW)), sds((1, LANES)), sds((1, DV)),
            sds((SIDE, hid, LANES), BF16), sds((SIDE, heads * DV, LANES), BF16), sds((2, hid, LANES)),
        ],
        [
            pltpu.VMEM((rows, heads * DV), F32), pltpu.VMEM((units, DV, DK), F32),
            pltpu.VMEM((heads, DV, DK), BF16), pltpu.VMEM((heads, DV, DK), F32),
            pltpu.VMEM((SIDE, heads, DV, DK), BF16), pltpu.VMEM((heads, DV, DK), BF16),
            pltpu.VMEM((SIDE, heads, DV, DK), BF16),
            pltpu.VMEM((PAD + rows, CONVW), F32), pltpu.VMEM((PAD + rows, CONVW), F32),
            pltpu.VMEM((units, DV, DK), F32), pltpu.VMEM((rows, DK), F32), pltpu.VMEM((rows, heads * CONVW), F32),
            pltpu.VMEM((units, BLK, BLK), F32), pltpu.VMEM((units, BLK, BLK), F32), pltpu.VMEM((units, BLK, DV), F32),
            pltpu.VMEM((units, BLK, DV), F32), pltpu.VMEM((units, BLK, DV), F32), pltpu.VMEM((units, BLK, DK), F32),
            pltpu.VMEM((units, BLK, DK), F32), pltpu.VMEM((units, BLK, LANES), F32),
            pltpu.VMEM((seq, hid, LANES), BF16), pltpu.VMEM((seq, heads * DV, LANES), BF16),
            pltpu.VMEM((SIDE, hid, LANES), BF16), pltpu.VMEM((SIDE, heads * DV, LANES), BF16),
            pltpu.VMEM((2, SIDE, hid, LANES), BF16), pltpu.VMEM((2, SIDE, heads * DV, LANES), BF16),
            pltpu.VMEM((2, SIDE, hid, LANES), BF16),
            sems(SIDE), sems(SIDE), sems(SIDE), sems(SIDE), sems(2 * SIDE * SIDE), sems(2 * SIDE * SIDE),
            sems(2 * SIDE), sems(2 * SIDE),
        ],
        4, 63, info, d_mixed, out_flat, head_out, projected, gain, qe, step, ga, ta, middle, cot_rows, gated_t, grads,
        conv, dec, inv, wu, states, rate_proj, halo, convw, dlog, dbias, scalars=(0,), nbytes=40_000_000,
    )
    rate_pad = jnp.pad(rate_weight.reshape(D, 2 * heads), ((0, 0), (0, LANES - 2 * heads)))
    n_gain, n_conv, n_last = D // LANES + PAD, KCONV * heads * CONVW // LANES + PAD, D // LANES
    n_y, n_z = n_gain + n_conv + SIDE * PAD, n_gain + n_conv + PAD

    def rows_of(*shape):
        return pltpu.VMEM(shape + (LANES,), F32)

    (
        layer_out, grad_tokens, grad_mixer, grad_mixer_gain, grad_feed_gain, grad_head_gain, grad_conv, grad_decay_log,
        grad_decay_bias, grad_rate, grad_down, grad_output,
    ) = reach(
        finish,
        [
            sds((own, D), BF16), sds((own, D)), sds((2, part, half)), sds((1, D)), sds((1, D)), sds((1, DV)),
            sds((KCONV, heads, CONVW)), sds((1, heads)), sds((1, heads)), sds((2, heads, LANES)), sds((hid, LANES)),
            sds((heads * DV, LANES)),
        ],
        [
            pltpu.VMEM((rows, heads * MIXW), BF16), pltpu.VMEM((D, heads * MIXW), BF16),
            pltpu.VMEM((PAD, heads * CONVW), F32), pltpu.VMEM((2, seq, part, half), BF16),
            pltpu.VMEM((2, SIDE, part, half), BF16), pltpu.VMEM((2, 2, SIDE, part, half), BF16),
            pltpu.VMEM((2, SIDE, part, half), BF16), pltpu.VMEM((2, SIDE, part, half), BF16), pltpu.VMEM((rows, D), BF16),
        ]
        + sums_of_head()
        + sums_of_head()
        + [
            pltpu.VMEM((SIDE, hid, LANES), BF16), pltpu.VMEM((SIDE, heads * DV, LANES), BF16),
            rows_of(n_gain), rows_of(n_head, n_gain), rows_of(SIDE, n_y), rows_of(SIDE, n_y), rows_of(SIDE, n_z),
            rows_of(SIDE, n_z), rows_of(n_last), rows_of(n_head, n_last), rows_of(n_last), rows_of(SIDE, n_last),
            rows_of(n_last), rows_of(SIDE, n_last),
            pltpu.SemaphoreType.DMA, pltpu.SemaphoreType.DMA, sems(2),
            sems(2 * SIDE * SIDE), sems(2 * SIDE * SIDE), sems(2 * SIDE), sems(2 * SIDE),
            sems(10), sems(10), sems(10), sems(10), sems(2 * SIDE), sems(2 * SIDE),
            pltpu.SemaphoreType.DMA((3, n_head)), pltpu.SemaphoreType.DMA((3, n_head)),
            pltpu.SemaphoreType.DMA((3, n_head)), pltpu.SemaphoreType.DMA((3, n_head)),
        ],
        5, 62, d_projected, gathered, mixer_flat, d_rate, rate_pad, d_tail, d_edge, feed, hidden, tokens,
        d_hidden, mixer_gain.reshape(1, D), d_convw, d_decay, g_feed_gain, g_head_gain, s_down, s_out,
        anywhere=(0, 2), nbytes=40_000_000,
    )
    results = [
        layer_out, grad_tokens, grad_mixer_gain, grad_feed_gain, grad_head_gain, grad_conv, grad_decay_log,
        grad_decay_bias, grad_rate, grad_down, grad_output, grad_gate_up, grad_mixer,
    ]
    (
        layer_out, grad_tokens, grad_mixer_gain, grad_feed_gain, grad_head_gain, grad_conv, grad_decay_log,
        grad_decay_bias, grad_rate, grad_down, grad_output, grad_gate_up, grad_mixer,
    ) = pl.pallas_call(
        hand_over,
        out_shape=[sds(v.shape, v.dtype) for v in results[:-1]] + [sds((part, heads, half))],
        in_specs=[pl.BlockSpec(memory_space=pl.ANY) for _ in results],
        out_specs=[VMEM for _ in results],
        scratch_shapes=[pltpu.VMEM((heads, part, half), F32), sems(len(results))],
        compiler_params=pltpu.CompilerParams(vmem_limit_bytes=60 << 20),
        cost_estimate=pl.CostEstimate(flops=0, bytes_accessed=6_000_000, transcendentals=0),
    )(*results)
    grad_gate_up = grad_gate_up.transpose(2, 0, 1)
    grad_output = grad_output.reshape(heads, DV, LANES)
    grad_rate = grad_rate.transpose(2, 0, 1)
    grad_mixer_gain, grad_feed_gain, grad_head_gain = (
        v.reshape(-1) for v in (grad_mixer_gain, grad_feed_gain, grad_head_gain)
    )
    grad_decay_log, grad_decay_bias = grad_decay_log.reshape(-1), grad_decay_bias.reshape(-1)
    return (
        layer_out, grad_tokens, grad_mixer_gain, grad_mixer, grad_rate, grad_conv, grad_decay_log, grad_decay_bias,
        grad_head_gain, grad_output, grad_feed_gain, grad_gate_up, grad_down,
    )


def solution(mesh):
    rows = P(("seq", "head"), None)
    return jax.shard_map(
        local,
        mesh=mesh,
        in_specs=(
            rows, P(), P(None, "head", None), P(None, None, "head"), P(None, "head", None), P("head"), P("head"),
            P(), P("head", None, None), P(), P(None, None, "head"), P("head", None), P(), rows,
        ),
        out_specs=(
            rows, rows, P(), P("seq", "head", None), P("seq", None, "head"), P(None, "head", None), P("head"),
            P("head"), P(), P("head", None, "seq"), P(), P("seq", None, "head"), P("head", "seq"),
        ),
        check_vma=False,
    )
```
